32 devices in a mesh: dp: 4 (over z), ctx: 4 (over y, core), tp: 2 (over x).
Axes of the slice: x: 2, y: 2, z: 4, core: 2. Of those that a mesh axis runs over, the one named last changes fastest.
Arguments:
- hidden_in: bfloat16 [12, 1024, 768], P('dp', 'ctx'), may hold values from -6 to 6
- doc_lengths: int32 [12, 18], P('dp'), may hold values from 0 to 800, as said below
- sticky_places: int32 [12, 256], P('dp'), may hold values from 0 to 1023
- attn_gain: float32 [768], replicated, may hold values from 0.5 to 1.5
- attn_shift: float32 [768], replicated, may hold values from -1.25 to 1.25
- qkv_weight: bfloat16 [768, 3, 768], P('dp', None, 'tp'), may hold values from -0.21875 to 0.21875
- qkv_bias: float32 [3, 768], P(None, 'tp'), may hold values from -1.25 to 1.25
- center_weight: float32 [12, 256], P('tp'), may hold values from -0.375 to 0.375
- spread_weight: float32 [12, 256], P('tp'), may hold values from -0.375 to 0.375
- out_weight: bfloat16 [768, 768], P('tp', 'dp'), may hold values from -0.625 to 0.625
- out_bias: float32 [768], replicated, may hold values from -1.25 to 1.25
- mlp_gain: float32 [768], replicated, may hold values from 0.5 to 1.5
- mlp_shift: float32 [768], replicated, may hold values from -1.25 to 1.25
- fc_weight: bfloat16 [768, 3072], P('dp', 'tp'), may hold values from -0.21875 to 0.21875
- fc_bias: float32 [3072], P('tp'), may hold values from -1.25 to 1.25
- proj_weight: bfloat16 [3072, 768], P('tp', 'dp'), may hold values from -0.109375 to 0.109375
- proj_bias: float32 [768], replicated, may hold values from -1.25 to 1.25
- cotangent: bfloat16 [12, 1024, 768], P('dp', 'ctx'), may hold values from -6 to 6
Outputs:
- block_out: bfloat16 [12, 1024, 768], P('dp', 'ctx')
- input_grad: bfloat16 [12, 1024, 768], P('dp', 'ctx')
- attn_gain_grad: float32 [768], replicated
- attn_shift_grad: float32 [768], replicated
- qkv_weight_grad: float32 [768, 3, 768], P('dp', None, 'tp')
- qkv_bias_grad: float32 [3, 768], P(None, 'tp')
- center_weight_grad: float32 [12, 256], P('tp')
- spread_weight_grad: float32 [12, 256], P('tp')
- out_weight_grad: float32 [768, 768], P('tp', 'dp')
- out_bias_grad: float32 [768], replicated
- mlp_gain_grad: float32 [768], replicated
- mlp_shift_grad: float32 [768], replicated
- fc_weight_grad: float32 [768, 3072], P('dp', 'tp')
- fc_bias_grad: float32 [3072], P('tp')
- proj_weight_grad: float32 [3072, 768], P('tp', 'dp')
- proj_bias_grad: float32 [768], replicated
The draws below stay inside these ranges and needn't reach their ends.
Inputs may be any that keep to these rules, and one draw needn't show every extreme that they name: `doc_lengths`: the entries of one sequence sum to 1024; zero entries are empty documents.
All inputs are finite; a program needn't handle non-finite values.
Results may differ from the reference program's by a relative error of at most 0.015.
The reference program's roundings to bfloat16 on the way count: a program that leaves them out, or rounds other values in their place, can miss the bound.
Values may be sent and summed in bfloat16 or wider, within the bound.
A program may use at most 128 MiB of HBM per device.

```python
import jax
import jax.numpy as jnp
from jax import lax

D = 768
H = 12
DH = 64
FF = 3072
NB = 256
STICKY = 256
WINDOW = 512
DOC_MIN = 60
DOC_MAX = 800
SEQ_DEV = 3
LEN = 1024
NDOC = 18
SEQUENCES = 12


def draw_doc_lengths(key, part):
    base_key = jax.random.fold_in(key, 7)
    key_raw, key_first, key_pick = jax.random.split(base_key, 3)
    raw_lengths = jax.random.randint(key_raw, (SEQUENCES, NDOC), DOC_MIN, DOC_MAX + 1, dtype=jnp.int32)
    starts = jnp.cumsum(raw_lengths, axis=1, dtype=jnp.int32) - raw_lengths
    ragged = jnp.clip(LEN - starts, 0, raw_lengths)
    first_length = jax.random.randint(key_first, (SEQUENCES, 1), DOC_MIN, LEN - DOC_MAX - DOC_MIN + 1, dtype=jnp.int32)
    spanning = jnp.concatenate([first_length, jnp.full((SEQUENCES, 1), DOC_MAX, jnp.int32), LEN - DOC_MAX - first_length, jnp.zeros((SEQUENCES, NDOC - 3), jnp.int32)], axis=1)
    groups = SEQUENCES // SEQ_DEV
    chosen = jax.random.randint(key_pick, (groups, 1), 0, SEQ_DEV, dtype=jnp.int32)
    member = (jnp.arange(SEQ_DEV, dtype=jnp.int32)[None, :] == chosen).reshape(SEQUENCES, 1)
    return jnp.where(member, spanning, ragged).astype(jnp.int32)


def plant(array, key, low, largest):
    dims = array.shape
    place = [jax.random.randint(jax.random.fold_in(key, axis), (), 0, dims[axis]) for axis in range(len(dims))]
    array = array.at[tuple(place)].set(low)
    longest = dims.index(max(dims))
    place[longest] = (place[longest] + 1) % dims[longest]
    return array.at[tuple(place)].set(largest)


def steps_of(stream_key, extent, cuts, smallest, largest):
    def one(dim, blocks):
        steps = jax.random.uniform(jax.random.fold_in(jax.random.fold_in(stream_key, 6), dim), (blocks,), jnp.float32, smallest / len(cuts), largest / len(cuts))
        return jnp.repeat(jnp.exp(steps), extent[dim] // blocks).reshape((-1,) + (1,) * (len(extent) - dim - 1))

    loudness = one(*cuts[0])
    for cut in cuts[1:]:
        loudness = loudness * one(*cut)
    return loudness


def bell_draw(rng, dims, scale, most, cuts=(), kind=jnp.bfloat16):
    level = steps_of(rng, dims, cuts, -0.22, 0.18) if cuts else 1.0
    array = jax.random.normal(rng, dims, jnp.float32) * scale * level
    return jnp.minimum(jnp.maximum(array, -most), most).astype(kind)


def setup_inputs(seed: int = 0) -> dict:
    splits = jax.random.split(jax.random.key(seed), 19)
    hidden_in = bell_draw(splits[0], (SEQUENCES, LEN, D), 1.0, 6.0, ((0, 4), (1, 4)))
    doc_lengths = draw_doc_lengths(jax.random.fold_in(splits[18], 71), 0)
    sticky_places = plant(jax.random.randint(splits[2], (SEQUENCES, STICKY), 0, LEN), jax.random.fold_in(splits[2], 1), 0, LEN - 1).astype(jnp.int32)
    attn_gain = jnp.clip(1.0 + 0.1 * jax.random.normal(splits[3], (D,), jnp.float32), 0.5, 1.5)
    attn_shift = bell_draw(splits[4], (D,), 0.2, 1.25, (), jnp.float32)
    qkv_weight = bell_draw(splits[5], (D, 3, D), D ** -0.5, 0.21875, ((0, 4), (2, 2)))
    qkv_bias = bell_draw(splits[6], (3, D), 0.2, 1.25, ((1, 2),), jnp.float32)
    center_weight = bell_draw(splits[7], (H, NB), NB ** -0.5, 0.375, ((0, 2),), jnp.float32)
    spread_weight = bell_draw(splits[8], (H, NB), NB ** -0.5, 0.375, ((0, 2),), jnp.float32)
    out_weight = bell_draw(splits[9], (D, D), (D // 8) ** -0.5, 0.625, ((0, 2), (1, 4)))
    out_bias = bell_draw(splits[10], (D,), 0.2, 1.25, (), jnp.float32)
    mlp_gain = jnp.clip(1.0 + 0.1 * jax.random.normal(splits[11], (D,), jnp.float32), 0.5, 1.5)
    mlp_shift = bell_draw(splits[12], (D,), 0.2, 1.25, (), jnp.float32)
    fc_weight = bell_draw(splits[13], (D, FF), D ** -0.5, 0.21875, ((0, 4), (1, 2)))
    fc_bias = bell_draw(splits[14], (FF,), 0.2, 1.25, ((0, 2),), jnp.float32)
    proj_weight = bell_draw(splits[15], (FF, D), FF ** -0.5, 0.109375, ((0, 2), (1, 4)))
    proj_bias = bell_draw(splits[16], (D,), 0.2, 1.25, (), jnp.float32)
    cotangent = bell_draw(splits[17], (SEQUENCES, LEN, D), 1.0, 6.0, ((0, 4), (1, 4)))
    return dict(hidden_in=hidden_in, doc_lengths=doc_lengths, sticky_places=sticky_places, attn_gain=attn_gain, attn_shift=attn_shift, qkv_weight=qkv_weight, qkv_bias=qkv_bias, center_weight=center_weight, spread_weight=spread_weight, out_weight=out_weight, out_bias=out_bias, mlp_gain=mlp_gain, mlp_shift=mlp_shift, fc_weight=fc_weight, fc_bias=fc_bias, proj_weight=proj_weight, proj_bias=proj_bias, cotangent=cotangent)


highest = lax.Precision.HIGHEST
eps_norm = 1e-05
ridge_term = 0.5
spread_scale = 0.02

@jax.custom_vjp
def low(v):
    return lax.optimization_barrier(v.astype(jnp.bfloat16)).astype(jnp.float32)

@jax.custom_vjp
def low_back(v):
    return v

def low_keep(v):
    return (low(v), None)

def low_pass(kept, grad):
    return (grad,)

def back_keep(v):
    return (v, None)

def back_low(kept, grad):
    return (low(grad),)
low.defvjp(low_keep, low_pass)
low_back.defvjp(back_keep, back_low)

def layer_norm(values, gain_vec, shift_vec):
    mean_value = lax.optimization_barrier(jnp.mean(values, axis=-1, keepdims=True))
    centred = values - mean_value
    variance = lax.optimization_barrier(jnp.mean(centred * centred, axis=-1, keepdims=True))
    return centred * lax.rsqrt(variance + eps_norm) * gain_vec + shift_vec

def gelu_tanh(values):
    return 0.5 * values * (1.0 + jnp.tanh(0.7978845608028654 * (values + 0.044715 * values * values * values)))

def softplus_smooth(values):
    return jnp.log1p(jnp.exp(values))

def ridge_fit(basis_count, sample_count):
    centers = (jnp.arange(basis_count, dtype=jnp.float32) + 0.5) / basis_count
    sample_times = (jnp.arange(sample_count, dtype=jnp.float32) + 0.5) / sample_count
    basis_width = 1.0 / basis_count
    design = jnp.exp(-jnp.square(sample_times[None, :] - centers[:, None]) / (2.0 * basis_width * basis_width))
    gram_matrix = jnp.dot(design, design.T, precision=highest) + ridge_term * jnp.eye(basis_count, dtype=jnp.float32)
    factor = jnp.linalg.cholesky(gram_matrix)
    return jax.scipy.linalg.cho_solve((factor, True), design)

def memory_reach(mem_scores, center_weight, spread_weight):
    basis_count = mem_scores.shape[-1]
    centers = (jnp.arange(basis_count, dtype=jnp.float32) + 0.5) / basis_count
    basis_width = 1.0 / basis_count
    center_logit = jnp.einsum('...hqj,hj->...hq', mem_scores, center_weight, precision=highest)
    spread_logit = jnp.einsum('...hqj,hj->...hq', mem_scores, spread_weight, precision=highest)
    middle = jax.nn.sigmoid(center_logit)[..., None]
    variance = (spread_scale * softplus_smooth(spread_logit) + basis_width * basis_width)[..., None]
    return basis_width * lax.rsqrt(variance) * jnp.exp(-jnp.square(middle - centers) / (2.0 * variance))

def one_sequence(params, fit_low, sequence_item):
    attn_gain, attn_shift, qkv_weight, qkv_bias, center_weight, spread_weight, out_weight, out_bias, mlp_gain, mlp_shift, fc_weight, fc_bias, proj_weight, proj_bias = params
    tokens, lengths, places = sequence_item
    length = tokens.shape[0]
    head_count = center_weight.shape[0]
    basis_count = center_weight.shape[1]
    score_scale = DH ** (-0.5)
    positions = jnp.arange(length, dtype=jnp.int32)
    doc_ends = jnp.cumsum(lengths.astype(jnp.int32), dtype=jnp.int32)
    segments = lax.optimization_barrier(jnp.sum((doc_ends[None, :] <= positions[:, None]).astype(jnp.int32), axis=1, dtype=jnp.int32))
    normed = low(layer_norm(tokens, attn_gain, attn_shift))
    qkv = jnp.einsum('pd,dke->pke', normed, qkv_weight, precision=highest) + qkv_bias
    qkv = low(low_back(qkv))
    model_width = qkv.shape[-1]
    queries = qkv[:, 0].reshape(length, head_count, DH)
    key_rows = qkv[:, 1].reshape(length, head_count, DH)
    value_rows = qkv[:, 2].reshape(length, head_count, DH)
    raw_scores = low_back(jnp.einsum('qhd,khd->hqk', queries, key_rows, precision=highest) * score_scale)
    allowed = (positions[None, :] <= positions[:, None]) & (positions[:, None] - positions[None, :] < WINDOW) & (segments[:, None] == segments[None, :])
    masked = jnp.where(allowed[None], raw_scores, -1e+30)
    row_max = lax.optimization_barrier(jnp.max(masked, axis=-1, keepdims=True))
    exp_terms = jnp.exp(masked - row_max)
    shares = exp_terms / lax.optimization_barrier(jnp.sum(exp_terms, axis=-1, keepdims=True))
    local_out = jnp.einsum('hqk,khd->qhd', low(shares), value_rows, precision=highest)
    sticky_count = places.shape[0]
    uniform = jnp.arange(sticky_count, dtype=jnp.int32) * length // sticky_count + length // (2 * sticky_count)
    all_places = jnp.concatenate([places.astype(jnp.int32), uniform.astype(jnp.int32)])
    sampled = qkv[all_places, 1:]
    memory = jnp.einsum('bm,mke->bke', fit_low, sampled, precision=highest)
    memory = low(low_back(memory))
    mem_keys = memory[:, 0].reshape(basis_count, head_count, DH)
    mem_values = memory[:, 1].reshape(basis_count, head_count, DH)
    mem_scores = low_back(jnp.einsum('qhd,bhd->hqb', queries, mem_keys, precision=highest) * score_scale)
    reach_low = low(memory_reach(mem_scores, center_weight, spread_weight))
    recalled = jnp.einsum('hqb,bhd->qhd', reach_low, mem_values, precision=highest)
    mixed_heads = low(low_back(local_out + recalled)).reshape(length, model_width)
    branch = low_back(jnp.dot(mixed_heads, out_weight, precision=highest))
    residual = tokens + branch + out_bias
    mlp_normed = low(layer_norm(residual, mlp_gain, mlp_shift))
    pre_act = low_back(jnp.dot(mlp_normed, fc_weight, precision=highest) + fc_bias)
    activated = low(gelu_tanh(pre_act))
    return residual + jnp.dot(activated, proj_weight, precision=highest) + proj_bias

def reference(hidden_in, doc_lengths, sticky_places, attn_gain, attn_shift, qkv_weight, qkv_bias, center_weight, spread_weight, out_weight, out_bias, mlp_gain, mlp_shift, fc_weight, fc_bias, proj_weight, proj_bias, cotangent):
    params = (attn_gain.astype(jnp.float32), attn_shift.astype(jnp.float32), qkv_weight.astype(jnp.float32), qkv_bias.astype(jnp.float32), center_weight.astype(jnp.float32), spread_weight.astype(jnp.float32), out_weight.astype(jnp.float32), out_bias.astype(jnp.float32), mlp_gain.astype(jnp.float32), mlp_shift.astype(jnp.float32), fc_weight.astype(jnp.float32), fc_bias.astype(jnp.float32), proj_weight.astype(jnp.float32), proj_bias.astype(jnp.float32))
    per_sequence = jax.checkpoint(one_sequence)
    lengths_all = doc_lengths.astype(jnp.int32)
    places_all = sticky_places.astype(jnp.int32)

    def forward(tokens, *weights):
        fit_low = low(ridge_fit(NB, 2 * STICKY))

        def apply_one(sequence_item):
            return per_sequence(weights, fit_low, sequence_item)
        return lax.map(apply_one, (tokens, lengths_all, places_all))
    block_value, pullback = jax.vjp(forward, hidden_in.astype(jnp.float32), *params)
    gradients = pullback(cotangent.astype(jnp.float32))
    return (block_value.astype(jnp.bfloat16), gradients[0].astype(jnp.bfloat16), gradients[1], gradients[2], gradients[3], gradients[4], gradients[5], gradients[6], gradients[7], gradients[8], gradients[9], gradients[10], gradients[11], gradients[12], gradients[13], gradients[14])
```

```python
import functools

import jax
import jax.numpy as jnp
import numpy as np
from jax import lax
from jax.experimental import pallas as pl
from jax.experimental.pallas import tpu as pltpu
from jax.sharding import PartitionSpec as P

DH = 64
WINDOW = 512
EPS = 1e-05
SPREAD = 0.02
SCALE = DH ** (-0.5)
VMEM_LIMIT = 58 * 1024 * 1024

bf16 = jnp.bfloat16
f32 = jnp.float32
MESH = pl.DeviceIdType.MESH


def dot_nn(a, b):
    return lax.dot_general(a, b, (((1,), (0,)), ((), ())), preferred_element_type=f32)


def dot_nt(a, b):
    return lax.dot_general(a, b, (((1,), (1,)), ((), ())), preferred_element_type=f32)


def dot_tn(a, b):
    return lax.dot_general(a, b, (((0,), (0,)), ((), ())), preferred_element_type=f32)


def ridge_fit(basis_count, sample_count):
    centers = (np.arange(basis_count) + 0.5) / basis_count
    times = (np.arange(sample_count) + 0.5) / sample_count
    width = 1.0 / basis_count
    design = np.exp(-np.square(times[None, :] - centers[:, None]) / (2.0 * width * width))
    gram = design @ design.T + 0.5 * np.eye(basis_count)
    return np.linalg.solve(gram, design).astype(bf16)


def place():
    c = lax.axis_index("ctx")
    side = c + 1 - 2 * lax.rem(c, 2)
    across = lax.rem(c + 2, 4)
    corner = lax.rem(side + 2, 4)
    return lax.axis_index("dp"), c, lax.axis_index("tp"), side, across, corner


def enter(devices):
    barrier = pltpu.get_barrier_semaphore()
    for device in devices:
        pl.semaphore_signal(barrier, inc=1, device_id=device, device_id_type=MESH)
    pl.semaphore_wait(barrier, len(devices))


def remote(src, dst, send, recv, device):
    return pltpu.make_async_remote_copy(
        src_ref=src,
        dst_ref=dst,
        send_sem=send,
        recv_sem=recv,
        device_id=device,
        device_id_type=MESH,
    )


def normalise(x, gain, shift):
    mean = jnp.mean(x, axis=-1, keepdims=True)
    centred = x - mean
    r = lax.rsqrt(jnp.mean(centred * centred, axis=-1, keepdims=True) + EPS)
    n = centred * r
    return n * gain + shift, n, r


def lowest_key(lengths, s, pos):
    low = jnp.maximum(pos - (WINDOW - 1), 0)
    end = jnp.int32(0)
    for e in range(lengths.shape[1]):
        end = end + lengths[s, e]
        low = jnp.maximum(low, jnp.where(pos >= end, end, 0))
    return low


def lanes(shape, dim):
    return lax.broadcasted_iota(jnp.int32, shape, dim)


def half_lanes(scale):
    lane = lanes((1, 2 * DH), 1)
    return [
        jnp.where(lane < DH, scale, 0.0).astype(bf16),
        jnp.where(lane >= DH, scale, 0.0).astype(bf16),
    ]


def mask_bias(lengths, s, c, rows, key_start, keys):
    pos = c * rows + lanes((rows, 1), 0)
    low = lowest_key(lengths, s, pos)
    key_pos = key_start + lanes((1, keys), 1)
    return jnp.where((key_pos <= pos) & (key_pos >= low), 0.0, -1e30)


def reach_terms(scores, center_row, spread_row, centers, width):
    center_logit = jnp.sum(scores * center_row, axis=-1, keepdims=True)
    spread_logit = jnp.sum(scores * spread_row, axis=-1, keepdims=True)
    mu = 1.0 / (1.0 + jnp.exp(-center_logit))
    grown = jnp.exp(spread_logit)
    var = SPREAD * jnp.log(1.0 + grown) + width * width
    inv = 1.0 / var
    diff = mu - centers
    reach = (width * lax.rsqrt(var)) * jnp.exp(-(diff * diff) * (0.5 * inv))
    return reach, mu, inv, diff, spread_logit


def forward_kernel(gather, refs):
    n = lax.axis_size("dp")
    if gather:
        (hid, lengths, places, gain, shift, wq_sh, wo_sh, wf_sh, wp_sh, qbias, cw, sw, fit,
         normed, q, kv, mem, lse, mixed, wq, wo, wf, wp,
         hoth, noth, bias, lsem,
         zs, zr, ys, yr, as_, ar, bs, br, os_, or_, hys, hyr, hxs, hxr, ks, kr, ms, mr) = refs
    else:
        (hid, lengths, places, gain, shift, wq, qbias, cw, sw, fit,
         normed, q, kv, mem, lse, mixed,
         hoth, noth, bias,
         hys, hyr, hxs, hxr, ks, kr, ms, mr) = refs
    z, c, t, side, across, corner = place()
    S, B, D = hid.shape
    HW = q.shape[2]
    NB = mem.shape[1]
    L = kv.shape[1]
    half = B // 2
    peers = [{"ctx": side}, {"ctx": across}, {"tp": 1 - t}]
    if gather:
        R = D // n
        Q = R // 4
        shards = [wq_sh, wo_sh, wf_sh, wp_sh]
        whole = [wq, wo.at[t], wf, wp]
        peers += [{"dp": lax.rem(z + i, n)} for i in range(1, n)]
    enter(peers)

    started = []

    def start(copies):
        for copy in copies:
            copy.start()
        started.extend(copies)
        return copies

    if gather:

        def rows(g, owner, quarter):
            return whole[g].at[pl.ds(pl.multiple_of(R * owner + Q * quarter, 16), Q)]

        def source(i):
            return lax.rem(z + n - i, n)

        def z_copies(g):
            src = shards[g].at[pl.ds(pl.multiple_of(Q * c, 16), Q)]
            return [
                remote(src, rows(g, z, c), zs.at[g, i - 1], zr.at[g, i - 1], {"dp": lax.rem(z + i, n)})
                for i in range(1, n)
            ]

        def own_copy(g):
            return pltpu.make_async_copy(
                shards[g], whole[g].at[pl.ds(pl.multiple_of(R * z, 16), R)], lsem.at[g]
            )

        def y_copies(g):
            return [
                remote(rows(g, source(i), c), rows(g, source(i), c), ys.at[g, i - 1], yr.at[g, i - 1], {"ctx": across})
                for i in range(1, n)
            ]

        def a_copies(g):
            return [
                remote(rows(g, source(i), c), rows(g, source(i), c), as_.at[g, i - 1], ar.at[g, i - 1], {"ctx": side})
                for i in range(1, n)
            ]

        def b_copies(g):
            return [
                remote(rows(g, source(i), across), rows(g, source(i), across), bs.at[g, i - 1], br.at[g, i - 1], {"ctx": side})
                for i in range(1, n)
            ]

        z_sent, y_sent, a_sent, b_sent, own_sent = {}, {}, {}, {}, {}

        def stage_z(g):
            own_sent[g] = own_copy(g)
            own_sent[g].start()
            z_sent[g] = start(z_copies(g))

        def stage_y(g):
            for copy in z_sent[g]:
                copy.wait_recv()
            y_sent[g] = start(y_copies(g))
            a_sent[g] = start(a_copies(g))

        def stage_b(g):
            for copy in y_sent[g]:
                copy.wait_recv()
            b_sent[g] = start(b_copies(g))

        def stage_end(g):
            for copy in a_sent[g] + b_sent[g]:
                copy.wait_recv()
            own_sent[g].wait()
    else:

        def stage_z(g):
            pass

        stage_y = stage_b = stage_end = stage_z

    def hidden_y(s):
        piece = pl.ds(pl.multiple_of(half * t, 16), half)
        return remote(hid.at[s, piece], hoth.at[s, piece], hys.at[s], hyr.at[s], {"ctx": across})

    def hidden_x(s):
        piece = pl.ds(pl.multiple_of(half * t, 16), half)
        return remote(hoth.at[s, piece], hoth.at[s, piece], hxs.at[s], hxr.at[s], {"tp": 1 - t})

    def block(s, owner):
        return kv.at[s, pl.ds(pl.multiple_of(owner * B, B), B)]

    def kv_copy(s, which):
        owner = c if which == 0 else across
        return remote(block(s, owner), block(s, owner), ks.at[s, which], kr.at[s, which], {"ctx": side})

    stage_z(0)
    hy = start([hidden_y(s) for s in range(S)])
    for g in (1, 2, 3):
        stage_z(g)

    gain_row = gain[...]
    shift_row = shift[...]
    for s in range(S):
        low, _, _ = normalise(hid[s].astype(f32), gain_row, shift_row)
        normed[s] = low.astype(bf16)
    hx = []
    for s in range(S):
        hy[s].wait_recv()
        hx += start([hidden_x(s)])
    stage_y(0)
    for s in range(S):
        hx[s].wait_recv()
        low, _, _ = normalise(hoth[s].astype(f32), gain_row, shift_row)
        noth[s] = low.astype(bf16)
    stage_b(0)
    stage_end(0)
    bias_row = qbias[...]
    kvs = []
    for s in range(S):
        part = (dot_nn(normed[s], wq[:, HW:]) + bias_row[:, HW:]).astype(bf16)
        kv[s, pl.ds(pl.multiple_of(c * B, B), B)] = part
        kvs += start([kv_copy(s, 0)])
    stage_y(1)
    for s in range(S):
        part = (dot_nn(noth[s], wq[:, HW:]) + bias_row[:, HW:]).astype(bf16)
        kv[s, pl.ds(pl.multiple_of(across * B, B), B)] = part
        kvs += start([kv_copy(s, 1)])
    stage_b(1)
    stage_y(2)
    for s in range(S):
        q[s] = (dot_nn(normed[s], wq[:, :HW]) + bias_row[:, :HW]).astype(bf16)
    stage_end(1)
    if gather:
        wo_sent = start([remote(wo.at[t], wo.at[t], os_, or_, {"tp": 1 - t})])

    key_start = pl.multiple_of(jnp.maximum(c - 2, 0) * B, B)
    keys = 3 * B
    M = places.shape[0]
    centers = (lanes((1, NB), 1).astype(f32) + 0.5) * (1.0 / NB)
    width = 1.0 / NB
    lane = lanes((1, 2 * DH), 1)
    scaled = half_lanes(SCALE)
    column = lanes((1, 2 * DH), 1)
    mx = []
    for s in range(S):
        kvs[s].wait_recv()
        kvs[S + s].wait_recv()
        key_row = lanes((1, L), 1)
        sticky = jnp.where(key_row == places[:, s : s + 1], 1.0, 0.0).astype(bf16)
        even = lanes((M, 1), 0) * L // M + L // (2 * M)
        steady = jnp.where(key_row == even, 1.0, 0.0).astype(bf16)
        spread_fit = dot_nn(fit[:, :M], sticky) + dot_nn(fit[:, M:], steady)
        high = spread_fit.astype(bf16)
        rest = (spread_fit - high.astype(f32)).astype(bf16)
        mem[s] = (dot_nn(high, kv[s]) + dot_nn(rest, kv[s])).astype(bf16)
        bias[...] = mask_bias(lengths, s, c, B, key_start, keys)

        def pair_step(p, log_rows, s=s):
            cols = pl.ds(pl.multiple_of(p * 2 * DH, 2 * DH), 2 * DH)
            vcols = pl.ds(pl.multiple_of(HW + p * 2 * DH, 2 * DH), 2 * DH)
            window = pl.ds(key_start, keys)
            qp = q[s, :, cols]
            kp = kv[s, window, cols]
            vp = kv[s, window, vcols]
            mk = mem[s, :, cols]
            mv = mem[s, :, vcols]
            outs = []
            for h in range(2):
                qh = qp * scaled[h]
                scores = dot_nt(qh, kp) + bias[...]
                top = jnp.max(scores, axis=-1, keepdims=True)
                e = jnp.exp(scores - top)
                total = jnp.sum(e, axis=-1, keepdims=True)
                share = (e * (1.0 / total)).astype(bf16)
                out = dot_nn(share, vp)
                log_rows = jnp.where(column == 2 * p + h, top + jnp.log(total), log_rows)
                mem_scores = dot_nt(qh, mk)
                reach, _, _, _, _ = reach_terms(
                    mem_scores, cw[pl.ds(2 * p + h, 1)], sw[pl.ds(2 * p + h, 1)], centers, width
                )
                outs.append(out + dot_nn(reach.astype(bf16), mv))
            mixed[t, s, :, cols] = jnp.where(lane < DH, outs[0], outs[1]).astype(bf16)
            return log_rows

        lse[s] = lax.fori_loop(0, HW // (2 * DH), pair_step, jnp.zeros((B, 2 * DH), f32))
        mx += start([remote(mixed.at[t, s], mixed.at[t, s], ms.at[s], mr.at[s], {"tp": 1 - t})])
        if s == 0:
            stage_b(2)
            stage_y(3)
        if s == 1:
            stage_b(3)
    stage_end(2)
    stage_end(3)
    if gather:
        wo_sent[0].wait_recv()
    for copy in mx:
        copy.wait_recv()
    for copy in started:
        copy.wait_send()


def forward(gather, hid, lengths, places, gain, shift, weights, qbias, cw, sw, fit):
    S, B, D = hid.shape
    HW = qbias.shape[1] // 3
    n = lax.axis_size("dp")
    L = B * lax.axis_size("ctx")
    NB = cw.shape[1]
    vm = pl.BlockSpec(memory_space=pltpu.VMEM)
    sm = pl.BlockSpec(memory_space=pltpu.SMEM)
    hb = pl.BlockSpec(memory_space=pl.ANY)
    out = [
        jax.ShapeDtypeStruct((S, B, D), bf16),
        jax.ShapeDtypeStruct((S, B, HW), bf16),
        jax.ShapeDtypeStruct((S, L, 2 * HW), bf16),
        jax.ShapeDtypeStruct((S, NB, 2 * HW), bf16),
        jax.ShapeDtypeStruct((S, B, 128), f32),
        jax.ShapeDtypeStruct((2, S, B, HW), bf16),
    ]
    out_specs = [vm] * 6
    sem = pltpu.SemaphoreType.DMA
    scratch = [
        pltpu.VMEM((S, B, D), bf16),
        pltpu.VMEM((S, B, D), bf16),
        pltpu.VMEM((B, 3 * B), f32),
    ]
    w_specs = [vm]
    if gather:
        FW = weights[2].shape[1]
        out += [
            jax.ShapeDtypeStruct((D, 3 * HW), bf16),
            jax.ShapeDtypeStruct((2, D, HW), bf16),
            jax.ShapeDtypeStruct((D, FW), bf16),
            jax.ShapeDtypeStruct((D, FW), bf16),
        ]
        out_specs += [vm, hb, hb, hb]
        w_specs = [vm, hb, hb, hb]
        scratch += [sem((4,))] + [sem((4, n - 1))] * 8 + [sem, sem]
    scratch += [sem((S,))] * 4 + [sem((S, 2))] * 2 + [sem((S,))] * 2
    return pl.pallas_call(
        lambda *refs: forward_kernel(gather, refs),
        out_shape=out,
        in_specs=[vm, sm, vm, vm, vm, *w_specs, vm, vm, vm, vm],
        out_specs=out_specs,
        scratch_shapes=scratch,
        compiler_params=pltpu.CompilerParams(
            collective_id=0, has_side_effects=True, vmem_limit_bytes=VMEM_LIMIT
        ),
        cost_estimate=pl.CostEstimate(flops=6_000_000_000, bytes_accessed=30_000_000, transcendentals=6_000_000),
        name="forward_part",
    )(hid, lengths, places, gain, shift, *weights, qbias, cw, sw, fit)


def layer_norm(values, gain_vec, shift_vec):
    mean_value = jnp.mean(values, axis=-1, keepdims=True)
    centred = values - mean_value
    variance = jnp.mean(centred * centred, axis=-1, keepdims=True)
    return centred * lax.rsqrt(variance + EPS) * gain_vec + shift_vec


def gelu_tanh(values):
    return (
        0.5
        * values
        * (1.0 + jnp.tanh(0.7978845608028654 * (values + 0.044715 * values * values * values)))
    )


def memory_reach(mem_scores, center_weight, spread_weight):
    highest = lax.Precision.HIGHEST
    basis_count = mem_scores.shape[-1]
    centers = (jnp.arange(basis_count, dtype=f32) + 0.5) / basis_count
    basis_width = 1.0 / basis_count
    center_logit = jnp.einsum("...hqj,hj->...hq", mem_scores, center_weight, precision=highest)
    spread_logit = jnp.einsum("...hqj,hj->...hq", mem_scores, spread_weight, precision=highest)
    middle = jax.nn.sigmoid(center_logit)[..., None]
    variance = (SPREAD * jnp.log1p(jnp.exp(spread_logit)) + basis_width * basis_width)[..., None]
    return basis_width * lax.rsqrt(variance) * jnp.exp(-jnp.square(middle - centers) / (2.0 * variance))


def attend_back(item):
    queries, key_rows, value_rows, bias, log_total, grad_mixed = item
    masked = jnp.einsum("qhd,khd->hqk", queries, key_rows, preferred_element_type=f32) * SCALE + bias[None]
    shares = jnp.exp(masked - log_total)
    grad_shares = jnp.einsum("qhd,khd->hqk", grad_mixed, value_rows, preferred_element_type=f32)
    grad_scores = (shares * (grad_shares - jnp.sum(shares * grad_shares, axis=-1, keepdims=True))).astype(bf16)
    grad_queries = jnp.einsum("hqk,khd->qhd", grad_scores, key_rows, preferred_element_type=f32) * SCALE
    grad_keys = jnp.einsum("hqk,qhd->khd", grad_scores, queries, preferred_element_type=f32) * SCALE
    grad_values = jnp.einsum("hqk,qhd->khd", shares.astype(bf16), grad_mixed, preferred_element_type=f32)
    return (grad_queries, grad_keys, grad_values)


def passed_along(value, axis, distance):
    devices = range(lax.axis_size(axis))
    return lax.ppermute(value, axis, [(i - distance, i) for i in devices if i - distance in devices])


def per_device(hidden_in, doc_lengths, sticky_places, attn_gain, attn_shift, qkv_weight, qkv_bias, center_weight,
               spread_weight, out_weight, out_bias, mlp_gain, mlp_shift, fc_weight, fc_bias, proj_weight, proj_bias, cotangent):
    S, B, D = hidden_in.shape
    n = lax.axis_size("dp")
    HW = qkv_bias.shape[1]
    H = HW // DH
    NB = center_weight.shape[1]
    c = lax.axis_index("ctx")
    t = lax.axis_index("tp")
    M = sticky_places.shape[1]
    L = B * lax.axis_size("ctx")
    fit = jnp.asarray(ridge_fit(NB, 2 * M))
    gather = D % (64 * n) == 0
    shards = [qkv_weight.reshape(D // n, 3 * HW), out_weight.T, fc_weight, proj_weight.T]
    if gather:
        weights = shards
    else:
        full = [lax.all_gather(w, "dp", axis=0, tiled=True) for w in shards]
        weights = full[:1]
    res = forward(gather, hidden_in, doc_lengths, sticky_places.T, attn_gain[None], attn_shift[None], weights,
                  qkv_bias.reshape(1, 3 * HW), center_weight, spread_weight, fit)
    normed_low, q, kv, memory, lse, mixed = res[:6]
    if gather:
        wq, wo, wf, wp = res[6:]
        wo = lax.dynamic_index_in_dim(wo, t, 0, keepdims=False)
    else:
        wq, wo, wf, wp = full
    qkv_full, out_full, fc_full, proj_full = wq.reshape(D, 3, HW), wo.T, wf, wp.T
    inputs_wide = hidden_in.astype(f32)
    _, norm_pull = jax.vjp(layer_norm, inputs_wide, attn_gain, attn_shift)
    queries = q.reshape(S, B, H, DH)
    key_start = jnp.maximum(c - 2, 0) * B
    win = lax.dynamic_slice_in_dim(kv, key_start, 3 * B, axis=1)
    key_rows = win[:, :, :HW].reshape(S, 3 * B, H, DH)
    value_rows = win[:, :, HW:].reshape(S, 3 * B, H, DH)
    pos = c * B + jnp.arange(B)
    kpos = key_start + jnp.arange(3 * B)
    ends = jnp.sum(jnp.where(jnp.tril(jnp.ones((doc_lengths.shape[1],) * 2, bool))[None], doc_lengths[:, None, :], 0), axis=2)
    qd = jnp.sum((ends[:, None, :] <= pos[None, :, None]).astype(jnp.int32), axis=2)
    kd = jnp.sum((ends[:, None, :] <= kpos[None, :, None]).astype(jnp.int32), axis=2)
    allowed = (kpos[None, None, :] <= pos[None, :, None]) & (pos[None, :, None] - kpos[None, None, :] < WINDOW) & (qd[:, :, None] == kd[:, None, :])
    bias = jnp.where(allowed, 0.0, -1e30)
    mem_keys = memory[:, :, :HW].reshape(S, NB, H, DH)
    mem_values = memory[:, :, HW:].reshape(S, NB, H, DH)
    mem_scores = jnp.einsum("sqhd,sbhd->shqb", queries, mem_keys, preferred_element_type=f32) * SCALE
    reach_weights, reach_pull = jax.vjp(memory_reach, mem_scores, center_weight, spread_weight)
    reach_low = reach_weights.astype(bf16)
    mixed_heads = lax.dynamic_index_in_dim(mixed, t, 0, keepdims=False)
    attn_part = jnp.einsum("sbe,ed->sbd", mixed_heads, out_full, preferred_element_type=f32)
    residual = inputs_wide + lax.psum(attn_part, "tp") + out_bias
    mlp_normed, mlp_pull = jax.vjp(layer_norm, residual, mlp_gain, mlp_shift)
    mlp_low = mlp_normed.astype(bf16)
    pre_act = jnp.einsum("sbd,df->sbf", mlp_low, fc_full, preferred_element_type=f32) + fc_bias
    activated, gelu_pull = jax.vjp(gelu_tanh, pre_act)
    activated_low = activated.astype(bf16)
    mlp_part = jnp.einsum("sbf,fd->sbd", activated_low, proj_full, preferred_element_type=f32)
    mlp_sum = lax.psum(mlp_part.astype(bf16), "tp").astype(f32)
    block_out = (residual + mlp_sum + proj_bias).astype(bf16)
    grad_out = cotangent.astype(f32)
    proj_grad = jnp.einsum("sbf,sbd->fd", activated_low, cotangent, preferred_element_type=f32)
    proj_bias_grad = jnp.sum(grad_out, axis=(0, 1))
    grad_activated = jnp.einsum("sbd,fd->sbf", cotangent, proj_full, preferred_element_type=f32)
    grad_pre = gelu_pull(grad_activated)[0].astype(bf16)
    fc_grad = jnp.einsum("sbd,sbf->df", mlp_low, grad_pre, preferred_element_type=f32)
    fc_bias_grad = jnp.sum(grad_pre, axis=(0, 1), dtype=f32)
    mlp_back_part = jnp.einsum("sbf,df->sbd", grad_pre, fc_full, preferred_element_type=f32)
    grad_mlp_normed = lax.psum(mlp_back_part, "tp")
    grad_residual, mlp_gain_grad, mlp_shift_grad = mlp_pull(grad_mlp_normed)
    grad_residual = grad_residual + grad_out
    out_bias_grad = jnp.sum(grad_residual, axis=(0, 1))
    grad_residual_low = grad_residual.astype(bf16)
    out_grad = jnp.einsum("sbe,sbd->ed", mixed_heads, grad_residual_low, preferred_element_type=f32)
    grad_mixed = jnp.einsum("sbd,ed->sbe", grad_residual_low, out_full, preferred_element_type=f32)
    grad_mixed = grad_mixed.astype(bf16).reshape(S, B, H, DH)
    log_total = jnp.swapaxes(lse[:, :, :H], 1, 2)[..., None]
    grad_queries, grad_keys, grad_values = lax.map(attend_back, (queries, key_rows, value_rows, bias, log_total, grad_mixed))
    grad_reach = jnp.einsum("sqhd,sbhd->shqb", grad_mixed, mem_values, preferred_element_type=f32)
    grad_mem_values = jnp.einsum("shqb,sqhd->sbhd", reach_low, grad_mixed, preferred_element_type=f32)
    grad_mem_scores, center_grad, spread_grad = reach_pull(grad_reach)
    grad_mem_scores = grad_mem_scores.astype(bf16)
    grad_queries = grad_queries + jnp.einsum("shqb,sbhd->sqhd", grad_mem_scores, mem_keys, preferred_element_type=f32) * SCALE
    grad_mem_keys = jnp.einsum("shqb,sqhd->sbhd", grad_mem_scores, queries, preferred_element_type=f32) * SCALE
    grad_memory_part = jnp.concatenate([grad_mem_keys.reshape(S, NB, HW), grad_mem_values.reshape(S, NB, HW)], axis=2)
    grad_memory = lax.psum(grad_memory_part.astype(bf16), "ctx")
    grad_sampled = jnp.einsum("bm,sbc->smc", fit, grad_memory, preferred_element_type=f32)
    uniform = jnp.arange(M, dtype=jnp.int32) * L // M + L // (2 * M)
    all_places = jnp.concatenate([sticky_places, jnp.broadcast_to(uniform, sticky_places.shape)], axis=1)
    local_index = all_places - c * B
    inside = (local_index >= 0) & (local_index < B)
    row_index = jnp.where(inside, local_index, B)
    seq_index = jnp.arange(S, dtype=jnp.int32)[:, None]
    grad_fit_rows = jnp.zeros((S, B, 2 * HW), f32).at[seq_index, row_index].add(grad_sampled, mode="drop")
    grad_win = jnp.concatenate([grad_keys.reshape(S, 3 * B, HW), grad_values.reshape(S, 3 * B, HW)], axis=2)
    grad_all = lax.dynamic_update_slice_in_dim(jnp.zeros((S, L, 2 * HW), f32), grad_win, key_start, axis=1)
    grad_own = lax.psum_scatter(grad_all, "ctx", scatter_dimension=1, tiled=True) + grad_fit_rows
    grad_qkv = jnp.concatenate([grad_queries.reshape(S, B, 1, HW), grad_own.reshape(S, B, 2, HW)], axis=2).astype(bf16)
    qkv_grad = jnp.einsum("sbd,sbke->dke", normed_low, grad_qkv, preferred_element_type=f32)
    qkv_bias_grad = jnp.sum(grad_qkv, axis=(0, 1), dtype=f32)
    grad_normed = lax.psum(jnp.einsum("sbke,dke->sbd", grad_qkv, qkv_full, preferred_element_type=f32).astype(bf16), "tp").astype(f32)
    grad_inputs, attn_gain_grad, attn_shift_grad = norm_pull(grad_normed)
    input_grad = (grad_inputs + grad_residual).astype(bf16)
    small = lax.psum((attn_gain_grad, attn_shift_grad, qkv_bias_grad, center_grad, spread_grad, out_bias_grad, mlp_gain_grad, mlp_shift_grad, fc_bias_grad, proj_bias_grad), ("dp", "ctx"))
    attn_gain_grad, attn_shift_grad, qkv_bias_grad, center_grad, spread_grad, out_bias_grad, mlp_gain_grad, mlp_shift_grad, fc_bias_grad, proj_bias_grad = small

    def reduced(grad, dim):
        part = lax.psum_scatter(grad.astype(bf16), "dp", scatter_dimension=dim, tiled=True)
        return lax.psum(part, "ctx").astype(f32)

    return (block_out, input_grad, attn_gain_grad, attn_shift_grad, reduced(qkv_grad, 0), qkv_bias_grad, center_grad, spread_grad,
            reduced(out_grad, 1), out_bias_grad, mlp_gain_grad, mlp_shift_grad, reduced(fc_grad, 0), fc_bias_grad, reduced(proj_grad, 1), proj_bias_grad)


def solution(mesh):
    in_specs = (
        P("dp", "ctx", None),
        P("dp", None),
        P("dp", None),
        P(),
        P(),
        P("dp", None, "tp"),
        P(None, "tp"),
        P("tp", None),
        P("tp", None),
        P("tp", "dp"),
        P(),
        P(),
        P(),
        P("dp", "tp"),
        P("tp"),
        P("tp", "dp"),
        P(),
        P("dp", "ctx", None),
    )
    out_specs = (
        P("dp", "ctx", None),
        P("dp", "ctx", None),
        P(),
        P(),
        P("dp", None, "tp"),
        P(None, "tp"),
        P("tp", None),
        P("tp", None),
        P("tp", "dp"),
        P(),
        P(),
        P(),
        P("dp", "tp"),
        P("tp"),
        P("tp", "dp"),
        P(),
    )
    return jax.shard_map(
        per_device, mesh=mesh, in_specs=in_specs, out_specs=out_specs, check_vma=False
    )
```

```python
import functools

import jax
import jax.numpy as jnp
import numpy as np
from jax import lax
from jax.experimental import pallas as pl
from jax.experimental.pallas import tpu as pltpu
from jax.sharding import PartitionSpec as P

DH = 64
WINDOW = 512
EPS = 1e-05
SPREAD = 0.02
SCALE = DH ** (-0.5)
VMEM_LIMIT = 60 * 1024 * 1024

bf16 = jnp.bfloat16
f32 = jnp.float32
MESH = pl.DeviceIdType.MESH


def dot_nn(a, b):
    return lax.dot_general(a, b, (((1,), (0,)), ((), ())), preferred_element_type=f32)


def dot_nt(a, b):
    return lax.dot_general(a, b, (((1,), (1,)), ((), ())), preferred_element_type=f32)


def dot_tn(a, b):
    return lax.dot_general(a, b, (((0,), (0,)), ((), ())), preferred_element_type=f32)


def ridge_fit(basis_count, sample_count):
    centers = (np.arange(basis_count) + 0.5) / basis_count
    times = (np.arange(sample_count) + 0.5) / sample_count
    width = 1.0 / basis_count
    design = np.exp(-np.square(times[None, :] - centers[:, None]) / (2.0 * width * width))
    gram = design @ design.T + 0.5 * np.eye(basis_count)
    return np.linalg.solve(gram, design).astype(bf16)


def place():
    c = lax.axis_index("ctx")
    side = c + 1 - 2 * lax.rem(c, 2)
    across = lax.rem(c + 2, 4)
    corner = lax.rem(side + 2, 4)
    return lax.axis_index("dp"), c, lax.axis_index("tp"), side, across, corner


def enter(devices):
    barrier = pltpu.get_barrier_semaphore()
    for device in devices:
        pl.semaphore_signal(barrier, inc=1, device_id=device, device_id_type=MESH)
    pl.semaphore_wait(barrier, len(devices))


def remote(src, dst, send, recv, device):
    return pltpu.make_async_remote_copy(
        src_ref=src,
        dst_ref=dst,
        send_sem=send,
        recv_sem=recv,
        device_id=device,
        device_id_type=MESH,
    )


def normalise(x, gain, shift):
    mean = jnp.mean(x, axis=-1, keepdims=True)
    centred = x - mean
    r = lax.rsqrt(jnp.mean(centred * centred, axis=-1, keepdims=True) + EPS)
    n = centred * r
    return n * gain + shift, n, r


def lowest_key(lengths, s, pos):
    low = jnp.maximum(pos - (WINDOW - 1), 0)
    end = jnp.int32(0)
    for e in range(lengths.shape[1]):
        end = end + lengths[s, e]
        low = jnp.maximum(low, jnp.where(pos >= end, end, 0))
    return low


def lanes(shape, dim):
    return lax.broadcasted_iota(jnp.int32, shape, dim)


def half_lanes(scale):
    lane = lanes((1, 2 * DH), 1)
    return [
        jnp.where(lane < DH, scale, 0.0).astype(bf16),
        jnp.where(lane >= DH, scale, 0.0).astype(bf16),
    ]


def mask_bias(lengths, s, c, rows, key_start, keys):
    pos = c * rows + lanes((rows, 1), 0)
    low = lowest_key(lengths, s, pos)
    key_pos = key_start + lanes((1, keys), 1)
    return jnp.where((key_pos <= pos) & (key_pos >= low), 0.0, -1e30)


def reach_terms(scores, center_row, spread_row, centers, width):
    center_logit = jnp.sum(scores * center_row, axis=-1, keepdims=True)
    spread_logit = jnp.sum(scores * spread_row, axis=-1, keepdims=True)
    mu = 1.0 / (1.0 + jnp.exp(-center_logit))
    grown = jnp.exp(spread_logit)
    var = SPREAD * jnp.log(1.0 + grown) + width * width
    inv = 1.0 / var
    diff = mu - centers
    reach = (width * lax.rsqrt(var)) * jnp.exp(-(diff * diff) * (0.5 * inv))
    return reach, mu, inv, diff, spread_logit


def forward_kernel(gather, refs):
    n = lax.axis_size("dp")
    if gather:
        (hid, lengths, places, gain, shift, wq_sh, wo_sh, wf_sh, wp_sh, qbias, cw, sw, fit,
         normed, q, kv, mem, lse, mixed, wq, wo, wf, wp,
         hoth, noth, bias, lsem,
         zs, zr, ys, yr, as_, ar, bs, br, os_, or_, hys, hyr, hxs, hxr, ks, kr, ms, mr) = refs
    else:
        (hid, lengths, places, gain, shift, wq, qbias, cw, sw, fit,
         normed, q, kv, mem, lse, mixed,
         hoth, noth, bias,
         hys, hyr, hxs, hxr, ks, kr, ms, mr) = refs
    z, c, t, side, across, corner = place()
    S, B, D = hid.shape
    HW = q.shape[2]
    NB = mem.shape[1]
    L = kv.shape[1]
    half = B // 2
    peers = [{"ctx": side}, {"ctx": across}, {"tp": 1 - t}]
    if gather:
        R = D // n
        Q = R // 4
        shards = [wq_sh, wo_sh, wf_sh, wp_sh]
        whole = [wq, wo.at[t], wf, wp]
        peers += [{"dp": lax.rem(z + i, n)} for i in range(1, n)]
    enter(peers)

    started = []

    def start(copies):
        for copy in copies:
            copy.start()
        started.extend(copies)
        return copies

    if gather:

        def rows(g, owner, quarter):
            return whole[g].at[pl.ds(pl.multiple_of(R * owner + Q * quarter, 16), Q)]

        def source(i):
            return lax.rem(z + n - i, n)

        def z_copies(g):
            src = shards[g].at[pl.ds(pl.multiple_of(Q * c, 16), Q)]
            return [
                remote(src, rows(g, z, c), zs.at[g, i - 1], zr.at[g, i - 1], {"dp": lax.rem(z + i, n)})
                for i in range(1, n)
            ]

        def own_copy(g):
            return pltpu.make_async_copy(
                shards[g], whole[g].at[pl.ds(pl.multiple_of(R * z, 16), R)], lsem.at[g]
            )

        def y_copies(g):
            return [
                remote(rows(g, source(i), c), rows(g, source(i), c), ys.at[g, i - 1], yr.at[g, i - 1], {"ctx": across})
                for i in range(1, n)
            ]

        def a_copies(g):
            return [
                remote(rows(g, source(i), c), rows(g, source(i), c), as_.at[g, i - 1], ar.at[g, i - 1], {"ctx": side})
                for i in range(1, n)
            ]

        def b_copies(g):
            return [
                remote(rows(g, source(i), across), rows(g, source(i), across), bs.at[g, i - 1], br.at[g, i - 1], {"ctx": side})
                for i in range(1, n)
            ]

        z_sent, y_sent, a_sent, b_sent, own_sent = {}, {}, {}, {}, {}

        def stage_z(g):
            own_sent[g] = own_copy(g)
            own_sent[g].start()
            z_sent[g] = start(z_copies(g))

        def stage_y(g):
            for copy in z_sent[g]:
                copy.wait_recv()
            y_sent[g] = start(y_copies(g))
            a_sent[g] = start(a_copies(g))

        def stage_b(g):
            for copy in y_sent[g]:
                copy.wait_recv()
            b_sent[g] = start(b_copies(g))

        def stage_end(g):
            for copy in a_sent[g] + b_sent[g]:
                copy.wait_recv()
            own_sent[g].wait()
    else:

        def stage_z(g):
            pass

        stage_y = stage_b = stage_end = stage_z

    def hidden_y(s):
        piece = pl.ds(pl.multiple_of(half * t, 16), half)
        return remote(hid.at[s, piece], hoth.at[s, piece], hys.at[s], hyr.at[s], {"ctx": across})

    def hidden_x(s):
        piece = pl.ds(pl.multiple_of(half * t, 16), half)
        return remote(hoth.at[s, piece], hoth.at[s, piece], hxs.at[s], hxr.at[s], {"tp": 1 - t})

    def block(s, owner):
        return kv.at[s, pl.ds(pl.multiple_of(owner * B, B), B)]

    def kv_copy(s, which):
        owner = c if which == 0 else across
        return remote(block(s, owner), block(s, owner), ks.at[s, which], kr.at[s, which], {"ctx": side})

    stage_z(0)
    hy = start([hidden_y(s) for s in range(S)])
    for g in (1, 2, 3):
        stage_z(g)

    gain_row = gain[...]
    shift_row = shift[...]
    for s in range(S):
        low, _, _ = normalise(hid[s].astype(f32), gain_row, shift_row)
        normed[s] = low.astype(bf16)
    hx = []
    for s in range(S):
        hy[s].wait_recv()
        hx += start([hidden_x(s)])
    stage_y(0)
    for s in range(S):
        hx[s].wait_recv()
        low, _, _ = normalise(hoth[s].astype(f32), gain_row, shift_row)
        noth[s] = low.astype(bf16)
    stage_b(0)
    stage_end(0)
    bias_row = qbias[...]
    kvs = []
    for s in range(S):
        part = (dot_nn(normed[s], wq[:, HW:]) + bias_row[:, HW:]).astype(bf16)
        kv[s, pl.ds(pl.multiple_of(c * B, B), B)] = part
        kvs += start([kv_copy(s, 0)])
    stage_y(1)
    for s in range(S):
        part = (dot_nn(noth[s], wq[:, HW:]) + bias_row[:, HW:]).astype(bf16)
        kv[s, pl.ds(pl.multiple_of(across * B, B), B)] = part
        kvs += start([kv_copy(s, 1)])
    stage_b(1)
    stage_y(2)
    for s in range(S):
        q[s] = (dot_nn(normed[s], wq[:, :HW]) + bias_row[:, :HW]).astype(bf16)
    stage_end(1)
    if gather:
        wo_sent = start([remote(wo.at[t], wo.at[t], os_, or_, {"tp": 1 - t})])

    key_start = pl.multiple_of(jnp.maximum(c - 2, 0) * B, B)
    keys = 3 * B
    M = places.shape[0]
    centers = (lanes((1, NB), 1).astype(f32) + 0.5) * (1.0 / NB)
    width = 1.0 / NB
    lane = lanes((1, 2 * DH), 1)
    scaled = half_lanes(SCALE)
    column = lanes((1, 2 * DH), 1)
    mx = []
    for s in range(S):
        kvs[s].wait_recv()
        kvs[S + s].wait_recv()
        key_row = lanes((1, L), 1)
        sticky = jnp.where(key_row == places[:, s : s + 1], 1.0, 0.0).astype(bf16)
        even = lanes((M, 1), 0) * L // M + L // (2 * M)
        steady = jnp.where(key_row == even, 1.0, 0.0).astype(bf16)
        spread_fit = dot_nn(fit[:, :M], sticky) + dot_nn(fit[:, M:], steady)
        high = spread_fit.astype(bf16)
        rest = (spread_fit - high.astype(f32)).astype(bf16)
        mem[s] = (dot_nn(high, kv[s]) + dot_nn(rest, kv[s])).astype(bf16)
        bias[...] = mask_bias(lengths, s, c, B, key_start, keys)

        def pair_step(p, log_rows, s=s):
            cols = pl.ds(pl.multiple_of(p * 2 * DH, 2 * DH), 2 * DH)
            vcols = pl.ds(pl.multiple_of(HW + p * 2 * DH, 2 * DH), 2 * DH)
            window = pl.ds(key_start, keys)
            qp = q[s, :, cols]
            kp = kv[s, window, cols]
            vp = kv[s, window, vcols]
            mk = mem[s, :, cols]
            mv = mem[s, :, vcols]
            outs = []
            for h in range(2):
                qh = qp * scaled[h]
                scores = dot_nt(qh, kp) + bias[...]
                top = jnp.max(scores, axis=-1, keepdims=True)
                e = jnp.exp(scores - top)
                total = jnp.sum(e, axis=-1, keepdims=True)
                share = (e * (1.0 / total)).astype(bf16)
                out = dot_nn(share, vp)
                log_rows = jnp.where(column == 2 * p + h, top + jnp.log(total), log_rows)
                mem_scores = dot_nt(qh, mk)
                reach, _, _, _, _ = reach_terms(
                    mem_scores, cw[pl.ds(2 * p + h, 1)], sw[pl.ds(2 * p + h, 1)], centers, width
                )
                outs.append(out + dot_nn(reach.astype(bf16), mv))
            mixed[t, s, :, cols] = jnp.where(lane < DH, outs[0], outs[1]).astype(bf16)
            return log_rows

        lse[s] = lax.fori_loop(0, HW // (2 * DH), pair_step, jnp.zeros((B, 2 * DH), f32))
        mx += start([remote(mixed.at[t, s], mixed.at[t, s], ms.at[s], mr.at[s], {"tp": 1 - t})])
        if s == 0:
            stage_b(2)
            stage_y(3)
        if s == 1:
            stage_b(3)
    stage_end(2)
    stage_end(3)
    if gather:
        wo_sent[0].wait_recv()
    for copy in mx:
        copy.wait_recv()
    for copy in started:
        copy.wait_send()


def forward(gather, hid, lengths, places, gain, shift, weights, qbias, cw, sw, fit):
    S, B, D = hid.shape
    HW = qbias.shape[1] // 3
    n = lax.axis_size("dp")
    L = B * lax.axis_size("ctx")
    NB = cw.shape[1]
    vm = pl.BlockSpec(memory_space=pltpu.VMEM)
    sm = pl.BlockSpec(memory_space=pltpu.SMEM)
    hb = pl.BlockSpec(memory_space=pl.ANY)
    out = [
        jax.ShapeDtypeStruct((S, B, D), bf16),
        jax.ShapeDtypeStruct((S, B, HW), bf16),
        jax.ShapeDtypeStruct((S, L, 2 * HW), bf16),
        jax.ShapeDtypeStruct((S, NB, 2 * HW), bf16),
        jax.ShapeDtypeStruct((S, B, 128), f32),
        jax.ShapeDtypeStruct((2, S, B, HW), bf16),
    ]
    out_specs = [vm] * 6
    sem = pltpu.SemaphoreType.DMA
    scratch = [
        pltpu.VMEM((S, B, D), bf16),
        pltpu.VMEM((S, B, D), bf16),
        pltpu.VMEM((B, 3 * B), f32),
    ]
    w_specs = [vm]
    if gather:
        FW = weights[2].shape[1]
        out += [
            jax.ShapeDtypeStruct((D, 3 * HW), bf16),
            jax.ShapeDtypeStruct((2, D, HW), bf16),
            jax.ShapeDtypeStruct((D, FW), bf16),
            jax.ShapeDtypeStruct((D, FW), bf16),
        ]
        out_specs += [vm, hb, hb, hb]
        w_specs = [vm, hb, hb, hb]
        scratch += [sem((4,))] + [sem((4, n - 1))] * 8 + [sem, sem]
    scratch += [sem((S,))] * 4 + [sem((S, 2))] * 2 + [sem((S,))] * 2
    return pl.pallas_call(
        lambda *refs: forward_kernel(gather, refs),
        out_shape=out,
        in_specs=[vm, sm, vm, vm, vm, *w_specs, vm, vm, vm, vm],
        out_specs=out_specs,
        scratch_shapes=scratch,
        compiler_params=pltpu.CompilerParams(
            collective_id=0, has_side_effects=True, vmem_limit_bytes=VMEM_LIMIT
        ),
        cost_estimate=pl.CostEstimate(flops=6_000_000_000, bytes_accessed=30_000_000, transcendentals=6_000_000),
        name="forward_part",
    )(hid, lengths, places, gain, shift, *weights, qbias, cw, sw, fit)


def quarter(c):
    return 2 * lax.rem(c, 2) + c // 2


class Reduction:
    def __init__(self, n, rows, full, half, half_in, own, own_in, sems):
        self.n, self.rows, self.piece = n, rows, rows // 4
        self.full, self.half, self.half_in, self.own, self.own_in = full, half, half_in, own, own_in
        self.sems = sems
        self.z, self.c, self.t, self.side, self.across, self.corner = place()
        self.started = []

    def at(self, offset, size):
        return pl.ds(pl.multiple_of(offset, 16), size)

    def send_side(self):
        two = 2 * self.piece
        core = lax.rem(self.c, 2)
        self.one = remote(
            self.full.at[:, self.at(two * (1 - core), two)], self.half_in, self.sems[0].at[0], self.sems[1].at[0], {"ctx": self.side}
        )
        self.one.start()
        self.started.append(self.one)

    def send_across(self):
        two, piece = 2 * self.piece, self.piece
        core, y = lax.rem(self.c, 2), self.c // 2
        self.one.wait_recv()
        for k in range(self.n):
            self.half[k] = (
                self.full[k, self.at(two * core, two)].astype(f32) + self.half_in[k].astype(f32)
            ).astype(bf16)
        self.two = remote(
            self.half.at[:, self.at(piece * (1 - y), piece)], self.own_in, self.sems[0].at[1], self.sems[1].at[1], {"ctx": self.across}
        )
        self.two.start()
        self.started.append(self.two)

    def take_across(self):
        y = self.c // 2
        self.two.wait_recv()
        for k in range(self.n):
            self.own[k] = (
                self.half[k, self.at(self.piece * y, self.piece)].astype(f32) + self.own_in[k].astype(f32)
            ).astype(bf16)

    def wait_sends(self):
        for copy in self.started:
            copy.wait_send()


def mlp_kernel(gather, refs):
    (hid, mixed, wo, wf, wp, obias, gain, shift, fbias, cot,
     residual, mlp_part, gres, gmixed, og, pg, fg, sums, fsum,
     *rest) = refs
    if gather:
        (low, act, gpre, gpart, gin, turned, glow, pfull, phalf, phalf_in, pown_in, ffull, fhalf, fhalf_in, fown_in,
         gs, gr, ps, pr, fs, fr) = rest
    else:
        low, act, gpre, gpart, gin, turned, glow, gs, gr = rest
        pfull, ffull = pg, fg
    z, c, t, side, across, corner = place()
    S, B, D = hid.shape
    FW = wf.shape[1]
    HW = mixed.shape[3]
    n, R = pfull.shape[:2]
    tile = 512
    enter([{"tp": 1 - t}] + ([{"ctx": side}, {"ctx": across}] if gather else []))
    fsum[...] = jnp.zeros_like(fsum)
    copies = []
    for s in range(S):
        branch = dot_nt(mixed[0, s], wo[0]) + dot_nt(mixed[1, s], wo[1])
        wide = hid[s].astype(f32) + branch + obias[...]
        residual[s] = wide
        value, _, _ = normalise(wide, gain[...], shift[...])
        low[s] = value.astype(bf16)

        def columns(j, carry, s=s):
            cols = pl.ds(pl.multiple_of(j * tile, tile), tile)
            pre = dot_nn(low[s], wf[:, cols]) + fbias[:, cols]
            square = pre * pre
            th = jnp.tanh(0.7978845608028654 * (pre + 0.044715 * (square * pre)))
            act[s, :, cols] = (0.5 * pre * (1.0 + th)).astype(bf16)
            slope = 0.5 * (1.0 + th) + (0.5 * pre) * (1.0 - th * th) * (
                0.7978845608028654 * (1.0 + 3.0 * 0.044715 * square)
            )
            grad = (dot_nn(cot[s], wp[:, cols]) * slope).astype(bf16)
            gpre[s, :, cols] = grad
            fsum[:, cols] += jnp.sum(grad.astype(f32), axis=0, keepdims=True)
            return carry

        lax.fori_loop(0, FW // tile, columns, 0)
        gpart[s] = dot_nt(gpre[s], wf[...]).astype(bf16)
        copies.append(remote(gpart.at[s], gin.at[s], gs.at[s], gr.at[s], {"tp": 1 - t}))
        copies[-1].start()

    def weight_grad(full, left, right, width, step):
        turned[...] = left.reshape(S * B, D).T

        def columns(j, carry):
            cols = pl.ds(pl.multiple_of(j * step, step), step)
            value = dot_nn(turned[...], right[:, :, cols].reshape(S * B, step)).astype(bf16)
            for k in range(n):
                full[k, :, cols] = value[k * R : (k + 1) * R]
            return carry

        lax.fori_loop(0, width // step, columns, 0)

    weight_grad(pfull, cot[...], act, FW, 256)
    if gather:
        proj = Reduction(n, R, pfull, phalf, phalf_in, pg, pown_in, (ps, pr))
        proj.send_side()
    weight_grad(ffull, low[...], gpre, FW, 256)
    if gather:
        fc = Reduction(n, R, ffull, fhalf, fhalf_in, fg, fown_in, (fs, fr))
        fc.send_side()
        proj.send_across()
    out_sum = jnp.zeros((1, D), f32)
    gain_sum = jnp.zeros((1, D), f32)
    shift_sum = jnp.zeros((1, D), f32)
    cot_sum = jnp.zeros((1, D), f32)
    for s in range(S):
        copies[s].wait_recv()
        grad = gpart[s].astype(f32) + gin[s].astype(f32)
        _, unit, r = normalise(residual[s], gain[...], shift[...])
        gain_sum += jnp.sum(grad * unit, axis=0, keepdims=True)
        shift_sum += jnp.sum(grad, axis=0, keepdims=True)
        a = grad * gain[...]
        wide_cot = cot[s].astype(f32)
        cot_sum += jnp.sum(wide_cot, axis=0, keepdims=True)
        total = wide_cot + r * (
            a - jnp.mean(a, axis=-1, keepdims=True) - unit * jnp.mean(a * unit, axis=-1, keepdims=True)
        )
        out_sum += jnp.sum(total, axis=0, keepdims=True)
        gres[s] = total
        glow[s] = total.astype(bf16)
        gmixed[s] = dot_nn(glow[s], wo[t]).astype(bf16)
        if s == 0 and gather:
            fc.send_across()
    sums[0:1] = out_sum
    sums[1:2] = gain_sum
    sums[2:3] = shift_sum
    sums[3:4] = cot_sum
    weight_grad(og, glow[...], mixed.at[t], HW, 384)
    for s in range(S):
        mlp_part[s] = dot_nt(act[s], wp[...]).astype(bf16)
    if gather:
        proj.take_across()
        fc.take_across()
        proj.wait_sends()
        fc.wait_sends()
    for copy in copies:
        copy.wait_send()


def mlp(gather, hid, mixed, wo, wf, wp, obias, gain, shift, fbias, cot):
    S, B, D = hid.shape
    HW = mixed.shape[3]
    FW = wf.shape[1]
    n = lax.axis_size("dp") if gather else 1
    R = D // n
    Q = R // 4
    vm = pl.BlockSpec(memory_space=pltpu.VMEM)
    sem = pltpu.SemaphoreType.DMA
    grad = (n, Q, FW) if gather else (n, R, FW)
    out = [
        jax.ShapeDtypeStruct((S, B, D), f32),
        jax.ShapeDtypeStruct((S, B, D), bf16),
        jax.ShapeDtypeStruct((S, B, D), f32),
        jax.ShapeDtypeStruct((S, B, HW), bf16),
        jax.ShapeDtypeStruct((n, R, HW), bf16),
        jax.ShapeDtypeStruct(grad, bf16),
        jax.ShapeDtypeStruct(grad, bf16),
        jax.ShapeDtypeStruct((4, D), f32),
        jax.ShapeDtypeStruct((1, FW), f32),
    ]
    scratch = [
        pltpu.VMEM((S, B, D), bf16),
        pltpu.VMEM((S, B, FW), bf16),
        pltpu.VMEM((S, B, FW), bf16),
        pltpu.VMEM((S, B, D), bf16),
        pltpu.VMEM((S, B, D), bf16),
        pltpu.VMEM((D, S * B), bf16),
        pltpu.VMEM((S, B, D), bf16),
    ]
    if gather:
        scratch += [
            pltpu.VMEM((n, R, FW), bf16),
            pltpu.VMEM((n, R // 2, FW), bf16),
            pltpu.VMEM((n, R // 2, FW), bf16),
            pltpu.VMEM((n, Q, FW), bf16),
        ] * 2
    scratch += [sem((S,)), sem((S,))]
    if gather:
        scratch += [sem((2,))] * 4
    return pl.pallas_call(
        lambda *refs: mlp_kernel(gather, refs),
        out_shape=out,
        in_specs=[vm] * 10,
        out_specs=[vm] * 9,
        scratch_shapes=scratch,
        compiler_params=pltpu.CompilerParams(
            collective_id=1, has_side_effects=True, vmem_limit_bytes=VMEM_LIMIT
        ),
        cost_estimate=pl.CostEstimate(flops=12_000_000_000, bytes_accessed=30_000_000, transcendentals=1_500_000),
        name="mlp_part",
    )(hid, mixed, wo, wf, wp, obias, gain, shift, fbias, cot)


def backward_kernel(gather, refs):
    (lengths, places, q, kv, mem, lse, gmixed, normed, wq, hid, gres, residual, mlp_part, pbias, gain, cw, sw, fit, sums, fsum,
     *rest) = refs
    if gather:
        (pown, fown, ofull, *rest) = rest
        (block_out, input_grad, small_out, wq_out, wo_out, wf_out, wp_out, *rest) = rest
    else:
        (block_out, input_grad, small_out, qfull, *rest) = rest
    (dkv, dmem, gqkv, hs1, hr1, hr2, m1in, m2out, m2in, gmem, turned, mlp_in, gnpart, gnin, bias, small,
     xs, xr, h1s, h1r, h2s, h2r, m1s, m1r, m2s, m2r, m3s, m3r, ns, nr, *rest) = rest
    if gather:
        (qfull, qhalf, qhalf_in, qown, qown_in, ohalf, ohalf_in, oown, oown_in,
         zin_q, zin_o, zin_f, zin_p, small_in, qs, qr, os_, or_, zs, zr, gs, gr, ss, sr) = rest
    z, c, t, side, across, corner = place()
    S, B, D = hid.shape
    HW = q.shape[2]
    NB = mem.shape[1]
    L = kv.shape[1]
    n, R = qfull.shape[:2]
    keys = 3 * B
    peers = [{"tp": 1 - t}, {"ctx": side}, {"ctx": across}]
    if gather:
        peers += [{"dp": lax.rem(z + i, n)} for i in range(1, n)]
    enter(peers)
    started = []

    def start(copy):
        copy.start()
        started.append(copy)
        return copy

    if gather:
        owns = {"q": qown, "o": oown, "f": fown, "p": pown}
        zins = {"q": zin_q, "o": zin_o, "f": zin_f, "p": zin_p}
        finals = {"q": wq_out, "o": wo_out, "f": wf_out, "p": wp_out}
        index = {"q": 0, "o": 1, "f": 2, "p": 3}
        Q = R // 4
        z_sent, g_sent = {}, {}

        def send_dp(g):
            j = index[g]
            z_sent[g] = [
                start(remote(owns[g].at[lax.rem(z + i, n)], zins[g].at[i - 1], zs.at[j, i - 1], zr.at[j, i - 1], {"dp": lax.rem(z + i, n)}))
                for i in range(1, n)
            ]

        def piece(g, device):
            return finals[g].at[pl.ds(pl.multiple_of(Q * quarter(device), 16), Q)]

        def take_dp(g):
            j = index[g]
            total = owns[g][z].astype(f32)
            for i in range(1, n):
                z_sent[g][i - 1].wait_recv()
                total = total + zins[g][i - 1].astype(f32)
            finals[g][pl.ds(pl.multiple_of(Q * quarter(c), 16), Q)] = total.astype(bf16)
            mine = piece(g, c)
            g_sent[g] = [
                start(remote(mine, mine, gs.at[j, 0], gr.at[j, 0], {"ctx": across})),
                start(remote(mine, mine, gs.at[j, 1], gr.at[j, 1], {"ctx": side})),
            ]

        def pass_on(g):
            j = index[g]
            g_sent[g][0].wait_recv()
            other = piece(g, across)
            g_sent[g].append(start(remote(other, other, gs.at[j, 2], gr.at[j, 2], {"ctx": side})))

        def take_all(g):
            g_sent[g][1].wait_recv()
            g_sent[g][2].wait_recv()

        send_dp("p")
        send_dp("f")
        out = Reduction(n, R, ofull, ohalf, ohalf_in, oown, oown_in, (os_, or_))
        out.send_side()

    mlp_sent = [
        start(remote(mlp_part.at[s], mlp_in.at[s], xs.at[s], xr.at[s], {"tp": 1 - t})) for s in range(S)
    ]

    key_start = pl.multiple_of(jnp.maximum(c - 2, 0) * B, B)
    lane = lanes((1, 2 * DH), 1)
    scaled = half_lanes(SCALE)
    plain = half_lanes(1.0)
    centers = (lanes((1, NB), 1).astype(f32) + 0.5) * (1.0 / NB)
    width = 1.0 / NB
    small[0] = jnp.zeros(small.shape[1:], f32)
    half = HW

    def attend_back(s):
        bias[...] = mask_bias(lengths, s, c, B, key_start, keys)

        def pair_step(p, carry):
            cols = pl.ds(pl.multiple_of(p * 2 * DH, 2 * DH), 2 * DH)
            vcols = pl.ds(pl.multiple_of(HW + p * 2 * DH, 2 * DH), 2 * DH)
            window = pl.ds(key_start, keys)
            qp = q[s, :, cols]
            gp = gmixed[s, :, cols]
            kp = kv[s, window, cols]
            vp = kv[s, window, vcols]
            mk = mem[s, :, cols]
            mv = mem[s, :, vcols]
            q_turned = (qp * SCALE).T
            g_turned = gp.T
            logs = lse[s]
            grad_q, dk, dv, dmk, dmv = [], [], [], [], []
            for h in range(2):
                row = 2 * p + h
                part = slice(h * DH, (h + 1) * DH)
                qh = qp * scaled[h]
                gh = gp * plain[h]
                log_total = jnp.sum(jnp.where(lane == row, logs, 0.0), axis=-1, keepdims=True)
                share = jnp.exp(dot_nt(qh, kp) + bias[...] - log_total)
                grad_share = dot_nt(gh, vp)
                delta = jnp.sum(share * grad_share, axis=-1, keepdims=True)
                grad_score = (share * (grad_share - delta)).astype(bf16)
                mem_scores = dot_nt(qh, mk)
                cw_row = cw[pl.ds(row, 1)]
                sw_row = sw[pl.ds(row, 1)]
                reach, mu, inv, diff, spread_logit = reach_terms(mem_scores, cw_row, sw_row, centers, width)
                grad_reach = dot_nt(gh, mv) * reach
                scaled_diff = diff * inv
                grad_mu = -jnp.sum(grad_reach * scaled_diff, axis=-1, keepdims=True)
                grad_var = jnp.sum(
                    grad_reach * (0.5 * scaled_diff * scaled_diff - 0.5 * inv), axis=-1, keepdims=True
                )
                gc = grad_mu * mu * (1.0 - mu)
                gw = SPREAD * grad_var * (1.0 / (1.0 + jnp.exp(-spread_logit)))
                small[0, pl.ds(8 + row, 1), 0:NB] += jnp.sum(gc * mem_scores, axis=0, keepdims=True)
                small[0, pl.ds(8 + row, 1), NB : 2 * NB] += jnp.sum(gw * mem_scores, axis=0, keepdims=True)
                grad_mem = (gc * cw_row + gw * sw_row).astype(bf16)
                grad_q.append((dot_nn(grad_score, kp) + dot_nn(grad_mem, mk)) * SCALE)
                dk.append(dot_nn(q_turned[part], grad_score))
                dv.append(dot_nn(g_turned[part], share.astype(bf16)))
                dmk.append(dot_nn(q_turned[part], grad_mem))
                dmv.append(dot_nn(g_turned[part], reach.astype(bf16)))
            gqkv[s, :, cols] = jnp.where(lane < DH, grad_q[0], grad_q[1]).astype(bf16)
            for h in range(2):
                rows = pl.ds(pl.multiple_of((2 * p + h) * DH, DH), DH)
                vrows = pl.ds(pl.multiple_of(HW + (2 * p + h) * DH, DH), DH)
                dkv[s, rows] = dk[h]
                dkv[s, vrows] = dv[h]
                dmem[s, rows] = dmk[h]
                dmem[s, vrows] = dmv[h]
            return carry

        lax.fori_loop(0, HW // (2 * DH), pair_step, 0)

    core = lax.rem(c, 2)
    y = c // 2
    own_half = pl.ds(pl.multiple_of(core * half, 16), half)
    side_half = pl.ds(pl.multiple_of((1 - core) * half, 16), half)
    give = pl.ds(pl.multiple_of(B * (1 - core * (1 - y)), 128), B)
    take = pl.ds(pl.multiple_of(B * lax.rem(c, 3), 128), B)
    own = pl.ds(pl.multiple_of(c * B - key_start, 128), B)
    one, two, three, first, second = {}, {}, {}, {}, {}

    def give_side(s):
        one[s] = start(remote(dmem.at[s, side_half], m1in.at[s], m1s.at[s], m1r.at[s], {"ctx": side}))
        hs1[s] = dkv[s, :, give].astype(bf16)
        first[s] = start(remote(hs1.at[s], hr1.at[s], h1s.at[s], h1r.at[s], {"ctx": side}))

    def second_copy(s):
        return remote(hr1.at[s], hr2.at[s], h2s.at[s], h2r.at[s], {"ctx": across})

    def give_across(s):
        one[s].wait_recv()
        m2out[s] = (dmem[s, own_half] + m1in[s]).astype(bf16)
        two[s] = start(remote(m2out.at[s], m2in.at[s], m2s.at[s], m2r.at[s], {"ctx": across}))
        first[s].wait_recv()
        dkv[s, :, take] = dkv[s, :, take] + hr1[s].astype(f32)

        @pl.when(y == 1)
        def _():
            hr1[s] = dkv[s, :, 0:B].astype(bf16)
            second_copy(s).start()

    def memory_back(s):
        two[s].wait_recv()
        gmem[s, own_half] = (m2out[s].astype(f32) + m2in[s].astype(f32)).astype(bf16)
        three[s] = start(remote(gmem.at[s, own_half], gmem.at[s, own_half], m3s.at[s], m3r.at[s], {"ctx": side}))

    M = places.shape[0]

    def finish_rows(s):
        three[s].wait_recv()
        token = c * B + lanes((1, B), 1)
        sticky = jnp.where(token == places[:, s : s + 1], 1.0, 0.0).astype(bf16)
        even = lanes((M, 1), 0) * L // M + L // (2 * M)
        steady = jnp.where(token == even, 1.0, 0.0).astype(bf16)
        spread_fit = dot_nn(fit[:, :M], sticky) + dot_nn(fit[:, M:], steady)
        high = spread_fit.astype(bf16)
        low = (spread_fit - high.astype(f32)).astype(bf16)
        dkv[s, :, own] = dkv[s, :, own] + dot_nn(gmem[s], high) + dot_nn(gmem[s], low)

        @pl.when(y == 0)
        def _():
            second_copy(s).wait_recv()
            dkv[s, :, own] = dkv[s, :, own] + hr2[s].astype(f32)

        gqkv[s, :, HW:] = dkv[s, :, own].T.astype(bf16)
        gnpart[s] = dot_nt(gqkv[s], wq[...]).astype(bf16)
        return start(remote(gnpart.at[s], gnin.at[s], ns.at[s], nr.at[s], {"tp": 1 - t}))

    def finish_block(s):
        mlp_sent[s].wait_recv()
        total = mlp_part[s].astype(f32) + mlp_in[s].astype(f32)
        block_out[s] = (residual[s] + total + pbias[...]).astype(bf16)

    attend_back(0)
    give_side(0)
    if gather:
        out.send_across()
        take_dp("p")
    attend_back(1)
    give_side(1)
    give_across(0)
    if gather:
        out.take_across()
        send_dp("o")
        pass_on("p")
        take_dp("f")
    attend_back(2)
    give_side(2)
    give_across(1)
    memory_back(0)
    give_across(2)
    turned[...] = normed[...].reshape(S * B, D).T
    memory_back(1)
    sent = [finish_rows(0)]
    memory_back(2)
    sent.append(finish_rows(1))
    sent.append(finish_rows(2))

    step = 384

    def columns(j, carry):
        cols = pl.ds(pl.multiple_of(j * step, 128), step)
        value = dot_nn(turned[...], gqkv[:, :, cols].reshape(S * B, step)).astype(bf16)
        for k in range(n):
            qfull[k, :, cols] = value[k * R : (k + 1) * R]
        return carry

    lax.fori_loop(0, 3 * HW // step, columns, 0)
    if gather:
        qkv = Reduction(n, R, qfull, qhalf, qhalf_in, qown, qown_in, (qs, qr))
        qkv.send_side()
        pass_on("f")
    small[0, 6:7, 0 : 3 * HW] = jnp.sum(gqkv[...].reshape(S * B, 3 * HW).astype(f32), axis=0, keepdims=True)
    small[0, 2:6, 0:D] = sums[...]
    small[0, 7:8] = fsum[...]
    if gather:
        qkv.send_across()
        take_dp("o")
    finish_block(0)
    finish_block(1)
    finish_block(2)
    gain_sum = jnp.zeros((1, D), f32)
    shift_sum = jnp.zeros((1, D), f32)
    for s in range(S):
        sent[s].wait_recv()
        grad = gnpart[s].astype(f32) + gnin[s].astype(f32)
        _, unit, r = normalise(hid[s].astype(f32), gain[...], gain[...])
        gain_sum += jnp.sum(grad * unit, axis=0, keepdims=True)
        shift_sum += jnp.sum(grad, axis=0, keepdims=True)
        a = grad * gain[...]
        back = r * (a - jnp.mean(a, axis=-1, keepdims=True) - unit * jnp.mean(a * unit, axis=-1, keepdims=True))
        input_grad[s] = (gres[s] + back).astype(bf16)
        if s == 0 and gather:
            qkv.take_across()
            send_dp("q")
            pass_on("o")
    small[0, 0:1, 0:D] = gain_sum
    small[0, 1:2, 0:D] = shift_sum
    if gather:
        near = z + 1 - 2 * lax.rem(z, 2)
        steps = [{"ctx": side}, {"ctx": across}, {"dp": near}, {"dp": lax.rem(z + 2, 4)}]
        for k, device in enumerate(steps):
            copy = start(remote(small.at[k], small_in.at[k], ss.at[k], sr.at[k], device))
            if k == 1:
                take_dp("q")
            if k == 3:
                pass_on("q")
            copy.wait_recv()
            total = small[k] + small_in[k]
            if k < 3:
                small[k + 1] = total
            else:
                small_out[...] = total
    if gather:
        for g in ("p", "f", "o", "q"):
            take_all(g)
        out.wait_sends()
        qkv.wait_sends()
    else:
        small_out[...] = small[0]
    for s in range(S):

        @pl.when(y == 1)
        def _(s=s):
            second_copy(s).wait_send()

    for copy in started:
        copy.wait_send()


def backward(gather, lengths, places, q, kv, mem, lse, gmixed, normed, wq, hid, gres, residual, mlp_part, pbias, gain, cw, sw,
             fit, sums, fsum, owned):
    S, B, D = hid.shape
    HW = q.shape[2]
    FW = fsum.shape[1]
    L = kv.shape[1]
    H, NB = cw.shape
    n = lax.axis_size("dp") if gather else 1
    R = D // n
    Q = R // 4
    rows = -(-(8 + H) // 8) * 8
    vm = pl.BlockSpec(memory_space=pltpu.VMEM)
    sm = pl.BlockSpec(memory_space=pltpu.SMEM)
    sem = pltpu.SemaphoreType.DMA
    out = [
        jax.ShapeDtypeStruct((S, B, D), bf16),
        jax.ShapeDtypeStruct((S, B, D), bf16),
        jax.ShapeDtypeStruct((rows, FW), f32),
    ]
    if gather:
        out += [jax.ShapeDtypeStruct((R, w), bf16) for w in (3 * HW, HW, FW, FW)]
    else:
        out += [jax.ShapeDtypeStruct((n, R, 3 * HW), bf16)]
    scratch = [
        pltpu.VMEM((S, 2 * HW, 3 * B), f32),
        pltpu.VMEM((S, 2 * HW, NB), f32),
        pltpu.VMEM((S, B, 3 * HW), bf16),
        *[pltpu.VMEM((S, 2 * HW, B), bf16)] * 3,
        pltpu.VMEM((S, HW, NB), f32),
        pltpu.VMEM((S, HW, NB), bf16),
        pltpu.VMEM((S, HW, NB), bf16),
        pltpu.VMEM((S, 2 * HW, NB), bf16),
        pltpu.VMEM((D, S * B), bf16),
        *[pltpu.VMEM((S, B, D), bf16)] * 3,
        pltpu.VMEM((B, 3 * B), f32),
        pltpu.VMEM((4, rows, FW), f32),
        *[sem((S,))] * 14,
    ]
    if gather:
        scratch += [
            pltpu.VMEM((n, R, 3 * HW), bf16),
            *[pltpu.VMEM((n, R // 2, 3 * HW), bf16)] * 2,
            *[pltpu.VMEM((n, Q, 3 * HW), bf16)] * 2,
            *[pltpu.VMEM((n, R // 2, HW), bf16)] * 2,
            *[pltpu.VMEM((n, Q, HW), bf16)] * 2,
            *[pltpu.VMEM((n - 1, Q, w), bf16) for w in (3 * HW, HW, FW, FW)],
            pltpu.VMEM((4, rows, FW), f32),
            *[sem((2,))] * 4,
            *[sem((4, n - 1))] * 2,
            *[sem((4, 3))] * 2,
            *[sem((4,))] * 2,
        ]
    args = [lengths, places, q, kv, mem, lse, gmixed, normed, wq, hid, gres, residual, mlp_part, pbias, gain, cw, sw, fit, sums,
            fsum, *owned]
    return pl.pallas_call(
        lambda *refs: backward_kernel(gather, refs),
        out_shape=out,
        in_specs=[sm] + [vm] * (len(args) - 1),
        out_specs=[vm] * len(out),
        scratch_shapes=scratch,
        compiler_params=pltpu.CompilerParams(
            collective_id=2, has_side_effects=True, vmem_limit_bytes=VMEM_LIMIT
        ),
        cost_estimate=pl.CostEstimate(flops=12_000_000_000, bytes_accessed=40_000_000, transcendentals=6_000_000),
        name="backward_part",
    )(*args)


def per_device(hidden_in, doc_lengths, sticky_places, attn_gain, attn_shift, qkv_weight, qkv_bias, center_weight,
               spread_weight, out_weight, out_bias, mlp_gain, mlp_shift, fc_weight, fc_bias, proj_weight, proj_bias,
               cotangent):
    S, B, D = hidden_in.shape
    n = lax.axis_size("dp")
    HW = qkv_bias.shape[1]
    H, NB = center_weight.shape
    M = sticky_places.shape[1]
    fit = jnp.asarray(ridge_fit(NB, 2 * M))
    places = sticky_places.T
    gather = n == 4 and D % (64 * n) == 0
    weights = [qkv_weight.reshape(D // n, 3 * HW), out_weight.T, fc_weight, proj_weight.T]
    if not gather:
        full = [lax.all_gather(w, "dp", axis=0, tiled=True) for w in weights]
        weights = full[:1]
    made = forward(gather, hidden_in, doc_lengths, places, attn_gain[None], attn_shift[None], weights,
                   qkv_bias.reshape(1, 3 * HW), center_weight, spread_weight, fit)
    normed, q, kv, mem, lse, mixed = made[:6]
    if gather:
        wq, wo, wf, wp = made[6:]
    else:
        wq, wo, wf, wp = full
        wo = lax.all_gather(wo, "tp", axis=0)
    made = mlp(gather, hidden_in, mixed, wo, wf, wp, out_bias[None], mlp_gain[None], mlp_shift[None], fc_bias[None], cotangent)
    residual, mlp_part, gres, gmixed, og, pg, fg, sums, fsum = made
    owned = [pg, fg, og] if gather else []
    made = backward(gather, doc_lengths, places, q, kv, mem, lse, gmixed, normed, wq, hidden_in, gres, residual, mlp_part,
                    proj_bias[None], attn_gain[None], center_weight, spread_weight, fit, sums, fsum, owned)
    block_out, input_grad, small = made[:3]
    if gather:
        wq_grad, wo_grad, wf_grad, wp_grad = [g.astype(f32) for g in made[3:]]
    else:
        small = lax.psum(small, ("dp", "ctx"))

        def reduced(grad):
            part = lax.psum_scatter(grad.reshape(D, -1), "dp", scatter_dimension=0, tiled=True)
            return lax.psum(part, "ctx").astype(f32)

        wq_grad, wo_grad, wf_grad, wp_grad = [reduced(g) for g in (made[3], og, fg, pg)]
    return (
        block_out,
        input_grad,
        small[0, :D],
        small[1, :D],
        wq_grad.reshape(D // n, 3, HW),
        small[6, : 3 * HW].reshape(3, HW),
        small[8 : 8 + H, :NB],
        small[8 : 8 + H, NB : 2 * NB],
        wo_grad.T,
        small[2, :D],
        small[3, :D],
        small[4, :D],
        wf_grad,
        small[7],
        wp_grad.T,
        small[5, :D],
    )


def solution(mesh):
    in_specs = (
        P("dp", "ctx", None),
        P("dp", None),
        P("dp", None),
        P(),
        P(),
        P("dp", None, "tp"),
        P(None, "tp"),
        P("tp", None),
        P("tp", None),
        P("tp", "dp"),
        P(),
        P(),
        P(),
        P("dp", "tp"),
        P("tp"),
        P("tp", "dp"),
        P(),
        P("dp", "ctx", None),
    )
    out_specs = (
        P("dp", "ctx", None),
        P("dp", "ctx", None),
        P(),
        P(),
        P("dp", None, "tp"),
        P(None, "tp"),
        P("tp", None),
        P("tp", None),
        P("tp", "dp"),
        P(),
        P(),
        P(),
        P("dp", "tp"),
        P("tp"),
        P("tp", "dp"),
        P(),
    )
    return jax.shard_map(
        per_device, mesh=mesh, in_specs=in_specs, out_specs=out_specs, check_vma=False
    )
```

```python
import functools

import jax
import jax.numpy as jnp
import numpy as np
from jax import lax
from jax.experimental import pallas as pl
from jax.experimental.pallas import tpu as pltpu
from jax.sharding import PartitionSpec as P

DH = 64
WINDOW = 512
EPS = 1e-05
SPREAD = 0.02
SCALE = DH ** (-0.5)
VMEM_LIMIT = 60 * 1024 * 1024

bf16 = jnp.bfloat16
f32 = jnp.float32
MESH = pl.DeviceIdType.MESH


def dot_nn(a, b):
    return lax.dot_general(a, b, (((1,), (0,)), ((), ())), preferred_element_type=f32)


def dot_nt(a, b):
    return lax.dot_general(a, b, (((1,), (1,)), ((), ())), preferred_element_type=f32)


def dot_tn(a, b):
    return lax.dot_general(a, b, (((0,), (0,)), ((), ())), preferred_element_type=f32)


def ridge_fit(basis_count, sample_count):
    centers = (np.arange(basis_count) + 0.5) / basis_count
    times = (np.arange(sample_count) + 0.5) / sample_count
    width = 1.0 / basis_count
    design = np.exp(-np.square(times[None, :] - centers[:, None]) / (2.0 * width * width))
    gram = design @ design.T + 0.5 * np.eye(basis_count)
    return np.linalg.solve(gram, design).astype(bf16)


def place():
    c = lax.axis_index("ctx")
    side = c + 1 - 2 * lax.rem(c, 2)
    across = lax.rem(c + 2, 4)
    corner = lax.rem(side + 2, 4)
    return lax.axis_index("dp"), c, lax.axis_index("tp"), side, across, corner


def enter(devices):
    barrier = pltpu.get_barrier_semaphore()
    for device in devices:
        pl.semaphore_signal(barrier, inc=1, device_id=device, device_id_type=MESH)
    pl.semaphore_wait(barrier, len(devices))


def remote(src, dst, send, recv, device):
    return pltpu.make_async_remote_copy(
        src_ref=src,
        dst_ref=dst,
        send_sem=send,
        recv_sem=recv,
        device_id=device,
        device_id_type=MESH,
    )


def normalise(x, gain, shift):
    mean = jnp.mean(x, axis=-1, keepdims=True)
    centred = x - mean
    r = lax.rsqrt(jnp.mean(centred * centred, axis=-1, keepdims=True) + EPS)
    n = centred * r
    return n * gain + shift, n, r


def lowest_key(lengths, s, pos):
    low = jnp.maximum(pos - (WINDOW - 1), 0)
    end = jnp.int32(0)
    for e in range(lengths.shape[1]):
        end = end + lengths[s, e]
        low = jnp.maximum(low, jnp.where(pos >= end, end, 0))
    return low


def lanes(shape, dim):
    return lax.broadcasted_iota(jnp.int32, shape, dim)


def half_lanes(scale):
    lane = lanes((1, 2 * DH), 1)
    return [
        jnp.where(lane < DH, scale, 0.0).astype(bf16),
        jnp.where(lane >= DH, scale, 0.0).astype(bf16),
    ]


def mask_bias(lengths, s, c, rows, key_start, keys):
    pos = c * rows + lanes((rows, 1), 0)
    low = lowest_key(lengths, s, pos)
    key_pos = key_start + lanes((1, keys), 1)
    return jnp.where((key_pos <= pos) & (key_pos >= low), 0.0, -1e30)


def fit_at(fit, places, s, tokens, length):
    M = places.shape[1]
    sticky = jnp.where(tokens == places[s : s + 1, :], 1.0, 0.0).astype(bf16)
    even = lanes((1, M), 1) * length // M + length // (2 * M)
    steady = jnp.where(tokens == even, 1.0, 0.0).astype(bf16)
    value = dot_nt(fit[:, :M], sticky) + dot_nt(fit[:, M:], steady)
    high = value.astype(bf16)
    return high, (value - high.astype(f32)).astype(bf16)


def reach_terms(scores, center_row, spread_row, centers, width):
    center_logit = jnp.sum(scores * center_row, axis=-1, keepdims=True)
    spread_logit = jnp.sum(scores * spread_row, axis=-1, keepdims=True)
    mu = 1.0 / (1.0 + jnp.exp(-center_logit))
    grown = jnp.exp(spread_logit)
    var = SPREAD * jnp.log(1.0 + grown) + width * width
    inv = 1.0 / var
    diff = mu - centers
    reach = (width * lax.rsqrt(var)) * jnp.exp(-(diff * diff) * (0.5 * inv))
    return reach, mu, inv, diff, spread_logit


def forward_kernel(gather, refs):
    n = lax.axis_size("dp")
    if gather:
        (hid, lengths, places, gain, shift, wq_sh, wo_sh, wf_sh, wp_sh, qbias, cw, sw, fit,
         normed_out, q_out, kv_out, mem, lse, mixed, wq_out, wo, wf, wp,
         normed, q, kv, hoth, noth, bias, os_, hys, hyr, hxs, hxr, ks, kr, ms, mr,
         wq, lsem, zs, zr, ys, yr, as_, ar, bs, br, oxs, oxr, lzs, lzr, lys, lyr, las, lar, lbs, lbr) = refs
    else:
        (hid, lengths, places, gain, shift, wq, qbias, cw, sw, fit,
         normed_out, q_out, kv_out, mem, lse, mixed,
         normed, q, kv, hoth, noth, bias, os_, hys, hyr, hxs, hxr, ks, kr, ms, mr) = refs
    z, c, t, side, across, corner = place()
    S, B, D = hid.shape
    HW = q.shape[2]
    NB = mem.shape[1]
    L = kv.shape[1]
    half = B // 2
    peers = [{"ctx": side}, {"ctx": across}, {"tp": 1 - t}]
    if gather:
        R = D // n
        Q = R // 4
        shards = [wq_sh, wo_sh, wf_sh, wp_sh]
        whole = [wq, wo.at[t], wf, wp, wo.at[1 - t]]
        peers += [{"dp": lax.rem(z + i, n)} for i in range(1, n)]
    enter(peers)

    started, kept = [], []

    def start(copies):
        for copy in copies:
            copy.start()
        started.extend(copies)
        return copies

    def keep(src, dst):
        copy = pltpu.make_async_copy(src, dst, os_.at[len(kept)])
        copy.start()
        kept.append(copy)

    if gather:
        groups = range(1, 5)

        def rows(g, owner, quarter):
            return whole[g].at[pl.ds(pl.multiple_of(R * owner + Q * quarter, 16), Q)]

        def source(i):
            return lax.rem(z + n - i, n)

        def first_z():
            src = wq_sh.at[pl.ds(pl.multiple_of(Q * c, 16), Q)]
            return start([
                remote(src, rows(0, z, c), zs.at[i - 1], zr.at[i - 1], {"dp": lax.rem(z + i, n)}) for i in range(1, n)
            ])

        def first_y(sent):
            for copy in sent:
                copy.wait_recv()
            here = [rows(0, source(i), c) for i in range(1, n)]
            over = start([remote(w, w, ys.at[i], yr.at[i], {"ctx": across}) for i, w in enumerate(here)])
            beside = start([remote(w, w, as_.at[i], ar.at[i], {"ctx": side}) for i, w in enumerate(here)])
            return over, beside

        def first_side(over):
            for copy in over:
                copy.wait_recv()
            there = [rows(0, source(i), across) for i in range(1, n)]
            return start([remote(w, w, bs.at[i], br.at[i], {"ctx": side}) for i, w in enumerate(there)])

        def sends(way, r):
            return ((z < n - 1) & (z >= r)) if way == 0 else ((z > 0) & (z + r < n))

        def takes(way, r):
            return (z > r) if way == 0 else (z + r < n - 1)

        def line_z(g, way, r):
            owner = z - r if way == 0 else z + r
            to = z + 1 if way == 0 else z - 1
            dst = rows(g, owner, c)
            src = shards[g].at[pl.ds(pl.multiple_of(Q * c, 16), Q)] if r == 0 and g < 4 else dst
            return remote(src, dst, lzs.at[g - 1, way, r], lzr.at[g - 1, way, r], {"dp": to})

        def line_copy(g, way, r, sems, quarter, device):
            part = rows(g, z - 1 - r if way == 0 else z + 1 + r, quarter)
            return remote(part, part, sems[0].at[g - 1, way, r], sems[1].at[g - 1, way, r], {"ctx": device})

        def line_y(g, way, r):
            return line_copy(g, way, r, (lys, lyr), c, across)

        def line_a(g, way, r):
            return line_copy(g, way, r, (las, lar), c, side)

        def line_b(g, way, r):
            return line_copy(g, way, r, (lbs, lbr), across, side)

        def line_send(r):
            for way in range(2):

                @pl.when(sends(way, r))
                def _(way=way):
                    for g in groups:
                        line_z(g, way, r).start()

        def line_take(r):
            for way in range(2):

                @pl.when(takes(way, r))
                def _(way=way):
                    for g in groups:
                        line_z(g, way, r).wait_recv()
                        line_y(g, way, r).start()
                        line_a(g, way, r).start()

        def line_pass(r):
            for way in range(2):

                @pl.when(takes(way, r))
                def _(way=way):
                    for g in groups:
                        line_y(g, way, r).wait_recv()
                        line_b(g, way, r).start()

        def line_end(r):
            for way in range(2):

                @pl.when(takes(way, r))
                def _(way=way):
                    for g in groups:
                        line_a(g, way, r).wait_recv()
                        line_b(g, way, r).wait_recv()
                        line_y(g, way, r).wait_send()
                        line_a(g, way, r).wait_send()
                        line_b(g, way, r).wait_send()

                @pl.when(sends(way, r))
                def _(way=way):
                    for g in groups:
                        line_z(g, way, r).wait_send()
    else:

        def line_send(r):
            pass

        line_take = line_pass = line_end = line_send

    def hidden_y(s):
        piece = pl.ds(pl.multiple_of(half * t, 16), half)
        return remote(hid.at[s, piece], hoth.at[s, piece], hys.at[s], hyr.at[s], {"ctx": across})

    def hidden_x(s):
        piece = pl.ds(pl.multiple_of(half * t, 16), half)
        return remote(hoth.at[s, piece], hoth.at[s, piece], hxs.at[s], hxr.at[s], {"tp": 1 - t})

    def block(s, owner):
        return kv.at[s, pl.ds(pl.multiple_of(owner * B, B), B)]

    def kv_copy(s, which):
        owner = c if which == 0 else across
        return remote(block(s, owner), block(s, owner), ks.at[s, which], kr.at[s, which], {"ctx": side})

    if gather:
        z_sent = first_z()
    hy = start([hidden_y(s) for s in range(S)])
    if gather:
        mine = pl.ds(pl.multiple_of(R * z, 16), R)
        owned = [pltpu.make_async_copy(shards[g], whole[g].at[mine], lsem.at[g]) for g in range(4)]
        for copy in owned:
            copy.start()
        crossed = start([remote(wo_sh, wo.at[t, mine], oxs, oxr, {"tp": 1 - t})])[0]

    gain_row = gain[...]
    shift_row = shift[...]
    for s in range(S):
        low, _, _ = normalise(hid[s].astype(f32), gain_row, shift_row)
        normed[s] = low.astype(bf16)
    keep(normed, normed_out)
    if gather:
        over, beside = first_y(z_sent)
        crossed.wait_recv()
    line_send(0)
    hx = []
    for s in range(S):
        hy[s].wait_recv()
        hx += start([hidden_x(s)])
    if gather:
        last = first_side(over)
    for s in range(S):
        hx[s].wait_recv()
        low, _, _ = normalise(hoth[s].astype(f32), gain_row, shift_row)
        noth[s] = low.astype(bf16)
    line_take(0)
    line_send(1)
    if gather:
        for copy in beside + last:
            copy.wait_recv()
        owned[0].wait()
        keep(wq, wq_out)
    kvs = []
    for which, rows_in, owner in ((0, normed, c), (1, noth, across)):
        for s in range(S):
            for k in (1, 2):
                part = dot_nn(rows_in[s], wq[:, k * HW : (k + 1) * HW]) + qbias[k : k + 1]
                kv[s, pl.ds(pl.multiple_of(owner * B, B), B), (k - 1) * HW : k * HW] = part.astype(bf16)
            kvs += start([kv_copy(s, which)])
    for s in range(S):
        q[s] = (dot_nn(normed[s], wq[:, :HW]) + qbias[0:1]).astype(bf16)
    keep(q, q_out)
    line_pass(0)
    line_take(1)
    line_send(2)

    key_start = pl.multiple_of(jnp.maximum(c - 2, 0) * B, B)
    keys = 3 * B
    centers = (lanes((1, NB), 1).astype(f32) + 0.5) * (1.0 / NB)
    width = 1.0 / NB
    lane = lanes((1, 2 * DH), 1)
    scaled = half_lanes(SCALE)
    mx = []
    for s in range(S):
        kvs[s].wait_recv()
        kvs[S + s].wait_recv()
        keep(kv.at[s], kv_out.at[s])
        high, rest = fit_at(fit, places, s, lanes((L, 1), 0), L)
        mem[s] = (dot_nn(high, kv[s]) + dot_nn(rest, kv[s])).astype(bf16)
        bias[...] = mask_bias(lengths, s, c, B, key_start, keys)

        def pair_step(p, log_rows, s=s):
            cols = pl.ds(pl.multiple_of(p * 2 * DH, 2 * DH), 2 * DH)
            vcols = pl.ds(pl.multiple_of(HW + p * 2 * DH, 2 * DH), 2 * DH)
            window = pl.ds(key_start, keys)
            qp = q[s, :, cols]
            kp = kv[s, window, cols]
            vp = kv[s, window, vcols]
            mk = mem[s, :, cols]
            mv = mem[s, :, vcols]
            outs = []
            for h in range(2):
                qh = qp * scaled[h]
                scores = dot_nt(qh, kp) + bias[...]
                top = jnp.max(scores, axis=-1, keepdims=True)
                e = jnp.exp(scores - top)
                total = jnp.sum(e, axis=-1, keepdims=True)
                share = (e * (1.0 / total)).astype(bf16)
                out = dot_nn(share, vp)
                log_rows = jnp.where(lane == 2 * p + h, top + jnp.log(total), log_rows)
                mem_scores = dot_nt(qh, mk)
                reach, _, _, _, _ = reach_terms(
                    mem_scores, cw[pl.ds(2 * p + h, 1)], sw[pl.ds(2 * p + h, 1)], centers, width
                )
                outs.append(out + dot_nn(reach.astype(bf16), mv))
            mixed[t, s, :, cols] = jnp.where(lane < DH, outs[0], outs[1]).astype(bf16)
            return log_rows

        lse[s] = lax.fori_loop(0, HW // (2 * DH), pair_step, jnp.zeros((B, 2 * DH), f32))
        mx += start([remote(mixed.at[t, s], mixed.at[t, s], ms.at[s], mr.at[s], {"tp": 1 - t})])
        if s == 0:
            line_take(2)
            line_pass(1)
        if s == 1:
            line_pass(2)
    for r in range(n - 1 if gather else 0):
        line_end(r)
    if gather:
        for copy in owned[1:]:
            copy.wait()
    for copy in mx:
        copy.wait_recv()
    for copy in started:
        copy.wait_send()
    for copy in kept:
        copy.wait()


def forward(gather, hid, lengths, places, gain, shift, weights, qbias, cw, sw, fit):
    S, B, D = hid.shape
    HW = qbias.shape[1]
    n = lax.axis_size("dp")
    L = B * lax.axis_size("ctx")
    NB = cw.shape[1]
    vm = pl.BlockSpec(memory_space=pltpu.VMEM)
    sm = pl.BlockSpec(memory_space=pltpu.SMEM)
    hb = pl.BlockSpec(memory_space=pl.ANY)
    out = [
        jax.ShapeDtypeStruct((S, B, D), bf16),
        jax.ShapeDtypeStruct((S, B, HW), bf16),
        jax.ShapeDtypeStruct((S, L, 2 * HW), bf16),
        jax.ShapeDtypeStruct((S, NB, 2 * HW), bf16),
        jax.ShapeDtypeStruct((S, B, 128), f32),
        jax.ShapeDtypeStruct((2, S, B, HW), bf16),
    ]
    out_specs = [hb] * 3 + [vm] * 3
    sem = pltpu.SemaphoreType.DMA
    scratch = [
        pltpu.VMEM((S, B, D), bf16),
        pltpu.VMEM((S, B, HW), bf16),
        pltpu.VMEM((S, L, 2 * HW), bf16),
        pltpu.VMEM((S, B, D), bf16),
        pltpu.VMEM((S, B, D), bf16),
        pltpu.VMEM((B, 3 * B), f32),
        sem((S + 3,)),
        *[sem((S,))] * 4,
        *[sem((S, 2))] * 2,
        *[sem((S,))] * 2,
    ]
    w_specs = [vm]
    if gather:
        FW = weights[2].shape[1]
        out += [
            jax.ShapeDtypeStruct((D, 3 * HW), bf16),
            jax.ShapeDtypeStruct((2, D, HW), bf16),
            jax.ShapeDtypeStruct((D, FW), bf16),
            jax.ShapeDtypeStruct((D, FW), bf16),
        ]
        out_specs += [hb] * 4
        w_specs = [vm] * 4
        scratch += [
            pltpu.VMEM((D, 3 * HW), bf16),
            sem((4,)),
            *[sem((n - 1,))] * 8,
            sem,
            sem,
            *[sem((4, 2, n - 1))] * 8,
        ]
    return pl.pallas_call(
        lambda *refs: forward_kernel(gather, refs),
        out_shape=out,
        in_specs=[vm, sm, vm, vm, vm, *w_specs, vm, vm, vm, vm],
        out_specs=out_specs,
        scratch_shapes=scratch,
        compiler_params=pltpu.CompilerParams(
            collective_id=0, has_side_effects=True, vmem_limit_bytes=VMEM_LIMIT
        ),
        cost_estimate=pl.CostEstimate(flops=6_000_000_000, bytes_accessed=30_000_000, transcendentals=6_000_000),
        name="forward_part",
    )(hid, lengths, places, gain, shift, *weights, qbias, cw, sw, fit)


def quarter(c):
    return 2 * lax.rem(c, 2) + c // 2


class Reduction:
    def __init__(self, n, rows, full, half, half_in, own, own_in, sems):
        self.n, self.rows, self.piece = n, rows, rows // 4
        self.full, self.half, self.half_in, self.own, self.own_in = full, half, half_in, own, own_in
        self.sems = sems
        self.z, self.c, self.t, self.side, self.across, self.corner = place()
        self.started = []

    def at(self, offset, size):
        return pl.ds(pl.multiple_of(offset, 16), size)

    def send_side(self):
        two = 2 * self.piece
        core = lax.rem(self.c, 2)
        self.one = remote(
            self.full.at[:, self.at(two * (1 - core), two)], self.half_in, self.sems[0].at[0], self.sems[1].at[0], {"ctx": self.side}
        )
        self.one.start()
        self.started.append(self.one)

    def sum_side(self):
        two = 2 * self.piece
        core = lax.rem(self.c, 2)
        self.one.wait_recv()
        for k in range(self.n):
            self.half[k] = (
                self.full[k, self.at(two * core, two)].astype(f32) + self.half_in[k].astype(f32)
            ).astype(bf16)

    def send_across(self):
        piece, y = self.piece, self.c // 2
        self.two = remote(
            self.half.at[:, self.at(piece * (1 - y), piece)], self.own_in, self.sems[0].at[1], self.sems[1].at[1], {"ctx": self.across}
        )
        self.two.start()
        self.started.append(self.two)

    def take_across(self):
        y = self.c // 2
        self.two.wait_recv()
        for k in range(self.n):
            self.own[k] = (
                self.half[k, self.at(self.piece * y, self.piece)].astype(f32) + self.own_in[k].astype(f32)
            ).astype(bf16)

    def wait_sends(self):
        for copy in self.started:
            copy.wait_send()


def mlp_kernel(gather, refs):
    (hid, mixed, wo, wf_far, wp_far, obias, gain, shift, fbias, cot_far,
     residual_out, mlp_out, gres_out, gmixed, og, pg, fg, sums, fsum,
     residual, mlp_part, gres, wf, wp, cot, low, act, gpre, gpart, gin, turned, glow, ls, outs, gs, gr, *rest) = refs
    if gather:
        pfull, phalf, phalf_in, pown_in, ffull, fhalf_in, ps, pr, fs, fr = rest
    else:
        pfull, ffull = pg, fg
    z, c, t, side, across, corner = place()
    S, B, D = hid.shape
    FW = wf.shape[1]
    HW = mixed.shape[3]
    n, R = pfull.shape[:2]
    tile = 512
    loads = [pltpu.make_async_copy(far, near, ls.at[i]) for i, (far, near) in enumerate(((wf_far, wf), (cot_far, cot), (wp_far, wp)))]
    for copy in loads:
        copy.start()
    kept = []

    def keep(src, dst):
        copy = pltpu.make_async_copy(src, dst, outs.at[len(kept)])
        copy.start()
        kept.append(copy)

    enter([{"tp": 1 - t}] + ([{"ctx": side}, {"ctx": across}] if gather else []))
    fsum[...] = jnp.zeros_like(fsum)
    copies = []
    for s in range(S):
        branch = dot_nt(mixed[0, s], wo[0]) + dot_nt(mixed[1, s], wo[1])
        wide = hid[s].astype(f32) + branch + obias[...]
        residual[s] = wide
        value, _, _ = normalise(wide, gain[...], shift[...])
        low[s] = value.astype(bf16)
        keep(residual.at[s], residual_out.at[s])
        if s == 0:
            for copy in loads:
                copy.wait()

        def columns(j, carry, s=s):
            cols = pl.ds(pl.multiple_of(j * tile, tile), tile)
            pre = dot_nn(low[s], wf[:, cols]) + fbias[:, cols]
            square = pre * pre
            th = jnp.tanh(0.7978845608028654 * (pre + 0.044715 * (square * pre)))
            act[s, :, cols] = (0.5 * pre * (1.0 + th)).astype(bf16)
            slope = 0.5 * (1.0 + th) + (0.5 * pre) * (1.0 - th * th) * (
                0.7978845608028654 * (1.0 + 3.0 * 0.044715 * square)
            )
            grad = (dot_nn(cot[s], wp[:, cols]) * slope).astype(bf16)
            gpre[s, :, cols] = grad
            fsum[:, cols] += jnp.sum(grad.astype(f32), axis=0, keepdims=True)
            return carry

        lax.fori_loop(0, FW // tile, columns, 0)
        gpart[s] = dot_nt(gpre[s], wf[...]).astype(bf16)
        copies.append(remote(gpart.at[s], gin.at[s], gs.at[s], gr.at[s], {"tp": 1 - t}))
        copies[-1].start()

    def weight_grad(full, left, right, width, step):
        turned[...] = left.reshape(S * B, D).T

        def columns(j, carry):
            cols = pl.ds(pl.multiple_of(j * step, step), step)
            value = dot_nn(turned[...], right[:, :, cols].reshape(S * B, step)).astype(bf16)
            for k in range(n):
                full[k, :, cols] = value[k * R : (k + 1) * R]
            return carry

        lax.fori_loop(0, width // step, columns, 0)

    weight_grad(pfull, cot[...], act, FW, 256)
    if gather:
        proj = Reduction(n, R, pfull, phalf, phalf_in, pg, pown_in, (ps, pr))
        proj.send_side()
    weight_grad(ffull, low[...], gpre, FW, 256)
    if gather:
        fc = Reduction(n, R, ffull, fg, fhalf_in, None, None, (fs, fr))
        fc.send_side()
        proj.sum_side()
        proj.send_across()
    for s in range(S):
        mlp_part[s] = dot_nt(act[s], wp[...]).astype(bf16)
        keep(mlp_part.at[s], mlp_out.at[s])
    out_sum = jnp.zeros((1, D), f32)
    gain_sum = jnp.zeros((1, D), f32)
    shift_sum = jnp.zeros((1, D), f32)
    cot_sum = jnp.zeros((1, D), f32)
    for s in range(S):
        copies[s].wait_recv()
        grad = gpart[s].astype(f32) + gin[s].astype(f32)
        _, unit, r = normalise(residual[s], gain[...], shift[...])
        gain_sum += jnp.sum(grad * unit, axis=0, keepdims=True)
        shift_sum += jnp.sum(grad, axis=0, keepdims=True)
        a = grad * gain[...]
        wide_cot = cot[s].astype(f32)
        cot_sum += jnp.sum(wide_cot, axis=0, keepdims=True)
        total = wide_cot + r * (
            a - jnp.mean(a, axis=-1, keepdims=True) - unit * jnp.mean(a * unit, axis=-1, keepdims=True)
        )
        out_sum += jnp.sum(total, axis=0, keepdims=True)
        gres[s] = total
        keep(gres.at[s], gres_out.at[s])
        glow[s] = total.astype(bf16)
        gmixed[s] = dot_nn(glow[s], wo[t]).astype(bf16)
        if s == 0 and gather:
            fc.sum_side()
    sums[0:1] = out_sum
    sums[1:2] = gain_sum
    sums[2:3] = shift_sum
    sums[3:4] = cot_sum
    weight_grad(og, glow[...], mixed.at[t], HW, 384)
    if gather:
        proj.take_across()
        proj.wait_sends()
        fc.wait_sends()
    for copy in copies:
        copy.wait_send()
    for copy in kept:
        copy.wait()


def mlp(gather, hid, mixed, wo, wf, wp, obias, gain, shift, fbias, cot):
    S, B, D = hid.shape
    HW = mixed.shape[3]
    FW = wf.shape[1]
    n = lax.axis_size("dp") if gather else 1
    R = D // n
    Q = R // 4
    vm = pl.BlockSpec(memory_space=pltpu.VMEM)
    sem = pltpu.SemaphoreType.DMA
    hb = pl.BlockSpec(memory_space=pl.ANY)
    pshape = (n, Q, FW) if gather else (n, R, FW)
    fshape = (n, 2 * Q, FW) if gather else (n, R, FW)
    out = [
        jax.ShapeDtypeStruct((S, B, D), f32),
        jax.ShapeDtypeStruct((S, B, D), bf16),
        jax.ShapeDtypeStruct((S, B, D), f32),
        jax.ShapeDtypeStruct((S, B, HW), bf16),
        jax.ShapeDtypeStruct((n, R, HW), bf16),
        jax.ShapeDtypeStruct(pshape, bf16),
        jax.ShapeDtypeStruct(fshape, bf16),
        jax.ShapeDtypeStruct((4, D), f32),
        jax.ShapeDtypeStruct((1, FW), f32),
    ]
    scratch = [
        pltpu.VMEM((S, B, D), f32),
        pltpu.VMEM((S, B, D), bf16),
        pltpu.VMEM((S, B, D), f32),
        pltpu.VMEM((D, FW), bf16),
        pltpu.VMEM((D, FW), bf16),
        pltpu.VMEM((S, B, D), bf16),
        pltpu.VMEM((S, B, D), bf16),
        pltpu.VMEM((S, B, FW), bf16),
        pltpu.VMEM((S, B, FW), bf16),
        pltpu.VMEM((S, B, D), bf16),
        pltpu.VMEM((S, B, D), bf16),
        pltpu.VMEM((D, S * B), bf16),
        pltpu.VMEM((S, B, D), bf16),
        sem((3,)),
        sem((3 * S,)),
        sem((S,)),
        sem((S,)),
    ]
    if gather:
        scratch += [
            pltpu.VMEM((n, R, FW), bf16),
            *[pltpu.VMEM((n, R // 2, FW), bf16)] * 2,
            pltpu.VMEM((n, Q, FW), bf16),
            pltpu.VMEM((n, R, FW), bf16),
            pltpu.VMEM((n, R // 2, FW), bf16),
            *[sem((2,))] * 4,
        ]
    return pl.pallas_call(
        lambda *refs: mlp_kernel(gather, refs),
        out_shape=out,
        in_specs=[vm, vm, vm, hb, hb, vm, vm, vm, vm, hb],
        out_specs=[hb, hb, hb, *[vm] * 6],
        scratch_shapes=scratch,
        compiler_params=pltpu.CompilerParams(
            collective_id=1, has_side_effects=True, vmem_limit_bytes=VMEM_LIMIT
        ),
        cost_estimate=pl.CostEstimate(flops=12_000_000_000, bytes_accessed=30_000_000, transcendentals=1_500_000),
        name="mlp_part",
    )(hid, mixed, wo, wf, wp, obias, gain, shift, fbias, cot)


def backward_kernel(gather, refs):
    (lengths, places, q, kv_far, mem, lse, gmixed, normed_far, wq_far, hid_far, gres_far, residual_far, mlp_far, pbias, gain,
     cw, sw, fit, sums, fsum, *rest) = refs
    if gather:
        (pown, fhalf, ofull, block_out, input_grad, early_out, late_out, fa, fk, fv, fo, ff, fp, *rest) = rest
    else:
        (block_out, input_grad, early_out, late_out, afull, kfull, vfull, *rest) = rest
    (kv, normed, wq, gres, residual, dkv, own_rows, dmem, gqkv, hs1, hr1, hs2, hr2, m1in, m2out, m2in, gmem,
     turned, mlp_in, gnpart, gnin, bias, early, ls, xs, xr, h1s, h1r, h2s, h2r, m1s, m1r, m2s, m2r, m3s, m3r, ns, nr,
     *rest) = rest
    if gather:
        (afull, kfull, vfull, ahalf_in, khalf_in, vhalf_in, ohalf_in, ahalf, khalf, vhalf, ohalf,
         aown, kown, vown, oown, fown, aown_in, kown_in, vown_in, oown_in, fown_in,
         zina, zink, zinv, zino, zinf, zinp, early_ctx, early_dp, late_ctx, late_dp,
         rs, rr, zs, zr, gs, gr, es, er) = rest
    z, c, t, side, across, corner = place()
    S, B, D = hid_far.shape
    HW = q.shape[2]
    NB = mem.shape[1]
    n, R = afull.shape[:2]
    L = kv_far.shape[1]
    keys = 3 * B
    key_start = pl.multiple_of(jnp.maximum(c - 2, 0) * B, B)
    pairs = [(kv_far.at[s, pl.ds(key_start, keys)], kv.at[s]) for s in range(S)] + [
        (normed_far, normed), (residual_far, residual), (wq_far, wq), (gres_far, gres)
    ]
    late_pairs = [(hid_far, kv.at[:, 0:B]), (mlp_far, kv.at[:, B : 2 * B])]
    loads = [pltpu.make_async_copy(far, near, ls.at[i]) for i, (far, near) in enumerate(pairs)]
    late_loads = [pltpu.make_async_copy(far, near, ls.at[S + 4 + i]) for i, (far, near) in enumerate(late_pairs)]
    for copy in loads:
        copy.start()
    peers = [{"tp": 1 - t}, {"ctx": side}, {"ctx": across}]
    if gather:
        peers += [{"ctx": corner}] + [{"dp": lax.rem(z + i, n)} for i in range(1, n)]
    enter(peers)
    started = []

    def start(copy):
        copy.start()
        started.append(copy)
        return copy

    if gather:
        Q = R // 4
        owns = {"a": aown, "k": kown, "v": vown, "o": oown, "f": fown, "p": pown}
        zins = {"a": zina, "k": zink, "v": zinv, "o": zino, "f": zinf, "p": zinp}
        finals = {"a": fa, "k": fk, "v": fv, "o": fo, "f": ff, "p": fp}
        index = {g: i for i, g in enumerate(owns)}
        z_sent, g_sent = {}, {}

        def send_dp(g):
            j = index[g]
            z_sent[g] = [
                start(remote(owns[g].at[lax.rem(z + i, n)], zins[g].at[i - 1], zs.at[j, i - 1], zr.at[j, i - 1], {"dp": lax.rem(z + i, n)}))
                for i in range(1, n)
            ]

        def piece(g, device):
            return finals[g].at[pl.ds(pl.multiple_of(Q * quarter(device), 16), Q)]

        def take_dp(g):
            j = index[g]
            total = owns[g][z].astype(f32)
            for i in range(1, n):
                z_sent[g][i - 1].wait_recv()
                total = total + zins[g][i - 1].astype(f32)
            finals[g][pl.ds(pl.multiple_of(Q * quarter(c), 16), Q)] = total.astype(bf16)
            mine = piece(g, c)
            g_sent[g] = [
                start(remote(mine, mine, gs.at[j, 0], gr.at[j, 0], {"ctx": across})),
                start(remote(mine, mine, gs.at[j, 1], gr.at[j, 1], {"ctx": side})),
            ]

        def pass_on(g):
            j = index[g]
            g_sent[g][0].wait_recv()
            other = piece(g, across)
            g_sent[g].append(start(remote(other, other, gs.at[j, 2], gr.at[j, 2], {"ctx": side})))

        def take_all(g):
            g_sent[g][1].wait_recv()
            g_sent[g][2].wait_recv()

        def reduction(g, full, half, half_in, own, own_in):
            return Reduction(n, R, full, half, half_in, own, own_in, (rs.at[index[g]], rr.at[index[g]]))

        red = {
            "a": reduction("a", afull, ahalf, ahalf_in, aown, aown_in),
            "k": reduction("k", kfull, khalf, khalf_in, kown, kown_in),
            "v": reduction("v", vfull, vhalf, vhalf_in, vown, vown_in),
            "o": reduction("o", ofull, ohalf, ohalf_in, oown, oown_in),
            "f": reduction("f", None, fhalf, None, fown, fown_in),
        }

        class Everywhere:
            def __init__(self, over_ctx, over_dp, which):
                self.over_ctx, self.over_dp, self.which = over_ctx, over_dp, which

            def send(self, slots, me, devices, step):
                j = 2 * self.which + step
                self.sent = [
                    start(remote(slots.at[me], slots.at[me], es.at[j, i], er.at[j, i], device)) for i, device in enumerate(devices)
                ]

            def first(self, value):
                self.over_ctx[c] = value
                self.send(self.over_ctx, c, [{"ctx": side}, {"ctx": across}, {"ctx": corner}], 0)

            def total(self, slots):
                for copy in self.sent:
                    copy.wait_recv()
                return (slots[0] + slots[1]) + (slots[2] + slots[3])

            def second(self):
                self.over_dp[z] = self.total(self.over_ctx)
                self.send(self.over_dp, z, [{"dp": lax.rem(z + i, n)} for i in range(1, n)], 1)

            def last(self, out):
                out[...] = self.total(self.over_dp)

        early_sum = Everywhere(early_ctx, early_dp, 0)
        late_sum = Everywhere(late_ctx, late_dp, 1)
        red["f"].send_across()
        send_dp("p")
        red["o"].send_side()

    mlp_sent = [
        start(remote(mlp_far.at[s], mlp_in.at[s], xs.at[s], xr.at[s], {"tp": 1 - t})) for s in range(S)
    ]

    lane = lanes((1, 2 * DH), 1)
    scaled = half_lanes(SCALE)
    plain = half_lanes(1.0)
    centers = (lanes((1, NB), 1).astype(f32) + 0.5) * (1.0 / NB)
    width = 1.0 / NB
    early[...] = jnp.zeros_like(early)
    half = HW
    core = lax.rem(c, 2)
    y = c // 2
    own_half = pl.ds(pl.multiple_of(core * half, 16), half)
    side_half = pl.ds(pl.multiple_of((1 - core) * half, 16), half)
    give = pl.ds(pl.multiple_of(B * (1 - core * (1 - y)), 128), B)
    own = pl.ds(pl.multiple_of(c * B - key_start, 128), B)
    one, two, three, first = {}, {}, {}, {}

    def second_copy(s):
        return remote(hs2.at[s], hr2.at[s], h2s.at[s], h2r.at[s], {"ctx": across})

    def attend_back(s):
        loads[s].wait()
        bias[...] = mask_bias(lengths, s, c, B, key_start, keys)

        def pair_step(p, carry):
            cols = pl.ds(pl.multiple_of(p * 2 * DH, 2 * DH), 2 * DH)
            vcols = pl.ds(pl.multiple_of(HW + p * 2 * DH, 2 * DH), 2 * DH)
            qp = q[s, :, cols]
            gp = gmixed[s, :, cols]
            kp = kv[s, :, cols]
            vp = kv[s, :, vcols]
            mk = mem[s, :, cols]
            mv = mem[s, :, vcols]
            q_turned = (qp * SCALE).T
            g_turned = gp.T
            logs = lse[s]
            grad_q, dk, dv, dmk, dmv = [], [], [], [], []
            for h in range(2):
                row = 2 * p + h
                part = slice(h * DH, (h + 1) * DH)
                qh = qp * scaled[h]
                gh = gp * plain[h]
                log_total = jnp.sum(jnp.where(lane == row, logs, 0.0), axis=-1, keepdims=True)
                share = jnp.exp(dot_nt(qh, kp) + bias[...] - log_total)
                grad_share = dot_nt(gh, vp)
                delta = jnp.sum(share * grad_share, axis=-1, keepdims=True)
                grad_score = (share * (grad_share - delta)).astype(bf16)
                mem_scores = dot_nt(qh, mk)
                cw_row = cw[pl.ds(row, 1)]
                sw_row = sw[pl.ds(row, 1)]
                reach, mu, inv, diff, spread_logit = reach_terms(mem_scores, cw_row, sw_row, centers, width)
                grad_reach = dot_nt(gh, mv) * reach
                scaled_diff = diff * inv
                grad_mu = -jnp.sum(grad_reach * scaled_diff, axis=-1, keepdims=True)
                grad_var = jnp.sum(
                    grad_reach * (0.5 * scaled_diff * scaled_diff - 0.5 * inv), axis=-1, keepdims=True
                )
                gc = grad_mu * mu * (1.0 - mu)
                gw = SPREAD * grad_var * (1.0 / (1.0 + jnp.exp(-spread_logit)))
                early[pl.ds(8 + row, 1), 0:NB] += jnp.sum(gc * mem_scores, axis=0, keepdims=True)
                early[pl.ds(8 + row, 1), NB : 2 * NB] += jnp.sum(gw * mem_scores, axis=0, keepdims=True)
                grad_mem = (gc * cw_row + gw * sw_row).astype(bf16)
                grad_q.append((dot_nn(grad_score, kp) + dot_nn(grad_mem, mk)) * SCALE)
                dk.append(dot_nn(q_turned[part], grad_score))
                dv.append(dot_nn(g_turned[part], share.astype(bf16)))
                dmk.append(dot_nn(q_turned[part], grad_mem))
                dmv.append(dot_nn(g_turned[part], reach.astype(bf16)))
            gqkv[s, :, cols] = jnp.where(lane < DH, grad_q[0], grad_q[1]).astype(bf16)
            for h in range(2):
                rows = pl.ds(pl.multiple_of((2 * p + h) * DH, DH), DH)
                vrows = pl.ds(pl.multiple_of(HW + (2 * p + h) * DH, DH), DH)
                dkv[rows] = dk[h]
                dkv[vrows] = dv[h]
                dmem[s, rows] = dmk[h]
                dmem[s, vrows] = dmv[h]
            return carry

        lax.fori_loop(0, HW // (2 * DH), pair_step, 0)
        one[s] = start(remote(dmem.at[s, side_half], m1in.at[s], m1s.at[s], m1r.at[s], {"ctx": side}))
        hs1[s] = dkv[:, give].astype(bf16)
        first[s] = start(remote(hs1.at[s], hr1.at[s], h1s.at[s], h1r.at[s], {"ctx": side}))
        own_rows[s] = dkv[:, own]
        hs2[s] = dkv[:, 0:B].astype(bf16)

    def give_across(s):
        one[s].wait_recv()
        m2out[s] = (dmem[s, own_half] + m1in[s]).astype(bf16)
        two[s] = start(remote(m2out.at[s], m2in.at[s], m2s.at[s], m2r.at[s], {"ctx": across}))
        first[s].wait_recv()

        @pl.when(c != 3)
        def _():
            own_rows[s] = own_rows[s] + hr1[s].astype(f32)

        @pl.when(c == 3)
        def _():
            hs2[s] = (hs2[s].astype(f32) + hr1[s].astype(f32)).astype(bf16)

        @pl.when(y == 1)
        def _():
            second_copy(s).start()

    def memory_back(s):
        two[s].wait_recv()
        gmem[s, own_half] = (m2out[s].astype(f32) + m2in[s].astype(f32)).astype(bf16)
        three[s] = start(remote(gmem.at[s, own_half], gmem.at[s, own_half], m3s.at[s], m3r.at[s], {"ctx": side}))

    sent = {}

    def finish_rows(s):
        three[s].wait_recv()
        high, low = fit_at(fit, places, s, c * B + lanes((B, 1), 0), L)
        value = own_rows[s] + dot_nn(gmem[s], high) + dot_nn(gmem[s], low)
        own_rows[s] = value

        @pl.when(y == 0)
        def _():
            second_copy(s).wait_recv()
            own_rows[s] = own_rows[s] + hr2[s].astype(f32)

        gqkv[s, :, HW:] = own_rows[s].T.astype(bf16)
        gnpart[s] = dot_nt(gqkv[s], wq[...]).astype(bf16)
        sent[s] = start(remote(gnpart.at[s], gnin.at[s], ns.at[s], nr.at[s], {"tp": 1 - t}))

    def finish_block(s):
        mlp_sent[s].wait_recv()
        total = kv[s, B : 2 * B].astype(f32) + mlp_in[s].astype(f32)
        block_out[s] = (residual[s] + total + pbias[...]).astype(bf16)

    def weight_grad(full, k):
        value = dot_nn(turned[...], gqkv[:, :, k * HW : (k + 1) * HW].reshape(S * B, HW)).astype(bf16)
        for i in range(n):
            full[i] = value[i * R : (i + 1) * R]

    column_sums = []

    def norm_back(s):
        sent[s].wait_recv()
        grad = gnpart[s].astype(f32) + gnin[s].astype(f32)
        _, unit, r = normalise(kv[s, 0:B].astype(f32), gain[...], gain[...])
        column_sums.append((jnp.sum(grad * unit, axis=0, keepdims=True), jnp.sum(grad, axis=0, keepdims=True)))
        a = grad * gain[...]
        back = r * (a - jnp.mean(a, axis=-1, keepdims=True) - unit * jnp.mean(a * unit, axis=-1, keepdims=True))
        input_grad[s] = (gres[s] + back).astype(bf16)

    attend_back(0)
    if gather:
        red["o"].sum_side()
        red["o"].send_across()
    attend_back(1)
    give_across(0)
    if gather:
        red["f"].take_across()
        send_dp("f")
        red["o"].take_across()
        send_dp("o")
    attend_back(2)
    for copy in late_loads:
        copy.start()
    give_across(1)
    memory_back(0)
    for copy in loads[S:] + late_loads:
        copy.wait()
    turned[...] = normed[...].reshape(S * B, D).T
    weight_grad(afull, 0)
    early[0:4, 0:D] = sums[...]
    early[4:5] = fsum[...]
    if gather:
        red["a"].send_side()
    give_across(2)
    memory_back(1)
    if gather:
        early_sum.first(early[...])
    finish_block(0)
    finish_block(1)
    if gather:
        red["a"].sum_side()
        red["a"].send_across()
    memory_back(2)
    finish_rows(0)
    finish_rows(1)
    finish_rows(2)
    weight_grad(kfull, 1)
    if gather:
        red["k"].send_side()
    weight_grad(vfull, 2)
    if gather:
        red["v"].send_side()
        red["a"].take_across()
        send_dp("a")
        red["k"].sum_side()
        red["k"].send_across()
        red["v"].sum_side()
        red["v"].send_across()
        early_sum.second()
    finish_block(2)
    norm_back(0)
    norm_back(1)
    if gather:
        red["k"].take_across()
        send_dp("k")
        red["v"].take_across()
        send_dp("v")
    norm_back(2)
    bias_sum = jnp.sum(gqkv[...].reshape(S * B, 3 * HW).astype(f32), axis=0, keepdims=True)
    room = late_ctx.at[c] if gather else late_out
    room[...] = jnp.zeros(room.shape, f32)
    room[0:1, 0:D] = column_sums[0][0] + column_sums[1][0] + column_sums[2][0]
    room[1:2, 0:D] = column_sums[0][1] + column_sums[1][1] + column_sums[2][1]
    room[2:3, 0 : 3 * HW] = bias_sum
    if gather:
        late_sum.send(late_ctx, c, [{"ctx": side}, {"ctx": across}, {"ctx": corner}], 0)
        for g in ("p", "f", "o", "a"):
            take_dp(g)
        late_sum.second()
        take_dp("k")
        take_dp("v")
        for g in ("p", "f", "o", "a", "k", "v"):
            pass_on(g)
        early_sum.last(early_out)
        late_sum.last(late_out)
        for g in ("p", "f", "o", "a", "k", "v"):
            take_all(g)
        for one_red in red.values():
            one_red.wait_sends()
    else:
        early_out[...] = early[...]
    for s in range(S):

        @pl.when(y == 1)
        def _(s=s):
            second_copy(s).wait_send()

    for copy in started:
        copy.wait_send()


def backward(gather, lengths, places, q, kv, mem, lse, gmixed, normed, wq, hid, gres, residual, mlp_part, pbias, gain, cw, sw,
             fit, sums, fsum, owned):
    S, B, D = hid.shape
    HW = q.shape[2]
    FW = fsum.shape[1]
    H, NB = cw.shape
    n = lax.axis_size("dp") if gather else 1
    R = D // n
    Q = R // 4
    rows = -(-(8 + H) // 8) * 8
    vm = pl.BlockSpec(memory_space=pltpu.VMEM)
    sm = pl.BlockSpec(memory_space=pltpu.SMEM)
    hb = pl.BlockSpec(memory_space=pl.ANY)
    sem = pltpu.SemaphoreType.DMA
    late = (8, max(D, 3 * HW))
    out = [
        jax.ShapeDtypeStruct((S, B, D), bf16),
        jax.ShapeDtypeStruct((S, B, D), bf16),
        jax.ShapeDtypeStruct((rows, FW), f32),
        jax.ShapeDtypeStruct(late, f32),
    ]
    if gather:
        out += [jax.ShapeDtypeStruct((R, w), bf16) for w in (HW, HW, HW, HW, FW, FW)]
    else:
        out += [jax.ShapeDtypeStruct((n, R, HW), bf16)] * 3
    scratch = [
        pltpu.VMEM((S, 3 * B, 2 * HW), bf16),
        pltpu.VMEM((S, B, D), bf16),
        pltpu.VMEM((D, 3 * HW), bf16),
        pltpu.VMEM((S, B, D), f32),
        pltpu.VMEM((S, B, D), f32),
        pltpu.VMEM((2 * HW, 3 * B), f32),
        pltpu.VMEM((S, 2 * HW, B), f32),
        pltpu.VMEM((S, 2 * HW, NB), f32),
        pltpu.VMEM((S, B, 3 * HW), bf16),
        *[pltpu.VMEM((S, 2 * HW, B), bf16)] * 4,
        pltpu.VMEM((S, HW, NB), f32),
        pltpu.VMEM((S, HW, NB), bf16),
        pltpu.VMEM((S, HW, NB), bf16),
        pltpu.VMEM((S, 2 * HW, NB), bf16),
        pltpu.VMEM((D, S * B), bf16),
        *[pltpu.VMEM((S, B, D), bf16)] * 3,
        pltpu.VMEM((B, 3 * B), f32),
        pltpu.VMEM((rows, FW), f32),
        sem((S + 6,)),
        *[sem((S,))] * 14,
    ]
    if gather:
        scratch += [
            *[pltpu.VMEM((n, R, HW), bf16)] * 3,
            *[pltpu.VMEM((n, 2 * Q, HW), bf16)] * 8,
            *[pltpu.VMEM((n, Q, HW), bf16)] * 4,
            pltpu.VMEM((n, Q, FW), bf16),
            *[pltpu.VMEM((n, Q, HW), bf16)] * 4,
            pltpu.VMEM((n, Q, FW), bf16),
            *[pltpu.VMEM((n - 1, Q, w), bf16) for w in (HW, HW, HW, HW, FW, FW)],
            *[pltpu.VMEM((4, rows, FW), f32)] * 2,
            *[pltpu.VMEM((4, *late), f32)] * 2,
            *[sem((6, 2))] * 2,
            *[sem((6, n - 1))] * 2,
            *[sem((6, 3))] * 2,
            *[sem((4, 3))] * 2,
        ]
    args = [lengths, places, q, kv, mem, lse, gmixed, normed, wq, hid, gres, residual, mlp_part, pbias, gain, cw, sw, fit, sums,
            fsum, *owned]
    far = (3, 7, 8, 9, 10, 11, 12)
    return pl.pallas_call(
        lambda *refs: backward_kernel(gather, refs),
        out_shape=out,
        in_specs=[sm] + [hb if i in far else vm for i in range(1, len(args))],
        out_specs=[vm] * len(out),
        scratch_shapes=scratch,
        compiler_params=pltpu.CompilerParams(
            collective_id=2, has_side_effects=True, vmem_limit_bytes=VMEM_LIMIT
        ),
        cost_estimate=pl.CostEstimate(flops=12_000_000_000, bytes_accessed=40_000_000, transcendentals=6_000_000),
        name="backward_part",
    )(*args)


def finish_kernel(fa, fk, fv, fo, ff, fp, early, late, qkv, out, fc, proj, qb, cgrad, sgrad, *vectors):
    HW = fa.shape[1]
    D = vectors[0].shape[1]
    NB = cgrad.shape[1]
    for k, part in enumerate((fa, fk, fv)):
        qkv[:, k, :] = part[...].astype(f32)
        qb[k : k + 1] = late[2:3, k * HW : (k + 1) * HW]
    out[...] = fo[...].astype(f32).T
    fc[...] = ff[...].astype(f32)
    proj[...] = fp[...].astype(f32).T
    H = cgrad.shape[0]
    cgrad[...] = early[8 : 8 + H, 0:NB]
    sgrad[...] = early[8 : 8 + H, NB : 2 * NB]
    vectors[0][...] = late[0:1, 0:D]
    vectors[1][...] = late[1:2, 0:D]
    for k in range(4):
        vectors[2 + k][...] = early[k : k + 1, 0:D]
    vectors[6][...] = early[4:5]


def finish(parts, early, late, D, H, NB):
    R, HW = parts[0].shape
    FW = parts[4].shape[1]
    vm = pl.BlockSpec(memory_space=pltpu.VMEM)
    shapes = [(R, 3, HW), (HW, R), (R, FW), (FW, R), (3, HW), (H, NB), (H, NB)] + [(1, D)] * 6 + [(1, FW)]
    return pl.pallas_call(
        finish_kernel,
        out_shape=[jax.ShapeDtypeStruct(shape, f32) for shape in shapes],
        in_specs=[vm] * 8,
        out_specs=[vm] * len(shapes),
        compiler_params=pltpu.CompilerParams(vmem_limit_bytes=VMEM_LIMIT),
        name="finish_part",
    )(*parts, early, late)


def per_device(hidden_in, doc_lengths, sticky_places, attn_gain, attn_shift, qkv_weight, qkv_bias, center_weight,
               spread_weight, out_weight, out_bias, mlp_gain, mlp_shift, fc_weight, fc_bias, proj_weight, proj_bias,
               cotangent):
    S, B, D = hidden_in.shape
    n = lax.axis_size("dp")
    HW = qkv_bias.shape[1]
    H, NB = center_weight.shape
    M = sticky_places.shape[1]
    fit = jnp.asarray(ridge_fit(NB, 2 * M))
    gather = n == 4 and D % (64 * n) == 0
    weights = [qkv_weight.reshape(D // n, 3 * HW), out_weight.T, fc_weight, proj_weight.T]
    if not gather:
        full = [lax.all_gather(w, "dp", axis=0, tiled=True) for w in weights]
        weights = full[:1]
    made = forward(gather, hidden_in, doc_lengths, sticky_places, attn_gain[None], attn_shift[None], weights,
                   qkv_bias, center_weight, spread_weight, fit)
    normed, q, kv, mem, lse, mixed = made[:6]
    if gather:
        wq, wo, wf, wp = made[6:]
    else:
        wq, wo, wf, wp = full
        wo = lax.all_gather(wo, "tp", axis=0)
    made = mlp(gather, hidden_in, mixed, wo, wf, wp, out_bias[None], mlp_gain[None], mlp_shift[None], fc_bias[None], cotangent)
    residual, mlp_part, gres, gmixed, og, pg, fg, sums, fsum = made
    owned = [pg, fg, og] if gather else []
    made = backward(gather, doc_lengths, sticky_places, q, kv, mem, lse, gmixed, normed, wq, hidden_in, gres, residual, mlp_part,
                    proj_bias[None], attn_gain[None], center_weight, spread_weight, fit, sums, fsum, owned)
    block_out, input_grad, early, late = made[:4]
    if gather:
        made = finish(made[4:], early, late, D, H, NB)
        qkv_grad, out_grad, fc_grad, proj_grad, qkv_bias_grad, center_grad, spread_grad = made[:7]
        gain_grad, shift_grad, out_bias_grad, mlp_gain_grad, mlp_shift_grad, proj_bias_grad, fc_bias_grad = [
            v.reshape(-1) for v in made[7:]
        ]
    else:
        early, late = lax.psum((early, late), ("dp", "ctx"))

        def reduced(grad):
            part = lax.psum_scatter(grad.reshape(D, -1), "dp", scatter_dimension=0, tiled=True)
            return lax.psum(part, "ctx").astype(f32)

        qkv_grad = jnp.stack([reduced(g) for g in made[4:]], axis=1)
        out_grad, fc_grad, proj_grad = reduced(og).T, reduced(fg), reduced(pg).T
        qkv_bias_grad = late[2, : 3 * HW].reshape(3, HW)
        center_grad, spread_grad = early[8 : 8 + H, :NB], early[8 : 8 + H, NB : 2 * NB]
        gain_grad, shift_grad = late[0, :D], late[1, :D]
        out_bias_grad, mlp_gain_grad, mlp_shift_grad, proj_bias_grad = [early[k, :D] for k in range(4)]
        fc_bias_grad = early[4]
    return (
        block_out,
        input_grad,
        gain_grad,
        shift_grad,
        qkv_grad,
        qkv_bias_grad,
        center_grad,
        spread_grad,
        out_grad,
        out_bias_grad,
        mlp_gain_grad,
        mlp_shift_grad,
        fc_grad,
        fc_bias_grad,
        proj_grad,
        proj_bias_grad,
    )


def solution(mesh):
    in_specs = (
        P("dp", "ctx", None),
        P("dp", None),
        P("dp", None),
        P(),
        P(),
        P("dp", None, "tp"),
        P(None, "tp"),
        P("tp", None),
        P("tp", None),
        P("tp", "dp"),
        P(),
        P(),
        P(),
        P("dp", "tp"),
        P("tp"),
        P("tp", "dp"),
        P(),
        P("dp", "ctx", None),
    )
    out_specs = (
        P("dp", "ctx", None),
        P("dp", "ctx", None),
        P(),
        P(),
        P("dp", None, "tp"),
        P(None, "tp"),
        P("tp", None),
        P("tp", None),
        P("tp", "dp"),
        P(),
        P(),
        P(),
        P("dp", "tp"),
        P("tp"),
        P("tp", "dp"),
        P(),
    )
    return jax.shard_map(
        per_device, mesh=mesh, in_specs=in_specs, out_specs=out_specs, check_vma=False
    )
```

```python
import functools

import jax
import jax.numpy as jnp
import numpy as np
from jax import lax
from jax.experimental import pallas as pl
from jax.experimental.pallas import tpu as pltpu
from jax.sharding import PartitionSpec as P

DH = 64
WINDOW = 512
EPS = 1e-05
SPREAD = 0.02
SCALE = DH ** (-0.5)
VMEM_LIMIT = 60 * 1024 * 1024

bf16 = jnp.bfloat16
f32 = jnp.float32
MESH = pl.DeviceIdType.MESH


def dot_nn(a, b):
    return lax.dot_general(a, b, (((1,), (0,)), ((), ())), preferred_element_type=f32)


def dot_nt(a, b):
    return lax.dot_general(a, b, (((1,), (1,)), ((), ())), preferred_element_type=f32)


def dot_tn(a, b):
    return lax.dot_general(a, b, (((0,), (0,)), ((), ())), preferred_element_type=f32)


def ridge_fit(basis_count, sample_count):
    centers = (np.arange(basis_count) + 0.5) / basis_count
    times = (np.arange(sample_count) + 0.5) / sample_count
    width = 1.0 / basis_count
    design = np.exp(-np.square(times[None, :] - centers[:, None]) / (2.0 * width * width))
    gram = design @ design.T + 0.5 * np.eye(basis_count)
    return np.linalg.solve(gram, design).astype(bf16)


def place():
    c = lax.axis_index("ctx")
    side = c + 1 - 2 * lax.rem(c, 2)
    across = lax.rem(c + 2, 4)
    corner = lax.rem(side + 2, 4)
    return lax.axis_index("dp"), c, lax.axis_index("tp"), side, across, corner


def enter(devices):
    barrier = pltpu.get_barrier_semaphore()
    for device in devices:
        pl.semaphore_signal(barrier, inc=1, device_id=device, device_id_type=MESH)
    pl.semaphore_wait(barrier, len(devices))


def remote(src, dst, send, recv, device):
    return pltpu.make_async_remote_copy(
        src_ref=src,
        dst_ref=dst,
        send_sem=send,
        recv_sem=recv,
        device_id=device,
        device_id_type=MESH,
    )


def normalise(x, gain, shift):
    mean = jnp.mean(x, axis=-1, keepdims=True)
    centred = x - mean
    r = lax.rsqrt(jnp.mean(centred * centred, axis=-1, keepdims=True) + EPS)
    n = centred * r
    return n * gain + shift, n, r


def lowest_key(lengths, s, pos):
    low = jnp.maximum(pos - (WINDOW - 1), 0)
    end = jnp.int32(0)
    for e in range(lengths.shape[1]):
        end = end + lengths[s, e]
        low = jnp.maximum(low, jnp.where(pos >= end, end, 0))
    return low


def row_of(vector):
    return vector[...].reshape(1, vector.shape[0])


def lanes(shape, dim):
    return lax.broadcasted_iota(jnp.int32, shape, dim)


def half_lanes(scale):
    lane = lanes((1, 2 * DH), 1)
    return [
        jnp.where(lane < DH, scale, 0.0).astype(bf16),
        jnp.where(lane >= DH, scale, 0.0).astype(bf16),
    ]


def mask_bias(lengths, s, c, rows, key_start, keys):
    pos = c * rows + lanes((rows, 1), 0)
    low = lowest_key(lengths, s, pos)
    key_pos = key_start + lanes((1, keys), 1)
    return jnp.where((key_pos <= pos) & (key_pos >= low), 0.0, -1e30)


def fit_at(fit, places, s, tokens, length):
    M = places.shape[1]
    sticky = jnp.where(tokens == places[s : s + 1, :], 1.0, 0.0).astype(bf16)
    even = lanes((1, M), 1) * length // M + length // (2 * M)
    steady = jnp.where(tokens == even, 1.0, 0.0).astype(bf16)
    value = dot_nt(fit[:, :M], sticky) + dot_nt(fit[:, M:], steady)
    high = value.astype(bf16)
    return high, (value - high.astype(f32)).astype(bf16)


def reach_terms(scores, center_row, spread_row, centers, width):
    center_logit = jnp.sum(scores * center_row, axis=-1, keepdims=True)
    spread_logit = jnp.sum(scores * spread_row, axis=-1, keepdims=True)
    mu = 1.0 / (1.0 + jnp.exp(-center_logit))
    grown = jnp.exp(spread_logit)
    var = SPREAD * jnp.log(1.0 + grown) + width * width
    inv = 1.0 / var
    diff = mu - centers
    reach = (width * lax.rsqrt(var)) * jnp.exp(-(diff * diff) * (0.5 * inv))
    return reach, mu, inv, diff, spread_logit


def forward_kernel(gather, refs):
    n = lax.axis_size("dp")
    if gather:
        (hid, lengths, places, gain, shift, wq_sh, wo_sh, wf_sh, wp_sh, qbias, cw, sw, fit,
         normed_out, q_out, kv_out, mem, lse, mixed, wq_out, wo, wf, wp,
         normed, q, kv, hoth, noth, bias, fits, os_, hys, hyr, hxs, hxr, ks, kr, ms, mr,
         wq, lsem, zs, zr, ys, yr, as_, ar, bs, br, oxs, oxr, lzs, lzr, lys, lyr, las, lar, lbs, lbr) = refs
    else:
        (hid, lengths, places, gain, shift, wq, qbias, cw, sw, fit,
         normed_out, q_out, kv_out, mem, lse, mixed,
         normed, q, kv, hoth, noth, bias, fits, os_, hys, hyr, hxs, hxr, ks, kr, ms, mr) = refs
    z, c, t, side, across, corner = place()
    S, B, D = hid.shape
    HW = q.shape[2]
    NB = mem.shape[1]
    L = kv.shape[1]
    half = B // 2
    peers = [{"ctx": side}, {"ctx": across}, {"tp": 1 - t}]
    if gather:
        R = D // n
        Q = R // 4
        shards = [wq_sh, wo_sh, wf_sh, wp_sh]
        whole = [wq, wo.at[t], wf, wp, wo.at[1 - t]]
        peers += [{"dp": lax.rem(z + i, n)} for i in range(1, n)]
    enter(peers)

    started, kept = [], []

    def start(copies):
        for copy in copies:
            copy.start()
        started.extend(copies)
        return copies

    def keep(src, dst):
        copy = pltpu.make_async_copy(src, dst, os_.at[len(kept)])
        copy.start()
        kept.append(copy)

    if gather:
        groups = range(1, 5)

        def rows(g, owner, quarter):
            part = pl.ds(pl.multiple_of(R * owner + Q * quarter, 16), Q)
            return wq.at[:, part] if g == 0 else whole[g].at[part]

        def source(i):
            return lax.rem(z + n - i, n)

        def first_z():
            src = wq_sh.at[:, pl.ds(pl.multiple_of(Q * c, 16), Q)]
            return start([
                remote(src, rows(0, z, c), zs.at[i - 1], zr.at[i - 1], {"dp": lax.rem(z + i, n)}) for i in range(1, n)
            ])

        def first_y(sent):
            for copy in sent:
                copy.wait_recv()
            here = [rows(0, source(i), c) for i in range(1, n)]
            over = start([remote(w, w, ys.at[i], yr.at[i], {"ctx": across}) for i, w in enumerate(here)])
            beside = start([remote(w, w, as_.at[i], ar.at[i], {"ctx": side}) for i, w in enumerate(here)])
            return over, beside

        def first_side(over):
            for copy in over:
                copy.wait_recv()
            there = [rows(0, source(i), across) for i in range(1, n)]
            return start([remote(w, w, bs.at[i], br.at[i], {"ctx": side}) for i, w in enumerate(there)])

        def sends(way, r):
            return ((z < n - 1) & (z >= r)) if way == 0 else ((z > 0) & (z + r < n))

        def takes(way, r):
            return (z > r) if way == 0 else (z + r < n - 1)

        def line_z(g, way, r):
            owner = z - r if way == 0 else z + r
            to = z + 1 if way == 0 else z - 1
            dst = rows(g, owner, c)
            src = shards[g].at[pl.ds(pl.multiple_of(Q * c, 16), Q)] if r == 0 and g < 4 else dst
            return remote(src, dst, lzs.at[g - 1, way, r], lzr.at[g - 1, way, r], {"dp": to})

        def line_copy(g, way, r, sems, quarter, device):
            part = rows(g, z - 1 - r if way == 0 else z + 1 + r, quarter)
            return remote(part, part, sems[0].at[g - 1, way, r], sems[1].at[g - 1, way, r], {"ctx": device})

        def line_y(g, way, r):
            return line_copy(g, way, r, (lys, lyr), c, across)

        def line_a(g, way, r):
            return line_copy(g, way, r, (las, lar), c, side)

        def line_b(g, way, r):
            return line_copy(g, way, r, (lbs, lbr), across, side)

        def line_send(r, some=groups):
            for way in range(2):

                @pl.when(sends(way, r))
                def _(way=way):
                    for g in some:
                        line_z(g, way, r).start()

        def line_take(r):
            for way in range(2):

                @pl.when(takes(way, r))
                def _(way=way):
                    for g in groups:
                        line_z(g, way, r).wait_recv()
                        line_y(g, way, r).start()
                        line_a(g, way, r).start()

        def line_pass(r):
            for way in range(2):

                @pl.when(takes(way, r))
                def _(way=way):
                    for g in groups:
                        line_y(g, way, r).wait_recv()
                        line_b(g, way, r).start()

        def line_end(r):
            for way in range(2):

                @pl.when(takes(way, r))
                def _(way=way):
                    for g in groups:
                        line_a(g, way, r).wait_recv()
                        line_b(g, way, r).wait_recv()
                        line_y(g, way, r).wait_send()
                        line_a(g, way, r).wait_send()
                        line_b(g, way, r).wait_send()

                @pl.when(sends(way, r))
                def _(way=way):
                    for g in groups:
                        line_z(g, way, r).wait_send()
    else:

        def line_send(r):
            pass

        line_take = line_pass = line_end = line_send

    def hidden_y(s):
        piece = pl.ds(pl.multiple_of(half * t, 16), half)
        return remote(hid.at[s, piece], hoth.at[s, piece], hys.at[s], hyr.at[s], {"ctx": across})

    def hidden_x(s):
        piece = pl.ds(pl.multiple_of(half * t, 16), half)
        return remote(hoth.at[s, piece], hoth.at[s, piece], hxs.at[s], hxr.at[s], {"tp": 1 - t})

    def block(s, owner):
        return kv.at[s, pl.ds(pl.multiple_of(owner * B, B), B)]

    def kv_copy(s, which):
        owner = c if which == 0 else across
        return remote(block(s, owner), block(s, owner), ks.at[s, which], kr.at[s, which], {"ctx": side})

    if gather:
        z_sent = first_z()
    hy = start([hidden_y(s) for s in range(S)])
    if gather:
        mine = pl.ds(pl.multiple_of(R * z, 16), R)
        owned = [
            pltpu.make_async_copy(shards[g], wq.at[:, mine] if g == 0 else whole[g].at[mine], lsem.at[g]) for g in range(4)
        ]
        for copy in owned:
            copy.start()
        crossed = start([remote(wo_sh, wo.at[t, mine], oxs, oxr, {"tp": 1 - t})])[0]
        line_send(0, (1, 2, 3))

    gain_row = row_of(gain)
    shift_row = row_of(shift)
    key_start = pl.multiple_of(jnp.maximum(c - 2, 0) * B, B)
    keys = 3 * B
    for s in range(S):
        low, _, _ = normalise(hid[s].astype(f32), gain_row, shift_row)
        normed[s] = low.astype(bf16)
    keep(normed, normed_out)
    for s in range(S):
        high, rest = fit_at(fit, places, s, lanes((L, 1), 0), L)
        fits[0, s] = high
        fits[1, s] = rest
    if gather:
        over, beside = first_y(z_sent)
        crossed.wait_recv()
        line_send(0, (4,))
    hx = []
    for s in range(S):
        hy[s].wait_recv()
        hx += start([hidden_x(s)])
    for s in range(S):
        bias[s] = mask_bias(lengths, s, c, B, key_start, keys)
    line_take(0)
    line_send(1)
    if gather:
        last = first_side(over)
    for s in range(S):
        hx[s].wait_recv()
        low, _, _ = normalise(hoth[s].astype(f32), gain_row, shift_row)
        noth[s] = low.astype(bf16)
    if gather:
        for copy in beside + last:
            copy.wait_recv()
        owned[0].wait()
        keep(wq, wq_out)
    kvs = []
    for s in range(S):
        for which, rows_in, owner in ((0, normed, c), (1, noth, across)):
            for k in (1, 2):
                part = dot_nn(rows_in[s], wq[k]) + qbias[k : k + 1]
                kv[s, pl.ds(pl.multiple_of(owner * B, B), B), (k - 1) * HW : k * HW] = part.astype(bf16)
            kvs += start([kv_copy(s, which)])
    for s in range(S):
        q[s] = (dot_nn(normed[s], wq[0]) + qbias[0:1]).astype(bf16)
    keep(q, q_out)
    line_take(1)
    line_send(2)

    centers = (lanes((1, NB), 1).astype(f32) + 0.5) * (1.0 / NB)
    width = 1.0 / NB
    lane = lanes((1, 2 * DH), 1)
    scaled = half_lanes(SCALE)
    mx = []
    for s in range(S):
        kvs[2 * s].wait_recv()
        kvs[2 * s + 1].wait_recv()
        keep(kv.at[s], kv_out.at[s])
        mem[s] = (dot_nn(fits[0, s], kv[s]) + dot_nn(fits[1, s], kv[s])).astype(bf16)

        def mixed_copy(s, p, cols):
            part = mixed.at[t, s, :, cols]
            return remote(part, part, ms.at[s, p], mr.at[s, p], {"tp": 1 - t})

        def pair_step(p, log_rows, s=s):
            cols = pl.ds(pl.multiple_of(p * 2 * DH, 2 * DH), 2 * DH)
            vcols = pl.ds(pl.multiple_of(HW + p * 2 * DH, 2 * DH), 2 * DH)
            window = pl.ds(key_start, keys)
            qp = q[s, :, cols]
            kp = kv[s, window, cols]
            vp = kv[s, window, vcols]
            mk = mem[s, :, cols]
            mv = mem[s, :, vcols]
            outs = []
            for h in range(2):
                qh = qp * scaled[h]
                scores = dot_nt(qh, kp) + bias[s]
                top = jnp.max(scores, axis=-1, keepdims=True)
                e = jnp.exp(scores - top)
                total = jnp.sum(e, axis=-1, keepdims=True)
                share = (e * (1.0 / total)).astype(bf16)
                out = dot_nn(share, vp)
                log_rows = jnp.where(lane == 2 * p + h, top + jnp.log(total), log_rows)
                mem_scores = dot_nt(qh, mk)
                reach, _, _, _, _ = reach_terms(
                    mem_scores, cw[pl.ds(2 * p + h, 1)], sw[pl.ds(2 * p + h, 1)], centers, width
                )
                outs.append(out + dot_nn(reach.astype(bf16), mv))
            mixed[t, s, :, cols] = jnp.where(lane < DH, outs[0], outs[1]).astype(bf16)
            mixed_copy(s, p, cols).start()
            return log_rows

        lse[s] = lax.fori_loop(0, HW // (2 * DH), pair_step, jnp.zeros((B, 2 * DH), f32))
        mx += [mixed_copy(s, p, pl.ds(p * 2 * DH, 2 * DH)) for p in range(HW // (2 * DH))]
        if s == 0:
            line_pass(0)
            line_take(2)
    line_pass(1)
    line_pass(2)
    for r in range(n - 1 if gather else 0):
        line_end(r)
    if gather:
        for copy in owned[1:]:
            copy.wait()
    for copy in mx:
        copy.wait_recv()
    for copy in started + mx:
        copy.wait_send()
    for copy in kept:
        copy.wait()


def forward(gather, hid, lengths, places, gain, shift, weights, qbias, cw, sw, fit):
    S, B, D = hid.shape
    HW = qbias.shape[1]
    n = lax.axis_size("dp")
    L = B * lax.axis_size("ctx")
    NB = cw.shape[1]
    vm = pl.BlockSpec(memory_space=pltpu.VMEM)
    sm = pl.BlockSpec(memory_space=pltpu.SMEM)
    hb = pl.BlockSpec(memory_space=pl.ANY)
    out = [
        jax.ShapeDtypeStruct((S, B, D), bf16),
        jax.ShapeDtypeStruct((S, B, HW), bf16),
        jax.ShapeDtypeStruct((S, L, 2 * HW), bf16),
        jax.ShapeDtypeStruct((S, NB, 2 * HW), bf16),
        jax.ShapeDtypeStruct((S, B, 128), f32),
        jax.ShapeDtypeStruct((2, S, B, HW), bf16),
    ]
    out_specs = [hb] * 3 + [vm] * 3
    sem = pltpu.SemaphoreType.DMA
    scratch = [
        pltpu.VMEM((S, B, D), bf16),
        pltpu.VMEM((S, B, HW), bf16),
        pltpu.VMEM((S, L, 2 * HW), bf16),
        pltpu.VMEM((S, B, D), bf16),
        pltpu.VMEM((S, B, D), bf16),
        pltpu.VMEM((S, B, 3 * B), f32),
        pltpu.VMEM((2, S, NB, L), bf16),
        sem((S + 3,)),
        *[sem((S,))] * 4,
        *[sem((S, 2))] * 2,
        *[sem((S, HW // (2 * DH)))] * 2,
    ]
    w_specs = [vm]
    if gather:
        FW = weights[2].shape[1]
        out += [
            jax.ShapeDtypeStruct((3, D, HW), bf16),
            jax.ShapeDtypeStruct((2, D, HW), bf16),
            jax.ShapeDtypeStruct((D, FW), bf16),
            jax.ShapeDtypeStruct((D, FW), bf16),
        ]
        out_specs += [hb] * 4
        w_specs = [vm] * 4
        scratch += [
            pltpu.VMEM((3, D, HW), bf16),
            sem((4,)),
            *[sem((n - 1,))] * 8,
            sem,
            sem,
            *[sem((4, 2, n - 1))] * 8,
        ]
    return pl.pallas_call(
        lambda *refs: forward_kernel(gather, refs),
        out_shape=out,
        in_specs=[vm, sm, vm, vm, vm, *w_specs, vm, vm, vm, vm],
        out_specs=out_specs,
        scratch_shapes=scratch,
        compiler_params=pltpu.CompilerParams(
            collective_id=0, has_side_effects=True, vmem_limit_bytes=VMEM_LIMIT
        ),
        cost_estimate=pl.CostEstimate(flops=6_000_000_000, bytes_accessed=30_000_000, transcendentals=6_000_000),
        name="forward_part",
    )(hid, lengths, places, gain, shift, *weights, qbias, cw, sw, fit)


def quarter(c):
    return 2 * lax.rem(c, 2) + c // 2


class Reduction:
    def __init__(self, n, rows, full, half, half_in, own, own_in, sems):
        self.n, self.rows, self.piece = n, rows, rows // 4
        self.full, self.half, self.half_in, self.own, self.own_in = full, half, half_in, own, own_in
        self.sems = sems
        self.z, self.c, self.t, self.side, self.across, self.corner = place()
        self.started = []

    def at(self, offset, size):
        return pl.ds(pl.multiple_of(offset, 16), size)

    def send_side(self):
        two = 2 * self.piece
        core = lax.rem(self.c, 2)
        self.one = remote(
            self.full.at[:, self.at(two * (1 - core), two)], self.half_in, self.sems[0].at[0], self.sems[1].at[0], {"ctx": self.side}
        )
        self.one.start()
        self.started.append(self.one)

    def sum_side(self):
        two = 2 * self.piece
        core = lax.rem(self.c, 2)
        self.one.wait_recv()
        for k in range(self.n):
            self.half[k] = (
                self.full[k, self.at(two * core, two)].astype(f32) + self.half_in[k].astype(f32)
            ).astype(bf16)

    def send_across(self):
        piece, y = self.piece, self.c // 2
        self.two = remote(
            self.half.at[:, self.at(piece * (1 - y), piece)], self.own_in, self.sems[0].at[1], self.sems[1].at[1], {"ctx": self.across}
        )
        self.two.start()
        self.started.append(self.two)

    def take_across(self):
        y = self.c // 2
        self.two.wait_recv()
        for k in range(self.n):
            self.own[k] = (
                self.half[k, self.at(self.piece * y, self.piece)].astype(f32) + self.own_in[k].astype(f32)
            ).astype(bf16)

    def wait_sends(self):
        for copy in self.started:
            copy.wait_send()


def mlp_kernel(gather, refs):
    (hid, mixed, wo, wf_far, wp_far, obias, gain, shift, fbias, cot_far,
     residual_out, mlp_out, gres_out, gmixed, og, pg, fg, sums, fsum,
     residual, mlp_part, gres, wf, wp, cot, low, act, gpre, gpart, gin, turned, glow, ls, outs, gs, gr, *rest) = refs
    if gather:
        pfull, phalf, phalf_in, pown_in, ffull, fhalf_in, ps, pr, fs, fr = rest
    else:
        pfull, ffull = pg, fg
    z, c, t, side, across, corner = place()
    S, B, D = hid.shape
    FW = wf.shape[1]
    HW = mixed.shape[3]
    n, R = pfull.shape[:2]
    tile = 512
    loads = [pltpu.make_async_copy(far, near, ls.at[i]) for i, (far, near) in enumerate(((wf_far, wf), (cot_far, cot), (wp_far, wp)))]
    for copy in loads:
        copy.start()
    kept = []

    def keep(src, dst):
        copy = pltpu.make_async_copy(src, dst, outs.at[len(kept)])
        copy.start()
        kept.append(copy)

    enter([{"tp": 1 - t}] + ([{"ctx": side}, {"ctx": across}] if gather else []))
    obias_row, gain_row, shift_row = row_of(obias), row_of(gain), row_of(shift)
    fsum[...] = jnp.zeros_like(fsum)
    copies = []
    for s in range(S):
        branch = dot_nt(mixed[0, s], wo[0]) + dot_nt(mixed[1, s], wo[1])
        wide = hid[s].astype(f32) + branch + obias_row
        residual[s] = wide
        value, _, _ = normalise(wide, gain_row, shift_row)
        low[s] = value.astype(bf16)
        keep(residual.at[s], residual_out.at[s])
        if s == 0:
            for copy in loads:
                copy.wait()

        def columns(j, carry, s=s):
            cols = pl.ds(pl.multiple_of(j * tile, tile), tile)
            pre = dot_nn(low[s], wf[:, cols]) + fbias[:, cols]
            square = pre * pre
            th = jnp.tanh(0.7978845608028654 * (pre + 0.044715 * (square * pre)))
            act[s, :, cols] = (0.5 * pre * (1.0 + th)).astype(bf16)
            slope = 0.5 * (1.0 + th) + (0.5 * pre) * (1.0 - th * th) * (
                0.7978845608028654 * (1.0 + 3.0 * 0.044715 * square)
            )
            grad = (dot_nn(cot[s], wp[:, cols]) * slope).astype(bf16)
            gpre[s, :, cols] = grad
            fsum[:, cols] += jnp.sum(grad.astype(f32), axis=0, keepdims=True)
            return carry

        lax.fori_loop(0, FW // tile, columns, 0)
        gpart[s] = dot_nt(gpre[s], wf[...]).astype(bf16)
        copies.append(remote(gpart.at[s], gin.at[s], gs.at[s], gr.at[s], {"tp": 1 - t}))
        copies[-1].start()

    def weight_grad(full, left, right, width, step):
        turned[...] = left.reshape(S * B, D).T

        def columns(j, carry):
            cols = pl.ds(pl.multiple_of(j * step, step), step)
            value = dot_nn(turned[...], right[:, :, cols].reshape(S * B, step)).astype(bf16)
            for k in range(n):
                full[k, :, cols] = value[k * R : (k + 1) * R]
            return carry

        lax.fori_loop(0, width // step, columns, 0)

    weight_grad(pfull, cot[...], act, FW, 256)
    if gather:
        proj = Reduction(n, R, pfull, phalf, phalf_in, pg, pown_in, (ps, pr))
        proj.send_side()
    weight_grad(ffull, low[...], gpre, FW, 256)
    if gather:
        fc = Reduction(n, R, ffull, fg, fhalf_in, None, None, (fs, fr))
        fc.send_side()
        proj.sum_side()
        proj.send_across()
    for s in range(S):
        mlp_part[s] = dot_nt(act[s], wp[...]).astype(bf16)
        keep(mlp_part.at[s], mlp_out.at[s])
    out_sum = jnp.zeros((1, D), f32)
    gain_sum = jnp.zeros((1, D), f32)
    shift_sum = jnp.zeros((1, D), f32)
    cot_sum = jnp.zeros((1, D), f32)
    for s in range(S):
        copies[s].wait_recv()
        grad = gpart[s].astype(f32) + gin[s].astype(f32)
        _, unit, r = normalise(residual[s], gain_row, shift_row)
        gain_sum += jnp.sum(grad * unit, axis=0, keepdims=True)
        shift_sum += jnp.sum(grad, axis=0, keepdims=True)
        a = grad * gain_row
        wide_cot = cot[s].astype(f32)
        cot_sum += jnp.sum(wide_cot, axis=0, keepdims=True)
        total = wide_cot + r * (
            a - jnp.mean(a, axis=-1, keepdims=True) - unit * jnp.mean(a * unit, axis=-1, keepdims=True)
        )
        out_sum += jnp.sum(total, axis=0, keepdims=True)
        gres[s] = total
        keep(gres.at[s], gres_out.at[s])
        glow[s] = total.astype(bf16)
        gmixed[s] = dot_nn(glow[s], wo[t]).astype(bf16)
        if s == 0 and gather:
            fc.sum_side()
    sums[0:1] = out_sum
    sums[1:2] = gain_sum
    sums[2:3] = shift_sum
    sums[3:4] = cot_sum
    weight_grad(og, glow[...], mixed.at[t], HW, 384)
    if gather:
        proj.take_across()
        proj.wait_sends()
        fc.wait_sends()
    for copy in copies:
        copy.wait_send()
    for copy in kept:
        copy.wait()


def mlp(gather, hid, mixed, wo, wf, wp, obias, gain, shift, fbias, cot):
    S, B, D = hid.shape
    HW = mixed.shape[3]
    FW = wf.shape[1]
    n = lax.axis_size("dp") if gather else 1
    R = D // n
    Q = R // 4
    vm = pl.BlockSpec(memory_space=pltpu.VMEM)
    sem = pltpu.SemaphoreType.DMA
    hb = pl.BlockSpec(memory_space=pl.ANY)
    pshape = (n, Q, FW) if gather else (n, R, FW)
    fshape = (n, 2 * Q, FW) if gather else (n, R, FW)
    out = [
        jax.ShapeDtypeStruct((S, B, D), f32),
        jax.ShapeDtypeStruct((S, B, D), bf16),
        jax.ShapeDtypeStruct((S, B, D), f32),
        jax.ShapeDtypeStruct((S, B, HW), bf16),
        jax.ShapeDtypeStruct((n, R, HW), bf16),
        jax.ShapeDtypeStruct(pshape, bf16),
        jax.ShapeDtypeStruct(fshape, bf16),
        jax.ShapeDtypeStruct((4, D), f32),
        jax.ShapeDtypeStruct((1, FW), f32),
    ]
    scratch = [
        pltpu.VMEM((S, B, D), f32),
        pltpu.VMEM((S, B, D), bf16),
        pltpu.VMEM((S, B, D), f32),
        pltpu.VMEM((D, FW), bf16),
        pltpu.VMEM((D, FW), bf16),
        pltpu.VMEM((S, B, D), bf16),
        pltpu.VMEM((S, B, D), bf16),
        pltpu.VMEM((S, B, FW), bf16),
        pltpu.VMEM((S, B, FW), bf16),
        pltpu.VMEM((S, B, D), bf16),
        pltpu.VMEM((S, B, D), bf16),
        pltpu.VMEM((D, S * B), bf16),
        pltpu.VMEM((S, B, D), bf16),
        sem((3,)),
        sem((3 * S,)),
        sem((S,)),
        sem((S,)),
    ]
    if gather:
        scratch += [
            pltpu.VMEM((n, R, FW), bf16),
            *[pltpu.VMEM((n, R // 2, FW), bf16)] * 2,
            pltpu.VMEM((n, Q, FW), bf16),
            pltpu.VMEM((n, R, FW), bf16),
            pltpu.VMEM((n, R // 2, FW), bf16),
            *[sem((2,))] * 4,
        ]
    return pl.pallas_call(
        lambda *refs: mlp_kernel(gather, refs),
        out_shape=out,
        in_specs=[vm, vm, vm, hb, hb, vm, vm, vm, vm, hb],
        out_specs=[hb, hb, hb, *[vm] * 6],
        scratch_shapes=scratch,
        compiler_params=pltpu.CompilerParams(
            collective_id=1, has_side_effects=True, vmem_limit_bytes=VMEM_LIMIT
        ),
        cost_estimate=pl.CostEstimate(flops=12_000_000_000, bytes_accessed=30_000_000, transcendentals=1_500_000),
        name="mlp_part",
    )(hid, mixed, wo, wf, wp, obias, gain, shift, fbias, cot)


def backward_kernel(gather, refs):
    (lengths, places, q, kv_far, mem, lse, gmixed, normed_far, wq_far, hid_far, gres_far, residual_far, mlp_far, pbias, gain,
     cw, sw, fit, sums, fsum, *rest) = refs
    if gather:
        (pown, fhalf, ofull, block_out, input_grad, early_out, late_out, fqkv, fo, ff, fp, *rest) = rest
    else:
        (block_out, input_grad, early_out, late_out, afull, kfull, vfull, *rest) = rest
    (kv, normed, wq, gres, residual, dkv, own_rows, dmem, gqkv, hs1, hr1, hs2, hr2, m1in, gmem, gfar,
     turned, mlp_in, gnpart, gnin, bias, early, ls, xs, xr, h1s, h1r, h2s, h2r, m1s, m1r, m2s, m2r, m3s, m3r, m4s, m4r, ns, nr,
     *rest) = rest
    if gather:
        (afull, kfull, vfull, ahalf_in, khalf_in, vhalf_in, ohalf_in, ahalf, khalf, vhalf, ohalf,
         aown, kown, vown, oown, fown, aown_in, kown_in, vown_in, oown_in, fown_in,
         zina, zink, zinv, zino, zinf, zinp, early_ctx, early_dp, late_ctx, late_dp,
         rs, rr, zs, zr, gs, gr, es, er) = rest
    z, c, t, side, across, corner = place()
    S, B, D = hid_far.shape
    HW = q.shape[2]
    NB = mem.shape[1]
    n, R = afull.shape[:2]
    L = kv_far.shape[1]
    keys = 3 * B
    key_start = pl.multiple_of(jnp.maximum(c - 2, 0) * B, B)
    pairs = [(kv_far.at[s, pl.ds(key_start, keys)], kv.at[s]) for s in range(S)] + [
        (normed_far, normed), (residual_far, residual), (wq_far, wq), (gres_far, gres)
    ]
    late_pairs = [(hid_far, kv.at[:, 0:B]), (mlp_far, kv.at[:, B : 2 * B])]
    loads = [pltpu.make_async_copy(far, near, ls.at[i]) for i, (far, near) in enumerate(pairs)]
    late_loads = [pltpu.make_async_copy(far, near, ls.at[S + 4 + i]) for i, (far, near) in enumerate(late_pairs)]
    for copy in loads:
        copy.start()
    peers = [{"tp": 1 - t}, {"ctx": side}, {"ctx": across}]
    if gather:
        peers += [{"ctx": corner}] + [{"dp": lax.rem(z + i, n)} for i in range(1, n)]
    enter(peers)
    started = []

    def start(copy):
        copy.start()
        started.append(copy)
        return copy

    if gather:
        Q = R // 4
        owns, zins, finals = {"p": pown, "f": fown}, {"p": zinp, "f": zinf}, {"p": fp, "f": ff}
        index = {g: i for i, g in enumerate("akvofp")}
        z_sent, g_sent = {}, {}

        def send_dp(g):
            j = index[g]
            z_sent[g] = [
                start(remote(owns[g].at[lax.rem(z + i, n)], zins[g].at[i - 1], zs.at[j, i - 1], zr.at[j, i - 1], {"dp": lax.rem(z + i, n)}))
                for i in range(1, n)
            ]

        def piece(g, device):
            return finals[g].at[pl.ds(pl.multiple_of(Q * quarter(device), 16), Q)]

        def take_dp(g):
            j = index[g]
            total = owns[g][z].astype(f32)
            for i in range(1, n):
                z_sent[g][i - 1].wait_recv()
                total = total + zins[g][i - 1].astype(f32)
            finals[g][pl.ds(pl.multiple_of(Q * quarter(c), 16), Q)] = total.astype(bf16)
            mine = piece(g, c)
            g_sent[g] = [
                start(remote(mine, mine, gs.at[j, 0], gr.at[j, 0], {"ctx": across})),
                start(remote(mine, mine, gs.at[j, 1], gr.at[j, 1], {"ctx": side})),
            ]

        def pass_on(g):
            j = index[g]
            g_sent[g][0].wait_recv()
            other = piece(g, across)
            g_sent[g].append(start(remote(other, other, gs.at[j, 2], gr.at[j, 2], {"ctx": side})))

        def take_all(g):
            g_sent[g][1].wait_recv()
            g_sent[g][2].wait_recv()

        class Chain(Reduction):
            def __init__(self, g, full, half, half_in, own, own_in, dp_in, final):
                j = index[g]
                super().__init__(n, R, full, half, half_in, own, own_in, (rs.at[j], rr.at[j]))
                self.j, self.dp_in, self.final = j, dp_in, final

            def send_dp(self):
                self.over = [
                    remote(self.half.at[lax.rem(z + i, n)], self.dp_in.at[i - 1], zs.at[self.j, i - 1], zr.at[self.j, i - 1], {"dp": lax.rem(z + i, n)})
                    for i in range(1, n)
                ]
                for copy in self.over:
                    start(copy)

            def take_dp(self):
                total = self.half[z].astype(f32)
                for i in range(1, n):
                    self.over[i - 1].wait_recv()
                    total = total + self.dp_in[i - 1].astype(f32)
                self.own[...] = total.astype(bf16)
                self.two = start(remote(self.own, self.own_in, gs.at[self.j, 0], gr.at[self.j, 0], {"ctx": across}))

            def take_across(self):
                self.two.wait_recv()
                mine = pl.ds(pl.multiple_of(2 * self.piece * lax.rem(c, 2), 16), 2 * self.piece)
                self.final[mine] = (self.own[...].astype(f32) + self.own_in[...].astype(f32)).astype(bf16)
                part = self.final.at[mine]
                self.three = start(remote(part, part, gs.at[self.j, 1], gr.at[self.j, 1], {"ctx": side}))

            def take_all(self):
                self.three.wait_recv()

        red = {
            "a": Chain("a", afull, ahalf, ahalf_in, aown, aown_in, zina, fqkv.at[0]),
            "k": Chain("k", kfull, khalf, khalf_in, kown, kown_in, zink, fqkv.at[1]),
            "v": Chain("v", vfull, vhalf, vhalf_in, vown, vown_in, zinv, fqkv.at[2]),
            "o": Chain("o", ofull, ohalf, ohalf_in, oown, oown_in, zino, fo),
        }
        fc = Reduction(n, R, None, fhalf, None, fown, fown_in, (rs.at[4], rr.at[4]))

        class Everywhere:
            def __init__(self, over_ctx, over_dp, which):
                self.over_ctx, self.over_dp, self.which = over_ctx, over_dp, which

            def send(self, slots, me, devices, step):
                j = 2 * self.which + step
                self.sent = [
                    start(remote(slots.at[me], slots.at[me], es.at[j, i], er.at[j, i], device)) for i, device in enumerate(devices)
                ]

            def first(self, value):
                self.over_ctx[c] = value
                self.send(self.over_ctx, c, [{"ctx": side}, {"ctx": across}, {"ctx": corner}], 0)

            def total(self, slots):
                for copy in self.sent:
                    copy.wait_recv()
                return (slots[0] + slots[1]) + (slots[2] + slots[3])

            def second(self):
                self.over_dp[z] = self.total(self.over_ctx)
                self.send(self.over_dp, z, [{"dp": lax.rem(z + i, n)} for i in range(1, n)], 1)

            def last(self, out):
                out[...] = self.total(self.over_dp)

        early_sum = Everywhere(early_ctx, early_dp, 0)
        late_sum = Everywhere(late_ctx, late_dp, 1)
        fc.send_across()
        send_dp("p")
        red["o"].send_side()

    mlp_sent = [
        start(remote(mlp_far.at[s], mlp_in.at[s], xs.at[s], xr.at[s], {"tp": 1 - t})) for s in range(S)
    ]

    lane = lanes((1, 2 * DH), 1)
    scaled = half_lanes(SCALE)
    plain = half_lanes(1.0)
    centers = (lanes((1, NB), 1).astype(f32) + 0.5) * (1.0 / NB)
    width = 1.0 / NB
    early[...] = jnp.zeros_like(early)
    half = HW
    core = lax.rem(c, 2)
    y = c // 2
    own_half = pl.ds(pl.multiple_of(core * half, 16), half)
    side_half = pl.ds(pl.multiple_of((1 - core) * half, 16), half)
    give = pl.ds(pl.multiple_of(B * (1 - core * (1 - y)), 128), B)
    own = pl.ds(pl.multiple_of(c * B - key_start, 128), B)
    one, two, three, first = {}, {}, {}, {}

    def second_copy(s):
        return remote(hs2.at[s], hr2.at[s], h2s.at[s], h2r.at[s], {"ctx": across})

    def memory_over(s):
        return remote(gmem.at[s, own_half], gfar.at[s, own_half], m2s.at[s], m2r.at[s], {"ctx": across})

    def memory_beside(s):
        return remote(gfar.at[s, own_half], gfar.at[s, own_half], m4s.at[s], m4r.at[s], {"ctx": side})

    def attend_back(s, between):
        loads[s].wait()
        bias[...] = mask_bias(lengths, s, c, B, key_start, keys)

        def pair_step(p, carry):
            cols = pl.ds(pl.multiple_of(p * 2 * DH, 2 * DH), 2 * DH)
            vcols = pl.ds(pl.multiple_of(HW + p * 2 * DH, 2 * DH), 2 * DH)
            qp = q[s, :, cols]
            gp = gmixed[s, :, cols]
            kp = kv[s, :, cols]
            vp = kv[s, :, vcols]
            mk = mem[s, :, cols]
            mv = mem[s, :, vcols]
            q_turned = (qp * SCALE).T
            g_turned = gp.T
            logs = lse[s]
            grad_q, dk, dv, dmk, dmv = [], [], [], [], []
            for h in range(2):
                row = 2 * p + h
                part = slice(h * DH, (h + 1) * DH)
                qh = qp * scaled[h]
                gh = gp * plain[h]
                log_total = jnp.sum(jnp.where(lane == row, logs, 0.0), axis=-1, keepdims=True)
                share = jnp.exp(dot_nt(qh, kp) + bias[...] - log_total)
                grad_share = dot_nt(gh, vp)
                delta = jnp.sum(share * grad_share, axis=-1, keepdims=True)
                grad_score = (share * (grad_share - delta)).astype(bf16)
                mem_scores = dot_nt(qh, mk)
                cw_row = cw[pl.ds(row, 1)]
                sw_row = sw[pl.ds(row, 1)]
                reach, mu, inv, diff, spread_logit = reach_terms(mem_scores, cw_row, sw_row, centers, width)
                grad_reach = dot_nt(gh, mv) * reach
                scaled_diff = diff * inv
                grad_mu = -jnp.sum(grad_reach * scaled_diff, axis=-1, keepdims=True)
                grad_var = jnp.sum(
                    grad_reach * (0.5 * scaled_diff * scaled_diff - 0.5 * inv), axis=-1, keepdims=True
                )
                gc = grad_mu * mu * (1.0 - mu)
                gw = SPREAD * grad_var * (1.0 / (1.0 + jnp.exp(-spread_logit)))
                early[pl.ds(8 + row, 1), 0:NB] += jnp.sum(gc * mem_scores, axis=0, keepdims=True)
                early[pl.ds(8 + row, 1), NB : 2 * NB] += jnp.sum(gw * mem_scores, axis=0, keepdims=True)
                grad_mem = (gc * cw_row + gw * sw_row).astype(bf16)
                grad_q.append((dot_nn(grad_score, kp) + dot_nn(grad_mem, mk)) * SCALE)
                dk.append(dot_nn(q_turned[part], grad_score))
                dv.append(dot_nn(g_turned[part], share.astype(bf16)))
                dmk.append(dot_nn(q_turned[part], grad_mem))
                dmv.append(dot_nn(g_turned[part], reach.astype(bf16)))
            gqkv[s, :, cols] = jnp.where(lane < DH, grad_q[0], grad_q[1]).astype(bf16)
            for h in range(2):
                rows = pl.ds(pl.multiple_of((2 * p + h) * DH, DH), DH)
                vrows = pl.ds(pl.multiple_of(HW + (2 * p + h) * DH, DH), DH)
                dkv[rows] = dk[h]
                dkv[vrows] = dv[h]
                dmem[s, rows] = dmk[h]
                dmem[s, vrows] = dmv[h]
            return carry

        lax.fori_loop(0, 1, pair_step, 0)
        between()
        lax.fori_loop(1, HW // (2 * DH), pair_step, 0)
        one[s] = start(remote(dmem.at[s, side_half], m1in.at[s], m1s.at[s], m1r.at[s], {"ctx": side}))
        hs1[s] = dkv[:, give].astype(bf16)
        first[s] = start(remote(hs1.at[s], hr1.at[s], h1s.at[s], h1r.at[s], {"ctx": side}))
        own_rows[s] = dkv[:, own]
        hs2[s] = dkv[:, 0:B].astype(bf16)

    def chip_memory(s):
        one[s].wait_recv()
        gmem[s, own_half] = (dmem[s, own_half] + m1in[s]).astype(bf16)
        three[s] = start(remote(gmem.at[s, own_half], gmem.at[s, own_half], m3s.at[s], m3r.at[s], {"ctx": side}))

        @pl.when(y == 0)
        def _():
            memory_over(s).start()

    def rows_of_memory(s, grad, owner):
        high, low = fit_at(fit, places, s, owner * B + lanes((B, 1), 0), L)
        return dot_nn(grad, high) + dot_nn(grad, low)

    def give_across(s):
        first[s].wait_recv()
        three[s].wait_recv()

        @pl.when(c != 3)
        def _():
            own_rows[s] = own_rows[s] + hr1[s].astype(f32)

        @pl.when(y == 1)
        def _():
            beside = jnp.where(c == 3, 1.0, 0.0)
            total = hs2[s].astype(f32) + beside * hr1[s].astype(f32) + rows_of_memory(s, gmem[s], across)
            hs2[s] = total.astype(bf16)
            second_copy(s).start()

    sent = {}

    def pass_memory(s):
        @pl.when(y == 1)
        def _():
            memory_over(s).wait_recv()
            memory_beside(s).start()

    def finish_rows(s):
        high, low = fit_at(fit, places, s, c * B + lanes((B, 1), 0), L)
        own_rows[s] = own_rows[s] + dot_nn(gmem[s], high) + dot_nn(gmem[s], low)

        @pl.when(y == 1)
        def _():
            memory_beside(s).wait_recv()
            own_rows[s] = own_rows[s] + dot_nn(gfar[s], high) + dot_nn(gfar[s], low)

        @pl.when(y == 0)
        def _():
            second_copy(s).wait_recv()
            own_rows[s] = own_rows[s] + hr2[s].astype(f32)

        gqkv[s, :, HW:] = own_rows[s].T.astype(bf16)
        parts = [dot_nt(gqkv[s, :, k * HW : (k + 1) * HW], wq[k]) for k in range(3)]
        gnpart[s] = (parts[0] + parts[1] + parts[2]).astype(bf16)
        sent[s] = start(remote(gnpart.at[s], gnin.at[s], ns.at[s], nr.at[s], {"tp": 1 - t}))

    def finish_block(s):
        mlp_sent[s].wait_recv()
        total = kv[s, B : 2 * B].astype(f32) + mlp_in[s].astype(f32)
        block_out[s] = (residual[s] + total + row_of(pbias)).astype(bf16)

    def weight_grad(full, k):
        value = dot_nn(turned[...], gqkv[:, :, k * HW : (k + 1) * HW].reshape(S * B, HW)).astype(bf16)
        for i in range(n):
            full[i] = value[i * R : (i + 1) * R]

    column_sums = []
    gain_row = row_of(gain)

    def norm_back(s):
        sent[s].wait_recv()
        grad = gnpart[s].astype(f32) + gnin[s].astype(f32)
        _, unit, r = normalise(kv[s, 0:B].astype(f32), gain_row, gain_row)
        column_sums.append((jnp.sum(grad * unit, axis=0, keepdims=True), jnp.sum(grad, axis=0, keepdims=True)))
        a = grad * gain_row
        back = r * (a - jnp.mean(a, axis=-1, keepdims=True) - unit * jnp.mean(a * unit, axis=-1, keepdims=True))
        input_grad[s] = (gres[s] + back).astype(bf16)

    attend_back(0, lambda: None)
    if gather:
        red["o"].sum_side()
        red["o"].send_dp()
    attend_back(1, lambda: chip_memory(0))
    if gather:
        fc.take_across()
        send_dp("f")
    give_across(0)
    pass_memory(0)
    attend_back(2, lambda: chip_memory(1))
    for copy in late_loads:
        copy.start()
    give_across(1)
    pass_memory(1)
    chip_memory(2)
    for copy in loads[S:]:
        copy.wait()
    finish_rows(0)
    give_across(2)
    turned[...] = normed[...].reshape(S * B, D).T
    weight_grad(afull, 0)
    if gather:
        red["a"].send_side()
    pass_memory(2)
    early[0:4, 0:D] = sums[...]
    for k in range(fsum.shape[1] // D):
        early[4 + k : 5 + k] = fsum[:, k * D : (k + 1) * D]
    if gather:
        early_sum.first(early[...])
    for copy in late_loads:
        copy.wait()
    finish_block(0)
    if gather:
        red["a"].sum_side()
        red["a"].send_dp()
    finish_block(1)
    finish_rows(1)
    finish_block(2)
    finish_rows(2)
    weight_grad(kfull, 1)
    if gather:
        red["k"].send_side()
    weight_grad(vfull, 2)
    if gather:
        red["v"].send_side()
        early_sum.second()
        red["k"].sum_side()
        red["k"].send_dp()
        red["v"].sum_side()
        red["v"].send_dp()
    norm_back(0)
    bias_sum = jnp.sum(gqkv[...].reshape(S * B, 3 * HW).astype(f32), axis=0, keepdims=True)
    norm_back(1)
    if gather:
        take_dp("p")
        take_dp("f")
        red["o"].take_dp()
        red["a"].take_dp()
    norm_back(2)
    room = late_ctx.at[c] if gather else late_out
    room[...] = jnp.zeros(room.shape, f32)
    room[0:1, 0:D] = column_sums[0][0] + column_sums[1][0] + column_sums[2][0]
    room[1:2, 0:D] = column_sums[0][1] + column_sums[1][1] + column_sums[2][1]
    room[2:3, 0 : 3 * HW] = bias_sum
    if gather:
        late_sum.send(late_ctx, c, [{"ctx": side}, {"ctx": across}, {"ctx": corner}], 0)
        pass_on("p")
        pass_on("f")
        for g in "oa":
            red[g].take_across()
        late_sum.second()
        red["k"].take_dp()
        red["v"].take_dp()
        early_sum.last(early_out)
        late_sum.last(late_out)
        red["k"].take_across()
        red["v"].take_across()
        take_all("p")
        take_all("f")
        fc.wait_sends()
        for chain in red.values():
            chain.take_all()
        for chain in red.values():
            chain.wait_sends()
    else:
        early_out[...] = early[...]
    for s in range(S):

        @pl.when(y == 1)
        def _(s=s):
            second_copy(s).wait_send()
            memory_beside(s).wait_send()

        @pl.when(y == 0)
        def _(s=s):
            memory_over(s).wait_send()

    for copy in started:
        copy.wait_send()


def backward(gather, lengths, places, q, kv, mem, lse, gmixed, normed, wq, hid, gres, residual, mlp_part, pbias, gain, cw, sw,
             fit, sums, fsum, owned):
    S, B, D = hid.shape
    HW = q.shape[2]
    FW = fsum.shape[1]
    H, NB = cw.shape
    n = lax.axis_size("dp") if gather else 1
    R = D // n
    Q = R // 4
    rows = -(-(8 + H) // 8) * 8
    vm = pl.BlockSpec(memory_space=pltpu.VMEM)
    sm = pl.BlockSpec(memory_space=pltpu.SMEM)
    hb = pl.BlockSpec(memory_space=pl.ANY)
    sem = pltpu.SemaphoreType.DMA
    late = (8, max(D, 3 * HW))
    out = [
        jax.ShapeDtypeStruct((S, B, D), bf16),
        jax.ShapeDtypeStruct((S, B, D), bf16),
        jax.ShapeDtypeStruct((rows, D), f32),
        jax.ShapeDtypeStruct(late, f32),
    ]
    if gather:
        out += [jax.ShapeDtypeStruct((3, R, HW), bf16)] + [jax.ShapeDtypeStruct((R, w), bf16) for w in (HW, FW, FW)]
    else:
        out += [jax.ShapeDtypeStruct((n, R, HW), bf16)] * 3
    scratch = [
        pltpu.VMEM((S, 3 * B, 2 * HW), bf16),
        pltpu.VMEM((S, B, D), bf16),
        pltpu.VMEM((3, D, HW), bf16),
        pltpu.VMEM((S, B, D), f32),
        pltpu.VMEM((S, B, D), f32),
        pltpu.VMEM((2 * HW, 3 * B), f32),
        pltpu.VMEM((S, 2 * HW, B), f32),
        pltpu.VMEM((S, 2 * HW, NB), f32),
        pltpu.VMEM((S, B, 3 * HW), bf16),
        *[pltpu.VMEM((S, 2 * HW, B), bf16)] * 4,
        pltpu.VMEM((S, HW, NB), f32),
        pltpu.VMEM((S, 2 * HW, NB), bf16),
        pltpu.VMEM((S, 2 * HW, NB), bf16),
        pltpu.VMEM((D, S * B), bf16),
        *[pltpu.VMEM((S, B, D), bf16)] * 3,
        pltpu.VMEM((B, 3 * B), f32),
        pltpu.VMEM((rows, D), f32),
        sem((S + 6,)),
        *[sem((S,))] * 16,
    ]
    if gather:
        scratch += [
            *[pltpu.VMEM((n, R, HW), bf16)] * 3,
            *[pltpu.VMEM((n, 2 * Q, HW), bf16)] * 8,
            *[pltpu.VMEM((2 * Q, HW), bf16)] * 4,
            pltpu.VMEM((n, Q, FW), bf16),
            *[pltpu.VMEM((2 * Q, HW), bf16)] * 4,
            pltpu.VMEM((n, Q, FW), bf16),
            *[pltpu.VMEM((n - 1, 2 * Q, HW), bf16)] * 4,
            *[pltpu.VMEM((n - 1, Q, FW), bf16)] * 2,
            *[pltpu.VMEM((4, rows, D), f32)] * 2,
            *[pltpu.VMEM((4, *late), f32)] * 2,
            *[sem((6, 2))] * 2,
            *[sem((6, n - 1))] * 2,
            *[sem((6, 3))] * 2,
            *[sem((4, 3))] * 2,
        ]
    args = [lengths, places, q, kv, mem, lse, gmixed, normed, wq, hid, gres, residual, mlp_part, pbias, gain, cw, sw, fit, sums,
            fsum, *owned]
    far = (3, 7, 8, 9, 10, 11, 12)
    return pl.pallas_call(
        lambda *refs: backward_kernel(gather, refs),
        out_shape=out,
        in_specs=[sm] + [hb if i in far else vm for i in range(1, len(args))],
        out_specs=[vm] * len(out),
        scratch_shapes=scratch,
        compiler_params=pltpu.CompilerParams(
            collective_id=2, has_side_effects=True, vmem_limit_bytes=VMEM_LIMIT
        ),
        cost_estimate=pl.CostEstimate(flops=12_000_000_000, bytes_accessed=40_000_000, transcendentals=6_000_000),
        name="backward_part",
    )(*args)


def finish_kernel(fqkv, fo, ff, fp, early, late, block_in, grad_in, qkv, out, fc, proj, block, grad, qb, cgrad, sgrad, *vectors):
    HW = fqkv.shape[2]
    D = vectors[0].shape[0]
    H, NB = cgrad.shape
    for k in range(3):
        qb[k : k + 1] = late[2:3, k * HW : (k + 1) * HW]
    qkv[...] = fqkv[...].astype(f32)
    out[...] = fo[...].astype(f32)
    fc[...] = ff[...].astype(f32)
    proj[...] = fp[...].astype(f32)
    block[...] = block_in[...]
    grad[...] = grad_in[...]
    cgrad[...] = early[8 : 8 + H, 0:NB]
    sgrad[...] = early[8 : 8 + H, NB : 2 * NB]
    rows = [late[k : k + 1, 0:D] for k in range(2)] + [early[k : k + 1, 0:D] for k in range(4)]
    for vector, row in zip(vectors, rows):
        vector[...] = row.reshape(vector.shape)
    for k in range(vectors[6].shape[0] // D):
        vectors[6][k * D : (k + 1) * D] = early[4 + k : 5 + k].reshape(D)


def finish(parts, early, late, block_out, input_grad, D, H, NB):
    _, R, HW = parts[0].shape
    FW = parts[2].shape[1]
    vm = pl.BlockSpec(memory_space=pltpu.VMEM)
    shapes = [(3, R, HW), (R, HW), (R, FW), (R, FW)]
    more = [(3, HW), (H, NB), (H, NB)] + [(D,)] * 6 + [(FW,)]
    copied = [jax.ShapeDtypeStruct(v.shape, v.dtype) for v in (block_out, input_grad)]
    return pl.pallas_call(
        finish_kernel,
        out_shape=[jax.ShapeDtypeStruct(v, f32) for v in shapes] + copied + [jax.ShapeDtypeStruct(v, f32) for v in more],
        in_specs=[vm] * 8,
        out_specs=[vm] * (len(shapes) + 2 + len(more)),
        compiler_params=pltpu.CompilerParams(vmem_limit_bytes=VMEM_LIMIT),
        name="finish_part",
    )(*parts, early, late, block_out, input_grad)


def per_device(hidden_in, doc_lengths, sticky_places, attn_gain, attn_shift, qkv_weight, qkv_bias, center_weight,
               spread_weight, out_weight, out_bias, mlp_gain, mlp_shift, fc_weight, fc_bias, proj_weight, proj_bias,
               cotangent):
    S, B, D = hidden_in.shape
    n = lax.axis_size("dp")
    HW = qkv_bias.shape[1]
    H, NB = center_weight.shape
    M = sticky_places.shape[1]
    fit = jnp.asarray(ridge_fit(NB, 2 * M))
    gather = n == 4 and D % (64 * n) == 0
    weights = [jnp.transpose(qkv_weight, (1, 0, 2)), out_weight.T, fc_weight, proj_weight.T]
    if not gather:
        full = [lax.all_gather(w, "dp", axis=w.ndim - 2, tiled=True) for w in weights]
        weights = full[:1]
    made = forward(gather, hidden_in, doc_lengths, sticky_places, attn_gain, attn_shift, weights,
                   qkv_bias, center_weight, spread_weight, fit)
    normed, q, kv, mem, lse, mixed = made[:6]
    if gather:
        wq, wo, wf, wp = made[6:]
    else:
        wq, wo, wf, wp = full
        wo = lax.all_gather(wo, "tp", axis=0)
    made = mlp(gather, hidden_in, mixed, wo, wf, wp, out_bias, mlp_gain, mlp_shift, fc_bias[None], cotangent)
    residual, mlp_part, gres, gmixed, og, pg, fg, sums, fsum = made
    owned = [pg, fg, og] if gather else []
    made = backward(gather, doc_lengths, sticky_places, q, kv, mem, lse, gmixed, normed, wq, hidden_in, gres, residual, mlp_part,
                    proj_bias, attn_gain, center_weight, spread_weight, fit, sums, fsum, owned)
    block_out, input_grad, early, late = made[:4]
    if gather:
        made = finish(made[4:], early, late, block_out, input_grad, D, H, NB)
        qkv_grad, out_grad, fc_grad, proj_grad, block_out, input_grad, qkv_bias_grad, center_grad, spread_grad = made[:9]
        gain_grad, shift_grad, out_bias_grad, mlp_gain_grad, mlp_shift_grad, proj_bias_grad, fc_bias_grad = made[9:]
        qkv_grad, out_grad, proj_grad = jnp.transpose(qkv_grad, (1, 0, 2)), out_grad.T, proj_grad.T
    else:
        early, late = lax.psum((early, late), ("dp", "ctx"))

        def reduced(grad):
            part = lax.psum_scatter(grad.reshape(D, -1), "dp", scatter_dimension=0, tiled=True)
            return lax.psum(part, "ctx").astype(f32)

        qkv_grad = jnp.stack([reduced(g) for g in made[4:]], axis=1)
        out_grad, fc_grad, proj_grad = reduced(og).T, reduced(fg), reduced(pg).T
        qkv_bias_grad = late[2, : 3 * HW].reshape(3, HW)
        center_grad, spread_grad = early[8 : 8 + H, :NB], early[8 : 8 + H, NB : 2 * NB]
        gain_grad, shift_grad = late[0, :D], late[1, :D]
        out_bias_grad, mlp_gain_grad, mlp_shift_grad, proj_bias_grad = [early[k, :D] for k in range(4)]
        fc_bias_grad = early[4 : 4 + fc_bias.shape[0] // D].reshape(-1)
    return (
        block_out,
        input_grad,
        gain_grad,
        shift_grad,
        qkv_grad,
        qkv_bias_grad,
        center_grad,
        spread_grad,
        out_grad,
        out_bias_grad,
        mlp_gain_grad,
        mlp_shift_grad,
        fc_grad,
        fc_bias_grad,
        proj_grad,
        proj_bias_grad,
    )


def solution(mesh):
    in_specs = (
        P("dp", "ctx", None),
        P("dp", None),
        P("dp", None),
        P(),
        P(),
        P("dp", None, "tp"),
        P(None, "tp"),
        P("tp", None),
        P("tp", None),
        P("tp", "dp"),
        P(),
        P(),
        P(),
        P("dp", "tp"),
        P("tp"),
        P("tp", "dp"),
        P(),
        P("dp", "ctx", None),
    )
    out_specs = (
        P("dp", "ctx", None),
        P("dp", "ctx", None),
        P(),
        P(),
        P("dp", None, "tp"),
        P(None, "tp"),
        P("tp", None),
        P("tp", None),
        P("tp", "dp"),
        P(),
        P(),
        P(),
        P("dp", "tp"),
        P("tp"),
        P("tp", "dp"),
        P(),
    )
    return jax.shard_map(
        per_device, mesh=mesh, in_specs=in_specs, out_specs=out_specs, check_vma=False
    )
```

```python
import functools

import jax
import jax.numpy as jnp
import numpy as np
from jax import lax
from jax.experimental import pallas as pl
from jax.experimental.pallas import tpu as pltpu
from jax.sharding import PartitionSpec as P

DH = 64
WINDOW = 512
EPS = 1e-05
SPREAD = 0.02
SCALE = DH ** (-0.5)
VMEM_LIMIT = 60 * 1024 * 1024

bf16 = jnp.bfloat16
f32 = jnp.float32
MESH = pl.DeviceIdType.MESH


def dot_nn(a, b):
    return lax.dot_general(a, b, (((1,), (0,)), ((), ())), preferred_element_type=f32)


def dot_nt(a, b):
    return lax.dot_general(a, b, (((1,), (1,)), ((), ())), preferred_element_type=f32)


def dot_tn(a, b):
    return lax.dot_general(a, b, (((0,), (0,)), ((), ())), preferred_element_type=f32)


def ridge_fit(basis_count, sample_count):
    centers = (np.arange(basis_count) + 0.5) / basis_count
    times = (np.arange(sample_count) + 0.5) / sample_count
    width = 1.0 / basis_count
    design = np.exp(-np.square(times[None, :] - centers[:, None]) / (2.0 * width * width))
    gram = design @ design.T + 0.5 * np.eye(basis_count)
    return np.linalg.solve(gram, design).astype(bf16)


def place():
    c = lax.axis_index("ctx")
    side = c + 1 - 2 * lax.rem(c, 2)
    across = lax.rem(c + 2, 4)
    corner = lax.rem(side + 2, 4)
    return lax.axis_index("dp"), c, lax.axis_index("tp"), side, across, corner


def knock(devices):
    barrier = pltpu.get_barrier_semaphore()
    for device in devices:
        pl.semaphore_signal(barrier, inc=1, device_id=device, device_id_type=MESH)
    return lambda: pl.semaphore_wait(barrier, len(devices))


def remote(src, dst, send, recv, device):
    return pltpu.make_async_remote_copy(
        src_ref=src,
        dst_ref=dst,
        send_sem=send,
        recv_sem=recv,
        device_id=device,
        device_id_type=MESH,
    )


def normalise(x, gain, shift):
    mean = jnp.mean(x, axis=-1, keepdims=True)
    centred = x - mean
    r = lax.rsqrt(jnp.mean(centred * centred, axis=-1, keepdims=True) + EPS)
    n = centred * r
    return n * gain + shift, n, r


def lowest_key(lengths, s, pos):
    low = jnp.maximum(pos - (WINDOW - 1), 0)
    end = jnp.int32(0)
    for e in range(lengths.shape[1]):
        end = end + lengths[s, e]
        low = jnp.maximum(low, jnp.where(pos >= end, end, 0))
    return low


def row_of(vector):
    return vector[...].reshape(1, vector.shape[0])


def lanes(shape, dim):
    return lax.broadcasted_iota(jnp.int32, shape, dim)


def half_lanes(scale):
    lane = lanes((1, 2 * DH), 1)
    return [
        jnp.where(lane < DH, scale, 0.0).astype(bf16),
        jnp.where(lane >= DH, scale, 0.0).astype(bf16),
    ]


def mask_bias(lengths, s, c, rows, key_start, keys):
    pos = c * rows + lanes((rows, 1), 0)
    low = lowest_key(lengths, s, pos)
    key_pos = key_start + lanes((1, keys), 1)
    return jnp.where((key_pos <= pos) & (key_pos >= low), 0.0, -1e30)


def fit_at(fit, places, s, tokens, length):
    M = places.shape[1]
    sticky = jnp.where(tokens == places[s : s + 1, :], 1.0, 0.0).astype(bf16)
    even = lanes((1, M), 1) * length // M + length // (2 * M)
    steady = jnp.where(tokens == even, 1.0, 0.0).astype(bf16)
    value = dot_nt(fit[:, :M], sticky) + dot_nt(fit[:, M:], steady)
    high = value.astype(bf16)
    return high, (value - high.astype(f32)).astype(bf16)


def reach_terms(scores, center_row, spread_row, centers, width):
    center_logit = jnp.sum(scores * center_row, axis=-1, keepdims=True)
    spread_logit = jnp.sum(scores * spread_row, axis=-1, keepdims=True)
    mu = 1.0 / (1.0 + jnp.exp(-center_logit))
    grown = jnp.exp(spread_logit)
    var = SPREAD * jnp.log(1.0 + grown) + width * width
    inv = 1.0 / var
    diff = mu - centers
    reach = (width * lax.rsqrt(var)) * jnp.exp(-(diff * diff) * (0.5 * inv))
    return reach, mu, inv, diff, spread_logit


def forward_kernel(gather, refs):
    n = lax.axis_size("dp")
    if gather:
        (hid, lengths, places, gain, shift, wq_sh, wo_sh, wf_sh, wp_sh, qbias, cw, sw, fit, cot_far,
         turned_out, cot_out, bias_out, q_out, kv_out, mem, lse, mixed, wq_out, wo, wf, wp,
         normed, q, kv, hoth, noth, bias, fits, turned, cot, cot_turned, cs, os_, hys, hyr, hxs, hxr, ks, kr, ms, mr,
         wq, lsem, zs, zr, ys, yr, as_, ar, bs, br, oxs, oxr, lzs, lzr, lys, lyr, las, lar, lbs, lbr) = refs
    else:
        (hid, lengths, places, gain, shift, wq, qbias, cw, sw, fit, cot_far,
         turned_out, cot_out, bias_out, q_out, kv_out, mem, lse, mixed,
         normed, q, kv, hoth, noth, bias, fits, turned, cot, cot_turned, cs, os_, hys, hyr, hxs, hxr, ks, kr, ms, mr) = refs
    z, c, t, side, across, corner = place()
    S, B, D = hid.shape
    HW = q.shape[2]
    NB = mem.shape[1]
    L = kv.shape[1]
    half = B // 2
    peers = [{"ctx": side}, {"ctx": across}, {"tp": 1 - t}]
    if gather:
        R = D // n
        Q = R // 4
        shards = [wq_sh, wo_sh, wf_sh, wp_sh]
        whole = [wq, wo.at[t], wf, wp, wo.at[1 - t]]
        peers += [{"dp": lax.rem(z + i, n)} for i in range(1, n)]
    wait_for_all = knock(peers)
    cot_copy = pltpu.make_async_copy(cot_far, cot, cs)
    cot_copy.start()
    wait_for_all()

    started, kept = [], []

    def start(copies):
        for copy in copies:
            copy.start()
        started.extend(copies)
        return copies

    def keep(src, dst):
        copy = pltpu.make_async_copy(src, dst, os_.at[len(kept)])
        copy.start()
        kept.append(copy)

    if gather:
        groups = range(1, 5)

        def rows(g, owner, quarter):
            part = pl.ds(pl.multiple_of(R * owner + Q * quarter, 16), Q)
            return wq.at[:, part] if g == 0 else whole[g].at[part]

        def source(i):
            return lax.rem(z + n - i, n)

        def part_rows(part, owner, quarter):
            rows_here = pl.ds(pl.multiple_of(R * owner + Q * quarter, 16), Q)
            return wq.at[1:3, rows_here] if part == 0 else wq.at[0:1, rows_here]

        def first_z(part):
            mine_here = pl.ds(pl.multiple_of(Q * c, 16), Q)
            src = wq_sh.at[1:3, mine_here] if part == 0 else wq_sh.at[0:1, mine_here]
            return start([
                remote(src, part_rows(part, z, c), zs.at[part, i - 1], zr.at[part, i - 1], {"dp": lax.rem(z + i, n)})
                for i in range(1, n)
            ])

        def first_y(part, sent):
            over, beside = [], []
            for i, copy in enumerate(sent):
                copy.wait_recv()
                w = part_rows(part, source(i + 1), c)
                over += start([remote(w, w, ys.at[part, i], yr.at[part, i], {"ctx": across})])
                beside += start([remote(w, w, as_.at[part, i], ar.at[part, i], {"ctx": side})])
            return over, beside

        def first_side(part, over):
            last = []
            for i, copy in enumerate(over):
                copy.wait_recv()
                w = part_rows(part, source(i + 1), across)
                last += start([remote(w, w, bs.at[part, i], br.at[part, i], {"ctx": side})])
            return last

        def sends(way, r):
            return ((z < n - 1) & (z >= r)) if way == 0 else ((z > 0) & (z + r < n))

        def takes(way, r):
            return (z > r) if way == 0 else (z + r < n - 1)

        def line_z(g, way, r):
            owner = z - r if way == 0 else z + r
            to = z + 1 if way == 0 else z - 1
            dst = rows(g, owner, c)
            src = shards[g].at[pl.ds(pl.multiple_of(Q * c, 16), Q)] if r == 0 and g < 4 else dst
            return remote(src, dst, lzs.at[g - 1, way, r], lzr.at[g - 1, way, r], {"dp": to})

        def line_copy(g, way, r, sems, quarter, device):
            part = rows(g, z - 1 - r if way == 0 else z + 1 + r, quarter)
            return remote(part, part, sems[0].at[g - 1, way, r], sems[1].at[g - 1, way, r], {"ctx": device})

        def line_y(g, way, r):
            return line_copy(g, way, r, (lys, lyr), c, across)

        def line_a(g, way, r):
            return line_copy(g, way, r, (las, lar), c, side)

        def line_b(g, way, r):
            return line_copy(g, way, r, (lbs, lbr), across, side)

        def line_send(r, some=groups):
            for way in range(2):

                @pl.when(sends(way, r))
                def _(way=way):
                    for g in some:
                        line_z(g, way, r).start()

        def line_take(r):
            for way in range(2):

                @pl.when(takes(way, r))
                def _(way=way):
                    for g in groups:
                        line_z(g, way, r).wait_recv()
                        line_y(g, way, r).start()
                        line_a(g, way, r).start()

        def line_pass(r):
            for way in range(2):

                @pl.when(takes(way, r))
                def _(way=way):
                    for g in groups:
                        line_y(g, way, r).wait_recv()
                        line_b(g, way, r).start()

        def line_end(r):
            for way in range(2):

                @pl.when(takes(way, r))
                def _(way=way):
                    for g in groups:
                        line_a(g, way, r).wait_recv()
                        line_b(g, way, r).wait_recv()
                        line_y(g, way, r).wait_send()
                        line_a(g, way, r).wait_send()
                        line_b(g, way, r).wait_send()

                @pl.when(sends(way, r))
                def _(way=way):
                    for g in groups:
                        line_z(g, way, r).wait_send()
    else:

        def line_send(r):
            pass

        line_take = line_pass = line_end = line_send

    def hidden_y(s):
        piece = pl.ds(pl.multiple_of(half * t, 16), half)
        return remote(hid.at[s, piece], hoth.at[s, piece], hys.at[s], hyr.at[s], {"ctx": across})

    def hidden_x(s):
        piece = pl.ds(pl.multiple_of(half * t, 16), half)
        return remote(hoth.at[s, piece], hoth.at[s, piece], hxs.at[s], hxr.at[s], {"tp": 1 - t})

    def block(s, owner):
        return kv.at[s, pl.ds(pl.multiple_of(owner * B, B), B)]

    def kv_copy(s, which):
        owner = c if which == 0 else across
        return remote(block(s, owner), block(s, owner), ks.at[s, which], kr.at[s, which], {"ctx": side})

    if gather:
        z_sent = [first_z(0)]
    hy = start([hidden_y(s) for s in range(S)])
    if gather:
        z_sent.append(first_z(1))
        mine = pl.ds(pl.multiple_of(R * z, 16), R)
        owned = [
            pltpu.make_async_copy(shards[g], wq.at[:, mine] if g == 0 else whole[g].at[mine], lsem.at[g]) for g in range(4)
        ]
        for copy in owned:
            copy.start()
        crossed = start([remote(wo_sh, wo.at[t, mine], oxs, oxr, {"tp": 1 - t})])[0]
        line_send(0, (1, 2, 3))

    gain_row = row_of(gain)
    shift_row = row_of(shift)
    key_start = pl.multiple_of(jnp.maximum(c - 2, 0) * B, B)
    keys = 3 * B
    for s in range(S):
        low, _, _ = normalise(hid[s].astype(f32), gain_row, shift_row)
        normed[s] = low.astype(bf16)
    turned[...] = normed[...].reshape(S * B, D).T
    keep(turned, turned_out)
    for s in range(S):
        high, rest = fit_at(fit, places, s, lanes((L, 1), 0), L)
        fits[0, s] = high
        fits[1, s] = rest
    if gather:
        over, beside = first_y(0, z_sent[0])
        crossed.wait_recv()
        line_send(0, (4,))
    hx = []
    for s in range(S):
        hy[s].wait_recv()
        hx += start([hidden_x(s)])
    if gather:
        over_q, beside_q = first_y(1, z_sent[1])
    for s in range(S):
        bias[s] = mask_bias(lengths, s, c, B, key_start, keys)
    keep(bias, bias_out)
    line_take(0)
    line_send(1)
    if gather:
        last = first_side(0, over)
    for s in range(S):
        hx[s].wait_recv()
        low, _, _ = normalise(hoth[s].astype(f32), gain_row, shift_row)
        noth[s] = low.astype(bf16)
    cot_copy.wait()
    cot_turned[...] = cot[...].reshape(S * B, D).T
    keep(cot_turned, cot_out)
    if gather:
        last_q = first_side(1, over_q)
        for copy in beside + last:
            copy.wait_recv()
        owned[0].wait()
    kvs = []
    for s in range(S):
        for which, rows_in, owner in ((0, normed, c), (1, noth, across)):
            for k in (1, 2):
                part = dot_nn(rows_in[s], wq[k]) + qbias[k : k + 1]
                kv[s, pl.ds(pl.multiple_of(owner * B, B), B), (k - 1) * HW : k * HW] = part.astype(bf16)
            kvs += start([kv_copy(s, which)])
    if gather:
        for copy in beside_q + last_q:
            copy.wait_recv()
        keep(wq, wq_out)
    for s in range(S):
        q[s] = (dot_nn(normed[s], wq[0]) + qbias[0:1]).astype(bf16)
    keep(q, q_out)
    line_take(1)
    line_send(2)

    centers = (lanes((1, NB), 1).astype(f32) + 0.5) * (1.0 / NB)
    width = 1.0 / NB
    lane = lanes((1, 2 * DH), 1)
    scaled = half_lanes(SCALE)
    mx = []
    for s in range(S):
        kvs[2 * s].wait_recv()
        kvs[2 * s + 1].wait_recv()
        keep(kv.at[s], kv_out.at[s])
        mem[s] = (dot_nn(fits[0, s], kv[s]) + dot_nn(fits[1, s], kv[s])).astype(bf16)

        def mixed_copy(s, p, cols):
            part = mixed.at[t, s, :, cols]
            return remote(part, part, ms.at[s, p], mr.at[s, p], {"tp": 1 - t})

        def pair_step(p, log_rows, s=s):
            cols = pl.ds(pl.multiple_of(p * 2 * DH, 2 * DH), 2 * DH)
            vcols = pl.ds(pl.multiple_of(HW + p * 2 * DH, 2 * DH), 2 * DH)
            window = pl.ds(key_start, keys)
            qp = q[s, :, cols]
            kp = kv[s, window, cols]
            vp = kv[s, window, vcols]
            mk = mem[s, :, cols]
            mv = mem[s, :, vcols]
            outs = []
            for h in range(2):
                qh = qp * scaled[h]
                scores = dot_nt(qh, kp) + bias[s]
                top = jnp.max(scores, axis=-1, keepdims=True)
                e = jnp.exp(scores - top)
                total = jnp.sum(e, axis=-1, keepdims=True)
                share = (e * (1.0 / total)).astype(bf16)
                out = dot_nn(share, vp)
                log_rows = jnp.where(lane == 2 * p + h, top + jnp.log(total), log_rows)
                mem_scores = dot_nt(qh, mk)
                reach, _, _, _, _ = reach_terms(
                    mem_scores, cw[pl.ds(2 * p + h, 1)], sw[pl.ds(2 * p + h, 1)], centers, width
                )
                outs.append(out + dot_nn(reach.astype(bf16), mv))
            mixed[t, s, :, cols] = jnp.where(lane < DH, outs[0], outs[1]).astype(bf16)
            mixed_copy(s, p, cols).start()
            return log_rows

        lse[s] = lax.fori_loop(0, HW // (2 * DH), pair_step, jnp.zeros((B, 2 * DH), f32))
        mx += [mixed_copy(s, p, pl.ds(p * 2 * DH, 2 * DH)) for p in range(HW // (2 * DH))]
        if s == 0:
            line_pass(0)
            line_take(2)
    line_pass(1)
    line_pass(2)
    for r in range(n - 1 if gather else 0):
        line_end(r)
    if gather:
        for copy in owned[1:]:
            copy.wait()
    for copy in mx:
        copy.wait_recv()
    for copy in started + mx:
        copy.wait_send()
    for copy in kept:
        copy.wait()


def forward(gather, hid, lengths, places, gain, shift, weights, qbias, cw, sw, fit, cot):
    S, B, D = hid.shape
    HW = qbias.shape[1]
    n = lax.axis_size("dp")
    L = B * lax.axis_size("ctx")
    NB = cw.shape[1]
    vm = pl.BlockSpec(memory_space=pltpu.VMEM)
    sm = pl.BlockSpec(memory_space=pltpu.SMEM)
    hb = pl.BlockSpec(memory_space=pl.ANY)
    out = [
        jax.ShapeDtypeStruct((D, S * B), bf16),
        jax.ShapeDtypeStruct((D, S * B), bf16),
        jax.ShapeDtypeStruct((S, B, 3 * B), f32),
        jax.ShapeDtypeStruct((S, B, HW), bf16),
        jax.ShapeDtypeStruct((S, L, 2 * HW), bf16),
        jax.ShapeDtypeStruct((S, NB, 2 * HW), bf16),
        jax.ShapeDtypeStruct((S, B, 128), f32),
        jax.ShapeDtypeStruct((2, S, B, HW), bf16),
    ]
    out_specs = [hb] * 5 + [vm] * 3
    sem = pltpu.SemaphoreType.DMA
    scratch = [
        pltpu.VMEM((S, B, D), bf16),
        pltpu.VMEM((S, B, HW), bf16),
        pltpu.VMEM((S, L, 2 * HW), bf16),
        pltpu.VMEM((S, B, D), bf16),
        pltpu.VMEM((S, B, D), bf16),
        pltpu.VMEM((S, B, 3 * B), f32),
        pltpu.VMEM((2, S, NB, L), bf16),
        pltpu.VMEM((D, S * B), bf16),
        pltpu.VMEM((S, B, D), bf16),
        pltpu.VMEM((D, S * B), bf16),
        sem,
        sem((S + 5,)),
        *[sem((S,))] * 4,
        *[sem((S, 2))] * 2,
        *[sem((S, HW // (2 * DH)))] * 2,
    ]
    w_specs = [vm]
    if gather:
        FW = weights[2].shape[1]
        out += [
            jax.ShapeDtypeStruct((3, D, HW), bf16),
            jax.ShapeDtypeStruct((2, D, HW), bf16),
            jax.ShapeDtypeStruct((D, FW), bf16),
            jax.ShapeDtypeStruct((D, FW), bf16),
        ]
        out_specs += [hb] * 4
        w_specs = [vm] * 4
        scratch += [
            pltpu.VMEM((3, D, HW), bf16),
            sem((4,)),
            *[sem((2, n - 1))] * 8,
            sem,
            sem,
            *[sem((4, 2, n - 1))] * 8,
        ]
    return pl.pallas_call(
        lambda *refs: forward_kernel(gather, refs),
        out_shape=out,
        in_specs=[vm, sm, vm, vm, vm, *w_specs, vm, vm, vm, vm, hb],
        out_specs=out_specs,
        scratch_shapes=scratch,
        compiler_params=pltpu.CompilerParams(
            collective_id=0, has_side_effects=True, vmem_limit_bytes=VMEM_LIMIT
        ),
        cost_estimate=pl.CostEstimate(flops=6_000_000_000, bytes_accessed=30_000_000, transcendentals=6_000_000),
        name="forward_part",
    )(hid, lengths, places, gain, shift, *weights, qbias, cw, sw, fit, cot)


def quarter(c):
    return 2 * lax.rem(c, 2) + c // 2


class Reduction:
    def __init__(self, n, rows, full, half, half_in, own, own_in, sems):
        self.n, self.rows, self.piece = n, rows, rows // 4
        self.full, self.half, self.half_in, self.own, self.own_in = full, half, half_in, own, own_in
        self.sems = sems
        self.z, self.c, self.t, self.side, self.across, self.corner = place()
        self.started = []

    def at(self, offset, size):
        return pl.ds(pl.multiple_of(offset, 16), size)

    def send_side(self):
        two = 2 * self.piece
        core = lax.rem(self.c, 2)
        self.one = remote(
            self.full.at[:, self.at(two * (1 - core), two)], self.half_in, self.sems[0].at[0], self.sems[1].at[0], {"ctx": self.side}
        )
        self.one.start()
        self.started.append(self.one)

    def sum_side(self):
        two = 2 * self.piece
        core = lax.rem(self.c, 2)
        self.one.wait_recv()
        for k in range(self.n):
            self.half[k] = (
                self.full[k, self.at(two * core, two)].astype(f32) + self.half_in[k].astype(f32)
            ).astype(bf16)

    def send_across(self):
        piece, y = self.piece, self.c // 2
        self.two = remote(
            self.half.at[:, self.at(piece * (1 - y), piece)], self.own_in, self.sems[0].at[1], self.sems[1].at[1], {"ctx": self.across}
        )
        self.two.start()
        self.started.append(self.two)

    def take_across(self):
        y = self.c // 2
        self.two.wait_recv()
        for k in range(self.n):
            self.own[k] = (
                self.half[k, self.at(self.piece * y, self.piece)].astype(f32) + self.own_in[k].astype(f32)
            ).astype(bf16)

    def wait_sends(self):
        for copy in self.started:
            copy.wait_send()


def mlp_kernel(gather, refs):
    (hid_far, mixed_far, wo_far, wf_far, wp_far, obias, gain, shift, fbias, cot_far, cot_turned_far,
     residual_out, mlp_out, gres_out, gmixed, og, pg, fg, sums, fsum,
     hid, mixed, wo, residual, mlp_part, gres, wf, wp, cot, low, act, gpre, gpart, gin, turned, glow, frow, cot_turned, ls, outs, gs, gr, *rest) = refs
    if gather:
        pfull, phalf, phalf_in, pown_in, ffull, fhalf_in, ps, pr, fs, fr = rest
    else:
        pfull, ffull = pg, fg
    z, c, t, side, across, corner = place()
    S, B, D = hid_far.shape
    FW = wf.shape[1]
    HW = mixed.shape[3]
    n, R = pfull.shape[:2]
    tile = 512
    pairs = [(mixed_far, mixed), (wo_far, wo), (hid_far, hid), (wf_far, wf), (cot_far, cot), (wp_far, wp), (cot_turned_far, cot_turned)]
    loads = [pltpu.make_async_copy(far, near, ls.at[i]) for i, (far, near) in enumerate(pairs)]
    for copy in loads[:6]:
        copy.start()
    kept = []

    def keep(src, dst):
        copy = pltpu.make_async_copy(src, dst, outs.at[len(kept)])
        copy.start()
        kept.append(copy)

    wait_for_all = knock([{"tp": 1 - t}] + ([{"ctx": side}, {"ctx": across}] if gather else []))
    obias_row, gain_row, shift_row = row_of(obias), row_of(gain), row_of(shift)
    frow[...] = row_of(fbias)
    fsum[...] = jnp.zeros_like(fsum)
    copies = []
    for copy in loads[:3]:
        copy.wait()
    for s in range(S):
        branch = dot_nt(mixed[0, s], wo[0]) + dot_nt(mixed[1, s], wo[1])
        wide = hid[s].astype(f32) + branch + obias_row
        residual[s] = wide
        value, _, _ = normalise(wide, gain_row, shift_row)
        low[s] = value.astype(bf16)
        keep(residual.at[s], residual_out.at[s])
        if s == 0:
            for copy in loads[3:6]:
                copy.wait()
            loads[6].start()

        def columns(j, carry, s=s):
            cols = pl.ds(pl.multiple_of(j * tile, tile), tile)
            pre = dot_nn(low[s], wf[:, cols]) + frow[:, cols]
            square = pre * pre
            th = jnp.tanh(0.7978845608028654 * (pre + 0.044715 * (square * pre)))
            act[s, :, cols] = (0.5 * pre * (1.0 + th)).astype(bf16)
            slope = 0.5 * (1.0 + th) + (0.5 * pre) * (1.0 - th * th) * (
                0.7978845608028654 * (1.0 + 3.0 * 0.044715 * square)
            )
            grad = (dot_nn(cot[s], wp[:, cols]) * slope).astype(bf16)
            gpre[s, :, cols] = grad
            fsum[:, cols] += jnp.sum(grad.astype(f32), axis=0, keepdims=True)
            return carry

        for j in range(FW // tile):
            columns(j, 0)
        gpart[s] = dot_nt(gpre[s], wf[...]).astype(bf16)
        if s == 0:
            wait_for_all()
        copies.append(remote(gpart.at[s], gin.at[s], gs.at[s], gr.at[s], {"tp": 1 - t}))
        copies[-1].start()

    def weight_grad(full, left, right, width, step):
        if left is None:
            loads[6].wait()
            across_left = cot_turned
        else:
            turned[...] = left.reshape(S * B, D).T
            across_left = turned

        def columns(j, carry):
            cols = pl.ds(pl.multiple_of(j * step, step), step)
            value = dot_nn(across_left[...], right[:, :, cols].reshape(S * B, step)).astype(bf16)
            for k in range(n):
                full[k, :, cols] = value[k * R : (k + 1) * R]
            return carry

        lax.fori_loop(0, width // step, columns, 0)

    weight_grad(pfull, None, act, FW, 512)
    if gather:
        proj = Reduction(n, R, pfull, phalf, phalf_in, pg, pown_in, (ps, pr))
        proj.send_side()
    weight_grad(ffull, low[...], gpre, FW, 512)
    if gather:
        fc = Reduction(n, R, ffull, fg, fhalf_in, None, None, (fs, fr))
        fc.send_side()
        proj.sum_side()
        proj.send_across()
    for s in range(S):
        mlp_part[s] = dot_nt(act[s], wp[...]).astype(bf16)
        keep(mlp_part.at[s], mlp_out.at[s])
    out_sum = jnp.zeros((1, D), f32)
    gain_sum = jnp.zeros((1, D), f32)
    shift_sum = jnp.zeros((1, D), f32)
    cot_sum = jnp.zeros((1, D), f32)
    for s in range(S):
        copies[s].wait_recv()
        grad = gpart[s].astype(f32) + gin[s].astype(f32)
        _, unit, r = normalise(residual[s], gain_row, shift_row)
        gain_sum += jnp.sum(grad * unit, axis=0, keepdims=True)
        shift_sum += jnp.sum(grad, axis=0, keepdims=True)
        a = grad * gain_row
        wide_cot = cot[s].astype(f32)
        cot_sum += jnp.sum(wide_cot, axis=0, keepdims=True)
        total = wide_cot + r * (
            a - jnp.mean(a, axis=-1, keepdims=True) - unit * jnp.mean(a * unit, axis=-1, keepdims=True)
        )
        out_sum += jnp.sum(total, axis=0, keepdims=True)
        gres[s] = total
        keep(gres.at[s], gres_out.at[s])
        glow[s] = total.astype(bf16)
        gmixed[s] = dot_nn(glow[s], wo[t]).astype(bf16)
        if s == 0 and gather:
            fc.sum_side()
    sums[0:1] = out_sum
    sums[1:2] = gain_sum
    sums[2:3] = shift_sum
    sums[3:4] = cot_sum
    weight_grad(og, glow[...], mixed.at[t], HW, 384)
    if gather:
        proj.take_across()
        proj.wait_sends()
        fc.wait_sends()
    for copy in copies:
        copy.wait_send()
    for copy in kept:
        copy.wait()


def mlp(gather, hid, mixed, wo, wf, wp, obias, gain, shift, fbias, cot, cot_turned):
    S, B, D = hid.shape
    HW = mixed.shape[3]
    FW = wf.shape[1]
    n = lax.axis_size("dp") if gather else 1
    R = D // n
    Q = R // 4
    vm = pl.BlockSpec(memory_space=pltpu.VMEM)
    sem = pltpu.SemaphoreType.DMA
    hb = pl.BlockSpec(memory_space=pl.ANY)
    pshape = (n, Q, FW) if gather else (n, R, FW)
    fshape = (n, 2 * Q, FW) if gather else (n, R, FW)
    out = [
        jax.ShapeDtypeStruct((S, B, D), f32),
        jax.ShapeDtypeStruct((S, B, D), bf16),
        jax.ShapeDtypeStruct((S, B, D), f32),
        jax.ShapeDtypeStruct((S, B, HW), bf16),
        jax.ShapeDtypeStruct((n, R, HW), bf16),
        jax.ShapeDtypeStruct(pshape, bf16),
        jax.ShapeDtypeStruct(fshape, bf16),
        jax.ShapeDtypeStruct((4, D), f32),
        jax.ShapeDtypeStruct((1, FW), f32),
    ]
    scratch = [
        pltpu.VMEM((S, B, D), bf16),
        pltpu.VMEM((2, S, B, HW), bf16),
        pltpu.VMEM((2, D, HW), bf16),
        pltpu.VMEM((S, B, D), f32),
        pltpu.VMEM((S, B, D), bf16),
        pltpu.VMEM((S, B, D), f32),
        pltpu.VMEM((D, FW), bf16),
        pltpu.VMEM((D, FW), bf16),
        pltpu.VMEM((S, B, D), bf16),
        pltpu.VMEM((S, B, D), bf16),
        pltpu.VMEM((S, B, FW), bf16),
        pltpu.VMEM((S, B, FW), bf16),
        pltpu.VMEM((S, B, D), bf16),
        pltpu.VMEM((S, B, D), bf16),
        pltpu.VMEM((D, S * B), bf16),
        pltpu.VMEM((S, B, D), bf16),
        pltpu.VMEM((1, FW), f32),
        pltpu.VMEM((D, S * B), bf16),
        sem((7,)),
        sem((3 * S,)),
        sem((S,)),
        sem((S,)),
    ]
    if gather:
        scratch += [
            pltpu.VMEM((n, R, FW), bf16),
            *[pltpu.VMEM((n, R // 2, FW), bf16)] * 2,
            pltpu.VMEM((n, Q, FW), bf16),
            pltpu.VMEM((n, R, FW), bf16),
            pltpu.VMEM((n, R // 2, FW), bf16),
            *[sem((2,))] * 4,
        ]
    return pl.pallas_call(
        lambda *refs: mlp_kernel(gather, refs),
        out_shape=out,
        in_specs=[hb, hb, hb, hb, hb, vm, vm, vm, vm, hb, hb],
        out_specs=[hb, hb, hb, *[vm] * 6],
        scratch_shapes=scratch,
        compiler_params=pltpu.CompilerParams(
            collective_id=1, has_side_effects=True, vmem_limit_bytes=VMEM_LIMIT
        ),
        cost_estimate=pl.CostEstimate(flops=12_000_000_000, bytes_accessed=30_000_000, transcendentals=1_500_000),
        name="mlp_part",
    )(hid, mixed, wo, wf, wp, obias, gain, shift, fbias, cot, cot_turned)


def backward_kernel(gather, refs):
    (bias_far, places, q, kv_far, mem, lse, gmixed, turned_far, wq_far, hid_far, gres_far, residual_far, mlp_far, pbias, gain,
     cw, sw, fit, sums, fsum, *rest) = refs
    if gather:
        (pown_far, fhalf_far, ofull_far, block_out, input_grad, early_out, late_out, fqkv, fo, ff, fp, *rest) = rest
    else:
        (block_out, input_grad, early_out, late_out, afull, kfull, vfull, *rest) = rest
    (kv, wq, gres, residual, dkv, own_rows, dmem, gqkv, hs1, hr1, hs2, hr2, m1in, gmem, gfar,
     turned, mlp_in, gnpart, gnin, bias, early, ls, xs, xr, h1s, h1r, h2s, h2r, m1s, m1r, m2s, m2r, m3s, m3r, m4s, m4r, ns, nr,
     *rest) = rest
    if gather:
        (pown, fhalf, ofull, afull, kfull, vfull, ahalf_in, khalf_in, vhalf_in, ohalf_in, ahalf, khalf, vhalf, ohalf,
         aown, kown, vown, oown, fown, aown_in, kown_in, vown_in, oown_in, fown_in,
         zina, zink, zinv, zino, zinf, zinp, early_ctx, early_dp, late_ctx, late_dp,
         rs, rr, zs, zr, gs, gr, es, er) = rest
    z, c, t, side, across, corner = place()
    S, B, D = hid_far.shape
    HW = q.shape[2]
    NB = mem.shape[1]
    n, R = afull.shape[:2]
    L = kv_far.shape[1]
    keys = 3 * B
    key_start = pl.multiple_of(jnp.maximum(c - 2, 0) * B, B)
    near_pairs = []
    for s in range(S):
        near_pairs += [(kv_far.at[s, pl.ds(key_start, keys)], kv.at[s]), (bias_far.at[s], bias.at[s])]
    if gather:
        near_pairs += [(fhalf_far, fhalf), (pown_far, pown), (ofull_far, ofull)]
    next_pairs = [(turned_far, turned), (wq_far, wq), (residual_far, residual), (gres_far, gres)]
    late_pairs = [(hid_far, kv.at[:, 0:B]), (mlp_far, kv.at[:, B : 2 * B])]
    copies = [pltpu.make_async_copy(far, near, ls.at[i]) for i, (far, near) in enumerate(near_pairs + next_pairs + late_pairs)]
    loads, next_loads, late_loads = copies[: len(near_pairs)], copies[len(near_pairs) : -2], copies[-2:]
    for copy in loads:
        copy.start()
    peers = [{"tp": 1 - t}, {"ctx": side}, {"ctx": across}]
    if gather:
        peers += [{"ctx": corner}] + [{"dp": lax.rem(z + i, n)} for i in range(1, n)]
    wait_for_all = knock(peers)
    started = []

    def start(copy):
        copy.start()
        started.append(copy)
        return copy

    if gather:
        Q = R // 4
        owns, zins = {"p": pown, "f": fown, "v": vown}, {"p": zinp, "f": zinf, "v": zinv}
        finals = {"p": fp, "f": ff, "v": fqkv.at[2]}
        index = {g: i for i, g in enumerate("akvofp")}
        z_sent, g_sent = {}, {}

        def send_dp(g):
            j = index[g]
            z_sent[g] = [
                start(remote(owns[g].at[lax.rem(z + i, n)], zins[g].at[i - 1], zs.at[j, i - 1], zr.at[j, i - 1], {"dp": lax.rem(z + i, n)}))
                for i in range(1, n)
            ]

        def piece(g, device):
            return finals[g].at[pl.ds(pl.multiple_of(Q * quarter(device), 16), Q)]

        def take_dp(g):
            j = index[g]
            total = owns[g][z].astype(f32)
            for i in range(1, n):
                z_sent[g][i - 1].wait_recv()
                total = total + zins[g][i - 1].astype(f32)
            finals[g][pl.ds(pl.multiple_of(Q * quarter(c), 16), Q)] = total.astype(bf16)
            mine = piece(g, c)
            g_sent[g] = [
                start(remote(mine, mine, gs.at[j, 0], gr.at[j, 0], {"ctx": across})),
                start(remote(mine, mine, gs.at[j, 1], gr.at[j, 1], {"ctx": side})),
            ]

        def pass_on(g):
            j = index[g]
            g_sent[g][0].wait_recv()
            other = piece(g, across)
            g_sent[g].append(start(remote(other, other, gs.at[j, 2], gr.at[j, 2], {"ctx": side})))

        def take_all(g):
            g_sent[g][1].wait_recv()
            g_sent[g][2].wait_recv()

        class Chain(Reduction):
            def __init__(self, g, full, half, half_in, own, own_in, dp_in, final):
                j = index[g]
                super().__init__(n, R, full, half, half_in, own, own_in, (rs.at[j], rr.at[j]))
                self.j, self.dp_in, self.final = j, dp_in, final

            def send_dp(self):
                self.over = [
                    remote(self.half.at[lax.rem(z + i, n)], self.dp_in.at[i - 1], zs.at[self.j, i - 1], zr.at[self.j, i - 1], {"dp": lax.rem(z + i, n)})
                    for i in range(1, n)
                ]
                for copy in self.over:
                    start(copy)

            def take_dp(self):
                total = self.half[z].astype(f32)
                for i in range(1, n):
                    self.over[i - 1].wait_recv()
                    total = total + self.dp_in[i - 1].astype(f32)
                self.own[...] = total.astype(bf16)
                self.two = start(remote(self.own, self.own_in, gs.at[self.j, 0], gr.at[self.j, 0], {"ctx": across}))

            def take_across(self):
                self.two.wait_recv()
                mine = pl.ds(pl.multiple_of(2 * self.piece * lax.rem(c, 2), 16), 2 * self.piece)
                self.final[mine] = (self.own[...].astype(f32) + self.own_in[...].astype(f32)).astype(bf16)
                part = self.final.at[mine]
                self.three = start(remote(part, part, gs.at[self.j, 1], gr.at[self.j, 1], {"ctx": side}))

            def take_all(self):
                self.three.wait_recv()

        red = {
            "a": Chain("a", afull, ahalf, ahalf_in, aown, aown_in, zina, fqkv.at[0]),
            "k": Chain("k", kfull, khalf, khalf_in, kown, kown_in, zink, fqkv.at[1]),
            "o": Chain("o", ofull, ohalf, ohalf_in, oown, oown_in, zino, fo),
        }
        vals = Reduction(n, R, vfull, vhalf, vhalf_in, vown, vown_in, (rs.at[2], rr.at[2]))
        fc = Reduction(n, R, None, fhalf, None, fown, fown_in, (rs.at[4], rr.at[4]))

        class Everywhere:
            def __init__(self, over_ctx, over_dp, which):
                self.over_ctx, self.over_dp, self.which = over_ctx, over_dp, which

            def send(self, slots, me, devices, step):
                j = 2 * self.which + step
                self.sent = [
                    start(remote(slots.at[me], slots.at[me], es.at[j, i], er.at[j, i], device)) for i, device in enumerate(devices)
                ]

            def first(self, value):
                self.over_ctx[c] = value
                self.send(self.over_ctx, c, [{"ctx": side}, {"ctx": across}, {"ctx": corner}], 0)

            def total(self, slots):
                for copy in self.sent:
                    copy.wait_recv()
                return (slots[0] + slots[1]) + (slots[2] + slots[3])

            def second(self):
                self.over_dp[z] = self.total(self.over_ctx)
                self.send(self.over_dp, z, [{"dp": lax.rem(z + i, n)} for i in range(1, n)], 1)

            def last(self, out):
                out[...] = self.total(self.over_dp)

        early_sum = Everywhere(early_ctx, early_dp, 0)
        late_sum = Everywhere(late_ctx, late_dp, 1)

    mlp_sent = []

    def open_transfers():
        for copy in next_loads:
            copy.start()
        wait_for_all()
        if gather:
            for copy in loads[2 * S :]:
                copy.wait()
            fc.send_across()
            send_dp("p")
            red["o"].send_side()
        for s in range(S):
            mlp_sent.append(start(remote(mlp_far.at[s], mlp_in.at[s], xs.at[s], xr.at[s], {"tp": 1 - t})))

    lane = lanes((1, 2 * DH), 1)
    scaled = half_lanes(SCALE)
    plain = half_lanes(1.0)
    centers = (lanes((1, NB), 1).astype(f32) + 0.5) * (1.0 / NB)
    width = 1.0 / NB
    early[...] = jnp.zeros_like(early)
    half = HW
    core = lax.rem(c, 2)
    y = c // 2
    own_half = pl.ds(pl.multiple_of(core * half, 16), half)
    side_half = pl.ds(pl.multiple_of((1 - core) * half, 16), half)
    give = pl.ds(pl.multiple_of(B * (1 - core * (1 - y)), 128), B)
    own = pl.ds(pl.multiple_of(c * B - key_start, 128), B)
    one, two, three, first = {}, {}, {}, {}

    def second_copy(s):
        return remote(hs2.at[s], hr2.at[s], h2s.at[s], h2r.at[s], {"ctx": across})

    def memory_over(s):
        return remote(gmem.at[s, own_half], gfar.at[s, own_half], m2s.at[s], m2r.at[s], {"ctx": across})

    def memory_beside(s):
        return remote(gfar.at[s, own_half], gfar.at[s, own_half], m4s.at[s], m4r.at[s], {"ctx": side})

    def attend_back(s, *between):
        loads[2 * s].wait()
        loads[2 * s + 1].wait()

        def pair_step(p, carry):
            cols = pl.ds(pl.multiple_of(p * 2 * DH, 2 * DH), 2 * DH)
            vcols = pl.ds(pl.multiple_of(HW + p * 2 * DH, 2 * DH), 2 * DH)
            qp = q[s, :, cols]
            gp = gmixed[s, :, cols]
            kp = kv[s, :, cols]
            vp = kv[s, :, vcols]
            mk = mem[s, :, cols]
            mv = mem[s, :, vcols]
            q_turned = (qp * SCALE).T
            g_turned = gp.T
            logs = lse[s]
            grad_q, dk, dv, dmk, dmv = [], [], [], [], []
            for h in range(2):
                row = 2 * p + h
                part = slice(h * DH, (h + 1) * DH)
                qh = qp * scaled[h]
                gh = gp * plain[h]
                log_total = jnp.sum(jnp.where(lane == row, logs, 0.0), axis=-1, keepdims=True)
                share = jnp.exp(dot_nt(qh, kp) + bias[s] - log_total)
                grad_share = dot_nt(gh, vp)
                delta = jnp.sum(share * grad_share, axis=-1, keepdims=True)
                grad_score = (share * (grad_share - delta)).astype(bf16)
                mem_scores = dot_nt(qh, mk)
                cw_row = cw[pl.ds(row, 1)]
                sw_row = sw[pl.ds(row, 1)]
                reach, mu, inv, diff, spread_logit = reach_terms(mem_scores, cw_row, sw_row, centers, width)
                grad_reach = dot_nt(gh, mv) * reach
                scaled_diff = diff * inv
                grad_mu = -jnp.sum(grad_reach * scaled_diff, axis=-1, keepdims=True)
                grad_var = jnp.sum(
                    grad_reach * (0.5 * scaled_diff * scaled_diff - 0.5 * inv), axis=-1, keepdims=True
                )
                gc = grad_mu * mu * (1.0 - mu)
                gw = SPREAD * grad_var * (1.0 / (1.0 + jnp.exp(-spread_logit)))
                early[pl.ds(8 + row, 1), 0:NB] += jnp.sum(gc * mem_scores, axis=0, keepdims=True)
                early[pl.ds(8 + row, 1), NB : 2 * NB] += jnp.sum(gw * mem_scores, axis=0, keepdims=True)
                grad_mem = (gc * cw_row + gw * sw_row).astype(bf16)
                grad_q.append((dot_nn(grad_score, kp) + dot_nn(grad_mem, mk)) * SCALE)
                dk.append(dot_nn(q_turned[part], grad_score))
                dv.append(dot_nn(g_turned[part], share.astype(bf16)))
                dmk.append(dot_nn(q_turned[part], grad_mem))
                dmv.append(dot_nn(g_turned[part], reach.astype(bf16)))
            gqkv[s, :, cols] = jnp.where(lane < DH, grad_q[0], grad_q[1]).astype(bf16)
            for h in range(2):
                rows = pl.ds(pl.multiple_of((2 * p + h) * DH, DH), DH)
                vrows = pl.ds(pl.multiple_of(HW + (2 * p + h) * DH, DH), DH)
                dkv[rows] = dk[h]
                dkv[vrows] = dv[h]
                dmem[s, rows] = dmk[h]
                dmem[s, vrows] = dmv[h]
            return carry

        done = 0
        for step in between:
            lax.fori_loop(done, done + 1, pair_step, 0)
            done += 1
            step()
        lax.fori_loop(done, HW // (2 * DH), pair_step, 0)
        one[s] = start(remote(dmem.at[s, side_half], m1in.at[s], m1s.at[s], m1r.at[s], {"ctx": side}))
        hs1[s] = dkv[:, give].astype(bf16)
        first[s] = start(remote(hs1.at[s], hr1.at[s], h1s.at[s], h1r.at[s], {"ctx": side}))
        own_rows[s] = dkv[:, own]
        hs2[s] = dkv[:, 0:B].astype(bf16)

    def chip_memory(s):
        one[s].wait_recv()
        gmem[s, own_half] = (dmem[s, own_half] + m1in[s]).astype(bf16)
        three[s] = start(remote(gmem.at[s, own_half], gmem.at[s, own_half], m3s.at[s], m3r.at[s], {"ctx": side}))

        @pl.when(y == 0)
        def _():
            memory_over(s).start()

    def rows_of_memory(s, grad, owner):
        high, low = fit_at(fit, places, s, owner * B + lanes((B, 1), 0), L)
        return dot_nn(grad, high) + dot_nn(grad, low)

    def give_across(s):
        first[s].wait_recv()
        three[s].wait_recv()

        @pl.when(c != 3)
        def _():
            own_rows[s] = own_rows[s] + hr1[s].astype(f32)

        @pl.when(y == 1)
        def _():
            beside = jnp.where(c == 3, 1.0, 0.0)
            total = hs2[s].astype(f32) + beside * hr1[s].astype(f32) + rows_of_memory(s, gmem[s], across)
            hs2[s] = total.astype(bf16)
            second_copy(s).start()

    sent = {}

    def pass_memory(s):
        @pl.when(y == 1)
        def _():
            memory_over(s).wait_recv()
            memory_beside(s).start()

    def finish_rows(s):
        high, low = fit_at(fit, places, s, c * B + lanes((B, 1), 0), L)
        own_rows[s] = own_rows[s] + dot_nn(gmem[s], high) + dot_nn(gmem[s], low)

        @pl.when(y == 1)
        def _():
            memory_beside(s).wait_recv()
            own_rows[s] = own_rows[s] + dot_nn(gfar[s], high) + dot_nn(gfar[s], low)

        @pl.when(y == 0)
        def _():
            second_copy(s).wait_recv()
            own_rows[s] = own_rows[s] + hr2[s].astype(f32)

        gqkv[s, :, HW:] = own_rows[s].T.astype(bf16)
        parts = [dot_nt(gqkv[s, :, k * HW : (k + 1) * HW], wq[k]) for k in range(3)]
        gnpart[s] = (parts[0] + parts[1] + parts[2]).astype(bf16)
        sent[s] = start(remote(gnpart.at[s], gnin.at[s], ns.at[s], nr.at[s], {"tp": 1 - t}))

    def finish_block(s):
        mlp_sent[s].wait_recv()
        total = kv[s, B : 2 * B].astype(f32) + mlp_in[s].astype(f32)
        block_out[s] = (residual[s] + total + row_of(pbias)).astype(bf16)

    def weight_grad(full, k):
        value = dot_nn(turned[...], gqkv[:, :, k * HW : (k + 1) * HW].reshape(S * B, HW)).astype(bf16)
        for i in range(n):
            full[i] = value[i * R : (i + 1) * R]

    column_sums = []
    gain_row = row_of(gain)

    def norm_back(s):
        sent[s].wait_recv()
        grad = gnpart[s].astype(f32) + gnin[s].astype(f32)
        _, unit, r = normalise(kv[s, 0:B].astype(f32), gain_row, gain_row)
        column_sums.append((jnp.sum(grad * unit, axis=0, keepdims=True), jnp.sum(grad, axis=0, keepdims=True)))
        a = grad * gain_row
        back = r * (a - jnp.mean(a, axis=-1, keepdims=True) - unit * jnp.mean(a * unit, axis=-1, keepdims=True))
        input_grad[s] = (gres[s] + back).astype(bf16)

    attend_back(0, open_transfers)
    if gather:
        red["o"].sum_side()
        red["o"].send_dp()
    attend_back(1, lambda: chip_memory(0), lambda: give_across(0))
    if gather:
        fc.take_across()
        send_dp("f")
    pass_memory(0)
    attend_back(2, lambda: chip_memory(1), lambda: give_across(1))
    for copy in late_loads:
        copy.start()
    for copy in next_loads:
        copy.wait()
    pass_memory(1)
    finish_rows(0)
    chip_memory(2)
    give_across(2)
    weight_grad(afull, 0)
    if gather:
        red["a"].send_side()
    pass_memory(2)
    early[0:4, 0:D] = sums[...]
    for k in range(fsum.shape[1] // D):
        early[4 + k : 5 + k] = fsum[:, k * D : (k + 1) * D]
    if gather:
        early_sum.first(early[...])
    for copy in late_loads:
        copy.wait()
    finish_block(0)
    if gather:
        red["a"].sum_side()
        red["a"].send_dp()
    finish_rows(1)
    finish_block(1)
    finish_block(2)
    if gather:
        take_dp("p")
        red["o"].take_dp()
        take_dp("f")
    finish_rows(2)
    weight_grad(vfull, 2)
    if gather:
        vals.send_side()
    weight_grad(kfull, 1)
    if gather:
        red["k"].send_side()
        vals.sum_side()
        vals.send_across()
        red["k"].sum_side()
        red["k"].send_dp()
        early_sum.second()
    norm_back(0)
    if gather:
        vals.take_across()
        send_dp("v")
    bias_sum = jnp.sum(gqkv[...].reshape(S * B, 3 * HW).astype(f32), axis=0, keepdims=True)
    norm_back(1)
    if gather:
        red["a"].take_dp()
        pass_on("p")
        pass_on("f")
        red["o"].take_across()
    norm_back(2)
    room = late_ctx.at[c] if gather else late_out
    room[...] = jnp.zeros(room.shape, f32)
    room[0:1, 0:D] = column_sums[0][0] + column_sums[1][0] + column_sums[2][0]
    room[1:2, 0:D] = column_sums[0][1] + column_sums[1][1] + column_sums[2][1]
    room[2:3, 0 : 3 * HW] = bias_sum
    if gather:
        late_sum.send(late_ctx, c, [{"ctx": side}, {"ctx": across}, {"ctx": corner}], 0)
        red["k"].take_dp()
        red["a"].take_across()
        late_sum.second()
        take_dp("v")
        red["k"].take_across()
        early_sum.last(early_out)
        pass_on("v")
        late_sum.last(late_out)
        for g in "pfv":
            take_all(g)
        for chain in red.values():
            chain.take_all()
        for chain in (*red.values(), fc, vals):
            chain.wait_sends()
    else:
        early_out[...] = early[...]
    for s in range(S):

        @pl.when(y == 1)
        def _(s=s):
            second_copy(s).wait_send()
            memory_beside(s).wait_send()

        @pl.when(y == 0)
        def _(s=s):
            memory_over(s).wait_send()

    for copy in started:
        copy.wait_send()


def backward(gather, bias, places, q, kv, mem, lse, gmixed, turned, wq, hid, gres, residual, mlp_part, pbias, gain, cw, sw,
             fit, sums, fsum, owned):
    S, B, D = hid.shape
    HW = q.shape[2]
    FW = fsum.shape[1]
    H, NB = cw.shape
    n = lax.axis_size("dp") if gather else 1
    R = D // n
    Q = R // 4
    rows = -(-(8 + H) // 8) * 8
    vm = pl.BlockSpec(memory_space=pltpu.VMEM)
    hb = pl.BlockSpec(memory_space=pl.ANY)
    sem = pltpu.SemaphoreType.DMA
    late = (8, max(D, 3 * HW))
    out = [
        jax.ShapeDtypeStruct((S, B, D), bf16),
        jax.ShapeDtypeStruct((S, B, D), bf16),
        jax.ShapeDtypeStruct((rows, D), f32),
        jax.ShapeDtypeStruct(late, f32),
    ]
    if gather:
        out += [jax.ShapeDtypeStruct((3, R, HW), bf16)] + [jax.ShapeDtypeStruct((R, w), bf16) for w in (HW, FW, FW)]
    else:
        out += [jax.ShapeDtypeStruct((n, R, HW), bf16)] * 3
    scratch = [
        pltpu.VMEM((S, 3 * B, 2 * HW), bf16),
        pltpu.VMEM((3, D, HW), bf16),
        pltpu.VMEM((S, B, D), f32),
        pltpu.VMEM((S, B, D), f32),
        pltpu.VMEM((2 * HW, 3 * B), f32),
        pltpu.VMEM((S, 2 * HW, B), f32),
        pltpu.VMEM((S, 2 * HW, NB), f32),
        pltpu.VMEM((S, B, 3 * HW), bf16),
        *[pltpu.VMEM((S, 2 * HW, B), bf16)] * 4,
        pltpu.VMEM((S, HW, NB), f32),
        pltpu.VMEM((S, 2 * HW, NB), bf16),
        pltpu.VMEM((S, 2 * HW, NB), bf16),
        pltpu.VMEM((D, S * B), bf16),
        *[pltpu.VMEM((S, B, D), bf16)] * 3,
        pltpu.VMEM((S, B, 3 * B), f32),
        pltpu.VMEM((rows, D), f32),
        sem((2 * S + 9,)),
        *[sem((S,))] * 16,
    ]
    if gather:
        scratch += [
            pltpu.VMEM((n, Q, FW), bf16),
            pltpu.VMEM((n, 2 * Q, FW), bf16),
            *[pltpu.VMEM((n, R, HW), bf16)] * 4,
            *[pltpu.VMEM((n, 2 * Q, HW), bf16)] * 8,
            *[pltpu.VMEM((2 * Q, HW), bf16)] * 2,
            pltpu.VMEM((n, Q, HW), bf16),
            pltpu.VMEM((2 * Q, HW), bf16),
            pltpu.VMEM((n, Q, FW), bf16),
            *[pltpu.VMEM((2 * Q, HW), bf16)] * 2,
            pltpu.VMEM((n, Q, HW), bf16),
            pltpu.VMEM((2 * Q, HW), bf16),
            pltpu.VMEM((n, Q, FW), bf16),
            *[pltpu.VMEM((n - 1, 2 * Q, HW), bf16)] * 2,
            pltpu.VMEM((n - 1, Q, HW), bf16),
            pltpu.VMEM((n - 1, 2 * Q, HW), bf16),
            *[pltpu.VMEM((n - 1, Q, FW), bf16)] * 2,
            *[pltpu.VMEM((4, rows, D), f32)] * 2,
            *[pltpu.VMEM((4, *late), f32)] * 2,
            *[sem((6, 2))] * 2,
            *[sem((6, n - 1))] * 2,
            *[sem((6, 3))] * 2,
            *[sem((4, 3))] * 2,
        ]
    args = [bias, places, q, kv, mem, lse, gmixed, turned, wq, hid, gres, residual, mlp_part, pbias, gain, cw, sw, fit, sums,
            fsum, *owned]
    far = (0, 3, 20, 21, 22, 7, 8, 9, 10, 11, 12)
    return pl.pallas_call(
        lambda *refs: backward_kernel(gather, refs),
        out_shape=out,
        in_specs=[hb if i in far else vm for i in range(len(args))],
        out_specs=[vm] * len(out),
        scratch_shapes=scratch,
        compiler_params=pltpu.CompilerParams(
            collective_id=2, has_side_effects=True, vmem_limit_bytes=VMEM_LIMIT
        ),
        cost_estimate=pl.CostEstimate(flops=12_000_000_000, bytes_accessed=40_000_000, transcendentals=6_000_000),
        name="backward_part",
    )(*args)


def finish_kernel(fqkv, fo, ff, fp, early, late, block_in, grad_in, qkv, out, fc, proj, block, grad, qb, cgrad, sgrad, *vectors):
    HW = fqkv.shape[2]
    D = vectors[0].shape[0]
    H, NB = cgrad.shape
    for k in range(3):
        qb[k : k + 1] = late[2:3, k * HW : (k + 1) * HW]
    qkv[...] = fqkv[...].astype(f32)
    out[...] = fo[...].astype(f32)
    fc[...] = ff[...].astype(f32)
    proj[...] = fp[...].astype(f32)
    block[...] = block_in[...]
    grad[...] = grad_in[...]
    cgrad[...] = early[8 : 8 + H, 0:NB]
    sgrad[...] = early[8 : 8 + H, NB : 2 * NB]
    rows = [late[k : k + 1, 0:D] for k in range(2)] + [early[k : k + 1, 0:D] for k in range(4)]
    for vector, row in zip(vectors, rows):
        vector[...] = row.reshape(vector.shape)
    for k in range(vectors[6].shape[0] // D):
        vectors[6][k * D : (k + 1) * D] = early[4 + k : 5 + k].reshape(D)


def finish(parts, early, late, block_out, input_grad, D, H, NB):
    _, R, HW = parts[0].shape
    FW = parts[2].shape[1]
    vm = pl.BlockSpec(memory_space=pltpu.VMEM)
    shapes = [(3, R, HW), (R, HW), (R, FW), (R, FW)]
    more = [(3, HW), (H, NB), (H, NB)] + [(D,)] * 6 + [(FW,)]
    copied = [jax.ShapeDtypeStruct(v.shape, v.dtype) for v in (block_out, input_grad)]
    return pl.pallas_call(
        finish_kernel,
        out_shape=[jax.ShapeDtypeStruct(v, f32) for v in shapes] + copied + [jax.ShapeDtypeStruct(v, f32) for v in more],
        in_specs=[vm] * 8,
        out_specs=[vm] * (len(shapes) + 2 + len(more)),
        compiler_params=pltpu.CompilerParams(vmem_limit_bytes=VMEM_LIMIT),
        name="finish_part",
    )(*parts, early, late, block_out, input_grad)


def per_device(hidden_in, doc_lengths, sticky_places, attn_gain, attn_shift, qkv_weight, qkv_bias, center_weight,
               spread_weight, out_weight, out_bias, mlp_gain, mlp_shift, fc_weight, fc_bias, proj_weight, proj_bias,
               cotangent):
    S, B, D = hidden_in.shape
    n = lax.axis_size("dp")
    HW = qkv_bias.shape[1]
    H, NB = center_weight.shape
    M = sticky_places.shape[1]
    fit = jnp.asarray(ridge_fit(NB, 2 * M))
    gather = n == 4 and D % (64 * n) == 0
    weights = [jnp.transpose(qkv_weight, (1, 0, 2)), out_weight.T, fc_weight, proj_weight.T]
    if not gather:
        full = [lax.all_gather(w, "dp", axis=w.ndim - 2, tiled=True) for w in weights]
        weights = full[:1]
    made = forward(gather, hidden_in, doc_lengths, sticky_places, attn_gain, attn_shift, weights,
                   qkv_bias, center_weight, spread_weight, fit, cotangent)
    turned, cot_turned, bias, q, kv, mem, lse, mixed = made[:8]
    if gather:
        wq, wo, wf, wp = made[8:]
    else:
        wq, wo, wf, wp = full
        wo = lax.all_gather(wo, "tp", axis=0)
    made = mlp(gather, hidden_in, mixed, wo, wf, wp, out_bias, mlp_gain, mlp_shift, fc_bias, cotangent, cot_turned)
    residual, mlp_part, gres, gmixed, og, pg, fg, sums, fsum = made
    owned = [pg, fg, og] if gather else []
    made = backward(gather, bias, sticky_places, q, kv, mem, lse, gmixed, turned, wq, hidden_in, gres, residual, mlp_part,
                    proj_bias, attn_gain, center_weight, spread_weight, fit, sums, fsum, owned)
    block_out, input_grad, early, late = made[:4]
    if gather:
        made = finish(made[4:], early, late, block_out, input_grad, D, H, NB)
        qkv_grad, out_grad, fc_grad, proj_grad, block_out, input_grad, qkv_bias_grad, center_grad, spread_grad = made[:9]
        gain_grad, shift_grad, out_bias_grad, mlp_gain_grad, mlp_shift_grad, proj_bias_grad, fc_bias_grad = made[9:]
        qkv_grad, out_grad, proj_grad = jnp.transpose(qkv_grad, (1, 0, 2)), out_grad.T, proj_grad.T
    else:
        early, late = lax.psum((early, late), ("dp", "ctx"))

        def reduced(grad):
            part = lax.psum_scatter(grad.reshape(D, -1), "dp", scatter_dimension=0, tiled=True)
            return lax.psum(part, "ctx").astype(f32)

        qkv_grad = jnp.stack([reduced(g) for g in made[4:]], axis=1)
        out_grad, fc_grad, proj_grad = reduced(og).T, reduced(fg), reduced(pg).T
        qkv_bias_grad = late[2, : 3 * HW].reshape(3, HW)
        center_grad, spread_grad = early[8 : 8 + H, :NB], early[8 : 8 + H, NB : 2 * NB]
        gain_grad, shift_grad = late[0, :D], late[1, :D]
        out_bias_grad, mlp_gain_grad, mlp_shift_grad, proj_bias_grad = [early[k, :D] for k in range(4)]
        fc_bias_grad = early[4 : 4 + fc_bias.shape[0] // D].reshape(-1)
    return (
        block_out,
        input_grad,
        gain_grad,
        shift_grad,
        qkv_grad,
        qkv_bias_grad,
        center_grad,
        spread_grad,
        out_grad,
        out_bias_grad,
        mlp_gain_grad,
        mlp_shift_grad,
        fc_grad,
        fc_bias_grad,
        proj_grad,
        proj_bias_grad,
    )


def solution(mesh):
    in_specs = (
        P("dp", "ctx", None),
        P("dp", None),
        P("dp", None),
        P(),
        P(),
        P("dp", None, "tp"),
        P(None, "tp"),
        P("tp", None),
        P("tp", None),
        P("tp", "dp"),
        P(),
        P(),
        P(),
        P("dp", "tp"),
        P("tp"),
        P("tp", "dp"),
        P(),
        P("dp", "ctx", None),
    )
    out_specs = (
        P("dp", "ctx", None),
        P("dp", "ctx", None),
        P(),
        P(),
        P("dp", None, "tp"),
        P(None, "tp"),
        P("tp", None),
        P("tp", None),
        P("tp", "dp"),
        P(),
        P(),
        P(),
        P("dp", "tp"),
        P("tp"),
        P("tp", "dp"),
        P(),
    )
    return jax.shard_map(
        per_device, mesh=mesh, in_specs=in_specs, out_specs=out_specs, check_vma=False
    )
```

```python
import functools

import jax
import jax.numpy as jnp
import numpy as np
from jax import lax
from jax.experimental import pallas as pl
from jax.experimental.pallas import tpu as pltpu
from jax.sharding import PartitionSpec as P

DH = 64
WINDOW = 512
EPS = 1e-05
SPREAD = 0.02
SCALE = DH ** (-0.5)
VMEM_LIMIT = 60 * 1024 * 1024

bf16 = jnp.bfloat16
f32 = jnp.float32
MESH = pl.DeviceIdType.MESH


def dot_nn(a, b):
    return lax.dot_general(a, b, (((1,), (0,)), ((), ())), preferred_element_type=f32)


def dot_nt(a, b):
    return lax.dot_general(a, b, (((1,), (1,)), ((), ())), preferred_element_type=f32)


def dot_tn(a, b):
    return lax.dot_general(a, b, (((0,), (0,)), ((), ())), preferred_element_type=f32)


def ridge_fit(basis_count, sample_count):
    centers = (np.arange(basis_count) + 0.5) / basis_count
    times = (np.arange(sample_count) + 0.5) / sample_count
    width = 1.0 / basis_count
    design = np.exp(-np.square(times[None, :] - centers[:, None]) / (2.0 * width * width))
    gram = design @ design.T + 0.5 * np.eye(basis_count)
    return np.linalg.solve(gram, design).astype(bf16)


def place():
    c = lax.axis_index("ctx")
    side = c + 1 - 2 * lax.rem(c, 2)
    across = lax.rem(c + 2, 4)
    corner = lax.rem(side + 2, 4)
    return lax.axis_index("dp"), c, lax.axis_index("tp"), side, across, corner


def knock(devices):
    barrier = pltpu.get_barrier_semaphore()
    for device in devices:
        pl.semaphore_signal(barrier, inc=1, device_id=device, device_id_type=MESH)
    return lambda: pl.semaphore_wait(barrier, len(devices))


def remote(src, dst, send, recv, device):
    return pltpu.make_async_remote_copy(
        src_ref=src,
        dst_ref=dst,
        send_sem=send,
        recv_sem=recv,
        device_id=device,
        device_id_type=MESH,
    )


def normalise(x, gain, shift):
    mean = jnp.mean(x, axis=-1, keepdims=True)
    centred = x - mean
    r = lax.rsqrt(jnp.mean(centred * centred, axis=-1, keepdims=True) + EPS)
    n = centred * r
    return n * gain + shift, n, r


def lowest_key(lengths, s, pos):
    low = jnp.maximum(pos - (WINDOW - 1), 0)
    end = jnp.int32(0)
    for e in range(lengths.shape[1]):
        end = end + lengths[s, e]
        low = jnp.maximum(low, jnp.where(pos >= end, end, 0))
    return low


def row_of(vector):
    return vector[...].reshape(1, vector.shape[0])


def lanes(shape, dim):
    return lax.broadcasted_iota(jnp.int32, shape, dim)


def half_lanes(scale):
    lane = lanes((1, 2 * DH), 1)
    return [
        jnp.where(lane < DH, scale, 0.0).astype(bf16),
        jnp.where(lane >= DH, scale, 0.0).astype(bf16),
    ]


def mask_bias(lengths, s, c, rows, key_start, keys):
    pos = c * rows + lanes((rows, 1), 0)
    low = lowest_key(lengths, s, pos)
    key_pos = key_start + lanes((1, keys), 1)
    return jnp.where((key_pos <= pos) & (key_pos >= low), 0.0, -1e30)


def fit_at(fit, places, s, tokens, length):
    M = places.shape[1]
    sticky = jnp.where(tokens == places[s : s + 1, :], 1.0, 0.0).astype(bf16)
    even = lanes((1, M), 1) * length // M + length // (2 * M)
    steady = jnp.where(tokens == even, 1.0, 0.0).astype(bf16)
    value = dot_nt(fit[:, :M], sticky) + dot_nt(fit[:, M:], steady)
    high = value.astype(bf16)
    return high, (value - high.astype(f32)).astype(bf16)


def reach_terms(scores, center_row, spread_row, centers, width):
    center_logit = jnp.sum(scores * center_row, axis=-1, keepdims=True)
    spread_logit = jnp.sum(scores * spread_row, axis=-1, keepdims=True)
    mu = 1.0 / (1.0 + jnp.exp(-center_logit))
    grown = jnp.exp(spread_logit)
    var = SPREAD * jnp.log(1.0 + grown) + width * width
    inv = 1.0 / var
    diff = mu - centers
    reach = (width * lax.rsqrt(var)) * jnp.exp(-(diff * diff) * (0.5 * inv))
    return reach, mu, inv, diff, spread_logit


def forward_kernel(gather, refs):
    n = lax.axis_size("dp")
    if gather:
        (hid_far, lengths, places, gain, shift, wq_sh, wo_sh, wf_sh, wp_sh, qbias, cw, sw, fit, cot_far,
         turned_out, cot_out, bias_out, q_out, kv_out, mem_out, lse_out, mixed, wq_out, wo, wf, wp,
         normed, q, kv, hoth, noth, bias, fits, mem, lse, hid, turned, cot, cot_turned, cs, os_, hys, hyr, hxs, hxr, ks, kr, ms, mr,
         wq, wo_own, wf_own, wp_own, lsem, zs, zr, ys, yr, as_, ar, bs, br, oxs, oxr, lzs, lzr, lys, lyr, las, lar, lbs, lbr) = refs
    else:
        (hid_far, lengths, places, gain, shift, wq, qbias, cw, sw, fit, cot_far,
         turned_out, cot_out, bias_out, q_out, kv_out, mem_out, lse_out, mixed,
         normed, q, kv, hoth, noth, bias, fits, mem, lse, hid, turned, cot, cot_turned, cs, os_, hys, hyr, hxs, hxr, ks, kr, ms, mr) = refs
    z, c, t, side, across, corner = place()
    S, B, D = hid_far.shape
    HW = q.shape[2]
    NB = mem.shape[1]
    L = kv.shape[1]
    half = B // 2
    peers = [{"ctx": side}, {"ctx": across}, {"tp": 1 - t}]
    if gather:
        R = D // n
        Q = R // 4
        shards = [wq_sh, wo_sh, wf_sh, wp_sh]
        whole = [wq, wo.at[t], wf, wp, wo.at[1 - t]]
        peers += [{"dp": lax.rem(z + i, n)} for i in range(1, n)]
    wait_for_all = knock(peers)
    hid_copy = pltpu.make_async_copy(hid_far, hid, cs.at[0])
    hid_copy.start()
    cot_copy = pltpu.make_async_copy(cot_far, cot, cs.at[1])
    if gather:
        own_in = [
            pltpu.make_async_copy(far, near, lsem.at[4 + i]) for i, (far, near) in enumerate(((wo_sh, wo_own), (wf_sh, wf_own), (wp_sh, wp_own)))
        ]
    wait_for_all()

    started, kept = [], []

    def start(copies):
        for copy in copies:
            copy.start()
        started.extend(copies)
        return copies

    def keep(src, dst):
        copy = pltpu.make_async_copy(src, dst, os_.at[len(kept)])
        copy.start()
        kept.append(copy)

    if gather:
        groups = range(1, 5)

        def rows(g, owner, quarter):
            part = pl.ds(pl.multiple_of(R * owner + Q * quarter, 16), Q)
            return wq.at[:, part] if g == 0 else whole[g].at[part]

        def source(i):
            return lax.rem(z + n - i, n)

        def part_rows(part, owner, quarter):
            rows_here = pl.ds(pl.multiple_of(R * owner + Q * quarter, 16), Q)
            return wq.at[1:3, rows_here] if part == 0 else wq.at[0:1, rows_here]

        def first_z(part):
            mine_here = pl.ds(pl.multiple_of(Q * c, 16), Q)
            src = wq_sh.at[1:3, mine_here] if part == 0 else wq_sh.at[0:1, mine_here]
            return start([
                remote(src, part_rows(part, z, c), zs.at[part, i - 1], zr.at[part, i - 1], {"dp": lax.rem(z + i, n)})
                for i in range(1, n)
            ])

        def first_y(part, sent):
            over, beside = [], []
            for i, copy in enumerate(sent):
                copy.wait_recv()
                w = part_rows(part, source(i + 1), c)
                over += start([remote(w, w, ys.at[part, i], yr.at[part, i], {"ctx": across})])
                beside += start([remote(w, w, as_.at[part, i], ar.at[part, i], {"ctx": side})])
            return over, beside

        def first_side(part, over):
            last = []
            for i, copy in enumerate(over):
                copy.wait_recv()
                w = part_rows(part, source(i + 1), across)
                last += start([remote(w, w, bs.at[part, i], br.at[part, i], {"ctx": side})])
            return last

        def sends(way, r):
            return ((z < n - 1) & (z >= r)) if way == 0 else ((z > 0) & (z + r < n))

        def takes(way, r):
            return (z > r) if way == 0 else (z + r < n - 1)

        def line_z(g, way, r):
            owner = z - r if way == 0 else z + r
            to = z + 1 if way == 0 else z - 1
            dst = rows(g, owner, c)
            src = shards[g].at[pl.ds(pl.multiple_of(Q * c, 16), Q)] if r == 0 and g < 4 else dst
            return remote(src, dst, lzs.at[g - 1, way, r], lzr.at[g - 1, way, r], {"dp": to})

        def line_copy(g, way, r, sems, quarter, device):
            part = rows(g, z - 1 - r if way == 0 else z + 1 + r, quarter)
            return remote(part, part, sems[0].at[g - 1, way, r], sems[1].at[g - 1, way, r], {"ctx": device})

        def line_y(g, way, r):
            return line_copy(g, way, r, (lys, lyr), c, across)

        def line_a(g, way, r):
            return line_copy(g, way, r, (las, lar), c, side)

        def line_b(g, way, r):
            return line_copy(g, way, r, (lbs, lbr), across, side)

        def line_send(r, some=groups):
            for way in range(2):

                @pl.when(sends(way, r))
                def _(way=way):
                    for g in some:
                        line_z(g, way, r).start()

        def line_take(r):
            for way in range(2):

                @pl.when(takes(way, r))
                def _(way=way):
                    for g in groups:
                        line_z(g, way, r).wait_recv()
                        line_y(g, way, r).start()
                        line_a(g, way, r).start()

        def line_pass(r):
            for way in range(2):

                @pl.when(takes(way, r))
                def _(way=way):
                    for g in groups:
                        line_y(g, way, r).wait_recv()
                        line_b(g, way, r).start()

        def line_end(r):
            for way in range(2):

                @pl.when(takes(way, r))
                def _(way=way):
                    for g in groups:
                        line_a(g, way, r).wait_recv()
                        line_b(g, way, r).wait_recv()
                        line_y(g, way, r).wait_send()
                        line_a(g, way, r).wait_send()
                        line_b(g, way, r).wait_send()

                @pl.when(sends(way, r))
                def _(way=way):
                    for g in groups:
                        line_z(g, way, r).wait_send()
    else:

        def line_send(r):
            pass

        line_take = line_pass = line_end = line_send

    def hidden_y(s):
        piece = pl.ds(pl.multiple_of(half * t, 16), half)
        return remote(hid_far.at[s, piece], hoth.at[s, piece], hys.at[s], hyr.at[s], {"ctx": across})

    def hidden_x(s):
        piece = pl.ds(pl.multiple_of(half * t, 16), half)
        return remote(hoth.at[s, piece], hoth.at[s, piece], hxs.at[s], hxr.at[s], {"tp": 1 - t})

    def block(s, owner):
        return kv.at[s, pl.ds(pl.multiple_of(owner * B, B), B)]

    def kv_copy(s, which):
        owner = c if which == 0 else across
        return remote(block(s, owner), block(s, owner), ks.at[s, which], kr.at[s, which], {"ctx": side})

    if gather:
        z_sent = [first_z(0)]
    hy = start([hidden_y(s) for s in range(S)])
    if gather:
        z_sent.append(first_z(1))
        mine = pl.ds(pl.multiple_of(R * z, 16), R)
        owned = [
            pltpu.make_async_copy(near, wq.at[:, mine] if g == 0 else whole[g].at[mine], lsem.at[g])
            for g, near in enumerate((wq_sh, wo_own, wf_own, wp_own))
        ]
        for copy in (owned[0], *own_in):
            copy.start()
        crossed = start([remote(wo_sh, wo.at[t, mine], oxs, oxr, {"tp": 1 - t})])[0]
        line_send(0, (1, 2, 3))

    gain_row = row_of(gain)
    shift_row = row_of(shift)
    key_start = pl.multiple_of(jnp.maximum(c - 2, 0) * B, B)
    keys = 3 * B
    cot_copy.start()
    hid_copy.wait()
    for s in range(S):
        low, _, _ = normalise(hid[s].astype(f32), gain_row, shift_row)
        normed[s] = low.astype(bf16)
    turned[...] = normed[...].reshape(S * B, D).T
    keep(turned, turned_out)
    if gather:
        for k in range(3):
            own_in[k].wait()
            owned[1 + k].start()
    for s in range(S):
        high, rest = fit_at(fit, places, s, lanes((L, 1), 0), L)
        fits[0, s] = high
        fits[1, s] = rest
    if gather:
        over, beside = first_y(0, z_sent[0])
        crossed.wait_recv()
        line_send(0, (4,))
    hx = []
    for s in range(S):
        hy[s].wait_recv()
        hx += start([hidden_x(s)])
    if gather:
        over_q, beside_q = first_y(1, z_sent[1])
    for s in range(S):
        bias[s] = mask_bias(lengths, s, c, B, key_start, keys)
    keep(bias, bias_out)
    line_take(0)
    line_send(1)
    if gather:
        last = first_side(0, over)
    for s in range(S):
        hx[s].wait_recv()
        low, _, _ = normalise(hoth[s].astype(f32), gain_row, shift_row)
        noth[s] = low.astype(bf16)
    cot_copy.wait()
    cot_turned[...] = cot[...].reshape(S * B, D).T
    keep(cot_turned, cot_out)
    if gather:
        last_q = first_side(1, over_q)
        for copy in beside + last:
            copy.wait_recv()
        owned[0].wait()
    kvs = []
    for s in range(S):
        for which, rows_in, owner in ((0, normed, c), (1, noth, across)):
            for k in (1, 2):
                part = dot_nn(rows_in[s], wq[k]) + qbias[k : k + 1]
                kv[s, pl.ds(pl.multiple_of(owner * B, B), B), (k - 1) * HW : k * HW] = part.astype(bf16)
            kvs += start([kv_copy(s, which)])
    if gather:
        for copy in beside_q + last_q:
            copy.wait_recv()
        keep(wq, wq_out)
    for s in range(S):
        q[s] = (dot_nn(normed[s], wq[0]) + qbias[0:1]).astype(bf16)
    keep(q, q_out)
    line_take(1)
    line_send(2)

    centers = (lanes((1, NB), 1).astype(f32) + 0.5) * (1.0 / NB)
    width = 1.0 / NB
    lane = lanes((1, 2 * DH), 1)
    scaled = half_lanes(SCALE)
    mx = []
    for s in range(S):
        kvs[2 * s].wait_recv()
        kvs[2 * s + 1].wait_recv()
        keep(kv.at[s], kv_out.at[s])
        mem[s] = (dot_nn(fits[0, s], kv[s]) + dot_nn(fits[1, s], kv[s])).astype(bf16)
        keep(mem.at[s], mem_out.at[s])

        def mixed_copy(s, p, cols):
            part = mixed.at[t, s, :, cols]
            return remote(part, part, ms.at[s, p], mr.at[s, p], {"tp": 1 - t})

        def pair_step(p, log_rows, s=s):
            cols = pl.ds(pl.multiple_of(p * 2 * DH, 2 * DH), 2 * DH)
            vcols = pl.ds(pl.multiple_of(HW + p * 2 * DH, 2 * DH), 2 * DH)
            window = pl.ds(key_start, keys)
            qp = q[s, :, cols]
            kp = kv[s, window, cols]
            vp = kv[s, window, vcols]
            mk = mem[s, :, cols]
            mv = mem[s, :, vcols]
            outs = []
            for h in range(2):
                qh = qp * scaled[h]
                scores = dot_nt(qh, kp) + bias[s]
                top = jnp.max(scores, axis=-1, keepdims=True)
                e = jnp.exp(scores - top)
                total = jnp.sum(e, axis=-1, keepdims=True)
                share = (e * (1.0 / total)).astype(bf16)
                out = dot_nn(share, vp)
                log_rows = jnp.where(lane == 2 * p + h, top + jnp.log(total), log_rows)
                mem_scores = dot_nt(qh, mk)
                reach, _, _, _, _ = reach_terms(
                    mem_scores, cw[pl.ds(2 * p + h, 1)], sw[pl.ds(2 * p + h, 1)], centers, width
                )
                outs.append(out + dot_nn(reach.astype(bf16), mv))
            mixed[t, s, :, cols] = jnp.where(lane < DH, outs[0], outs[1]).astype(bf16)
            mixed_copy(s, p, cols).start()
            return log_rows

        lse[s] = lax.fori_loop(0, HW // (2 * DH), pair_step, jnp.zeros((B, 2 * DH), f32))
        keep(lse.at[s], lse_out.at[s])
        mx += [mixed_copy(s, p, pl.ds(p * 2 * DH, 2 * DH)) for p in range(HW // (2 * DH))]
        if s == 0:
            line_pass(0)
            line_take(2)
    line_pass(1)
    line_pass(2)
    for r in range(n - 1 if gather else 0):
        line_end(r)
    if gather:
        for copy in owned[1:]:
            copy.wait()
    for copy in mx:
        copy.wait_recv()
    for copy in started + mx:
        copy.wait_send()
    for copy in kept:
        copy.wait()


def forward(gather, hid, lengths, places, gain, shift, weights, qbias, cw, sw, fit, cot):
    S, B, D = hid.shape
    HW = qbias.shape[1]
    n = lax.axis_size("dp")
    L = B * lax.axis_size("ctx")
    NB = cw.shape[1]
    vm = pl.BlockSpec(memory_space=pltpu.VMEM)
    sm = pl.BlockSpec(memory_space=pltpu.SMEM)
    hb = pl.BlockSpec(memory_space=pl.ANY)
    out = [
        jax.ShapeDtypeStruct((D, S * B), bf16),
        jax.ShapeDtypeStruct((D, S * B), bf16),
        jax.ShapeDtypeStruct((S, B, 3 * B), f32),
        jax.ShapeDtypeStruct((S, B, HW), bf16),
        jax.ShapeDtypeStruct((S, L, 2 * HW), bf16),
        jax.ShapeDtypeStruct((S, NB, 2 * HW), bf16),
        jax.ShapeDtypeStruct((S, B, 128), f32),
        jax.ShapeDtypeStruct((2, S, B, HW), bf16),
    ]
    out_specs = [hb] * 7 + [vm]
    sem = pltpu.SemaphoreType.DMA
    scratch = [
        pltpu.VMEM((S, B, D), bf16),
        pltpu.VMEM((S, B, HW), bf16),
        pltpu.VMEM((S, L, 2 * HW), bf16),
        pltpu.VMEM((S, B, D), bf16),
        pltpu.VMEM((S, B, D), bf16),
        pltpu.VMEM((S, B, 3 * B), f32),
        pltpu.VMEM((2, S, NB, L), bf16),
        pltpu.VMEM((S, NB, 2 * HW), bf16),
        pltpu.VMEM((S, B, 128), f32),
        pltpu.VMEM((S, B, D), bf16),
        pltpu.VMEM((D, S * B), bf16),
        pltpu.VMEM((S, B, D), bf16),
        pltpu.VMEM((D, S * B), bf16),
        sem((2,)),
        sem((3 * S + 5,)),
        *[sem((S,))] * 4,
        *[sem((S, 2))] * 2,
        *[sem((S, HW // (2 * DH)))] * 2,
    ]
    w_specs = [vm]
    if gather:
        FW = weights[2].shape[1]
        out += [
            jax.ShapeDtypeStruct((3, D, HW), bf16),
            jax.ShapeDtypeStruct((2, D, HW), bf16),
            jax.ShapeDtypeStruct((D, FW), bf16),
            jax.ShapeDtypeStruct((D, FW), bf16),
        ]
        out_specs += [hb] * 4
        w_specs = [hb] * 4
        scratch += [
            pltpu.VMEM((3, D, HW), bf16),
            *[pltpu.VMEM((D // n, w), bf16) for w in (HW, FW, FW)],
            sem((7,)),
            *[sem((2, n - 1))] * 8,
            sem,
            sem,
            *[sem((4, 2, n - 1))] * 8,
        ]
    return pl.pallas_call(
        lambda *refs: forward_kernel(gather, refs),
        out_shape=out,
        in_specs=[hb, sm, vm, vm, vm, *w_specs, vm, vm, vm, vm, hb],
        out_specs=out_specs,
        scratch_shapes=scratch,
        compiler_params=pltpu.CompilerParams(
            collective_id=0, has_side_effects=True, vmem_limit_bytes=VMEM_LIMIT
        ),
        cost_estimate=pl.CostEstimate(flops=6_000_000_000, bytes_accessed=30_000_000, transcendentals=6_000_000),
        name="forward_part",
    )(hid, lengths, places, gain, shift, *weights, qbias, cw, sw, fit, cot)


def quarter(c):
    return 2 * lax.rem(c, 2) + c // 2


class Reduction:
    def __init__(self, n, rows, full, half, half_in, own, own_in, sems):
        self.n, self.rows, self.piece = n, rows, rows // 4
        self.full, self.half, self.half_in, self.own, self.own_in = full, half, half_in, own, own_in
        self.sems = sems
        self.z, self.c, self.t, self.side, self.across, self.corner = place()
        self.started = []

    def at(self, offset, size):
        return pl.ds(pl.multiple_of(offset, 16), size)

    def send_side(self):
        two = 2 * self.piece
        core = lax.rem(self.c, 2)
        self.one = remote(
            self.full.at[:, self.at(two * (1 - core), two)], self.half_in, self.sems[0].at[0], self.sems[1].at[0], {"ctx": self.side}
        )
        self.one.start()
        self.started.append(self.one)

    def sum_side(self):
        two = 2 * self.piece
        core = lax.rem(self.c, 2)
        self.one.wait_recv()
        for k in range(self.n):
            self.half[k] = (
                self.full[k, self.at(two * core, two)].astype(f32) + self.half_in[k].astype(f32)
            ).astype(bf16)

    def send_across(self):
        piece, y = self.piece, self.c // 2
        self.two = remote(
            self.half.at[:, self.at(piece * (1 - y), piece)], self.own_in, self.sems[0].at[1], self.sems[1].at[1], {"ctx": self.across}
        )
        self.two.start()
        self.started.append(self.two)

    def take_across(self):
        y = self.c // 2
        self.two.wait_recv()
        for k in range(self.n):
            self.own[k] = (
                self.half[k, self.at(self.piece * y, self.piece)].astype(f32) + self.own_in[k].astype(f32)
            ).astype(bf16)

    def wait_sends(self):
        for copy in self.started:
            copy.wait_send()


def mlp_kernel(gather, refs):
    (hid_far, mixed_far, wo_far, wf_far, wp_far, obias, gain, shift, fbias, cot_far, cot_turned_far,
     residual_out, mlp_out, gres_out, gmixed, og, pg, fg, sums, fsum,
     hid, mixed, wo, residual, mlp_part, gres, wf, wp, cot, low, act, gpre, gpart, gin, turned, glow, frow, cot_turned, ls, outs, gs, gr, *rest) = refs
    if gather:
        pfull, phalf, phalf_in, pown_in, ffull, fhalf_in, ps, pr, fs, fr = rest
    else:
        pfull, ffull = pg, fg
    z, c, t, side, across, corner = place()
    S, B, D = hid_far.shape
    FW = wf.shape[1]
    HW = mixed.shape[3]
    n, R = pfull.shape[:2]
    tile = 512
    pairs = [(mixed_far, mixed), (wo_far, wo), (hid_far, hid), (wf_far, wf), (cot_far, cot), (wp_far, wp), (cot_turned_far, cot_turned)]
    loads = [pltpu.make_async_copy(far, near, ls.at[i]) for i, (far, near) in enumerate(pairs)]
    for copy in loads[:6]:
        copy.start()
    kept = []

    def keep(src, dst):
        copy = pltpu.make_async_copy(src, dst, outs.at[len(kept)])
        copy.start()
        kept.append(copy)

    wait_for_all = knock([{"tp": 1 - t}] + ([{"ctx": side}, {"ctx": across}] if gather else []))
    obias_row, gain_row, shift_row = row_of(obias), row_of(gain), row_of(shift)
    frow[...] = row_of(fbias)
    fsum[...] = jnp.zeros_like(fsum)
    copies = []
    for copy in loads[:3]:
        copy.wait()
    for s in range(S):
        branch = dot_nt(mixed[0, s], wo[0]) + dot_nt(mixed[1, s], wo[1])
        wide = hid[s].astype(f32) + branch + obias_row
        residual[s] = wide
        value, _, _ = normalise(wide, gain_row, shift_row)
        low[s] = value.astype(bf16)
        keep(residual.at[s], residual_out.at[s])
        if s == 0:
            for copy in loads[3:6]:
                copy.wait()
            loads[6].start()

        def columns(j, carry, s=s):
            cols = pl.ds(pl.multiple_of(j * tile, tile), tile)
            pre = dot_nn(low[s], wf[:, cols]) + frow[:, cols]
            square = pre * pre
            th = jnp.tanh(0.7978845608028654 * (pre + 0.044715 * (square * pre)))
            act[s, :, cols] = (0.5 * pre * (1.0 + th)).astype(bf16)
            slope = 0.5 * (1.0 + th) + (0.5 * pre) * (1.0 - th * th) * (
                0.7978845608028654 * (1.0 + 3.0 * 0.044715 * square)
            )
            grad = (dot_nn(cot[s], wp[:, cols]) * slope).astype(bf16)
            gpre[s, :, cols] = grad
            fsum[:, cols] += jnp.sum(grad.astype(f32), axis=0, keepdims=True)
            return carry

        for j in range(FW // tile):
            columns(j, 0)
        gpart[s] = dot_nt(gpre[s], wf[...]).astype(bf16)
        if s == 0:
            wait_for_all()
        copies.append(remote(gpart.at[s], gin.at[s], gs.at[s], gr.at[s], {"tp": 1 - t}))
        copies[-1].start()

    def weight_grad(full, left, right, width, step):
        if left is None:
            loads[6].wait()
            across_left = cot_turned
        else:
            turned[...] = left.reshape(S * B, D).T
            across_left = turned

        def columns(j, carry):
            cols = pl.ds(pl.multiple_of(j * step, step), step)
            value = dot_nn(across_left[...], right[:, :, cols].reshape(S * B, step)).astype(bf16)
            for k in range(n):
                full[k, :, cols] = value[k * R : (k + 1) * R]
            return carry

        lax.fori_loop(0, width // step, columns, 0)

    weight_grad(pfull, None, act, FW, 512)
    if gather:
        proj = Reduction(n, R, pfull, phalf, phalf_in, pg, pown_in, (ps, pr))
        proj.send_side()
    weight_grad(ffull, low[...], gpre, FW, 512)
    if gather:
        fc = Reduction(n, R, ffull, fg, fhalf_in, None, None, (fs, fr))
        fc.send_side()
        proj.sum_side()
        proj.send_across()
    for s in range(S):
        mlp_part[s] = dot_nt(act[s], wp[...]).astype(bf16)
        keep(mlp_part.at[s], mlp_out.at[s])
    out_sum = jnp.zeros((1, D), f32)
    gain_sum = jnp.zeros((1, D), f32)
    shift_sum = jnp.zeros((1, D), f32)
    cot_sum = jnp.zeros((1, D), f32)
    for s in range(S):
        copies[s].wait_recv()
        grad = gpart[s].astype(f32) + gin[s].astype(f32)
        _, unit, r = normalise(residual[s], gain_row, shift_row)
        gain_sum += jnp.sum(grad * unit, axis=0, keepdims=True)
        shift_sum += jnp.sum(grad, axis=0, keepdims=True)
        a = grad * gain_row
        wide_cot = cot[s].astype(f32)
        cot_sum += jnp.sum(wide_cot, axis=0, keepdims=True)
        total = wide_cot + r * (
            a - jnp.mean(a, axis=-1, keepdims=True) - unit * jnp.mean(a * unit, axis=-1, keepdims=True)
        )
        out_sum += jnp.sum(total, axis=0, keepdims=True)
        gres[s] = total
        keep(gres.at[s], gres_out.at[s])
        glow[s] = total.astype(bf16)
        gmixed[s] = dot_nn(glow[s], wo[t]).astype(bf16)
        if s == 0 and gather:
            fc.sum_side()
    sums[0:1] = out_sum
    sums[1:2] = gain_sum
    sums[2:3] = shift_sum
    sums[3:4] = cot_sum
    weight_grad(og, glow[...], mixed.at[t], HW, 384)
    if gather:
        proj.take_across()
        proj.wait_sends()
        fc.wait_sends()
    for copy in copies:
        copy.wait_send()
    for copy in kept:
        copy.wait()


def mlp(gather, hid, mixed, wo, wf, wp, obias, gain, shift, fbias, cot, cot_turned):
    S, B, D = hid.shape
    HW = mixed.shape[3]
    FW = wf.shape[1]
    n = lax.axis_size("dp") if gather else 1
    R = D // n
    Q = R // 4
    vm = pl.BlockSpec(memory_space=pltpu.VMEM)
    sem = pltpu.SemaphoreType.DMA
    hb = pl.BlockSpec(memory_space=pl.ANY)
    pshape = (n, Q, FW) if gather else (n, R, FW)
    fshape = (n, 2 * Q, FW) if gather else (n, R, FW)
    out = [
        jax.ShapeDtypeStruct((S, B, D), f32),
        jax.ShapeDtypeStruct((S, B, D), bf16),
        jax.ShapeDtypeStruct((S, B, D), f32),
        jax.ShapeDtypeStruct((S, B, HW), bf16),
        jax.ShapeDtypeStruct((n, R, HW), bf16),
        jax.ShapeDtypeStruct(pshape, bf16),
        jax.ShapeDtypeStruct(fshape, bf16),
        jax.ShapeDtypeStruct((4, D), f32),
        jax.ShapeDtypeStruct((1, FW), f32),
    ]
    scratch = [
        pltpu.VMEM((S, B, D), bf16),
        pltpu.VMEM((2, S, B, HW), bf16),
        pltpu.VMEM((2, D, HW), bf16),
        pltpu.VMEM((S, B, D), f32),
        pltpu.VMEM((S, B, D), bf16),
        pltpu.VMEM((S, B, D), f32),
        pltpu.VMEM((D, FW), bf16),
        pltpu.VMEM((D, FW), bf16),
        pltpu.VMEM((S, B, D), bf16),
        pltpu.VMEM((S, B, D), bf16),
        pltpu.VMEM((S, B, FW), bf16),
        pltpu.VMEM((S, B, FW), bf16),
        pltpu.VMEM((S, B, D), bf16),
        pltpu.VMEM((S, B, D), bf16),
        pltpu.VMEM((D, S * B), bf16),
        pltpu.VMEM((S, B, D), bf16),
        pltpu.VMEM((1, FW), f32),
        pltpu.VMEM((D, S * B), bf16),
        sem((7,)),
        sem((3 * S,)),
        sem((S,)),
        sem((S,)),
    ]
    if gather:
        scratch += [
            pltpu.VMEM((n, R, FW), bf16),
            *[pltpu.VMEM((n, R // 2, FW), bf16)] * 2,
            pltpu.VMEM((n, Q, FW), bf16),
            pltpu.VMEM((n, R, FW), bf16),
            pltpu.VMEM((n, R // 2, FW), bf16),
            *[sem((2,))] * 4,
        ]
    return pl.pallas_call(
        lambda *refs: mlp_kernel(gather, refs),
        out_shape=out,
        in_specs=[hb, hb, hb, hb, hb, vm, vm, vm, vm, hb, hb],
        out_specs=[hb, hb, hb, *[vm] * 6],
        scratch_shapes=scratch,
        compiler_params=pltpu.CompilerParams(
            collective_id=1, has_side_effects=True, vmem_limit_bytes=VMEM_LIMIT
        ),
        cost_estimate=pl.CostEstimate(flops=12_000_000_000, bytes_accessed=30_000_000, transcendentals=1_500_000),
        name="mlp_part",
    )(hid, mixed, wo, wf, wp, obias, gain, shift, fbias, cot, cot_turned)


def backward_kernel(gather, refs):
    (bias_far, places, q_far, kv_far, mem_far, lse_far, gmixed_far, turned_far, wq_far, hid_far, gres_far, residual_far, mlp_far, pbias, gain,
     cw, sw, fit, sums, fsum, *rest) = refs
    if gather:
        (pown_far, fhalf_far, ofull_far, block_out, input_grad, early_out, late_out, fqkv, fo, ff, fp, *rest) = rest
    else:
        (block_out, input_grad, early_out, late_out, afull, kfull, vfull, *rest) = rest
    (q, mem, lse, gmixed, kv, wq, gres, residual, dkv, own_rows, dmem, gqkv, hs1, hr1, hs2, hr2, m1in, gmem, gfar,
     turned, mlp_in, gnpart, gnin, bias, early, ls, xs, xr, h1s, h1r, h2s, h2r, m1s, m1r, m2s, m2r, m3s, m3r, m4s, m4r, ns, nr,
     *rest) = rest
    if gather:
        (pown, fhalf, ofull, afull, kfull, vfull, ahalf_in, khalf_in, vhalf_in, ohalf_in, ahalf, khalf, vhalf, ohalf,
         aown, kown, vown, oown, fown, aown_in, kown_in, vown_in, oown_in, fown_in,
         zina, zink, zinv, zino, zinf, zinp, early_ctx, early_dp, late_ctx, late_dp,
         rs, rr, zs, zr, gs, gr, es, er) = rest
    z, c, t, side, across, corner = place()
    S, B, D = hid_far.shape
    HW = q.shape[2]
    NB = mem.shape[1]
    n, R = afull.shape[:2]
    L = kv_far.shape[1]
    keys = 3 * B
    key_start = pl.multiple_of(jnp.maximum(c - 2, 0) * B, B)
    near_pairs = []
    for s in range(S):
        near_pairs += [(far.at[s], near.at[s]) for far, near in ((q_far, q), (gmixed_far, gmixed), (lse_far, lse), (mem_far, mem))]
        near_pairs += [(kv_far.at[s, pl.ds(key_start, keys)], kv.at[s]), (bias_far.at[s], bias.at[s])]
    if gather:
        near_pairs += [(fhalf_far, fhalf), (pown_far, pown), (ofull_far, ofull)]
    next_pairs = [(turned_far, turned), (wq_far, wq), (residual_far, residual), (gres_far, gres)]
    late_pairs = [(hid_far, kv.at[:, 0:B]), (mlp_far, kv.at[:, B : 2 * B])]
    copies = [pltpu.make_async_copy(far, near, ls.at[i]) for i, (far, near) in enumerate(near_pairs + next_pairs + late_pairs)]
    loads, next_loads, late_loads = copies[: len(near_pairs)], copies[len(near_pairs) : -2], copies[-2:]
    for copy in loads:
        copy.start()
    peers = [{"tp": 1 - t}, {"ctx": side}, {"ctx": across}]
    if gather:
        peers += [{"ctx": corner}] + [{"dp": lax.rem(z + i, n)} for i in range(1, n)]
    wait_for_all = knock(peers)
    started = []

    def start(copy):
        copy.start()
        started.append(copy)
        return copy

    if gather:
        Q = R // 4
        owns, zins = {"p": pown, "f": fown, "v": vown}, {"p": zinp, "f": zinf, "v": zinv}
        finals = {"p": fp, "f": ff, "v": fqkv.at[2]}
        index = {g: i for i, g in enumerate("akvofp")}
        z_sent, g_sent = {}, {}

        def send_dp(g):
            j = index[g]
            z_sent[g] = [
                start(remote(owns[g].at[lax.rem(z + i, n)], zins[g].at[i - 1], zs.at[j, i - 1], zr.at[j, i - 1], {"dp": lax.rem(z + i, n)}))
                for i in range(1, n)
            ]

        def piece(g, device):
            return finals[g].at[pl.ds(pl.multiple_of(Q * quarter(device), 16), Q)]

        def take_dp(g):
            j = index[g]
            total = owns[g][z].astype(f32)
            for i in range(1, n):
                z_sent[g][i - 1].wait_recv()
                total = total + zins[g][i - 1].astype(f32)
            finals[g][pl.ds(pl.multiple_of(Q * quarter(c), 16), Q)] = total.astype(bf16)
            mine = piece(g, c)
            g_sent[g] = [
                start(remote(mine, mine, gs.at[j, 0], gr.at[j, 0], {"ctx": across})),
                start(remote(mine, mine, gs.at[j, 1], gr.at[j, 1], {"ctx": side})),
            ]

        def pass_on(g):
            j = index[g]
            g_sent[g][0].wait_recv()
            other = piece(g, across)
            g_sent[g].append(start(remote(other, other, gs.at[j, 2], gr.at[j, 2], {"ctx": side})))

        def take_all(g):
            g_sent[g][1].wait_recv()
            g_sent[g][2].wait_recv()

        class Chain(Reduction):
            def __init__(self, g, full, half, half_in, own, own_in, dp_in, final):
                j = index[g]
                super().__init__(n, R, full, half, half_in, own, own_in, (rs.at[j], rr.at[j]))
                self.j, self.dp_in, self.final = j, dp_in, final

            def send_dp(self):
                self.over = [
                    remote(self.half.at[lax.rem(z + i, n)], self.dp_in.at[i - 1], zs.at[self.j, i - 1], zr.at[self.j, i - 1], {"dp": lax.rem(z + i, n)})
                    for i in range(1, n)
                ]
                for copy in self.over:
                    start(copy)

            def take_dp(self):
                total = self.half[z].astype(f32)
                for i in range(1, n):
                    self.over[i - 1].wait_recv()
                    total = total + self.dp_in[i - 1].astype(f32)
                self.own[...] = total.astype(bf16)
                self.two = start(remote(self.own, self.own_in, gs.at[self.j, 0], gr.at[self.j, 0], {"ctx": across}))

            def take_across(self):
                self.two.wait_recv()
                mine = pl.ds(pl.multiple_of(2 * self.piece * lax.rem(c, 2), 16), 2 * self.piece)
                self.final[mine] = (self.own[...].astype(f32) + self.own_in[...].astype(f32)).astype(bf16)
                part = self.final.at[mine]
                self.three = start(remote(part, part, gs.at[self.j, 1], gr.at[self.j, 1], {"ctx": side}))

            def take_all(self):
                self.three.wait_recv()

        red = {
            "a": Chain("a", afull, ahalf, ahalf_in, aown, aown_in, zina, fqkv.at[0]),
            "k": Chain("k", kfull, khalf, khalf_in, kown, kown_in, zink, fqkv.at[1]),
            "o": Chain("o", ofull, ohalf, ohalf_in, oown, oown_in, zino, fo),
        }
        vals = Reduction(n, R, vfull, vhalf, vhalf_in, vown, vown_in, (rs.at[2], rr.at[2]))
        fc = Reduction(n, R, None, fhalf, None, fown, fown_in, (rs.at[4], rr.at[4]))

        class Everywhere:
            def __init__(self, over_ctx, over_dp, which):
                self.over_ctx, self.over_dp, self.which = over_ctx, over_dp, which

            def send(self, slots, me, devices, step):
                j = 2 * self.which + step
                self.sent = [
                    start(remote(slots.at[me], slots.at[me], es.at[j, i], er.at[j, i], device)) for i, device in enumerate(devices)
                ]

            def over(self, axis, value, step):
                if axis == "ctx":
                    self.over_ctx[c] = value
                    self.send(self.over_ctx, c, [{"ctx": side}, {"ctx": across}, {"ctx": corner}], step)
                else:
                    self.over_dp[z] = value
                    self.send(self.over_dp, z, [{"dp": lax.rem(z + i, n)} for i in range(1, n)], step)

            def total(self, axis):
                for copy in self.sent:
                    copy.wait_recv()
                slots = self.over_ctx if axis == "ctx" else self.over_dp
                return (slots[0] + slots[1]) + (slots[2] + slots[3])

        early_sum = Everywhere(early_ctx, early_dp, 0)
        late_sum = Everywhere(late_ctx, late_dp, 1)

    mlp_sent = []

    def open_transfers():
        for copy in next_loads:
            copy.start()
        wait_for_all()
        if gather:
            for copy in loads[6 * S :]:
                copy.wait()
            fc.send_across()
            send_dp("p")
            red["o"].send_side()
        for s in range(S):
            mlp_sent.append(start(remote(mlp_far.at[s], mlp_in.at[s], xs.at[s], xr.at[s], {"tp": 1 - t})))

    lane = lanes((1, 2 * DH), 1)
    scaled = half_lanes(SCALE)
    plain = half_lanes(1.0)
    centers = (lanes((1, NB), 1).astype(f32) + 0.5) * (1.0 / NB)
    width = 1.0 / NB
    early[...] = jnp.zeros_like(early)
    half = HW
    core = lax.rem(c, 2)
    y = c // 2
    own_half = pl.ds(pl.multiple_of(core * half, 16), half)
    side_half = pl.ds(pl.multiple_of((1 - core) * half, 16), half)
    give = pl.ds(pl.multiple_of(B * (1 - core * (1 - y)), 128), B)
    own = pl.ds(pl.multiple_of(c * B - key_start, 128), B)
    one, two, three, first = {}, {}, {}, {}

    hb = B // 2

    def second_copy(s, k):
        part = pl.ds(k * hb, hb)
        return remote(hs2.at[s, :, part], hr2.at[s, :, part], h2s.at[s, k], h2r.at[s, k], {"ctx": across})

    def memory_over(s):
        return remote(gmem.at[s, own_half], gfar.at[s, own_half], m2s.at[s], m2r.at[s], {"ctx": across})

    def memory_beside(s):
        return remote(gfar.at[s, own_half], gfar.at[s, own_half], m4s.at[s], m4r.at[s], {"ctx": side})

    def attend_back(s, *between):
        for copy in loads[6 * s : 6 * s + 6]:
            copy.wait()

        def pair_step(p, carry):
            cols = pl.ds(pl.multiple_of(p * 2 * DH, 2 * DH), 2 * DH)
            vcols = pl.ds(pl.multiple_of(HW + p * 2 * DH, 2 * DH), 2 * DH)
            qp = q[s, :, cols]
            gp = gmixed[s, :, cols]
            kp = kv[s, :, cols]
            vp = kv[s, :, vcols]
            mk = mem[s, :, cols]
            mv = mem[s, :, vcols]
            q_turned = (qp * SCALE).T
            g_turned = gp.T
            logs = lse[s]
            both = jnp.concatenate([qp * scaled[0], qp * scaled[1]], axis=0)
            both_g = jnp.concatenate([gp * plain[0], gp * plain[1]], axis=0)
            all_scores = dot_nt(both, kp)
            all_grads = dot_nt(both_g, vp)
            all_mem = dot_nt(both, mk)
            all_reach = dot_nt(both_g, mv)
            grad_scores, grad_mems, dk, dv, dmk, dmv = [], [], [], [], [], []
            for h in range(2):
                row = 2 * p + h
                part = slice(h * DH, (h + 1) * DH)
                these = slice(h * B, (h + 1) * B)
                log_total = jnp.sum(jnp.where(lane == row, logs, 0.0), axis=-1, keepdims=True)
                share = jnp.exp(all_scores[these] + bias[s] - log_total)
                grad_share = all_grads[these]
                delta = jnp.sum(share * grad_share, axis=-1, keepdims=True)
                grad_score = (share * (grad_share - delta)).astype(bf16)
                mem_scores = all_mem[these]
                cw_row = cw[pl.ds(row, 1)]
                sw_row = sw[pl.ds(row, 1)]
                reach, mu, inv, diff, spread_logit = reach_terms(mem_scores, cw_row, sw_row, centers, width)
                grad_reach = all_reach[these] * reach
                scaled_diff = diff * inv
                product = grad_reach * scaled_diff
                grad_mu = -jnp.sum(product, axis=-1, keepdims=True)
                grad_var = 0.5 * (
                    jnp.sum(product * scaled_diff, axis=-1, keepdims=True) - inv * jnp.sum(grad_reach, axis=-1, keepdims=True)
                )
                gc = grad_mu * mu * (1.0 - mu)
                gw = SPREAD * grad_var * (1.0 / (1.0 + jnp.exp(-spread_logit)))
                early[pl.ds(8 + row, 1), 0:NB] += jnp.sum(gc * mem_scores, axis=0, keepdims=True)
                early[pl.ds(8 + row, 1), NB : 2 * NB] += jnp.sum(gw * mem_scores, axis=0, keepdims=True)
                grad_mem = (gc * cw_row + gw * sw_row).astype(bf16)
                grad_scores.append(grad_score)
                grad_mems.append(grad_mem)
                dk.append(dot_nn(q_turned[part], grad_score))
                dv.append(dot_nn(g_turned[part], share.astype(bf16)))
                dmk.append(dot_nn(q_turned[part], grad_mem))
                dmv.append(dot_nn(g_turned[part], reach.astype(bf16)))
            grad_q = dot_nn(jnp.concatenate(grad_scores, axis=0), kp) + dot_nn(jnp.concatenate(grad_mems, axis=0), mk)
            gqkv[s, :, cols] = (jnp.where(lane < DH, grad_q[:B], grad_q[B:]) * SCALE).astype(bf16)
            for h in range(2):
                rows = pl.ds(pl.multiple_of((2 * p + h) * DH, DH), DH)
                vrows = pl.ds(pl.multiple_of(HW + (2 * p + h) * DH, DH), DH)
                dkv[rows] = dk[h]
                dkv[vrows] = dv[h]
                dmem[s, rows] = dmk[h]
                dmem[s, vrows] = dmv[h]
            return carry

        done = 0
        for step in between:
            lax.fori_loop(done, done + 1, pair_step, 0)
            done += 1
            step()
        lax.fori_loop(done, HW // (2 * DH), pair_step, 0)
        one[s] = start(remote(dmem.at[s, side_half], m1in.at[s], m1s.at[s], m1r.at[s], {"ctx": side}))
        hs1[s] = dkv[:, give].astype(bf16)
        first[s] = start(remote(hs1.at[s], hr1.at[s], h1s.at[s], h1r.at[s], {"ctx": side}))
        own_rows[s] = dkv[:, own]
        hs2[s] = dkv[:, 0:B].astype(bf16)

    def chip_memory(s):
        one[s].wait_recv()
        gmem[s, own_half] = (dmem[s, own_half] + m1in[s]).astype(bf16)
        three[s] = start(remote(gmem.at[s, own_half], gmem.at[s, own_half], m3s.at[s], m3r.at[s], {"ctx": side}))

        @pl.when(y == 0)
        def _():
            memory_over(s).start()

    def rows_of_memory(s, grad, owner):
        high, low = fit_at(fit, places, s, owner * B + lanes((B, 1), 0), L)
        return dot_nn(grad, high) + dot_nn(grad, low)

    def give_across(s):
        first[s].wait_recv()
        three[s].wait_recv()

        @pl.when(c != 3)
        def _():
            own_rows[s] = own_rows[s] + hr1[s].astype(f32)

        @pl.when(y == 1)
        def _():
            beside = jnp.where(c == 3, 1.0, 0.0)
            total = hs2[s].astype(f32) + beside * hr1[s].astype(f32) + rows_of_memory(s, gmem[s], across)
            hs2[s] = total.astype(bf16)
            for k in range(2):
                second_copy(s, k).start()

    sent = {}

    def pass_memory(s):
        @pl.when(y == 1)
        def _():
            memory_over(s).wait_recv()
            memory_beside(s).start()

    def prepare_rows(s):
        high, low = fit_at(fit, places, s, c * B + lanes((B, 1), 0), L)
        own_rows[s] = own_rows[s] + dot_nn(gmem[s], high) + dot_nn(gmem[s], low)

        @pl.when(y == 1)
        def _():
            memory_beside(s).wait_recv()
            own_rows[s] = own_rows[s] + dot_nn(gfar[s], high) + dot_nn(gfar[s], low)

    def finish_rows(s):
        for k in range(2):
            part = slice(k * hb, (k + 1) * hb)

            @pl.when(y == 0)
            def _(k=k, part=part):
                second_copy(s, k).wait_recv()
                own_rows[s, :, part] = own_rows[s, :, part] + hr2[s, :, part].astype(f32)

            gqkv[s, part, HW:] = own_rows[s, :, part].T.astype(bf16)
            sums_here = [dot_nt(gqkv[s, part, i * HW : (i + 1) * HW], wq[i]) for i in range(3)]
            gnpart[s, part] = (sums_here[0] + sums_here[1] + sums_here[2]).astype(bf16)
            sent[s, k] = start(remote(gnpart.at[s, part], gnin.at[s, part], ns.at[s, k], nr.at[s, k], {"tp": 1 - t}))

    def finish_block(s):
        mlp_sent[s].wait_recv()
        total = kv[s, B : 2 * B].astype(f32) + mlp_in[s].astype(f32)
        block_out[s] = (residual[s] + total + row_of(pbias)).astype(bf16)

    def weight_grad(full, k):
        value = dot_nn(turned[...], gqkv[:, :, k * HW : (k + 1) * HW].reshape(S * B, HW)).astype(bf16)
        for i in range(n):
            full[i] = value[i * R : (i + 1) * R]

    column_sums = []
    gain_row = row_of(gain)

    def norm_back(s):
        sent[s, 0].wait_recv()
        sent[s, 1].wait_recv()
        grad = gnpart[s].astype(f32) + gnin[s].astype(f32)
        _, unit, r = normalise(kv[s, 0:B].astype(f32), gain_row, gain_row)
        column_sums.append((jnp.sum(grad * unit, axis=0, keepdims=True), jnp.sum(grad, axis=0, keepdims=True)))
        a = grad * gain_row
        back = r * (a - jnp.mean(a, axis=-1, keepdims=True) - unit * jnp.mean(a * unit, axis=-1, keepdims=True))
        input_grad[s] = (gres[s] + back).astype(bf16)

    attend_back(0, open_transfers)
    if gather:
        red["o"].sum_side()
        red["o"].send_dp()
    attend_back(1, lambda: chip_memory(0), lambda: give_across(0))
    if gather:
        fc.take_across()
        send_dp("f")
    pass_memory(0)
    attend_back(2, lambda: chip_memory(1), lambda: give_across(1))
    for copy in late_loads:
        copy.start()
    for copy in next_loads:
        copy.wait()
    pass_memory(1)
    prepare_rows(0)
    finish_rows(0)
    chip_memory(2)
    give_across(2)
    weight_grad(afull, 0)
    if gather:
        red["a"].send_side()
    pass_memory(2)
    early[0:4, 0:D] = sums[...]
    for k in range(fsum.shape[1] // D):
        early[4 + k : 5 + k] = fsum[:, k * D : (k + 1) * D]
    if gather:
        early_sum.over("dp", early[...], 0)
    for copy in late_loads:
        copy.wait()
    finish_block(0)
    if gather:
        red["a"].sum_side()
        red["a"].send_dp()
    prepare_rows(1)
    finish_rows(1)
    prepare_rows(2)
    finish_block(1)
    finish_block(2)
    if gather:
        take_dp("p")
        red["o"].take_dp()
        take_dp("f")
    finish_rows(2)
    if gather:
        early_sum.over("ctx", early_sum.total("dp"), 1)
    weight_grad(vfull, 2)
    if gather:
        vals.send_side()
    weight_grad(kfull, 1)
    if gather:
        red["k"].send_side()
        vals.sum_side()
        vals.send_across()
        red["k"].sum_side()
        red["k"].send_dp()
    bias_sum = jnp.sum(gqkv[...].reshape(S * B, 3 * HW).astype(f32), axis=0, keepdims=True)
    norm_back(0)
    if gather:
        vals.take_across()
        send_dp("v")
    if gather:
        red["a"].take_dp()
        pass_on("p")
        pass_on("f")
        red["o"].take_across()
    norm_back(1)
    norm_back(2)
    per = D // HW
    room = late_ctx.at[c] if gather else late_out
    room[...] = jnp.zeros(room.shape, f32)
    for which in range(2):
        whole_row = column_sums[0][which] + column_sums[1][which] + column_sums[2][which]
        for k in range(per):
            room[which * per + k : which * per + k + 1] = whole_row[:, k * HW : (k + 1) * HW]
    for k in range(3):
        room[2 * per + k : 2 * per + k + 1] = bias_sum[:, k * HW : (k + 1) * HW]
    if gather:
        late_sum.send(late_ctx, c, [{"ctx": side}, {"ctx": across}, {"ctx": corner}], 0)
        early_out[...] = early_sum.total("ctx")
        red["k"].take_dp()
        late_sum.over("dp", late_sum.total("ctx"), 1)
        red["a"].take_across()
        take_dp("v")
        red["k"].take_across()
        pass_on("v")
        late_out[...] = late_sum.total("dp")
        for g in "pfv":
            take_all(g)
        for chain in red.values():
            chain.take_all()
        for chain in (*red.values(), fc, vals):
            chain.wait_sends()
    else:
        early_out[...] = early[...]
    for s in range(S):

        @pl.when(y == 1)
        def _(s=s):
            second_copy(s, 0).wait_send()
            second_copy(s, 1).wait_send()
            memory_beside(s).wait_send()

        @pl.when(y == 0)
        def _(s=s):
            memory_over(s).wait_send()

    for copy in started:
        copy.wait_send()


def backward(gather, bias, places, q, kv, mem, lse, gmixed, turned, wq, hid, gres, residual, mlp_part, pbias, gain, cw, sw,
             fit, sums, fsum, owned):
    S, B, D = hid.shape
    HW = q.shape[2]
    FW = fsum.shape[1]
    H, NB = cw.shape
    n = lax.axis_size("dp") if gather else 1
    R = D // n
    Q = R // 4
    rows = -(-(8 + H) // 8) * 8
    vm = pl.BlockSpec(memory_space=pltpu.VMEM)
    hb = pl.BlockSpec(memory_space=pl.ANY)
    sem = pltpu.SemaphoreType.DMA
    late = (-(-(2 * (D // HW) + 3) // 8) * 8, HW)
    out = [
        jax.ShapeDtypeStruct((S, B, D), bf16),
        jax.ShapeDtypeStruct((S, B, D), bf16),
        jax.ShapeDtypeStruct((rows, D), f32),
        jax.ShapeDtypeStruct(late, f32),
    ]
    if gather:
        out += [jax.ShapeDtypeStruct((3, R, HW), bf16)] + [jax.ShapeDtypeStruct((R, w), bf16) for w in (HW, FW, FW)]
    else:
        out += [jax.ShapeDtypeStruct((n, R, HW), bf16)] * 3
    scratch = [
        pltpu.VMEM((S, B, HW), bf16),
        pltpu.VMEM((S, NB, 2 * HW), bf16),
        pltpu.VMEM((S, B, 128), f32),
        pltpu.VMEM((S, B, HW), bf16),
        pltpu.VMEM((S, 3 * B, 2 * HW), bf16),
        pltpu.VMEM((3, D, HW), bf16),
        pltpu.VMEM((S, B, D), f32),
        pltpu.VMEM((S, B, D), f32),
        pltpu.VMEM((2 * HW, 3 * B), f32),
        pltpu.VMEM((S, 2 * HW, B), f32),
        pltpu.VMEM((S, 2 * HW, NB), f32),
        pltpu.VMEM((S, B, 3 * HW), bf16),
        *[pltpu.VMEM((S, 2 * HW, B), bf16)] * 4,
        pltpu.VMEM((S, HW, NB), f32),
        pltpu.VMEM((S, 2 * HW, NB), bf16),
        pltpu.VMEM((S, 2 * HW, NB), bf16),
        pltpu.VMEM((D, S * B), bf16),
        *[pltpu.VMEM((S, B, D), bf16)] * 3,
        pltpu.VMEM((S, B, 3 * B), f32),
        pltpu.VMEM((rows, D), f32),
        sem((6 * S + 9,)),
        *[sem((S,))] * 4,
        *[sem((S, 2))] * 2,
        *[sem((S,))] * 8,
        *[sem((S, 2))] * 2,
    ]
    if gather:
        scratch += [
            pltpu.VMEM((n, Q, FW), bf16),
            pltpu.VMEM((n, 2 * Q, FW), bf16),
            *[pltpu.VMEM((n, R, HW), bf16)] * 4,
            *[pltpu.VMEM((n, 2 * Q, HW), bf16)] * 8,
            *[pltpu.VMEM((2 * Q, HW), bf16)] * 2,
            pltpu.VMEM((n, Q, HW), bf16),
            pltpu.VMEM((2 * Q, HW), bf16),
            pltpu.VMEM((n, Q, FW), bf16),
            *[pltpu.VMEM((2 * Q, HW), bf16)] * 2,
            pltpu.VMEM((n, Q, HW), bf16),
            pltpu.VMEM((2 * Q, HW), bf16),
            pltpu.VMEM((n, Q, FW), bf16),
            *[pltpu.VMEM((n - 1, 2 * Q, HW), bf16)] * 2,
            pltpu.VMEM((n - 1, Q, HW), bf16),
            pltpu.VMEM((n - 1, 2 * Q, HW), bf16),
            *[pltpu.VMEM((n - 1, Q, FW), bf16)] * 2,
            *[pltpu.VMEM((4, rows, D), f32)] * 2,
            *[pltpu.VMEM((4, *late), f32)] * 2,
            *[sem((6, 2))] * 2,
            *[sem((6, n - 1))] * 2,
            *[sem((6, 3))] * 2,
            *[sem((4, 3))] * 2,
        ]
    args = [bias, places, q, kv, mem, lse, gmixed, turned, wq, hid, gres, residual, mlp_part, pbias, gain, cw, sw, fit, sums,
            fsum, *owned]
    far = (0, 2, 3, 4, 5, 6, 20, 21, 22, 7, 8, 9, 10, 11, 12)
    return pl.pallas_call(
        lambda *refs: backward_kernel(gather, refs),
        out_shape=out,
        in_specs=[hb if i in far else vm for i in range(len(args))],
        out_specs=[vm] * len(out),
        scratch_shapes=scratch,
        compiler_params=pltpu.CompilerParams(
            collective_id=2, has_side_effects=True, vmem_limit_bytes=VMEM_LIMIT
        ),
        cost_estimate=pl.CostEstimate(flops=12_000_000_000, bytes_accessed=40_000_000, transcendentals=6_000_000),
        name="backward_part",
    )(*args)


def finish_kernel(fqkv, fo, ff, fp, early, late, block_in, grad_in, qkv, out, fc, proj, block, grad, qb, cgrad, sgrad, *vectors):
    HW = fqkv.shape[2]
    D = vectors[0].shape[0]
    H, NB = cgrad.shape
    per = D // HW
    for k in range(3):
        qb[k : k + 1] = late[2 * per + k : 2 * per + k + 1]
    qkv[...] = fqkv[...].astype(f32)
    out[...] = fo[...].astype(f32)
    fc[...] = ff[...].astype(f32)
    proj[...] = fp[...].astype(f32)
    block[...] = block_in[...]
    grad[...] = grad_in[...]
    cgrad[...] = early[8 : 8 + H, 0:NB]
    sgrad[...] = early[8 : 8 + H, NB : 2 * NB]
    for which in range(2):
        for k in range(per):
            vectors[which][k * HW : (k + 1) * HW] = late[which * per + k : which * per + k + 1].reshape(HW)
    for k in range(4):
        vectors[2 + k][...] = early[k : k + 1, 0:D].reshape(D)
    for k in range(vectors[6].shape[0] // D):
        vectors[6][k * D : (k + 1) * D] = early[4 + k : 5 + k].reshape(D)


def finish(parts, early, late, block_out, input_grad, D, H, NB):
    _, R, HW = parts[0].shape
    FW = parts[2].shape[1]
    vm = pl.BlockSpec(memory_space=pltpu.VMEM)
    shapes = [(3, R, HW), (R, HW), (R, FW), (R, FW)]
    more = [(3, HW), (H, NB), (H, NB)] + [(D,)] * 6 + [(FW,)]
    copied = [jax.ShapeDtypeStruct(v.shape, v.dtype) for v in (block_out, input_grad)]
    return pl.pallas_call(
        finish_kernel,
        out_shape=[jax.ShapeDtypeStruct(v, f32) for v in shapes] + copied + [jax.ShapeDtypeStruct(v, f32) for v in more],
        in_specs=[vm] * 8,
        out_specs=[vm] * (len(shapes) + 2 + len(more)),
        compiler_params=pltpu.CompilerParams(vmem_limit_bytes=VMEM_LIMIT),
        name="finish_part",
    )(*parts, early, late, block_out, input_grad)


def per_device(hidden_in, doc_lengths, sticky_places, attn_gain, attn_shift, qkv_weight, qkv_bias, center_weight,
               spread_weight, out_weight, out_bias, mlp_gain, mlp_shift, fc_weight, fc_bias, proj_weight, proj_bias,
               cotangent):
    S, B, D = hidden_in.shape
    n = lax.axis_size("dp")
    HW = qkv_bias.shape[1]
    H, NB = center_weight.shape
    M = sticky_places.shape[1]
    fit = jnp.asarray(ridge_fit(NB, 2 * M))
    gather = n == 4 and D % (64 * n) == 0
    weights = [jnp.transpose(qkv_weight, (1, 0, 2)), out_weight.T, fc_weight, proj_weight.T]
    if not gather:
        full = [lax.all_gather(w, "dp", axis=w.ndim - 2, tiled=True) for w in weights]
        weights = full[:1]
    made = forward(gather, hidden_in, doc_lengths, sticky_places, attn_gain, attn_shift, weights,
                   qkv_bias, center_weight, spread_weight, fit, cotangent)
    turned, cot_turned, bias, q, kv, mem, lse, mixed = made[:8]
    if gather:
        wq, wo, wf, wp = made[8:]
    else:
        wq, wo, wf, wp = full
        wo = lax.all_gather(wo, "tp", axis=0)
    made = mlp(gather, hidden_in, mixed, wo, wf, wp, out_bias, mlp_gain, mlp_shift, fc_bias, cotangent, cot_turned)
    residual, mlp_part, gres, gmixed, og, pg, fg, sums, fsum = made
    owned = [pg, fg, og] if gather else []
    made = backward(gather, bias, sticky_places, q, kv, mem, lse, gmixed, turned, wq, hidden_in, gres, residual, mlp_part,
                    proj_bias, attn_gain, center_weight, spread_weight, fit, sums, fsum, owned)
    block_out, input_grad, early, late = made[:4]
    if gather:
        made = finish(made[4:], early, late, block_out, input_grad, D, H, NB)
        qkv_grad, out_grad, fc_grad, proj_grad, block_out, input_grad, qkv_bias_grad, center_grad, spread_grad = made[:9]
        gain_grad, shift_grad, out_bias_grad, mlp_gain_grad, mlp_shift_grad, proj_bias_grad, fc_bias_grad = made[9:]
        qkv_grad, out_grad, proj_grad = jnp.transpose(qkv_grad, (1, 0, 2)), out_grad.T, proj_grad.T
    else:
        early, late = lax.psum((early, late), ("dp", "ctx"))

        def reduced(grad):
            part = lax.psum_scatter(grad.reshape(D, -1), "dp", scatter_dimension=0, tiled=True)
            return lax.psum(part, "ctx").astype(f32)

        qkv_grad = jnp.stack([reduced(g) for g in made[4:]], axis=1)
        out_grad, fc_grad, proj_grad = reduced(og).T, reduced(fg), reduced(pg).T
        per = D // HW
        qkv_bias_grad = late[2 * per : 2 * per + 3]
        center_grad, spread_grad = early[8 : 8 + H, :NB], early[8 : 8 + H, NB : 2 * NB]
        gain_grad, shift_grad = late[:per].reshape(-1), late[per : 2 * per].reshape(-1)
        out_bias_grad, mlp_gain_grad, mlp_shift_grad, proj_bias_grad = [early[k, :D] for k in range(4)]
        fc_bias_grad = early[4 : 4 + fc_bias.shape[0] // D].reshape(-1)
    return (
        block_out,
        input_grad,
        gain_grad,
        shift_grad,
        qkv_grad,
        qkv_bias_grad,
        center_grad,
        spread_grad,
        out_grad,
        out_bias_grad,
        mlp_gain_grad,
        mlp_shift_grad,
        fc_grad,
        fc_bias_grad,
        proj_grad,
        proj_bias_grad,
    )


def solution(mesh):
    in_specs = (
        P("dp", "ctx", None),
        P("dp", None),
        P("dp", None),
        P(),
        P(),
        P("dp", None, "tp"),
        P(None, "tp"),
        P("tp", None),
        P("tp", None),
        P("tp", "dp"),
        P(),
        P(),
        P(),
        P("dp", "tp"),
        P("tp"),
        P("tp", "dp"),
        P(),
        P("dp", "ctx", None),
    )
    out_specs = (
        P("dp", "ctx", None),
        P("dp", "ctx", None),
        P(),
        P(),
        P("dp", None, "tp"),
        P(None, "tp"),
        P("tp", None),
        P("tp", None),
        P("tp", "dp"),
        P(),
        P(),
        P(),
        P("dp", "tp"),
        P("tp"),
        P("tp", "dp"),
        P(),
    )
    return jax.shard_map(
        per_device, mesh=mesh, in_specs=in_specs, out_specs=out_specs, check_vma=False
    )
```

```python
import functools

import jax
import jax.numpy as jnp
import numpy as np
from jax import lax
from jax.experimental import pallas as pl
from jax.experimental.pallas import tpu as pltpu
from jax.sharding import PartitionSpec as P

DH = 64
WINDOW = 512
EPS = 1e-05
SPREAD = 0.02
SCALE = DH ** (-0.5)
VMEM_LIMIT = 60 * 1024 * 1024

bf16 = jnp.bfloat16
f32 = jnp.float32
MESH = pl.DeviceIdType.MESH


def dot_nn(a, b):
    return lax.dot_general(a, b, (((1,), (0,)), ((), ())), preferred_element_type=f32)


def dot_nt(a, b):
    return lax.dot_general(a, b, (((1,), (1,)), ((), ())), preferred_element_type=f32)


def dot_tn(a, b):
    return lax.dot_general(a, b, (((0,), (0,)), ((), ())), preferred_element_type=f32)


def ridge_fit(basis_count, sample_count):
    centers = (np.arange(basis_count) + 0.5) / basis_count
    times = (np.arange(sample_count) + 0.5) / sample_count
    width = 1.0 / basis_count
    design = np.exp(-np.square(times[None, :] - centers[:, None]) / (2.0 * width * width))
    gram = design @ design.T + 0.5 * np.eye(basis_count)
    return np.linalg.solve(gram, design).astype(bf16)


def place():
    c = lax.axis_index("ctx")
    side = c + 1 - 2 * lax.rem(c, 2)
    across = lax.rem(c + 2, 4)
    corner = lax.rem(side + 2, 4)
    return lax.axis_index("dp"), c, lax.axis_index("tp"), side, across, corner


def knock(devices):
    barrier = pltpu.get_barrier_semaphore()
    for device in devices:
        pl.semaphore_signal(barrier, inc=1, device_id=device, device_id_type=MESH)
    return lambda: pl.semaphore_wait(barrier, len(devices))


def remote(src, dst, send, recv, device):
    return pltpu.make_async_remote_copy(
        src_ref=src,
        dst_ref=dst,
        send_sem=send,
        recv_sem=recv,
        device_id=device,
        device_id_type=MESH,
    )


def normalise(x, gain, shift):
    mean = jnp.mean(x, axis=-1, keepdims=True)
    centred = x - mean
    r = lax.rsqrt(jnp.mean(centred * centred, axis=-1, keepdims=True) + EPS)
    n = centred * r
    return n * gain + shift, n, r


def lowest_key(lengths, s, pos):
    low = jnp.maximum(pos - (WINDOW - 1), 0)
    end = jnp.int32(0)
    for e in range(lengths.shape[1]):
        end = end + lengths[s, e]
        low = jnp.maximum(low, jnp.where(pos >= end, end, 0))
    return low


def row_of(vector):
    return vector[...].reshape(1, vector.shape[0])


def lanes(shape, dim):
    return lax.broadcasted_iota(jnp.int32, shape, dim)


def half_lanes(scale):
    lane = lanes((1, 2 * DH), 1)
    return [
        jnp.where(lane < DH, scale, 0.0).astype(bf16),
        jnp.where(lane >= DH, scale, 0.0).astype(bf16),
    ]


def mask_bias(lengths, s, c, rows, key_start, keys):
    pos = c * rows + lanes((rows, 1), 0)
    low = lowest_key(lengths, s, pos)
    key_pos = key_start + lanes((1, keys), 1)
    return jnp.where((key_pos <= pos) & (key_pos >= low), 0.0, -1e30)


def fit_at(fit, places, s, tokens, length):
    M = places.shape[1]
    sticky = jnp.where(tokens == places[s : s + 1, :], 1.0, 0.0).astype(bf16)
    even = lanes((1, M), 1) * length // M + length // (2 * M)
    steady = jnp.where(tokens == even, 1.0, 0.0).astype(bf16)
    value = dot_nt(fit[:, :M], sticky) + dot_nt(fit[:, M:], steady)
    high = value.astype(bf16)
    return high, (value - high.astype(f32)).astype(bf16)


def reach_terms(scores, center_row, spread_row, centers, width):
    center_logit = jnp.sum(scores * center_row, axis=-1, keepdims=True)
    spread_logit = jnp.sum(scores * spread_row, axis=-1, keepdims=True)
    mu = 1.0 / (1.0 + jnp.exp(-center_logit))
    grown = jnp.exp(spread_logit)
    var = SPREAD * jnp.log(1.0 + grown) + width * width
    inv = 1.0 / var
    diff = mu - centers
    reach = (width * lax.rsqrt(var)) * jnp.exp(-(diff * diff) * (0.5 * inv))
    return reach, mu, inv, diff, spread_logit


def forward_kernel(gather, refs):
    n = lax.axis_size("dp")
    if gather:
        (hid_far, lengths, places, gain, shift, wq_sh, wo_sh, wf_sh, wp_sh, qbias, cw, sw, fit, cot_far,
         turned_out, cot_out, bias_out, q_out, kv_out, mem_out, lse_out, mixed, wq_out, wo, wf, wp,
         normed, q, kv, hoth, noth, bias, fits, mem, lse, hid, turned, cot, cot_turned, cs, os_, hys, hyr, hxs, hxr, ks, kr, ms, mr,
         wq, wo_own, wf_own, wp_own, lsem, zs, zr, ys, yr, as_, ar, bs, br, oxs, oxr, lzs, lzr, lys, lyr, las, lar, lbs, lbr) = refs
    else:
        (hid_far, lengths, places, gain, shift, wq, qbias, cw, sw, fit, cot_far,
         turned_out, cot_out, bias_out, q_out, kv_out, mem_out, lse_out, mixed,
         normed, q, kv, hoth, noth, bias, fits, mem, lse, hid, turned, cot, cot_turned, cs, os_, hys, hyr, hxs, hxr, ks, kr, ms, mr) = refs
    z, c, t, side, across, corner = place()
    S, B, D = hid_far.shape
    HW = q.shape[2]
    NB = mem.shape[1]
    L = kv.shape[1]
    half = B // 2
    peers = [{"ctx": side}, {"ctx": across}, {"tp": 1 - t}]
    if gather:
        R = D // n
        Q = R // 4
        shards = [wq_sh, wo_sh, wf_sh, wp_sh]
        whole = [wq, wo.at[t], wf, wp, wo.at[1 - t]]
        peers += [{"dp": lax.rem(z + i, n)} for i in range(1, n)]
    wait_for_all = knock(peers)
    hid_copy = pltpu.make_async_copy(hid_far, hid, cs.at[0])
    hid_copy.start()
    cot_copy = pltpu.make_async_copy(cot_far, cot, cs.at[1])
    if gather:
        own_in = [
            pltpu.make_async_copy(far, near, lsem.at[4 + i]) for i, (far, near) in enumerate(((wo_sh, wo_own), (wf_sh, wf_own), (wp_sh, wp_own)))
        ]
    wait_for_all()

    started, kept = [], []

    def start(copies):
        for copy in copies:
            copy.start()
        started.extend(copies)
        return copies

    def keep(src, dst):
        copy = pltpu.make_async_copy(src, dst, os_.at[len(kept)])
        copy.start()
        kept.append(copy)

    if gather:
        groups = range(1, 5)

        def rows(g, owner, quarter):
            part = pl.ds(pl.multiple_of(R * owner + Q * quarter, 16), Q)
            return wq.at[:, part] if g == 0 else whole[g].at[part]

        def source(i):
            return lax.rem(z + n - i, n)

        def part_rows(part, owner, quarter):
            rows_here = pl.ds(pl.multiple_of(R * owner + Q * quarter, 16), Q)
            return wq.at[1:3, rows_here] if part == 0 else wq.at[0:1, rows_here]

        def first_z(part):
            mine_here = pl.ds(pl.multiple_of(Q * c, 16), Q)
            src = wq_sh.at[1:3, mine_here] if part == 0 else wq_sh.at[0:1, mine_here]
            return start([
                remote(src, part_rows(part, z, c), zs.at[part, i - 1], zr.at[part, i - 1], {"dp": lax.rem(z + i, n)})
                for i in range(1, n)
            ])

        def first_y(part, sent):
            over, beside = [], []
            for i, copy in enumerate(sent):
                copy.wait_recv()
                w = part_rows(part, source(i + 1), c)
                over += start([remote(w, w, ys.at[part, i], yr.at[part, i], {"ctx": across})])
                beside += start([remote(w, w, as_.at[part, i], ar.at[part, i], {"ctx": side})])
            return over, beside

        def first_side(part, over):
            last = []
            for i, copy in enumerate(over):
                copy.wait_recv()
                w = part_rows(part, source(i + 1), across)
                last += start([remote(w, w, bs.at[part, i], br.at[part, i], {"ctx": side})])
            return last

        def sends(way, r):
            return ((z < n - 1) & (z >= r)) if way == 0 else ((z > 0) & (z + r < n))

        def takes(way, r):
            return (z > r) if way == 0 else (z + r < n - 1)

        def line_z(g, way, r):
            owner = z - r if way == 0 else z + r
            to = z + 1 if way == 0 else z - 1
            dst = rows(g, owner, c)
            src = shards[g].at[pl.ds(pl.multiple_of(Q * c, 16), Q)] if r == 0 and g < 4 else dst
            return remote(src, dst, lzs.at[g - 1, way, r], lzr.at[g - 1, way, r], {"dp": to})

        def line_copy(g, way, r, sems, quarter, device):
            part = rows(g, z - 1 - r if way == 0 else z + 1 + r, quarter)
            return remote(part, part, sems[0].at[g - 1, way, r], sems[1].at[g - 1, way, r], {"ctx": device})

        def line_y(g, way, r):
            return line_copy(g, way, r, (lys, lyr), c, across)

        def line_a(g, way, r):
            return line_copy(g, way, r, (las, lar), c, side)

        def line_b(g, way, r):
            return line_copy(g, way, r, (lbs, lbr), across, side)

        def line_send(r, some=groups):
            for way in range(2):

                @pl.when(sends(way, r))
                def _(way=way):
                    for g in some:
                        line_z(g, way, r).start()

        def line_take(r):
            for way in range(2):

                @pl.when(takes(way, r))
                def _(way=way):
                    for g in groups:
                        line_z(g, way, r).wait_recv()
                        line_y(g, way, r).start()
                        line_a(g, way, r).start()

        def line_pass(r):
            for way in range(2):

                @pl.when(takes(way, r))
                def _(way=way):
                    for g in groups:
                        line_y(g, way, r).wait_recv()
                        line_b(g, way, r).start()

        def line_end(r):
            for way in range(2):

                @pl.when(takes(way, r))
                def _(way=way):
                    for g in groups:
                        line_a(g, way, r).wait_recv()
                        line_b(g, way, r).wait_recv()
                        line_y(g, way, r).wait_send()
                        line_a(g, way, r).wait_send()
                        line_b(g, way, r).wait_send()

                @pl.when(sends(way, r))
                def _(way=way):
                    for g in groups:
                        line_z(g, way, r).wait_send()
    else:

        def line_send(r):
            pass

        line_take = line_pass = line_end = line_send

    def hidden_y(s):
        piece = pl.ds(pl.multiple_of(half * t, 16), half)
        return remote(hid_far.at[s, piece], hoth.at[s, piece], hys.at[s], hyr.at[s], {"ctx": across})

    def hidden_x(s):
        piece = pl.ds(pl.multiple_of(half * t, 16), half)
        return remote(hoth.at[s, piece], hoth.at[s, piece], hxs.at[s], hxr.at[s], {"tp": 1 - t})

    def block(s, owner):
        return kv.at[s, pl.ds(pl.multiple_of(owner * B, B), B)]

    def kv_copy(s, which):
        owner = c if which == 0 else across
        return remote(block(s, owner), block(s, owner), ks.at[s, which], kr.at[s, which], {"ctx": side})

    if gather:
        z_sent = [first_z(0)]
    hy = start([hidden_y(s) for s in range(S)])
    if gather:
        z_sent.append(first_z(1))
        mine = pl.ds(pl.multiple_of(R * z, 16), R)
        owned = [
            pltpu.make_async_copy(near, wq.at[:, mine] if g == 0 else whole[g].at[mine], lsem.at[g])
            for g, near in enumerate((wq_sh, wo_own, wf_own, wp_own))
        ]
        for copy in (owned[0], *own_in):
            copy.start()
        crossed = start([remote(wo_sh, wo.at[t, mine], oxs, oxr, {"tp": 1 - t})])[0]
        line_send(0, (1, 2, 3))

    gain_row = row_of(gain)
    shift_row = row_of(shift)
    key_start = pl.multiple_of(jnp.maximum(c - 2, 0) * B, B)
    keys = 3 * B
    cot_copy.start()
    hid_copy.wait()
    for s in range(S):
        low, _, _ = normalise(hid[s].astype(f32), gain_row, shift_row)
        normed[s] = low.astype(bf16)
    turned[...] = normed[...].reshape(S * B, D).T
    keep(turned, turned_out)
    if gather:
        for k in range(3):
            own_in[k].wait()
            owned[1 + k].start()
    hx = []

    def forward_hidden(s):
        hy[s].wait_recv()
        hx.extend(start([hidden_x(s)]))

    for s in range(S):
        if s < S - 1:
            forward_hidden(s)
        high, rest = fit_at(fit, places, s, lanes((L, 1), 0), L)
        fits[0, s] = high
        fits[1, s] = rest
    if gather:
        over, beside = first_y(0, z_sent[0])
        crossed.wait_recv()
        line_send(0, (4,))
    forward_hidden(S - 1)
    cot_copy.wait()
    cot_turned[...] = cot[...].reshape(S * B, D).T
    keep(cot_turned, cot_out)
    if gather:
        over_q, beside_q = first_y(1, z_sent[1])
    for s in range(S):
        bias[s] = mask_bias(lengths, s, c, B, key_start, keys)
    keep(bias, bias_out)
    line_take(0)
    line_send(1)
    if gather:
        last = first_side(0, over)
    for s in range(S):
        hx[s].wait_recv()
        low, _, _ = normalise(hoth[s].astype(f32), gain_row, shift_row)
        noth[s] = low.astype(bf16)
    if gather:
        last_q = first_side(1, over_q)
        for copy in beside + last:
            copy.wait_recv()
        owned[0].wait()
    kvs = []
    for s in range(S):
        for which, rows_in, owner in ((0, normed, c), (1, noth, across)):
            for k in (1, 2):
                part = dot_nn(rows_in[s], wq[k]) + qbias[k : k + 1]
                kv[s, pl.ds(pl.multiple_of(owner * B, B), B), (k - 1) * HW : k * HW] = part.astype(bf16)
            kvs += start([kv_copy(s, which)])
    if gather:
        for copy in beside_q + last_q:
            copy.wait_recv()
        keep(wq, wq_out)
    for s in range(S):
        q[s] = (dot_nn(normed[s], wq[0]) + qbias[0:1]).astype(bf16)
    keep(q, q_out)
    line_take(1)
    line_send(2)

    centers = (lanes((1, NB), 1).astype(f32) + 0.5) * (1.0 / NB)
    width = 1.0 / NB
    lane = lanes((1, 2 * DH), 1)
    scaled = half_lanes(SCALE)
    mx = []
    for s in range(S):
        kvs[2 * s].wait_recv()
        kvs[2 * s + 1].wait_recv()
        keep(kv.at[s], kv_out.at[s])
        mem[s] = (dot_nn(fits[0, s], kv[s]) + dot_nn(fits[1, s], kv[s])).astype(bf16)
        keep(mem.at[s], mem_out.at[s])

        def mixed_copy(s, p, cols):
            part = mixed.at[t, s, :, cols]
            return remote(part, part, ms.at[s, p], mr.at[s, p], {"tp": 1 - t})

        def pair_step(p, log_rows, s=s):
            cols = pl.ds(pl.multiple_of(p * 2 * DH, 2 * DH), 2 * DH)
            vcols = pl.ds(pl.multiple_of(HW + p * 2 * DH, 2 * DH), 2 * DH)
            window = pl.ds(key_start, keys)
            qp = q[s, :, cols]
            kp = kv[s, window, cols]
            vp = kv[s, window, vcols]
            mk = mem[s, :, cols]
            mv = mem[s, :, vcols]
            outs = []
            for h in range(2):
                qh = qp * scaled[h]
                scores = dot_nt(qh, kp) + bias[s]
                top = jnp.max(scores, axis=-1, keepdims=True)
                e = jnp.exp(scores - top)
                total = jnp.sum(e, axis=-1, keepdims=True)
                share = (e * (1.0 / total)).astype(bf16)
                out = dot_nn(share, vp)
                log_rows = jnp.where(lane == 2 * p + h, top + jnp.log(total), log_rows)
                mem_scores = dot_nt(qh, mk)
                reach, _, _, _, _ = reach_terms(
                    mem_scores, cw[pl.ds(2 * p + h, 1)], sw[pl.ds(2 * p + h, 1)], centers, width
                )
                outs.append(out + dot_nn(reach.astype(bf16), mv))
            mixed[t, s, :, cols] = jnp.where(lane < DH, outs[0], outs[1]).astype(bf16)
            mixed_copy(s, p, cols).start()
            return log_rows

        lse[s] = lax.fori_loop(0, HW // (2 * DH), pair_step, jnp.zeros((B, 2 * DH), f32))
        keep(lse.at[s], lse_out.at[s])
        mx += [mixed_copy(s, p, pl.ds(p * 2 * DH, 2 * DH)) for p in range(HW // (2 * DH))]
        if s == 0:
            line_pass(0)
            line_take(2)
    line_pass(1)
    line_pass(2)
    for r in range(n - 1 if gather else 0):
        line_end(r)
    if gather:
        for copy in owned[1:]:
            copy.wait()
    for copy in mx:
        copy.wait_recv()
    for copy in started + mx:
        copy.wait_send()
    for copy in kept:
        copy.wait()


def forward(gather, hid, lengths, places, gain, shift, weights, qbias, cw, sw, fit, cot):
    S, B, D = hid.shape
    HW = qbias.shape[1]
    n = lax.axis_size("dp")
    L = B * lax.axis_size("ctx")
    NB = cw.shape[1]
    vm = pl.BlockSpec(memory_space=pltpu.VMEM)
    sm = pl.BlockSpec(memory_space=pltpu.SMEM)
    hb = pl.BlockSpec(memory_space=pl.ANY)
    out = [
        jax.ShapeDtypeStruct((D, S * B), bf16),
        jax.ShapeDtypeStruct((D, S * B), bf16),
        jax.ShapeDtypeStruct((S, B, 3 * B), f32),
        jax.ShapeDtypeStruct((S, B, HW), bf16),
        jax.ShapeDtypeStruct((S, L, 2 * HW), bf16),
        jax.ShapeDtypeStruct((S, NB, 2 * HW), bf16),
        jax.ShapeDtypeStruct((S, B, 128), f32),
        jax.ShapeDtypeStruct((2, S, B, HW), bf16),
    ]
    out_specs = [hb] * 7 + [vm]
    sem = pltpu.SemaphoreType.DMA
    scratch = [
        pltpu.VMEM((S, B, D), bf16),
        pltpu.VMEM((S, B, HW), bf16),
        pltpu.VMEM((S, L, 2 * HW), bf16),
        pltpu.VMEM((S, B, D), bf16),
        pltpu.VMEM((S, B, D), bf16),
        pltpu.VMEM((S, B, 3 * B), f32),
        pltpu.VMEM((2, S, NB, L), bf16),
        pltpu.VMEM((S, NB, 2 * HW), bf16),
        pltpu.VMEM((S, B, 128), f32),
        pltpu.VMEM((S, B, D), bf16),
        pltpu.VMEM((D, S * B), bf16),
        pltpu.VMEM((S, B, D), bf16),
        pltpu.VMEM((D, S * B), bf16),
        sem((2,)),
        sem((3 * S + 5,)),
        *[sem((S,))] * 4,
        *[sem((S, 2))] * 2,
        *[sem((S, HW // (2 * DH)))] * 2,
    ]
    w_specs = [vm]
    if gather:
        FW = weights[2].shape[1]
        out += [
            jax.ShapeDtypeStruct((3, D, HW), bf16),
            jax.ShapeDtypeStruct((2, D, HW), bf16),
            jax.ShapeDtypeStruct((D, FW), bf16),
            jax.ShapeDtypeStruct((D, FW), bf16),
        ]
        out_specs += [hb] * 4
        w_specs = [hb] * 4
        scratch += [
            pltpu.VMEM((3, D, HW), bf16),
            *[pltpu.VMEM((D // n, w), bf16) for w in (HW, FW, FW)],
            sem((7,)),
            *[sem((2, n - 1))] * 8,
            sem,
            sem,
            *[sem((4, 2, n - 1))] * 8,
        ]
    return pl.pallas_call(
        lambda *refs: forward_kernel(gather, refs),
        out_shape=out,
        in_specs=[hb, sm, vm, vm, vm, *w_specs, vm, vm, vm, vm, hb],
        out_specs=out_specs,
        scratch_shapes=scratch,
        compiler_params=pltpu.CompilerParams(
            collective_id=0, has_side_effects=True, vmem_limit_bytes=VMEM_LIMIT
        ),
        cost_estimate=pl.CostEstimate(flops=6_000_000_000, bytes_accessed=30_000_000, transcendentals=6_000_000),
        name="forward_part",
    )(hid, lengths, places, gain, shift, *weights, qbias, cw, sw, fit, cot)


def quarter(c):
    return 2 * lax.rem(c, 2) + c // 2


class Reduction:
    def __init__(self, n, rows, full, half, half_in, own, own_in, sems):
        self.n, self.rows, self.piece = n, rows, rows // 4
        self.full, self.half, self.half_in, self.own, self.own_in = full, half, half_in, own, own_in
        self.sems = sems
        self.z, self.c, self.t, self.side, self.across, self.corner = place()
        self.started = []

    def at(self, offset, size):
        return pl.ds(pl.multiple_of(offset, 16), size)

    def send_side(self):
        two = 2 * self.piece
        core = lax.rem(self.c, 2)
        self.one = remote(
            self.full.at[:, self.at(two * (1 - core), two)], self.half_in, self.sems[0].at[0], self.sems[1].at[0], {"ctx": self.side}
        )
        self.one.start()
        self.started.append(self.one)

    def sum_side(self):
        two = 2 * self.piece
        core = lax.rem(self.c, 2)
        self.one.wait_recv()
        for k in range(self.n):
            self.half[k] = (
                self.full[k, self.at(two * core, two)].astype(f32) + self.half_in[k].astype(f32)
            ).astype(bf16)

    def send_across(self):
        piece, y = self.piece, self.c // 2
        self.two = remote(
            self.half.at[:, self.at(piece * (1 - y), piece)], self.own_in, self.sems[0].at[1], self.sems[1].at[1], {"ctx": self.across}
        )
        self.two.start()
        self.started.append(self.two)

    def take_across(self):
        y = self.c // 2
        self.two.wait_recv()
        for k in range(self.n):
            self.own[k] = (
                self.half[k, self.at(self.piece * y, self.piece)].astype(f32) + self.own_in[k].astype(f32)
            ).astype(bf16)

    def wait_sends(self):
        for copy in self.started:
            copy.wait_send()


def mlp_kernel(gather, refs):
    (hid_far, mixed_far, wo_far, wf_far, wp_far, obias, gain, shift, fbias, cot_far, cot_turned_far,
     residual_out, mlp_out, gres_out, gmixed, og, pg, fg, sums, fsum,
     hid, mixed, wo, residual, mlp_part, gres, wf, wp, cot, low, act, gpre, gpart, gin, turned, glow, frow, cot_turned, ls, outs, gs, gr, *rest) = refs
    if gather:
        pfull, phalf, phalf_in, pown_in, ffull, fhalf_in, ps, pr, fs, fr = rest
    else:
        pfull, ffull = pg, fg
    z, c, t, side, across, corner = place()
    S, B, D = hid_far.shape
    FW = wf.shape[1]
    HW = mixed.shape[3]
    n, R = pfull.shape[:2]
    tile = 512
    pairs = [
        (wo_far, wo), (mixed_far.at[:, 0], mixed.at[:, 0]), (hid_far.at[0], hid.at[0]), (wf_far, wf), (wp_far, wp), (cot_far, cot),
        (mixed_far.at[:, 1:S], mixed.at[:, 1:S]), (hid_far.at[1:S], hid.at[1:S]), (cot_turned_far, cot_turned)
    ]
    loads = [pltpu.make_async_copy(far, near, ls.at[i]) for i, (far, near) in enumerate(pairs)]
    for copy in loads[:8]:
        copy.start()
    kept = []

    def keep(src, dst):
        copy = pltpu.make_async_copy(src, dst, outs.at[len(kept)])
        copy.start()
        kept.append(copy)

    wait_for_all = knock([{"tp": 1 - t}] + ([{"ctx": side}, {"ctx": across}] if gather else []))
    obias_row, gain_row, shift_row = row_of(obias), row_of(gain), row_of(shift)
    frow[...] = row_of(fbias)
    fsum[...] = jnp.zeros_like(fsum)
    copies = []
    for copy in loads[:3]:
        copy.wait()
    for s in range(S):
        if s == 1:
            loads[6].wait()
            loads[7].wait()
        branch = dot_nt(mixed[0, s], wo[0]) + dot_nt(mixed[1, s], wo[1])
        wide = hid[s].astype(f32) + branch + obias_row
        residual[s] = wide
        value, _, _ = normalise(wide, gain_row, shift_row)
        low[s] = value.astype(bf16)
        keep(residual.at[s], residual_out.at[s])
        if s == 0:
            loads[3].wait()
            loads[8].start()

        def columns(j, carry, s=s):
            cols = pl.ds(pl.multiple_of(j * tile, tile), tile)
            pre = dot_nn(low[s], wf[:, cols]) + frow[:, cols]
            square = pre * pre
            th = jnp.tanh(0.7978845608028654 * (pre + 0.044715 * (square * pre)))
            act[s, :, cols] = (0.5 * pre * (1.0 + th)).astype(bf16)
            slope = 0.5 * (1.0 + th) + (0.5 * pre) * (1.0 - th * th) * (
                0.7978845608028654 * (1.0 + 3.0 * 0.044715 * square)
            )
            if s == 0 and j == 0:
                loads[4].wait()
                loads[5].wait()
            grad = (dot_nn(cot[s], wp[:, cols]) * slope).astype(bf16)
            gpre[s, :, cols] = grad
            fsum[:, cols] += jnp.sum(grad.astype(f32), axis=0, keepdims=True)
            return carry

        for j in range(FW // tile):
            columns(j, 0)
        gpart[s] = dot_nt(gpre[s], wf[...]).astype(bf16)
        if s == 0:
            wait_for_all()
        copies.append(remote(gpart.at[s], gin.at[s], gs.at[s], gr.at[s], {"tp": 1 - t}))
        copies[-1].start()

    def weight_grad(full, left, right, width, step):
        if left is None:
            loads[8].wait()
            across_left = cot_turned
        else:
            turned[...] = left.reshape(S * B, D).T
            across_left = turned

        def columns(j, carry):
            cols = pl.ds(pl.multiple_of(j * step, step), step)
            value = dot_nn(across_left[...], right[:, :, cols].reshape(S * B, step)).astype(bf16)
            for k in range(n):
                full[k, :, cols] = value[k * R : (k + 1) * R]
            return carry

        lax.fori_loop(0, width // step, columns, 0)

    weight_grad(pfull, None, act, FW, 512)
    if gather:
        proj = Reduction(n, R, pfull, phalf, phalf_in, pg, pown_in, (ps, pr))
        proj.send_side()
    weight_grad(ffull, low[...], gpre, FW, 512)
    if gather:
        fc = Reduction(n, R, ffull, fg, fhalf_in, None, None, (fs, fr))
        fc.send_side()
        proj.sum_side()
        proj.send_across()
    for s in range(S):
        mlp_part[s] = dot_nt(act[s], wp[...]).astype(bf16)
        keep(mlp_part.at[s], mlp_out.at[s])
    out_sum = jnp.zeros((1, D), f32)
    gain_sum = jnp.zeros((1, D), f32)
    shift_sum = jnp.zeros((1, D), f32)
    cot_sum = jnp.zeros((1, D), f32)
    out_grad = jnp.zeros((D, HW), f32)
    for s in range(S):
        copies[s].wait_recv()
        grad = gpart[s].astype(f32) + gin[s].astype(f32)
        _, unit, r = normalise(residual[s], gain_row, shift_row)
        gain_sum += jnp.sum(grad * unit, axis=0, keepdims=True)
        shift_sum += jnp.sum(grad, axis=0, keepdims=True)
        a = grad * gain_row
        wide_cot = cot[s].astype(f32)
        cot_sum += jnp.sum(wide_cot, axis=0, keepdims=True)
        total = wide_cot + r * (
            a - jnp.mean(a, axis=-1, keepdims=True) - unit * jnp.mean(a * unit, axis=-1, keepdims=True)
        )
        out_sum += jnp.sum(total, axis=0, keepdims=True)
        gres[s] = total
        keep(gres.at[s], gres_out.at[s])
        glow[s] = total.astype(bf16)
        gmixed[s] = dot_nn(glow[s], wo[t]).astype(bf16)
        out_grad += dot_tn(glow[s], mixed[t, s])
        if s == 0 and gather:
            fc.sum_side()
    sums[0:1] = out_sum
    sums[1:2] = gain_sum
    sums[2:3] = shift_sum
    sums[3:4] = cot_sum
    for k in range(n):
        og[k] = out_grad[k * R : (k + 1) * R].astype(bf16)
    if gather:
        proj.take_across()
        proj.wait_sends()
        fc.wait_sends()
    for copy in copies:
        copy.wait_send()
    for copy in kept:
        copy.wait()


def mlp(gather, hid, mixed, wo, wf, wp, obias, gain, shift, fbias, cot, cot_turned):
    S, B, D = hid.shape
    HW = mixed.shape[3]
    FW = wf.shape[1]
    n = lax.axis_size("dp") if gather else 1
    R = D // n
    Q = R // 4
    vm = pl.BlockSpec(memory_space=pltpu.VMEM)
    sem = pltpu.SemaphoreType.DMA
    hb = pl.BlockSpec(memory_space=pl.ANY)
    pshape = (n, Q, FW) if gather else (n, R, FW)
    fshape = (n, 2 * Q, FW) if gather else (n, R, FW)
    out = [
        jax.ShapeDtypeStruct((S, B, D), f32),
        jax.ShapeDtypeStruct((S, B, D), bf16),
        jax.ShapeDtypeStruct((S, B, D), f32),
        jax.ShapeDtypeStruct((S, B, HW), bf16),
        jax.ShapeDtypeStruct((n, R, HW), bf16),
        jax.ShapeDtypeStruct(pshape, bf16),
        jax.ShapeDtypeStruct(fshape, bf16),
        jax.ShapeDtypeStruct((4, D), f32),
        jax.ShapeDtypeStruct((1, FW), f32),
    ]
    scratch = [
        pltpu.VMEM((S, B, D), bf16),
        pltpu.VMEM((2, S, B, HW), bf16),
        pltpu.VMEM((2, D, HW), bf16),
        pltpu.VMEM((S, B, D), f32),
        pltpu.VMEM((S, B, D), bf16),
        pltpu.VMEM((S, B, D), f32),
        pltpu.VMEM((D, FW), bf16),
        pltpu.VMEM((D, FW), bf16),
        pltpu.VMEM((S, B, D), bf16),
        pltpu.VMEM((S, B, D), bf16),
        pltpu.VMEM((S, B, FW), bf16),
        pltpu.VMEM((S, B, FW), bf16),
        pltpu.VMEM((S, B, D), bf16),
        pltpu.VMEM((S, B, D), bf16),
        pltpu.VMEM((D, S * B), bf16),
        pltpu.VMEM((S, B, D), bf16),
        pltpu.VMEM((1, FW), f32),
        pltpu.VMEM((D, S * B), bf16),
        sem((9,)),
        sem((3 * S,)),
        sem((S,)),
        sem((S,)),
    ]
    if gather:
        scratch += [
            pltpu.VMEM((n, R, FW), bf16),
            *[pltpu.VMEM((n, R // 2, FW), bf16)] * 2,
            pltpu.VMEM((n, Q, FW), bf16),
            pltpu.VMEM((n, R, FW), bf16),
            pltpu.VMEM((n, R // 2, FW), bf16),
            *[sem((2,))] * 4,
        ]
    return pl.pallas_call(
        lambda *refs: mlp_kernel(gather, refs),
        out_shape=out,
        in_specs=[hb, hb, hb, hb, hb, vm, vm, vm, vm, hb, hb],
        out_specs=[hb, hb, hb, *[vm] * 6],
        scratch_shapes=scratch,
        compiler_params=pltpu.CompilerParams(
            collective_id=1, has_side_effects=True, vmem_limit_bytes=VMEM_LIMIT
        ),
        cost_estimate=pl.CostEstimate(flops=12_000_000_000, bytes_accessed=30_000_000, transcendentals=1_500_000),
        name="mlp_part",
    )(hid, mixed, wo, wf, wp, obias, gain, shift, fbias, cot, cot_turned)


def backward_kernel(gather, refs):
    (bias_far, places, q_far, kv_far, mem_far, lse_far, gmixed_far, turned_far, wq_far, hid_far, gres_far, residual_far, mlp_far, pbias, gain,
     cw, sw, fit, sums, fsum, *rest) = refs
    if gather:
        (pown_far, fhalf_far, ofull_far, block_out, input_grad, early_out, late_out, fqkv, fo, ff, fp, *rest) = rest
    else:
        (block_out, input_grad, early_out, late_out, afull, kfull, vfull, *rest) = rest
    (q, mem, lse, gmixed, kv, wq, gres, residual, dkv, own_rows, dmem, gqkv, hs1, hr1, hs2, hr2, m1in, gmem, gfar,
     turned, mlp_in, gnpart, gnin, bias, early, ls, xs, xr, h1s, h1r, h2s, h2r, m1s, m1r, m2s, m2r, m3s, m3r, m4s, m4r, ns, nr,
     *rest) = rest
    if gather:
        (pown, fhalf, ofull, afull, kfull, vfull, ahalf_in, khalf_in, vhalf_in, ohalf_in, ahalf, khalf, vhalf, ohalf,
         aown, kown, vown, oown, fown, aown_in, kown_in, vown_in, oown_in, fown_in,
         zina, zink, zinv, zino, zinf, zinp, early_ctx, early_dp, late_ctx, late_dp,
         rs, rr, zs, zr, gs, gr, es, er) = rest
    z, c, t, side, across, corner = place()
    S, B, D = hid_far.shape
    HW = q.shape[2]
    NB = mem.shape[1]
    n, R = afull.shape[:2]
    L = kv_far.shape[1]
    keys = 3 * B
    key_start = pl.multiple_of(jnp.maximum(c - 2, 0) * B, B)
    near_pairs = []
    for s in range(S):
        near_pairs += [(far.at[s], near.at[s]) for far, near in ((q_far, q), (gmixed_far, gmixed), (lse_far, lse), (mem_far, mem))]
        near_pairs += [(kv_far.at[s, pl.ds(key_start, keys)], kv.at[s]), (bias_far.at[s], bias.at[s])]
    if gather:
        near_pairs += [(fhalf_far, fhalf), (pown_far, pown), (ofull_far, ofull)]
    next_pairs = [(turned_far, turned), (wq_far, wq), (residual_far, residual), (gres_far, gres)]
    late_pairs = [(hid_far, kv.at[:, 0:B]), (mlp_far, kv.at[:, B : 2 * B])]
    copies = [pltpu.make_async_copy(far, near, ls.at[i]) for i, (far, near) in enumerate(near_pairs + next_pairs + late_pairs)]
    loads, next_loads, late_loads = copies[: len(near_pairs)], copies[len(near_pairs) : -2], copies[-2:]
    for copy in loads:
        copy.start()
    peers = [{"tp": 1 - t}, {"ctx": side}, {"ctx": across}]
    if gather:
        peers += [{"ctx": corner}] + [{"dp": lax.rem(z + i, n)} for i in range(1, n)]
    wait_for_all = knock(peers)
    started = []

    def start(copy):
        copy.start()
        started.append(copy)
        return copy

    if gather:
        Q = R // 4
        owns, zins = {"p": pown, "f": fown, "v": vown}, {"p": zinp, "f": zinf, "v": zinv}
        finals = {"p": fp, "f": ff, "v": fqkv.at[2]}
        index = {g: i for i, g in enumerate("akvofp")}
        z_sent, g_sent = {}, {}

        def send_dp(g):
            j = index[g]
            z_sent[g] = [
                start(remote(owns[g].at[lax.rem(z + i, n)], zins[g].at[i - 1], zs.at[j, i - 1], zr.at[j, i - 1], {"dp": lax.rem(z + i, n)}))
                for i in range(1, n)
            ]

        def piece(g, device):
            return finals[g].at[pl.ds(pl.multiple_of(Q * quarter(device), 16), Q)]

        def take_dp(g):
            j = index[g]
            total = owns[g][z].astype(f32)
            for i in range(1, n):
                z_sent[g][i - 1].wait_recv()
                total = total + zins[g][i - 1].astype(f32)
            finals[g][pl.ds(pl.multiple_of(Q * quarter(c), 16), Q)] = total.astype(bf16)
            mine = piece(g, c)
            g_sent[g] = [
                start(remote(mine, mine, gs.at[j, 0], gr.at[j, 0], {"ctx": across})),
                start(remote(mine, mine, gs.at[j, 1], gr.at[j, 1], {"ctx": side})),
            ]

        def pass_on(g):
            j = index[g]
            g_sent[g][0].wait_recv()
            other = piece(g, across)
            g_sent[g].append(start(remote(other, other, gs.at[j, 2], gr.at[j, 2], {"ctx": side})))

        def take_all(g):
            g_sent[g][1].wait_recv()
            g_sent[g][2].wait_recv()

        class Chain(Reduction):
            def __init__(self, g, full, half, half_in, own, own_in, dp_in, final):
                j = index[g]
                super().__init__(n, R, full, half, half_in, own, own_in, (rs.at[j], rr.at[j]))
                self.j, self.dp_in, self.final = j, dp_in, final

            def send_dp(self):
                self.over = [
                    remote(self.half.at[lax.rem(z + i, n)], self.dp_in.at[i - 1], zs.at[self.j, i - 1], zr.at[self.j, i - 1], {"dp": lax.rem(z + i, n)})
                    for i in range(1, n)
                ]
                for copy in self.over:
                    start(copy)

            def take_dp(self):
                total = self.half[z].astype(f32)
                for i in range(1, n):
                    self.over[i - 1].wait_recv()
                    total = total + self.dp_in[i - 1].astype(f32)
                self.own[...] = total.astype(bf16)
                self.two = start(remote(self.own, self.own_in, gs.at[self.j, 0], gr.at[self.j, 0], {"ctx": across}))

            def take_across(self):
                self.two.wait_recv()
                mine = pl.ds(pl.multiple_of(2 * self.piece * lax.rem(c, 2), 16), 2 * self.piece)
                self.final[mine] = (self.own[...].astype(f32) + self.own_in[...].astype(f32)).astype(bf16)
                part = self.final.at[mine]
                self.three = start(remote(part, part, gs.at[self.j, 1], gr.at[self.j, 1], {"ctx": side}))

            def take_all(self):
                self.three.wait_recv()

        red = {
            "a": Chain("a", afull, ahalf, ahalf_in, aown, aown_in, zina, fqkv.at[0]),
            "k": Chain("k", kfull, khalf, khalf_in, kown, kown_in, zink, fqkv.at[1]),
            "o": Chain("o", ofull, ohalf, ohalf_in, oown, oown_in, zino, fo),
        }
        vals = Reduction(n, R, vfull, vhalf, vhalf_in, vown, vown_in, (rs.at[2], rr.at[2]))
        fc = Reduction(n, R, None, fhalf, None, fown, fown_in, (rs.at[4], rr.at[4]))

        class Everywhere:
            def __init__(self, over_ctx, over_dp, which):
                self.over_ctx, self.over_dp, self.which = over_ctx, over_dp, which

            def send(self, slots, me, devices, step):
                j = 2 * self.which + step
                self.sent = [
                    start(remote(slots.at[me], slots.at[me], es.at[j, i], er.at[j, i], device)) for i, device in enumerate(devices)
                ]

            def over(self, axis, value, step):
                if axis == "ctx":
                    self.over_ctx[c] = value
                    self.send(self.over_ctx, c, [{"ctx": side}, {"ctx": across}, {"ctx": corner}], step)
                else:
                    self.over_dp[z] = value
                    self.send(self.over_dp, z, [{"dp": lax.rem(z + i, n)} for i in range(1, n)], step)

            def total(self, axis):
                for copy in self.sent:
                    copy.wait_recv()
                slots = self.over_ctx if axis == "ctx" else self.over_dp
                return (slots[0] + slots[1]) + (slots[2] + slots[3])

        early_sum = Everywhere(early_ctx, early_dp, 0)
        late_sum = Everywhere(late_ctx, late_dp, 1)

    mlp_sent = []

    def open_transfers():
        for copy in next_loads:
            copy.start()
        wait_for_all()
        if gather:
            for copy in loads[6 * S :]:
                copy.wait()
            fc.send_across()
            send_dp("p")
            red["o"].send_side()
        for s in range(S):
            mlp_sent.append(start(remote(mlp_far.at[s], mlp_in.at[s], xs.at[s], xr.at[s], {"tp": 1 - t})))

    lane = lanes((1, 2 * DH), 1)
    scaled = half_lanes(SCALE)
    plain = half_lanes(1.0)
    centers = (lanes((1, NB), 1).astype(f32) + 0.5) * (1.0 / NB)
    width = 1.0 / NB
    early[...] = jnp.zeros_like(early)
    half = HW
    core = lax.rem(c, 2)
    y = c // 2
    own_half = pl.ds(pl.multiple_of(core * half, 16), half)
    side_half = pl.ds(pl.multiple_of((1 - core) * half, 16), half)
    give = pl.ds(pl.multiple_of(B * (1 - core * (1 - y)), 128), B)
    own = pl.ds(pl.multiple_of(c * B - key_start, 128), B)
    one, two, three, first = {}, {}, {}, {}

    hb = B // 2

    def second_copy(s, k):
        part = pl.ds(k * hb, hb)
        return remote(hs2.at[s, :, part], hr2.at[s, :, part], h2s.at[s, k], h2r.at[s, k], {"ctx": across})

    def memory_over(s):
        return remote(gmem.at[s, own_half], gfar.at[s, own_half], m2s.at[s], m2r.at[s], {"ctx": across})

    def memory_beside(s):
        return remote(gfar.at[s, own_half], gfar.at[s, own_half], m4s.at[s], m4r.at[s], {"ctx": side})

    def attend_back(s, *between):
        for copy in loads[6 * s : 6 * s + 6]:
            copy.wait()

        def pair_step(p, carry):
            cols = pl.ds(pl.multiple_of(p * 2 * DH, 2 * DH), 2 * DH)
            vcols = pl.ds(pl.multiple_of(HW + p * 2 * DH, 2 * DH), 2 * DH)
            qp = q[s, :, cols]
            gp = gmixed[s, :, cols]
            kp = kv[s, :, cols]
            vp = kv[s, :, vcols]
            mk = mem[s, :, cols]
            mv = mem[s, :, vcols]
            q_turned = (qp * SCALE).T
            g_turned = gp.T
            logs = lse[s]
            both = jnp.concatenate([qp * scaled[0], qp * scaled[1]], axis=0)
            both_g = jnp.concatenate([gp * plain[0], gp * plain[1]], axis=0)
            all_scores = dot_nt(both, kp)
            all_grads = dot_nt(both_g, vp)
            all_mem = dot_nt(both, mk)
            all_reach = dot_nt(both_g, mv)
            grad_scores, grad_mems, dk, dv, dmk, dmv = [], [], [], [], [], []
            for h in range(2):
                row = 2 * p + h
                part = slice(h * DH, (h + 1) * DH)
                these = slice(h * B, (h + 1) * B)
                log_total = jnp.sum(jnp.where(lane == row, logs, 0.0), axis=-1, keepdims=True)
                share = jnp.exp(all_scores[these] + bias[s] - log_total)
                grad_share = all_grads[these]
                delta = jnp.sum(share * grad_share, axis=-1, keepdims=True)
                grad_score = (share * (grad_share - delta)).astype(bf16)
                mem_scores = all_mem[these]
                cw_row = cw[pl.ds(row, 1)]
                sw_row = sw[pl.ds(row, 1)]
                reach, mu, inv, diff, spread_logit = reach_terms(mem_scores, cw_row, sw_row, centers, width)
                grad_reach = all_reach[these] * reach
                scaled_diff = diff * inv
                product = grad_reach * scaled_diff
                grad_mu = -jnp.sum(product, axis=-1, keepdims=True)
                grad_var = 0.5 * (
                    jnp.sum(product * scaled_diff, axis=-1, keepdims=True) - inv * jnp.sum(grad_reach, axis=-1, keepdims=True)
                )
                gc = grad_mu * mu * (1.0 - mu)
                gw = SPREAD * grad_var * (1.0 / (1.0 + jnp.exp(-spread_logit)))
                early[pl.ds(8 + row, 1), 0:NB] += jnp.sum(gc * mem_scores, axis=0, keepdims=True)
                early[pl.ds(8 + row, 1), NB : 2 * NB] += jnp.sum(gw * mem_scores, axis=0, keepdims=True)
                grad_mem = (gc * cw_row + gw * sw_row).astype(bf16)
                grad_scores.append(grad_score)
                grad_mems.append(grad_mem)
                dk.append(dot_nn(q_turned[part], grad_score))
                dv.append(dot_nn(g_turned[part], share.astype(bf16)))
                dmk.append(dot_nn(q_turned[part], grad_mem))
                dmv.append(dot_nn(g_turned[part], reach.astype(bf16)))
            grad_q = dot_nn(jnp.concatenate(grad_scores, axis=0), kp) + dot_nn(jnp.concatenate(grad_mems, axis=0), mk)
            gqkv[s, :, cols] = (jnp.where(lane < DH, grad_q[:B], grad_q[B:]) * SCALE).astype(bf16)
            for h in range(2):
                rows = pl.ds(pl.multiple_of((2 * p + h) * DH, DH), DH)
                vrows = pl.ds(pl.multiple_of(HW + (2 * p + h) * DH, DH), DH)
                dkv[rows] = dk[h]
                dkv[vrows] = dv[h]
                dmem[s, rows] = dmk[h]
                dmem[s, vrows] = dmv[h]
            return carry

        done = 0
        for step in between:
            lax.fori_loop(done, done + 1, pair_step, 0)
            done += 1
            step()
        lax.fori_loop(done, HW // (2 * DH), pair_step, 0)
        one[s] = start(remote(dmem.at[s, side_half], m1in.at[s], m1s.at[s], m1r.at[s], {"ctx": side}))
        hs1[s] = dkv[:, give].astype(bf16)
        first[s] = start(remote(hs1.at[s], hr1.at[s], h1s.at[s], h1r.at[s], {"ctx": side}))
        own_rows[s] = dkv[:, own]
        hs2[s] = dkv[:, 0:B].astype(bf16)

    def chip_memory(s):
        one[s].wait_recv()
        gmem[s, own_half] = (dmem[s, own_half] + m1in[s]).astype(bf16)
        three[s] = start(remote(gmem.at[s, own_half], gmem.at[s, own_half], m3s.at[s], m3r.at[s], {"ctx": side}))

        @pl.when(y == 0)
        def _():
            memory_over(s).start()

    def rows_of_memory(s, grad, owner):
        high, low = fit_at(fit, places, s, owner * B + lanes((B, 1), 0), L)
        return dot_nn(grad, high) + dot_nn(grad, low)

    def give_across(s):
        first[s].wait_recv()
        three[s].wait_recv()

        @pl.when(c != 3)
        def _():
            own_rows[s] = own_rows[s] + hr1[s].astype(f32)

        @pl.when(y == 1)
        def _():
            beside = jnp.where(c == 3, 1.0, 0.0)
            total = hs2[s].astype(f32) + beside * hr1[s].astype(f32) + rows_of_memory(s, gmem[s], across)
            hs2[s] = total.astype(bf16)
            for k in range(2):
                second_copy(s, k).start()

    sent = {}

    def pass_memory(s):
        @pl.when(y == 1)
        def _():
            memory_over(s).wait_recv()
            memory_beside(s).start()

    def prepare_rows(s):
        high, low = fit_at(fit, places, s, c * B + lanes((B, 1), 0), L)
        own_rows[s] = own_rows[s] + dot_nn(gmem[s], high) + dot_nn(gmem[s], low)

        @pl.when(y == 1)
        def _():
            memory_beside(s).wait_recv()
            own_rows[s] = own_rows[s] + dot_nn(gfar[s], high) + dot_nn(gfar[s], low)

    def finish_rows(s):
        for k in range(2):
            part = slice(k * hb, (k + 1) * hb)

            @pl.when(y == 0)
            def _(k=k, part=part):
                second_copy(s, k).wait_recv()
                own_rows[s, :, part] = own_rows[s, :, part] + hr2[s, :, part].astype(f32)

            gqkv[s, part, HW:] = own_rows[s, :, part].T.astype(bf16)
            sums_here = [dot_nt(gqkv[s, part, i * HW : (i + 1) * HW], wq[i]) for i in range(3)]
            gnpart[s, part] = (sums_here[0] + sums_here[1] + sums_here[2]).astype(bf16)
            sent[s, k] = start(remote(gnpart.at[s, part], gnin.at[s, part], ns.at[s, k], nr.at[s, k], {"tp": 1 - t}))

    def finish_block(s):
        mlp_sent[s].wait_recv()
        total = kv[s, B : 2 * B].astype(f32) + mlp_in[s].astype(f32)
        block_out[s] = (residual[s] + total + row_of(pbias)).astype(bf16)

    def weight_grad(full, k):
        value = dot_nn(turned[...], gqkv[:, :, k * HW : (k + 1) * HW].reshape(S * B, HW)).astype(bf16)
        for i in range(n):
            full[i] = value[i * R : (i + 1) * R]

    column_sums = []
    gain_row = row_of(gain)

    def norm_back(s):
        sent[s, 0].wait_recv()
        sent[s, 1].wait_recv()
        grad = gnpart[s].astype(f32) + gnin[s].astype(f32)
        _, unit, r = normalise(kv[s, 0:B].astype(f32), gain_row, gain_row)
        column_sums.append((jnp.sum(grad * unit, axis=0, keepdims=True), jnp.sum(grad, axis=0, keepdims=True)))
        a = grad * gain_row
        back = r * (a - jnp.mean(a, axis=-1, keepdims=True) - unit * jnp.mean(a * unit, axis=-1, keepdims=True))
        input_grad[s] = (gres[s] + back).astype(bf16)

    attend_back(0, open_transfers)
    if gather:
        red["o"].sum_side()
        red["o"].send_dp()
    attend_back(1, lambda: chip_memory(0), lambda: give_across(0))
    if gather:
        fc.take_across()
        send_dp("f")
    pass_memory(0)
    attend_back(2, lambda: chip_memory(1), lambda: give_across(1))
    for copy in late_loads:
        copy.start()
    for copy in next_loads:
        copy.wait()
    pass_memory(1)
    prepare_rows(0)
    finish_rows(0)
    chip_memory(2)
    give_across(2)
    weight_grad(afull, 0)
    if gather:
        red["a"].send_side()
    pass_memory(2)
    early[0:4, 0:D] = sums[...]
    for k in range(fsum.shape[1] // D):
        early[4 + k : 5 + k] = fsum[:, k * D : (k + 1) * D]
    if gather:
        early_sum.over("dp", early[...], 0)
    for copy in late_loads:
        copy.wait()
    finish_block(0)
    if gather:
        red["a"].sum_side()
        red["a"].send_dp()
    prepare_rows(1)
    finish_rows(1)
    prepare_rows(2)
    finish_block(1)
    finish_block(2)
    if gather:
        take_dp("p")
        red["o"].take_dp()
        take_dp("f")
    finish_rows(2)
    if gather:
        early_sum.over("ctx", early_sum.total("dp"), 1)
    weight_grad(vfull, 2)
    if gather:
        vals.send_side()
    weight_grad(kfull, 1)
    if gather:
        red["k"].send_side()
        vals.sum_side()
        vals.send_across()
        red["k"].sum_side()
        red["k"].send_dp()
    bias_sum = jnp.sum(gqkv[...].reshape(S * B, 3 * HW).astype(f32), axis=0, keepdims=True)
    norm_back(0)
    if gather:
        vals.take_across()
        send_dp("v")
    if gather:
        red["a"].take_dp()
        pass_on("p")
        pass_on("f")
        red["o"].take_across()
    norm_back(1)
    norm_back(2)
    per = D // HW
    room = late_ctx.at[c] if gather else late_out
    room[...] = jnp.zeros(room.shape, f32)
    for which in range(2):
        whole_row = column_sums[0][which] + column_sums[1][which] + column_sums[2][which]
        for k in range(per):
            room[which * per + k : which * per + k + 1] = whole_row[:, k * HW : (k + 1) * HW]
    for k in range(3):
        room[2 * per + k : 2 * per + k + 1] = bias_sum[:, k * HW : (k + 1) * HW]
    if gather:
        late_sum.send(late_ctx, c, [{"ctx": side}, {"ctx": across}, {"ctx": corner}], 0)
        early_out[...] = early_sum.total("ctx")
        red["k"].take_dp()
        late_sum.over("dp", late_sum.total("ctx"), 1)
        red["a"].take_across()
        take_dp("v")
        red["k"].take_across()
        pass_on("v")
        late_out[...] = late_sum.total("dp")
        for g in "pfv":
            take_all(g)
        for chain in red.values():
            chain.take_all()
        for chain in (*red.values(), fc, vals):
            chain.wait_sends()
    else:
        early_out[...] = early[...]
    for s in range(S):

        @pl.when(y == 1)
        def _(s=s):
            second_copy(s, 0).wait_send()
            second_copy(s, 1).wait_send()
            memory_beside(s).wait_send()

        @pl.when(y == 0)
        def _(s=s):
            memory_over(s).wait_send()

    for copy in started:
        copy.wait_send()


def backward(gather, bias, places, q, kv, mem, lse, gmixed, turned, wq, hid, gres, residual, mlp_part, pbias, gain, cw, sw,
             fit, sums, fsum, owned):
    S, B, D = hid.shape
    HW = q.shape[2]
    FW = fsum.shape[1]
    H, NB = cw.shape
    n = lax.axis_size("dp") if gather else 1
    R = D // n
    Q = R // 4
    rows = -(-(8 + H) // 8) * 8
    vm = pl.BlockSpec(memory_space=pltpu.VMEM)
    hb = pl.BlockSpec(memory_space=pl.ANY)
    sem = pltpu.SemaphoreType.DMA
    late = (-(-(2 * (D // HW) + 3) // 8) * 8, HW)
    out = [
        jax.ShapeDtypeStruct((S, B, D), bf16),
        jax.ShapeDtypeStruct((S, B, D), bf16),
        jax.ShapeDtypeStruct((rows, D), f32),
        jax.ShapeDtypeStruct(late, f32),
    ]
    if gather:
        out += [jax.ShapeDtypeStruct((3, R, HW), bf16)] + [jax.ShapeDtypeStruct((R, w), bf16) for w in (HW, FW, FW)]
    else:
        out += [jax.ShapeDtypeStruct((n, R, HW), bf16)] * 3
    scratch = [
        pltpu.VMEM((S, B, HW), bf16),
        pltpu.VMEM((S, NB, 2 * HW), bf16),
        pltpu.VMEM((S, B, 128), f32),
        pltpu.VMEM((S, B, HW), bf16),
        pltpu.VMEM((S, 3 * B, 2 * HW), bf16),
        pltpu.VMEM((3, D, HW), bf16),
        pltpu.VMEM((S, B, D), f32),
        pltpu.VMEM((S, B, D), f32),
        pltpu.VMEM((2 * HW, 3 * B), f32),
        pltpu.VMEM((S, 2 * HW, B), f32),
        pltpu.VMEM((S, 2 * HW, NB), f32),
        pltpu.VMEM((S, B, 3 * HW), bf16),
        *[pltpu.VMEM((S, 2 * HW, B), bf16)] * 4,
        pltpu.VMEM((S, HW, NB), f32),
        pltpu.VMEM((S, 2 * HW, NB), bf16),
        pltpu.VMEM((S, 2 * HW, NB), bf16),
        pltpu.VMEM((D, S * B), bf16),
        *[pltpu.VMEM((S, B, D), bf16)] * 3,
        pltpu.VMEM((S, B, 3 * B), f32),
        pltpu.VMEM((rows, D), f32),
        sem((6 * S + 9,)),
        *[sem((S,))] * 4,
        *[sem((S, 2))] * 2,
        *[sem((S,))] * 8,
        *[sem((S, 2))] * 2,
    ]
    if gather:
        scratch += [
            pltpu.VMEM((n, Q, FW), bf16),
            pltpu.VMEM((n, 2 * Q, FW), bf16),
            *[pltpu.VMEM((n, R, HW), bf16)] * 4,
            *[pltpu.VMEM((n, 2 * Q, HW), bf16)] * 8,
            *[pltpu.VMEM((2 * Q, HW), bf16)] * 2,
            pltpu.VMEM((n, Q, HW), bf16),
            pltpu.VMEM((2 * Q, HW), bf16),
            pltpu.VMEM((n, Q, FW), bf16),
            *[pltpu.VMEM((2 * Q, HW), bf16)] * 2,
            pltpu.VMEM((n, Q, HW), bf16),
            pltpu.VMEM((2 * Q, HW), bf16),
            pltpu.VMEM((n, Q, FW), bf16),
            *[pltpu.VMEM((n - 1, 2 * Q, HW), bf16)] * 2,
            pltpu.VMEM((n - 1, Q, HW), bf16),
            pltpu.VMEM((n - 1, 2 * Q, HW), bf16),
            *[pltpu.VMEM((n - 1, Q, FW), bf16)] * 2,
            *[pltpu.VMEM((4, rows, D), f32)] * 2,
            *[pltpu.VMEM((4, *late), f32)] * 2,
            *[sem((6, 2))] * 2,
            *[sem((6, n - 1))] * 2,
            *[sem((6, 3))] * 2,
            *[sem((4, 3))] * 2,
        ]
    args = [bias, places, q, kv, mem, lse, gmixed, turned, wq, hid, gres, residual, mlp_part, pbias, gain, cw, sw, fit, sums,
            fsum, *owned]
    far = (0, 2, 3, 4, 5, 6, 20, 21, 22, 7, 8, 9, 10, 11, 12)
    return pl.pallas_call(
        lambda *refs: backward_kernel(gather, refs),
        out_shape=out,
        in_specs=[hb if i in far else vm for i in range(len(args))],
        out_specs=[vm] * len(out),
        scratch_shapes=scratch,
        compiler_params=pltpu.CompilerParams(
            collective_id=2, has_side_effects=True, vmem_limit_bytes=VMEM_LIMIT
        ),
        cost_estimate=pl.CostEstimate(flops=12_000_000_000, bytes_accessed=40_000_000, transcendentals=6_000_000),
        name="backward_part",
    )(*args)


def finish_kernel(fqkv, fo, ff, fp, early, late, block_in, grad_in, qkv, out, fc, proj, block, grad, qb, cgrad, sgrad, *vectors):
    HW = fqkv.shape[2]
    D = vectors[0].shape[0]
    H, NB = cgrad.shape
    per = D // HW
    for k in range(3):
        qb[k : k + 1] = late[2 * per + k : 2 * per + k + 1]
    qkv[...] = fqkv[...].astype(f32)
    out[...] = fo[...].astype(f32)
    fc[...] = ff[...].astype(f32)
    proj[...] = fp[...].astype(f32)
    block[...] = block_in[...]
    grad[...] = grad_in[...]
    cgrad[...] = early[8 : 8 + H, 0:NB]
    sgrad[...] = early[8 : 8 + H, NB : 2 * NB]
    for which in range(2):
        for k in range(per):
            vectors[which][k * HW : (k + 1) * HW] = late[which * per + k : which * per + k + 1].reshape(HW)
    for k in range(4):
        vectors[2 + k][...] = early[k : k + 1, 0:D].reshape(D)
    for k in range(vectors[6].shape[0] // D):
        vectors[6][k * D : (k + 1) * D] = early[4 + k : 5 + k].reshape(D)


def finish(parts, early, late, block_out, input_grad, D, H, NB):
    _, R, HW = parts[0].shape
    FW = parts[2].shape[1]
    vm = pl.BlockSpec(memory_space=pltpu.VMEM)
    shapes = [(3, R, HW), (R, HW), (R, FW), (R, FW)]
    more = [(3, HW), (H, NB), (H, NB)] + [(D,)] * 6 + [(FW,)]
    copied = [jax.ShapeDtypeStruct(v.shape, v.dtype) for v in (block_out, input_grad)]
    return pl.pallas_call(
        finish_kernel,
        out_shape=[jax.ShapeDtypeStruct(v, f32) for v in shapes] + copied + [jax.ShapeDtypeStruct(v, f32) for v in more],
        in_specs=[vm] * 8,
        out_specs=[vm] * (len(shapes) + 2 + len(more)),
        compiler_params=pltpu.CompilerParams(vmem_limit_bytes=VMEM_LIMIT),
        name="finish_part",
    )(*parts, early, late, block_out, input_grad)


def per_device(hidden_in, doc_lengths, sticky_places, attn_gain, attn_shift, qkv_weight, qkv_bias, center_weight,
               spread_weight, out_weight, out_bias, mlp_gain, mlp_shift, fc_weight, fc_bias, proj_weight, proj_bias,
               cotangent):
    S, B, D = hidden_in.shape
    n = lax.axis_size("dp")
    HW = qkv_bias.shape[1]
    H, NB = center_weight.shape
    M = sticky_places.shape[1]
    fit = jnp.asarray(ridge_fit(NB, 2 * M))
    gather = n == 4 and D % (64 * n) == 0
    weights = [jnp.transpose(qkv_weight, (1, 0, 2)), out_weight.T, fc_weight, proj_weight.T]
    if not gather:
        full = [lax.all_gather(w, "dp", axis=w.ndim - 2, tiled=True) for w in weights]
        weights = full[:1]
    made = forward(gather, hidden_in, doc_lengths, sticky_places, attn_gain, attn_shift, weights,
                   qkv_bias, center_weight, spread_weight, fit, cotangent)
    turned, cot_turned, bias, q, kv, mem, lse, mixed = made[:8]
    if gather:
        wq, wo, wf, wp = made[8:]
    else:
        wq, wo, wf, wp = full
        wo = lax.all_gather(wo, "tp", axis=0)
    made = mlp(gather, hidden_in, mixed, wo, wf, wp, out_bias, mlp_gain, mlp_shift, fc_bias, cotangent, cot_turned)
    residual, mlp_part, gres, gmixed, og, pg, fg, sums, fsum = made
    owned = [pg, fg, og] if gather else []
    made = backward(gather, bias, sticky_places, q, kv, mem, lse, gmixed, turned, wq, hidden_in, gres, residual, mlp_part,
                    proj_bias, attn_gain, center_weight, spread_weight, fit, sums, fsum, owned)
    block_out, input_grad, early, late = made[:4]
    if gather:
        made = finish(made[4:], early, late, block_out, input_grad, D, H, NB)
        qkv_grad, out_grad, fc_grad, proj_grad, block_out, input_grad, qkv_bias_grad, center_grad, spread_grad = made[:9]
        gain_grad, shift_grad, out_bias_grad, mlp_gain_grad, mlp_shift_grad, proj_bias_grad, fc_bias_grad = made[9:]
        qkv_grad, out_grad, proj_grad = jnp.transpose(qkv_grad, (1, 0, 2)), out_grad.T, proj_grad.T
    else:
        early, late = lax.psum((early, late), ("dp", "ctx"))

        def reduced(grad):
            part = lax.psum_scatter(grad.reshape(D, -1), "dp", scatter_dimension=0, tiled=True)
            return lax.psum(part, "ctx").astype(f32)

        qkv_grad = jnp.stack([reduced(g) for g in made[4:]], axis=1)
        out_grad, fc_grad, proj_grad = reduced(og).T, reduced(fg), reduced(pg).T
        per = D // HW
        qkv_bias_grad = late[2 * per : 2 * per + 3]
        center_grad, spread_grad = early[8 : 8 + H, :NB], early[8 : 8 + H, NB : 2 * NB]
        gain_grad, shift_grad = late[:per].reshape(-1), late[per : 2 * per].reshape(-1)
        out_bias_grad, mlp_gain_grad, mlp_shift_grad, proj_bias_grad = [early[k, :D] for k in range(4)]
        fc_bias_grad = early[4 : 4 + fc_bias.shape[0] // D].reshape(-1)
    return (
        block_out,
        input_grad,
        gain_grad,
        shift_grad,
        qkv_grad,
        qkv_bias_grad,
        center_grad,
        spread_grad,
        out_grad,
        out_bias_grad,
        mlp_gain_grad,
        mlp_shift_grad,
        fc_grad,
        fc_bias_grad,
        proj_grad,
        proj_bias_grad,
    )


def solution(mesh):
    in_specs = (
        P("dp", "ctx", None),
        P("dp", None),
        P("dp", None),
        P(),
        P(),
        P("dp", None, "tp"),
        P(None, "tp"),
        P("tp", None),
        P("tp", None),
        P("tp", "dp"),
        P(),
        P(),
        P(),
        P("dp", "tp"),
        P("tp"),
        P("tp", "dp"),
        P(),
        P("dp", "ctx", None),
    )
    out_specs = (
        P("dp", "ctx", None),
        P("dp", "ctx", None),
        P(),
        P(),
        P("dp", None, "tp"),
        P(None, "tp"),
        P("tp", None),
        P("tp", None),
        P("tp", "dp"),
        P(),
        P(),
        P(),
        P("dp", "tp"),
        P("tp"),
        P("tp", "dp"),
        P(),
    )
    return jax.shard_map(
        per_device, mesh=mesh, in_specs=in_specs, out_specs=out_specs, check_vma=False
    )
```

```python
import functools

import jax
import jax.numpy as jnp
import numpy as np
from jax import lax
from jax.experimental import pallas as pl
from jax.experimental.pallas import tpu as pltpu
from jax.sharding import PartitionSpec as P

DH = 64
WINDOW = 512
EPS = 1e-05
SPREAD = 0.02
SCALE = DH ** (-0.5)
VMEM_LIMIT = 60 * 1024 * 1024

bf16 = jnp.bfloat16
f32 = jnp.float32
MESH = pl.DeviceIdType.MESH


def dot_nn(a, b):
    return lax.dot_general(a, b, (((1,), (0,)), ((), ())), preferred_element_type=f32)


def dot_nt(a, b):
    return lax.dot_general(a, b, (((1,), (1,)), ((), ())), preferred_element_type=f32)


def dot_tn(a, b):
    return lax.dot_general(a, b, (((0,), (0,)), ((), ())), preferred_element_type=f32)


def ridge_fit(basis_count, sample_count):
    centers = (np.arange(basis_count) + 0.5) / basis_count
    times = (np.arange(sample_count) + 0.5) / sample_count
    width = 1.0 / basis_count
    design = np.exp(-np.square(times[None, :] - centers[:, None]) / (2.0 * width * width))
    gram = design @ design.T + 0.5 * np.eye(basis_count)
    return np.linalg.solve(gram, design).astype(bf16)


def place():
    c = lax.axis_index("ctx")
    side = c + 1 - 2 * lax.rem(c, 2)
    across = lax.rem(c + 2, 4)
    corner = lax.rem(side + 2, 4)
    return lax.axis_index("dp"), c, lax.axis_index("tp"), side, across, corner


def knock(devices):
    barrier = pltpu.get_barrier_semaphore()
    for device in devices:
        pl.semaphore_signal(barrier, inc=1, device_id=device, device_id_type=MESH)
    return lambda: pl.semaphore_wait(barrier, len(devices))


def remote(src, dst, send, recv, device):
    return pltpu.make_async_remote_copy(
        src_ref=src,
        dst_ref=dst,
        send_sem=send,
        recv_sem=recv,
        device_id=device,
        device_id_type=MESH,
    )


def normalise(x, gain, shift):
    mean = jnp.mean(x, axis=-1, keepdims=True)
    centred = x - mean
    r = lax.rsqrt(jnp.mean(centred * centred, axis=-1, keepdims=True) + EPS)
    n = centred * r
    return n * gain + shift, n, r


def lowest_key(lengths, s, pos):
    low = jnp.maximum(pos - (WINDOW - 1), 0)
    end = jnp.int32(0)
    for e in range(lengths.shape[1]):
        end = end + lengths[s, e]
        low = jnp.maximum(low, jnp.where(pos >= end, end, 0))
    return low


def row_of(vector):
    return vector[...].reshape(1, vector.shape[0])


def lanes(shape, dim):
    return lax.broadcasted_iota(jnp.int32, shape, dim)


def half_lanes(scale):
    lane = lanes((1, 2 * DH), 1)
    return [
        jnp.where(lane < DH, scale, 0.0).astype(bf16),
        jnp.where(lane >= DH, scale, 0.0).astype(bf16),
    ]


def mask_bias(lengths, s, c, rows, key_start, keys):
    pos = c * rows + lanes((rows, 1), 0)
    low = lowest_key(lengths, s, pos)
    key_pos = key_start + lanes((1, keys), 1)
    return jnp.where((key_pos <= pos) & (key_pos >= low), 0.0, -1e30)


def fit_at(fit, places, s, tokens, length):
    M = places.shape[1]
    sticky = jnp.where(tokens == places[s : s + 1, :], 1.0, 0.0).astype(bf16)
    even = lanes((1, M), 1) * length // M + length // (2 * M)
    steady = jnp.where(tokens == even, 1.0, 0.0).astype(bf16)
    value = dot_nt(fit[:, :M], sticky) + dot_nt(fit[:, M:], steady)
    high = value.astype(bf16)
    return high, (value - high.astype(f32)).astype(bf16)


def reach_terms(scores, center_row, spread_row, centers, width):
    center_logit = jnp.sum(scores * center_row, axis=-1, keepdims=True)
    spread_logit = jnp.sum(scores * spread_row, axis=-1, keepdims=True)
    mu = 1.0 / (1.0 + jnp.exp(-center_logit))
    grown = jnp.exp(spread_logit)
    var = SPREAD * jnp.log(1.0 + grown) + width * width
    inv = 1.0 / var
    diff = mu - centers
    reach = (width * lax.rsqrt(var)) * jnp.exp(-(diff * diff) * (0.5 * inv))
    return reach, mu, inv, diff, spread_logit


def forward_kernel(gather, refs):
    n = lax.axis_size("dp")
    if gather:
        (hid_far, lengths, places, gain, shift, wq_sh, wo_sh, wf_sh, wp_sh, qbias, cw, sw, fit, cot_far,
         turned_out, cot_out, bias_out, q_out, kv_out, mem_out, lse_out, mixed, wq_out, wo, wf, wp,
         normed, q, kv, hoth, noth, bias, fits, mem, lse, hid, turned, cot, cot_turned, cs, os_, hys, hyr, hxs, hxr, ks, kr, ms, mr,
         wq, wo_own, wf_own, wp_own, lsem, zs, zr, ys, yr, as_, ar, bs, br, oxs, oxr, lzs, lzr, lys, lyr, las, lar, lbs, lbr) = refs
    else:
        (hid_far, lengths, places, gain, shift, wq, qbias, cw, sw, fit, cot_far,
         turned_out, cot_out, bias_out, q_out, kv_out, mem_out, lse_out, mixed,
         normed, q, kv, hoth, noth, bias, fits, mem, lse, hid, turned, cot, cot_turned, cs, os_, hys, hyr, hxs, hxr, ks, kr, ms, mr) = refs
    z, c, t, side, across, corner = place()
    S, B, D = hid_far.shape
    HW = q.shape[2]
    NB = mem.shape[1]
    L = kv.shape[1]
    half = B // 2
    peers = [{"ctx": side}, {"ctx": across}, {"tp": 1 - t}]
    if gather:
        R = D // n
        Q = R // 4
        shards = [wq_sh, wo_sh, wf_sh, wp_sh]
        whole = [wq, wo.at[t], wf, wp, wo.at[1 - t]]
        peers += [{"dp": lax.rem(z + i, n)} for i in range(1, n)]
    wait_for_all = knock(peers)
    hid_copy = pltpu.make_async_copy(hid_far, hid, cs.at[0])
    hid_copy.start()
    cot_copy = pltpu.make_async_copy(cot_far, cot, cs.at[1])
    if gather:
        own_in = [
            pltpu.make_async_copy(far, near, lsem.at[4 + i]) for i, (far, near) in enumerate(((wo_sh, wo_own), (wf_sh, wf_own), (wp_sh, wp_own)))
        ]
    wait_for_all()

    started, kept = [], []

    def start(copies):
        for copy in copies:
            copy.start()
        started.extend(copies)
        return copies

    def keep(src, dst):
        copy = pltpu.make_async_copy(src, dst, os_.at[len(kept)])
        copy.start()
        kept.append(copy)

    if gather:
        groups = range(1, 5)

        def rows(g, owner, quarter):
            part = pl.ds(pl.multiple_of(R * owner + Q * quarter, 16), Q)
            return wq.at[:, part] if g == 0 else whole[g].at[part]

        def source(i):
            return lax.rem(z + n - i, n)

        def part_rows(part, owner, quarter):
            rows_here = pl.ds(pl.multiple_of(R * owner + Q * quarter, 16), Q)
            return wq.at[1:3, rows_here] if part == 0 else wq.at[0:1, rows_here]

        def first_z(part):
            mine_here = pl.ds(pl.multiple_of(Q * c, 16), Q)
            src = wq_sh.at[1:3, mine_here] if part == 0 else wq_sh.at[0:1, mine_here]
            return start([
                remote(src, part_rows(part, z, c), zs.at[part, i - 1], zr.at[part, i - 1], {"dp": lax.rem(z + i, n)})
                for i in range(1, n)
            ])

        def first_y(part, sent):
            over, beside = [], []
            for i, copy in enumerate(sent):
                copy.wait_recv()
                w = part_rows(part, source(i + 1), c)
                over += start([remote(w, w, ys.at[part, i], yr.at[part, i], {"ctx": across})])
                beside += start([remote(w, w, as_.at[part, i], ar.at[part, i], {"ctx": side})])
            return over, beside

        def first_side(part, over):
            last = []
            for i, copy in enumerate(over):
                copy.wait_recv()
                w = part_rows(part, source(i + 1), across)
                last += start([remote(w, w, bs.at[part, i], br.at[part, i], {"ctx": side})])
            return last

        def sends(way, r):
            return ((z < n - 1) & (z >= r)) if way == 0 else ((z > 0) & (z + r < n))

        def takes(way, r):
            return (z > r) if way == 0 else (z + r < n - 1)

        def line_z(g, way, r):
            owner = z - r if way == 0 else z + r
            to = z + 1 if way == 0 else z - 1
            dst = rows(g, owner, c)
            src = shards[g].at[pl.ds(pl.multiple_of(Q * c, 16), Q)] if r == 0 and g < 4 else dst
            return remote(src, dst, lzs.at[g - 1, way, r], lzr.at[g - 1, way, r], {"dp": to})

        def line_copy(g, way, r, sems, quarter, device):
            part = rows(g, z - 1 - r if way == 0 else z + 1 + r, quarter)
            return remote(part, part, sems[0].at[g - 1, way, r], sems[1].at[g - 1, way, r], {"ctx": device})

        def line_y(g, way, r):
            return line_copy(g, way, r, (lys, lyr), c, across)

        def line_a(g, way, r):
            return line_copy(g, way, r, (las, lar), c, side)

        def line_b(g, way, r):
            return line_copy(g, way, r, (lbs, lbr), across, side)

        def line_send(r, some=groups):
            for way in range(2):

                @pl.when(sends(way, r))
                def _(way=way):
                    for g in some:
                        line_z(g, way, r).start()

        def line_take(r):
            for way in range(2):

                @pl.when(takes(way, r))
                def _(way=way):
                    for g in groups:
                        line_z(g, way, r).wait_recv()
                        line_y(g, way, r).start()
                        line_a(g, way, r).start()

        def line_pass(r):
            for way in range(2):

                @pl.when(takes(way, r))
                def _(way=way):
                    for g in groups:
                        line_y(g, way, r).wait_recv()
                        line_b(g, way, r).start()

        def line_end(r):
            for way in range(2):

                @pl.when(takes(way, r))
                def _(way=way):
                    for g in groups:
                        line_a(g, way, r).wait_recv()
                        line_b(g, way, r).wait_recv()
                        line_y(g, way, r).wait_send()
                        line_a(g, way, r).wait_send()
                        line_b(g, way, r).wait_send()

                @pl.when(sends(way, r))
                def _(way=way):
                    for g in groups:
                        line_z(g, way, r).wait_send()
    else:

        def line_send(r):
            pass

        line_take = line_pass = line_end = line_send

    def hidden_y(s):
        piece = pl.ds(pl.multiple_of(half * t, 16), half)
        return remote(hid_far.at[s, piece], hoth.at[s, piece], hys.at[s], hyr.at[s], {"ctx": across})

    def hidden_x(s):
        piece = pl.ds(pl.multiple_of(half * t, 16), half)
        return remote(hoth.at[s, piece], hoth.at[s, piece], hxs.at[s], hxr.at[s], {"tp": 1 - t})

    def block(s, owner):
        return kv.at[s, pl.ds(pl.multiple_of(owner * B, B), B)]

    def kv_copy(s, which):
        owner = c if which == 0 else across
        return remote(block(s, owner), block(s, owner), ks.at[s, which], kr.at[s, which], {"ctx": side})

    if gather:
        z_sent = [first_z(0)]
    hy = start([hidden_y(s) for s in range(S)])
    if gather:
        z_sent.append(first_z(1))
        mine = pl.ds(pl.multiple_of(R * z, 16), R)
        owned = [
            pltpu.make_async_copy(near, wq.at[:, mine] if g == 0 else whole[g].at[mine], lsem.at[g])
            for g, near in enumerate((wq_sh, wo_own, wf_own, wp_own))
        ]
        for copy in (owned[0], *own_in):
            copy.start()
        crossed = start([remote(wo_sh, wo.at[t, mine], oxs, oxr, {"tp": 1 - t})])[0]
        line_send(0, (1, 2, 3))

    gain_row = row_of(gain)
    shift_row = row_of(shift)
    key_start = pl.multiple_of(jnp.maximum(c - 2, 0) * B, B)
    keys = 3 * B
    cot_copy.start()
    hid_copy.wait()
    for s in range(S):
        low, _, _ = normalise(hid[s].astype(f32), gain_row, shift_row)
        normed[s] = low.astype(bf16)
    turned[...] = normed[...].reshape(S * B, D).T
    keep(turned, turned_out)
    if gather:
        for k in range(3):
            own_in[k].wait()
            owned[1 + k].start()
    hx = []

    def forward_hidden(s):
        hy[s].wait_recv()
        hx.extend(start([hidden_x(s)]))

    for s in range(S):
        if s < S - 1:
            forward_hidden(s)
        high, rest = fit_at(fit, places, s, lanes((L, 1), 0), L)
        fits[0, s] = high
        fits[1, s] = rest
    if gather:
        over, beside = first_y(0, z_sent[0])
        crossed.wait_recv()
        line_send(0, (4,))
    forward_hidden(S - 1)
    cot_copy.wait()
    cot_turned[...] = cot[...].reshape(S * B, D).T
    keep(cot_turned, cot_out)
    if gather:
        over_q, beside_q = first_y(1, z_sent[1])
    for s in range(S):
        bias[s] = mask_bias(lengths, s, c, B, key_start, keys)
    keep(bias, bias_out)
    line_take(0)
    line_send(1)
    if gather:
        last = first_side(0, over)
    for s in range(S):
        hx[s].wait_recv()
        low, _, _ = normalise(hoth[s].astype(f32), gain_row, shift_row)
        noth[s] = low.astype(bf16)
    if gather:
        last_q = first_side(1, over_q)
        for copy in beside + last:
            copy.wait_recv()
        owned[0].wait()
    kvs = []
    for s in range(S):
        for which, rows_in, owner in ((0, normed, c), (1, noth, across)):
            for k in (1, 2):
                part = dot_nn(rows_in[s], wq[k]) + qbias[k : k + 1]
                kv[s, pl.ds(pl.multiple_of(owner * B, B), B), (k - 1) * HW : k * HW] = part.astype(bf16)
            kvs += start([kv_copy(s, which)])
    if gather:
        for copy in beside_q + last_q:
            copy.wait_recv()
        keep(wq, wq_out)
    for s in range(S):
        q[s] = (dot_nn(normed[s], wq[0]) + qbias[0:1]).astype(bf16)
    keep(q, q_out)
    line_take(1)
    line_send(2)

    centers = (lanes((1, NB), 1).astype(f32) + 0.5) * (1.0 / NB)
    width = 1.0 / NB
    lane = lanes((1, 2 * DH), 1)
    scaled = half_lanes(SCALE)
    mx = []
    for s in range(S):
        kvs[2 * s].wait_recv()
        kvs[2 * s + 1].wait_recv()
        keep(kv.at[s], kv_out.at[s])
        mem[s] = (dot_nn(fits[0, s], kv[s]) + dot_nn(fits[1, s], kv[s])).astype(bf16)
        keep(mem.at[s], mem_out.at[s])

        def mixed_copy(s, p, cols):
            part = mixed.at[t, s, :, cols]
            return remote(part, part, ms.at[s, p], mr.at[s, p], {"tp": 1 - t})

        def pair_step(p, log_rows, s=s):
            cols = pl.ds(pl.multiple_of(p * 2 * DH, 2 * DH), 2 * DH)
            vcols = pl.ds(pl.multiple_of(HW + p * 2 * DH, 2 * DH), 2 * DH)
            window = pl.ds(key_start, keys)
            qp = q[s, :, cols]
            kp = kv[s, window, cols]
            vp = kv[s, window, vcols]
            mk = mem[s, :, cols]
            mv = mem[s, :, vcols]
            outs = []
            for h in range(2):
                qh = qp * scaled[h]
                scores = dot_nt(qh, kp) + bias[s]
                top = jnp.max(scores, axis=-1, keepdims=True)
                e = jnp.exp(scores - top)
                total = jnp.sum(e, axis=-1, keepdims=True)
                share = (e * (1.0 / total)).astype(bf16)
                out = dot_nn(share, vp)
                log_rows = jnp.where(lane == 2 * p + h, top + jnp.log(total), log_rows)
                mem_scores = dot_nt(qh, mk)
                reach, _, _, _, _ = reach_terms(
                    mem_scores, cw[pl.ds(2 * p + h, 1)], sw[pl.ds(2 * p + h, 1)], centers, width
                )
                outs.append(out + dot_nn(reach.astype(bf16), mv))
            mixed[t, s, :, cols] = jnp.where(lane < DH, outs[0], outs[1]).astype(bf16)
            mixed_copy(s, p, cols).start()
            return log_rows

        lse[s] = lax.fori_loop(0, HW // (2 * DH), pair_step, jnp.zeros((B, 2 * DH), f32))
        keep(lse.at[s], lse_out.at[s])
        mx += [mixed_copy(s, p, pl.ds(p * 2 * DH, 2 * DH)) for p in range(HW // (2 * DH))]
        if s == 0:
            line_pass(0)
            line_take(2)
    line_pass(1)
    line_pass(2)
    for r in range(n - 1 if gather else 0):
        line_end(r)
    if gather:
        for copy in owned[1:]:
            copy.wait()
    for copy in mx:
        copy.wait_recv()
    for copy in started + mx:
        copy.wait_send()
    for copy in kept:
        copy.wait()


def forward(gather, hid, lengths, places, gain, shift, weights, qbias, cw, sw, fit, cot):
    S, B, D = hid.shape
    HW = qbias.shape[1]
    n = lax.axis_size("dp")
    L = B * lax.axis_size("ctx")
    NB = cw.shape[1]
    vm = pl.BlockSpec(memory_space=pltpu.VMEM)
    sm = pl.BlockSpec(memory_space=pltpu.SMEM)
    hb = pl.BlockSpec(memory_space=pl.ANY)
    out = [
        jax.ShapeDtypeStruct((D, S * B), bf16),
        jax.ShapeDtypeStruct((D, S * B), bf16),
        jax.ShapeDtypeStruct((S, B, 3 * B), f32),
        jax.ShapeDtypeStruct((S, B, HW), bf16),
        jax.ShapeDtypeStruct((S, L, 2 * HW), bf16),
        jax.ShapeDtypeStruct((S, NB, 2 * HW), bf16),
        jax.ShapeDtypeStruct((S, B, 128), f32),
        jax.ShapeDtypeStruct((2, S, B, HW), bf16),
    ]
    out_specs = [hb] * 7 + [vm]
    sem = pltpu.SemaphoreType.DMA
    scratch = [
        pltpu.VMEM((S, B, D), bf16),
        pltpu.VMEM((S, B, HW), bf16),
        pltpu.VMEM((S, L, 2 * HW), bf16),
        pltpu.VMEM((S, B, D), bf16),
        pltpu.VMEM((S, B, D), bf16),
        pltpu.VMEM((S, B, 3 * B), f32),
        pltpu.VMEM((2, S, NB, L), bf16),
        pltpu.VMEM((S, NB, 2 * HW), bf16),
        pltpu.VMEM((S, B, 128), f32),
        pltpu.VMEM((S, B, D), bf16),
        pltpu.VMEM((D, S * B), bf16),
        pltpu.VMEM((S, B, D), bf16),
        pltpu.VMEM((D, S * B), bf16),
        sem((2,)),
        sem((3 * S + 5,)),
        *[sem((S,))] * 4,
        *[sem((S, 2))] * 2,
        *[sem((S, HW // (2 * DH)))] * 2,
    ]
    w_specs = [vm]
    if gather:
        FW = weights[2].shape[1]
        out += [
            jax.ShapeDtypeStruct((3, D, HW), bf16),
            jax.ShapeDtypeStruct((2, D, HW), bf16),
            jax.ShapeDtypeStruct((D, FW), bf16),
            jax.ShapeDtypeStruct((D, FW), bf16),
        ]
        out_specs += [hb] * 4
        w_specs = [hb] * 4
        scratch += [
            pltpu.VMEM((3, D, HW), bf16),
            *[pltpu.VMEM((D // n, w), bf16) for w in (HW, FW, FW)],
            sem((7,)),
            *[sem((2, n - 1))] * 8,
            sem,
            sem,
            *[sem((4, 2, n - 1))] * 8,
        ]
    return pl.pallas_call(
        lambda *refs: forward_kernel(gather, refs),
        out_shape=out,
        in_specs=[hb, sm, vm, vm, vm, *w_specs, vm, vm, vm, vm, hb],
        out_specs=out_specs,
        scratch_shapes=scratch,
        compiler_params=pltpu.CompilerParams(
            collective_id=0, has_side_effects=True, vmem_limit_bytes=VMEM_LIMIT
        ),
        cost_estimate=pl.CostEstimate(flops=6_000_000_000, bytes_accessed=30_000_000, transcendentals=6_000_000),
        name="forward_part",
    )(hid, lengths, places, gain, shift, *weights, qbias, cw, sw, fit, cot)


def quarter(c):
    return 2 * lax.rem(c, 2) + c // 2


class Reduction:
    def __init__(self, n, rows, full, half, half_in, own, own_in, sems):
        self.n, self.rows, self.piece = n, rows, rows // 4
        self.full, self.half, self.half_in, self.own, self.own_in = full, half, half_in, own, own_in
        self.sems = sems
        self.z, self.c, self.t, self.side, self.across, self.corner = place()
        self.started = []

    def at(self, offset, size):
        return pl.ds(pl.multiple_of(offset, 16), size)

    def send_side(self):
        two = 2 * self.piece
        core = lax.rem(self.c, 2)
        self.one = remote(
            self.full.at[:, self.at(two * (1 - core), two)], self.half_in, self.sems[0].at[0], self.sems[1].at[0], {"ctx": self.side}
        )
        self.one.start()
        self.started.append(self.one)

    def sum_side(self):
        two = 2 * self.piece
        core = lax.rem(self.c, 2)
        self.one.wait_recv()
        for k in range(self.n):
            self.half[k] = (
                self.full[k, self.at(two * core, two)].astype(f32) + self.half_in[k].astype(f32)
            ).astype(bf16)

    def send_across(self):
        piece, y = self.piece, self.c // 2
        self.two = remote(
            self.half.at[:, self.at(piece * (1 - y), piece)], self.own_in, self.sems[0].at[1], self.sems[1].at[1], {"ctx": self.across}
        )
        self.two.start()
        self.started.append(self.two)

    def take_across(self):
        y = self.c // 2
        self.two.wait_recv()
        for k in range(self.n):
            self.own[k] = (
                self.half[k, self.at(self.piece * y, self.piece)].astype(f32) + self.own_in[k].astype(f32)
            ).astype(bf16)

    def wait_sends(self):
        for copy in self.started:
            copy.wait_send()


def mlp_kernel(gather, refs):
    (hid_far, mixed_far, wo_far, wf_far, wp_far, obias, gain, shift, fbias, cot_far, cot_turned_far,
     residual_out, mlp_out, gres_out, gmixed, og, pg, fg, sums, fsum,
     hid, mixed, wo, residual, mlp_part, gres, wf, wp, cot, low, act, gpre, gpart, gin, turned, glow, frow, cot_turned, ls, outs, gs, gr, *rest) = refs
    if gather:
        pfull, phalf, phalf_in, pown_in, ffull, fhalf_in, ps, pr, fs, fr = rest
    else:
        pfull, ffull = pg, fg
    z, c, t, side, across, corner = place()
    S, B, D = hid_far.shape
    FW = wf.shape[1]
    HW = mixed.shape[3]
    n, R = pfull.shape[:2]
    tile = 512
    pairs = [
        (wo_far, wo), (mixed_far.at[:, 0], mixed.at[:, 0]), (hid_far.at[0], hid.at[0]), (wf_far, wf), (wp_far, wp), (cot_far, cot),
        (mixed_far.at[:, 1:S], mixed.at[:, 1:S]), (hid_far.at[1:S], hid.at[1:S]), (cot_turned_far, cot_turned)
    ]
    loads = [pltpu.make_async_copy(far, near, ls.at[i]) for i, (far, near) in enumerate(pairs)]
    for copy in loads[:8]:
        copy.start()
    kept = []

    def keep(src, dst):
        copy = pltpu.make_async_copy(src, dst, outs.at[len(kept)])
        copy.start()
        kept.append(copy)

    wait_for_all = knock([{"tp": 1 - t}] + ([{"ctx": side}, {"ctx": across}] if gather else []))
    obias_row, gain_row, shift_row = row_of(obias), row_of(gain), row_of(shift)
    frow[...] = row_of(fbias)
    fsum[...] = jnp.zeros_like(fsum)
    copies = []
    for copy in loads[:3]:
        copy.wait()
    for s in range(S):
        if s == 1:
            loads[6].wait()
            loads[7].wait()
        branch = dot_nt(mixed[0, s], wo[0]) + dot_nt(mixed[1, s], wo[1])
        wide = hid[s].astype(f32) + branch + obias_row
        residual[s] = wide
        value, _, _ = normalise(wide, gain_row, shift_row)
        low[s] = value.astype(bf16)
        keep(residual.at[s], residual_out.at[s])
        if s == 0:
            loads[3].wait()
            loads[8].start()

        def columns(j, carry, s=s):
            cols = pl.ds(pl.multiple_of(j * tile, tile), tile)
            pre = dot_nn(low[s], wf[:, cols]) + frow[:, cols]
            square = pre * pre
            th = jnp.tanh(0.7978845608028654 * (pre + 0.044715 * (square * pre)))
            act[s, :, cols] = (0.5 * pre * (1.0 + th)).astype(bf16)
            slope = 0.5 * (1.0 + th) + (0.5 * pre) * (1.0 - th * th) * (
                0.7978845608028654 * (1.0 + 3.0 * 0.044715 * square)
            )
            if s == 0 and j == 0:
                loads[4].wait()
                loads[5].wait()
            grad = (dot_nn(cot[s], wp[:, cols]) * slope).astype(bf16)
            gpre[s, :, cols] = grad
            fsum[:, cols] += jnp.sum(grad.astype(f32), axis=0, keepdims=True)
            return carry

        for j in range(FW // tile):
            columns(j, 0)
        gpart[s] = dot_nt(gpre[s], wf[...]).astype(bf16)
        if s == 0:
            wait_for_all()
        copies.append(remote(gpart.at[s], gin.at[s], gs.at[s], gr.at[s], {"tp": 1 - t}))
        copies[-1].start()

    def weight_grad(full, left, right, width, step):
        if left is None:
            loads[8].wait()
            across_left = cot_turned
        else:
            turned[...] = left.reshape(S * B, D).T
            across_left = turned

        def columns(j, carry):
            cols = pl.ds(pl.multiple_of(j * step, step), step)
            value = dot_nn(across_left[...], right[:, :, cols].reshape(S * B, step)).astype(bf16)
            for k in range(n):
                full[k, :, cols] = value[k * R : (k + 1) * R]
            return carry

        lax.fori_loop(0, width // step, columns, 0)

    weight_grad(pfull, None, act, FW, 512)
    if gather:
        proj = Reduction(n, R, pfull, phalf, phalf_in, pg, pown_in, (ps, pr))
        proj.send_side()
    weight_grad(ffull, low[...], gpre, FW, 512)
    if gather:
        fc = Reduction(n, R, ffull, fg, fhalf_in, None, None, (fs, fr))
        fc.send_side()
        proj.sum_side()
        proj.send_across()
    for s in range(S):
        mlp_part[s] = dot_nt(act[s], wp[...]).astype(bf16)
        keep(mlp_part.at[s], mlp_out.at[s])
    out_sum = jnp.zeros((1, D), f32)
    gain_sum = jnp.zeros((1, D), f32)
    shift_sum = jnp.zeros((1, D), f32)
    cot_sum = jnp.zeros((1, D), f32)
    out_grad = jnp.zeros((D, HW), f32)
    for s in range(S):
        copies[s].wait_recv()
        grad = gpart[s].astype(f32) + gin[s].astype(f32)
        _, unit, r = normalise(residual[s], gain_row, shift_row)
        gain_sum += jnp.sum(grad * unit, axis=0, keepdims=True)
        shift_sum += jnp.sum(grad, axis=0, keepdims=True)
        a = grad * gain_row
        wide_cot = cot[s].astype(f32)
        cot_sum += jnp.sum(wide_cot, axis=0, keepdims=True)
        total = wide_cot + r * (
            a - jnp.mean(a, axis=-1, keepdims=True) - unit * jnp.mean(a * unit, axis=-1, keepdims=True)
        )
        out_sum += jnp.sum(total, axis=0, keepdims=True)
        gres[s] = total
        keep(gres.at[s], gres_out.at[s])
        glow[s] = total.astype(bf16)
        gmixed[s] = dot_nn(glow[s], wo[t]).astype(bf16)
        out_grad += dot_tn(glow[s], mixed[t, s])
        if s == 0 and gather:
            fc.sum_side()
    sums[0:1] = out_sum
    sums[1:2] = gain_sum
    sums[2:3] = shift_sum
    sums[3:4] = cot_sum
    for k in range(n):
        og[k] = out_grad[k * R : (k + 1) * R].astype(bf16)
    if gather:
        proj.take_across()
        proj.wait_sends()
        fc.wait_sends()
    for copy in copies:
        copy.wait_send()
    for copy in kept:
        copy.wait()


def mlp(gather, hid, mixed, wo, wf, wp, obias, gain, shift, fbias, cot, cot_turned):
    S, B, D = hid.shape
    HW = mixed.shape[3]
    FW = wf.shape[1]
    n = lax.axis_size("dp") if gather else 1
    R = D // n
    Q = R // 4
    vm = pl.BlockSpec(memory_space=pltpu.VMEM)
    sem = pltpu.SemaphoreType.DMA
    hb = pl.BlockSpec(memory_space=pl.ANY)
    pshape = (n, Q, FW) if gather else (n, R, FW)
    fshape = (n, 2 * Q, FW) if gather else (n, R, FW)
    out = [
        jax.ShapeDtypeStruct((S, B, D), f32),
        jax.ShapeDtypeStruct((S, B, D), bf16),
        jax.ShapeDtypeStruct((S, B, D), f32),
        jax.ShapeDtypeStruct((S, B, HW), bf16),
        jax.ShapeDtypeStruct((n, R, HW), bf16),
        jax.ShapeDtypeStruct(pshape, bf16),
        jax.ShapeDtypeStruct(fshape, bf16),
        jax.ShapeDtypeStruct((4, D), f32),
        jax.ShapeDtypeStruct((1, FW), f32),
    ]
    scratch = [
        pltpu.VMEM((S, B, D), bf16),
        pltpu.VMEM((2, S, B, HW), bf16),
        pltpu.VMEM((2, D, HW), bf16),
        pltpu.VMEM((S, B, D), f32),
        pltpu.VMEM((S, B, D), bf16),
        pltpu.VMEM((S, B, D), f32),
        pltpu.VMEM((D, FW), bf16),
        pltpu.VMEM((D, FW), bf16),
        pltpu.VMEM((S, B, D), bf16),
        pltpu.VMEM((S, B, D), bf16),
        pltpu.VMEM((S, B, FW), bf16),
        pltpu.VMEM((S, B, FW), bf16),
        pltpu.VMEM((S, B, D), bf16),
        pltpu.VMEM((S, B, D), bf16),
        pltpu.VMEM((D, S * B), bf16),
        pltpu.VMEM((S, B, D), bf16),
        pltpu.VMEM((1, FW), f32),
        pltpu.VMEM((D, S * B), bf16),
        sem((9,)),
        sem((3 * S,)),
        sem((S,)),
        sem((S,)),
    ]
    if gather:
        scratch += [
            pltpu.VMEM((n, R, FW), bf16),
            *[pltpu.VMEM((n, R // 2, FW), bf16)] * 2,
            pltpu.VMEM((n, Q, FW), bf16),
            pltpu.VMEM((n, R, FW), bf16),
            pltpu.VMEM((n, R // 2, FW), bf16),
            *[sem((2,))] * 4,
        ]
    return pl.pallas_call(
        lambda *refs: mlp_kernel(gather, refs),
        out_shape=out,
        in_specs=[hb, hb, hb, hb, hb, vm, vm, vm, vm, hb, hb],
        out_specs=[hb, hb, hb, *[vm] * 6],
        scratch_shapes=scratch,
        compiler_params=pltpu.CompilerParams(
            collective_id=1, has_side_effects=True, vmem_limit_bytes=VMEM_LIMIT
        ),
        cost_estimate=pl.CostEstimate(flops=12_000_000_000, bytes_accessed=30_000_000, transcendentals=1_500_000),
        name="mlp_part",
    )(hid, mixed, wo, wf, wp, obias, gain, shift, fbias, cot, cot_turned)


def backward_kernel(gather, refs):
    (bias_far, places, q_far, kv_far, mem_far, lse_far, gmixed_far, turned_far, wq_far, hid_far, gres_far, residual_far, mlp_far, pbias, gain,
     cw, sw, fit, sums, fsum, *rest) = refs
    if gather:
        (pown_far, fhalf_far, ofull_far, block_out, input_grad, early_out, late_out, fqkv, fo, ff, fp, *rest) = rest
    else:
        (block_out, input_grad, early_out, late_out, afull, kfull, vfull, *rest) = rest
    (q, mem, lse, gmixed, kv, wq, gres, residual, dkv, own_rows, dmem, gqkv, hs1, hr1, hs2, hr2, m1in, gmem, gfar,
     turned, mlp_in, gnpart, gnin, bias, early, ls, xs, xr, h1s, h1r, h2s, h2r, m1s, m1r, m2s, m2r, m3s, m3r, m4s, m4r, ns, nr,
     *rest) = rest
    if gather:
        (pown, fhalf, ofull, afull, kfull, vfull, ahalf_in, khalf_in, vhalf_in, ohalf_in, ahalf, khalf, vhalf, ohalf,
         aown, kown, vown, oown, fown, aown_in, kown_in, vown_in, oown_in, fown_in,
         zina, zink, zinv, zino, zinf, zinp, early_ctx, early_dp, late_ctx, late_dp,
         rs, rr, zs, zr, gs, gr, es, er) = rest
    z, c, t, side, across, corner = place()
    S, B, D = hid_far.shape
    HW = q.shape[2]
    NB = mem.shape[1]
    n, R = afull.shape[:2]
    L = kv_far.shape[1]
    keys = 3 * B
    key_start = pl.multiple_of(jnp.maximum(c - 2, 0) * B, B)
    near_pairs = []
    for s in range(S):
        if s == 1 and gather:
            near_pairs += [(fhalf_far, fhalf), (pown_far, pown), (ofull_far, ofull)]
        near_pairs += [(far.at[s], near.at[s]) for far, near in ((q_far, q), (gmixed_far, gmixed), (lse_far, lse), (mem_far, mem))]
        near_pairs += [(kv_far.at[s, pl.ds(key_start, keys)], kv.at[s]), (bias_far.at[s], bias.at[s])]
    next_pairs = [(turned_far, turned), (wq_far, wq), (residual_far, residual), (gres_far, gres)]
    late_pairs = [(hid_far, kv.at[:, 0:B]), (mlp_far, kv.at[:, B : 2 * B])]
    copies = [pltpu.make_async_copy(far, near, ls.at[i]) for i, (far, near) in enumerate(near_pairs + next_pairs + late_pairs)]
    loads, next_loads, late_loads = copies[: len(near_pairs)], copies[len(near_pairs) : -2], copies[-2:]
    for copy in loads:
        copy.start()
    peers = [{"tp": 1 - t}, {"ctx": side}, {"ctx": across}]
    if gather:
        peers += [{"ctx": corner}] + [{"dp": lax.rem(z + i, n)} for i in range(1, n)]
    wait_for_all = knock(peers)
    started = []

    def start(copy):
        copy.start()
        started.append(copy)
        return copy

    if gather:
        Q = R // 4
        owns, zins = {"p": pown, "f": fown, "v": vown}, {"p": zinp, "f": zinf, "v": zinv}
        finals = {"p": fp, "f": ff, "v": fqkv.at[2]}
        index = {g: i for i, g in enumerate("akvofp")}
        z_sent, g_sent = {}, {}

        def send_dp(g):
            j = index[g]
            z_sent[g] = [
                start(remote(owns[g].at[lax.rem(z + i, n)], zins[g].at[i - 1], zs.at[j, i - 1], zr.at[j, i - 1], {"dp": lax.rem(z + i, n)}))
                for i in range(1, n)
            ]

        def piece(g, device):
            return finals[g].at[pl.ds(pl.multiple_of(Q * quarter(device), 16), Q)]

        def take_dp(g):
            j = index[g]
            total = owns[g][z].astype(f32)
            for i in range(1, n):
                z_sent[g][i - 1].wait_recv()
                total = total + zins[g][i - 1].astype(f32)
            finals[g][pl.ds(pl.multiple_of(Q * quarter(c), 16), Q)] = total.astype(bf16)
            mine = piece(g, c)
            g_sent[g] = [
                start(remote(mine, mine, gs.at[j, 0], gr.at[j, 0], {"ctx": across})),
                start(remote(mine, mine, gs.at[j, 1], gr.at[j, 1], {"ctx": side})),
            ]

        def pass_on(g):
            j = index[g]
            g_sent[g][0].wait_recv()
            other = piece(g, across)
            g_sent[g].append(start(remote(other, other, gs.at[j, 2], gr.at[j, 2], {"ctx": side})))

        def take_all(g):
            g_sent[g][1].wait_recv()
            g_sent[g][2].wait_recv()

        class Chain(Reduction):
            def __init__(self, g, full, half, half_in, own, own_in, dp_in, final):
                j = index[g]
                super().__init__(n, R, full, half, half_in, own, own_in, (rs.at[j], rr.at[j]))
                self.j, self.dp_in, self.final = j, dp_in, final

            def send_dp(self):
                self.over = [
                    remote(self.half.at[lax.rem(z + i, n)], self.dp_in.at[i - 1], zs.at[self.j, i - 1], zr.at[self.j, i - 1], {"dp": lax.rem(z + i, n)})
                    for i in range(1, n)
                ]
                for copy in self.over:
                    start(copy)

            def take_dp(self):
                total = self.half[z].astype(f32)
                for i in range(1, n):
                    self.over[i - 1].wait_recv()
                    total = total + self.dp_in[i - 1].astype(f32)
                self.own[...] = total.astype(bf16)
                self.two = start(remote(self.own, self.own_in, gs.at[self.j, 0], gr.at[self.j, 0], {"ctx": across}))

            def take_across(self):
                self.two.wait_recv()
                mine = pl.ds(pl.multiple_of(2 * self.piece * lax.rem(c, 2), 16), 2 * self.piece)
                self.final[mine] = (self.own[...].astype(f32) + self.own_in[...].astype(f32)).astype(bf16)
                part = self.final.at[mine]
                self.three = start(remote(part, part, gs.at[self.j, 1], gr.at[self.j, 1], {"ctx": side}))

            def take_all(self):
                self.three.wait_recv()

        red = {
            "a": Chain("a", afull, ahalf, ahalf_in, aown, aown_in, zina, fqkv.at[0]),
            "k": Chain("k", kfull, khalf, khalf_in, kown, kown_in, zink, fqkv.at[1]),
            "o": Chain("o", ofull, ohalf, ohalf_in, oown, oown_in, zino, fo),
        }
        vals = Reduction(n, R, vfull, vhalf, vhalf_in, vown, vown_in, (rs.at[2], rr.at[2]))
        fc = Reduction(n, R, None, fhalf, None, fown, fown_in, (rs.at[4], rr.at[4]))

        class Everywhere:
            def __init__(self, over_ctx, over_dp, which):
                self.over_ctx, self.over_dp, self.which = over_ctx, over_dp, which

            def send(self, slots, me, devices, step):
                j = 2 * self.which + step
                self.sent = [
                    start(remote(slots.at[me], slots.at[me], es.at[j, i], er.at[j, i], device)) for i, device in enumerate(devices)
                ]

            def over(self, axis, value, step):
                if axis == "ctx":
                    self.over_ctx[c] = value
                    self.send(self.over_ctx, c, [{"ctx": side}, {"ctx": across}, {"ctx": corner}], step)
                else:
                    self.over_dp[z] = value
                    self.send(self.over_dp, z, [{"dp": lax.rem(z + i, n)} for i in range(1, n)], step)

            def total(self, axis):
                for copy in self.sent:
                    copy.wait_recv()
                slots = self.over_ctx if axis == "ctx" else self.over_dp
                return (slots[0] + slots[1]) + (slots[2] + slots[3])

        early_sum = Everywhere(early_ctx, early_dp, 0)
        late_sum = Everywhere(late_ctx, late_dp, 1)

    mlp_sent = []

    def open_transfers():
        wait_for_all()
        for s in range(S):
            mlp_sent.append(start(remote(mlp_far.at[s], mlp_in.at[s], xs.at[s], xr.at[s], {"tp": 1 - t})))
        for copy in next_loads:
            copy.start()
        if gather:
            for copy in loads[6:9]:
                copy.wait()
            fc.send_across()
            send_dp("p")
            red["o"].send_side()

    lane = lanes((1, 2 * DH), 1)
    scaled = half_lanes(SCALE)
    plain = half_lanes(1.0)
    centers = (lanes((1, NB), 1).astype(f32) + 0.5) * (1.0 / NB)
    width = 1.0 / NB
    early[...] = jnp.zeros_like(early)
    half = HW
    core = lax.rem(c, 2)
    y = c // 2
    own_half = pl.ds(pl.multiple_of(core * half, 16), half)
    side_half = pl.ds(pl.multiple_of((1 - core) * half, 16), half)
    give = pl.ds(pl.multiple_of(B * (1 - core * (1 - y)), 128), B)
    own = pl.ds(pl.multiple_of(c * B - key_start, 128), B)
    one, two, three, first = {}, {}, {}, {}

    hb = B // 2

    def second_copy(s, k):
        part = pl.ds(k * hb, hb)
        return remote(hs2.at[s, :, part], hr2.at[s, :, part], h2s.at[s, k], h2r.at[s, k], {"ctx": across})

    def memory_over(s):
        return remote(gmem.at[s, own_half], gfar.at[s, own_half], m2s.at[s], m2r.at[s], {"ctx": across})

    def memory_beside(s):
        return remote(gfar.at[s, own_half], gfar.at[s, own_half], m4s.at[s], m4r.at[s], {"ctx": side})

    def attend_back(s, *between):
        skip = 3 if s > 0 and gather else 0
        for copy in loads[6 * s + skip : 6 * s + skip + 6]:
            copy.wait()

        def pair_step(p, carry):
            cols = pl.ds(pl.multiple_of(p * 2 * DH, 2 * DH), 2 * DH)
            vcols = pl.ds(pl.multiple_of(HW + p * 2 * DH, 2 * DH), 2 * DH)
            qp = q[s, :, cols]
            gp = gmixed[s, :, cols]
            kp = kv[s, :, cols]
            vp = kv[s, :, vcols]
            mk = mem[s, :, cols]
            mv = mem[s, :, vcols]
            q_turned = (qp * SCALE).T
            g_turned = gp.T
            logs = lse[s]
            both = jnp.concatenate([qp * scaled[0], qp * scaled[1]], axis=0)
            both_g = jnp.concatenate([gp * plain[0], gp * plain[1]], axis=0)
            all_scores = dot_nt(both, kp)
            all_grads = dot_nt(both_g, vp)
            all_mem = dot_nt(both, mk)
            all_reach = dot_nt(both_g, mv)
            grad_scores, grad_mems, dk, dv, dmk, dmv = [], [], [], [], [], []
            for h in range(2):
                row = 2 * p + h
                part = slice(h * DH, (h + 1) * DH)
                these = slice(h * B, (h + 1) * B)
                log_total = jnp.sum(jnp.where(lane == row, logs, 0.0), axis=-1, keepdims=True)
                share = jnp.exp(all_scores[these] + bias[s] - log_total)
                grad_share = all_grads[these]
                delta = jnp.sum(share * grad_share, axis=-1, keepdims=True)
                grad_score = (share * (grad_share - delta)).astype(bf16)
                mem_scores = all_mem[these]
                cw_row = cw[pl.ds(row, 1)]
                sw_row = sw[pl.ds(row, 1)]
                reach, mu, inv, diff, spread_logit = reach_terms(mem_scores, cw_row, sw_row, centers, width)
                grad_reach = all_reach[these] * reach
                scaled_diff = diff * inv
                product = grad_reach * scaled_diff
                grad_mu = -jnp.sum(product, axis=-1, keepdims=True)
                grad_var = 0.5 * (
                    jnp.sum(product * scaled_diff, axis=-1, keepdims=True) - inv * jnp.sum(grad_reach, axis=-1, keepdims=True)
                )
                gc = grad_mu * mu * (1.0 - mu)
                gw = SPREAD * grad_var * (1.0 / (1.0 + jnp.exp(-spread_logit)))
                early[pl.ds(8 + row, 1), 0:NB] += jnp.sum(gc * mem_scores, axis=0, keepdims=True)
                early[pl.ds(8 + row, 1), NB : 2 * NB] += jnp.sum(gw * mem_scores, axis=0, keepdims=True)
                grad_mem = (gc * cw_row + gw * sw_row).astype(bf16)
                grad_scores.append(grad_score)
                grad_mems.append(grad_mem)
                dk.append(dot_nn(q_turned[part], grad_score))
                dv.append(dot_nn(g_turned[part], share.astype(bf16)))
                dmk.append(dot_nn(q_turned[part], grad_mem))
                dmv.append(dot_nn(g_turned[part], reach.astype(bf16)))
            grad_q = dot_nn(jnp.concatenate(grad_scores, axis=0), kp) + dot_nn(jnp.concatenate(grad_mems, axis=0), mk)
            gqkv[s, :, cols] = (jnp.where(lane < DH, grad_q[:B], grad_q[B:]) * SCALE).astype(bf16)
            for h in range(2):
                rows = pl.ds(pl.multiple_of((2 * p + h) * DH, DH), DH)
                vrows = pl.ds(pl.multiple_of(HW + (2 * p + h) * DH, DH), DH)
                dkv[rows] = dk[h]
                dkv[vrows] = dv[h]
                dmem[s, rows] = dmk[h]
                dmem[s, vrows] = dmv[h]
            return carry

        done = 0
        for step in between:
            lax.fori_loop(done, done + 1, pair_step, 0)
            done += 1
            step()
        lax.fori_loop(done, HW // (2 * DH), pair_step, 0)
        one[s] = start(remote(dmem.at[s, side_half], m1in.at[s], m1s.at[s], m1r.at[s], {"ctx": side}))
        hs1[s] = dkv[:, give].astype(bf16)
        first[s] = start(remote(hs1.at[s], hr1.at[s], h1s.at[s], h1r.at[s], {"ctx": side}))
        own_rows[s] = dkv[:, own]
        hs2[s] = dkv[:, 0:B].astype(bf16)

    def chip_memory(s):
        one[s].wait_recv()
        gmem[s, own_half] = (dmem[s, own_half] + m1in[s]).astype(bf16)
        three[s] = start(remote(gmem.at[s, own_half], gmem.at[s, own_half], m3s.at[s], m3r.at[s], {"ctx": side}))

        @pl.when(y == 0)
        def _():
            memory_over(s).start()

    def rows_of_memory(s, grad, owner):
        high, low = fit_at(fit, places, s, owner * B + lanes((B, 1), 0), L)
        return dot_nn(grad, high) + dot_nn(grad, low)

    def give_across(s):
        first[s].wait_recv()
        three[s].wait_recv()

        @pl.when(c != 3)
        def _():
            own_rows[s] = own_rows[s] + hr1[s].astype(f32)

        @pl.when(y == 1)
        def _():
            beside = jnp.where(c == 3, 1.0, 0.0)
            total = hs2[s].astype(f32) + beside * hr1[s].astype(f32) + rows_of_memory(s, gmem[s], across)
            hs2[s] = total.astype(bf16)
            for k in range(2):
                second_copy(s, k).start()

    sent = {}

    def pass_memory(s):
        @pl.when(y == 1)
        def _():
            memory_over(s).wait_recv()
            memory_beside(s).start()

    def prepare_rows(s):
        high, low = fit_at(fit, places, s, c * B + lanes((B, 1), 0), L)
        own_rows[s] = own_rows[s] + dot_nn(gmem[s], high) + dot_nn(gmem[s], low)

        @pl.when(y == 1)
        def _():
            memory_beside(s).wait_recv()
            own_rows[s] = own_rows[s] + dot_nn(gfar[s], high) + dot_nn(gfar[s], low)

    def finish_rows(s):
        for k in range(2):
            part = slice(k * hb, (k + 1) * hb)

            @pl.when(y == 0)
            def _(k=k, part=part):
                second_copy(s, k).wait_recv()
                own_rows[s, :, part] = own_rows[s, :, part] + hr2[s, :, part].astype(f32)

            gqkv[s, part, HW:] = own_rows[s, :, part].T.astype(bf16)
            sums_here = [dot_nt(gqkv[s, part, i * HW : (i + 1) * HW], wq[i]) for i in range(3)]
            gnpart[s, part] = (sums_here[0] + sums_here[1] + sums_here[2]).astype(bf16)
            sent[s, k] = start(remote(gnpart.at[s, part], gnin.at[s, part], ns.at[s, k], nr.at[s, k], {"tp": 1 - t}))

    def finish_block(s):
        mlp_sent[s].wait_recv()
        total = kv[s, B : 2 * B].astype(f32) + mlp_in[s].astype(f32)
        block_out[s] = (residual[s] + total + row_of(pbias)).astype(bf16)

    def weight_grad(full, k):
        value = dot_nn(turned[...], gqkv[:, :, k * HW : (k + 1) * HW].reshape(S * B, HW)).astype(bf16)
        for i in range(n):
            full[i] = value[i * R : (i + 1) * R]

    column_sums = []
    gain_row = row_of(gain)

    def norm_back(s):
        sent[s, 0].wait_recv()
        sent[s, 1].wait_recv()
        grad = gnpart[s].astype(f32) + gnin[s].astype(f32)
        _, unit, r = normalise(kv[s, 0:B].astype(f32), gain_row, gain_row)
        column_sums.append((jnp.sum(grad * unit, axis=0, keepdims=True), jnp.sum(grad, axis=0, keepdims=True)))
        a = grad * gain_row
        back = r * (a - jnp.mean(a, axis=-1, keepdims=True) - unit * jnp.mean(a * unit, axis=-1, keepdims=True))
        input_grad[s] = (gres[s] + back).astype(bf16)

    open_transfers()
    attend_back(0)
    if gather:
        red["o"].sum_side()
        red["o"].send_dp()
    attend_back(1, lambda: chip_memory(0), lambda: give_across(0))
    if gather:
        fc.take_across()
        send_dp("f")
    pass_memory(0)
    attend_back(2, lambda: chip_memory(1), lambda: give_across(1))
    for copy in late_loads:
        copy.start()
    for copy in next_loads:
        copy.wait()
    pass_memory(1)
    prepare_rows(0)
    finish_rows(0)
    chip_memory(2)
    give_across(2)
    weight_grad(afull, 0)
    if gather:
        red["a"].send_side()
    pass_memory(2)
    early[0:4, 0:D] = sums[...]
    for k in range(fsum.shape[1] // D):
        early[4 + k : 5 + k] = fsum[:, k * D : (k + 1) * D]
    if gather:
        early_sum.over("dp", early[...], 0)
    for copy in late_loads:
        copy.wait()
    finish_block(0)
    if gather:
        red["a"].sum_side()
        red["a"].send_dp()
    prepare_rows(1)
    finish_rows(1)
    prepare_rows(2)
    finish_block(1)
    finish_block(2)
    if gather:
        take_dp("p")
        red["o"].take_dp()
        take_dp("f")
    finish_rows(2)
    if gather:
        early_sum.over("ctx", early_sum.total("dp"), 1)
    weight_grad(vfull, 2)
    if gather:
        vals.send_side()
    weight_grad(kfull, 1)
    if gather:
        red["k"].send_side()
        vals.sum_side()
        vals.send_across()
        red["k"].sum_side()
        red["k"].send_dp()
    bias_sum = jnp.sum(gqkv[...].reshape(S * B, 3 * HW).astype(f32), axis=0, keepdims=True)
    norm_back(0)
    if gather:
        vals.take_across()
        send_dp("v")
    if gather:
        red["a"].take_dp()
        pass_on("p")
        pass_on("f")
        red["o"].take_across()
    norm_back(1)
    norm_back(2)
    per = D // HW
    room = late_ctx.at[c] if gather else late_out
    room[...] = jnp.zeros(room.shape, f32)
    for which in range(2):
        whole_row = column_sums[0][which] + column_sums[1][which] + column_sums[2][which]
        for k in range(per):
            room[which * per + k : which * per + k + 1] = whole_row[:, k * HW : (k + 1) * HW]
    for k in range(3):
        room[2 * per + k : 2 * per + k + 1] = bias_sum[:, k * HW : (k + 1) * HW]
    if gather:
        late_sum.send(late_ctx, c, [{"ctx": side}, {"ctx": across}, {"ctx": corner}], 0)
        early_out[...] = early_sum.total("ctx")
        red["k"].take_dp()
        late_sum.over("dp", late_sum.total("ctx"), 1)
        red["a"].take_across()
        take_dp("v")
        red["k"].take_across()
        pass_on("v")
        late_out[...] = late_sum.total("dp")
        for g in "pfv":
            take_all(g)
        for chain in red.values():
            chain.take_all()
        for chain in (*red.values(), fc, vals):
            chain.wait_sends()
    else:
        early_out[...] = early[...]
    for s in range(S):

        @pl.when(y == 1)
        def _(s=s):
            second_copy(s, 0).wait_send()
            second_copy(s, 1).wait_send()
            memory_beside(s).wait_send()

        @pl.when(y == 0)
        def _(s=s):
            memory_over(s).wait_send()

    for copy in started:
        copy.wait_send()


def backward(gather, bias, places, q, kv, mem, lse, gmixed, turned, wq, hid, gres, residual, mlp_part, pbias, gain, cw, sw,
             fit, sums, fsum, owned):
    S, B, D = hid.shape
    HW = q.shape[2]
    FW = fsum.shape[1]
    H, NB = cw.shape
    n = lax.axis_size("dp") if gather else 1
    R = D // n
    Q = R // 4
    rows = -(-(8 + H) // 8) * 8
    vm = pl.BlockSpec(memory_space=pltpu.VMEM)
    hb = pl.BlockSpec(memory_space=pl.ANY)
    sem = pltpu.SemaphoreType.DMA
    late = (-(-(2 * (D // HW) + 3) // 8) * 8, HW)
    out = [
        jax.ShapeDtypeStruct((S, B, D), bf16),
        jax.ShapeDtypeStruct((S, B, D), bf16),
        jax.ShapeDtypeStruct((rows, D), f32),
        jax.ShapeDtypeStruct(late, f32),
    ]
    if gather:
        out += [jax.ShapeDtypeStruct((3, R, HW), bf16)] + [jax.ShapeDtypeStruct((R, w), bf16) for w in (HW, FW, FW)]
    else:
        out += [jax.ShapeDtypeStruct((n, R, HW), bf16)] * 3
    scratch = [
        pltpu.VMEM((S, B, HW), bf16),
        pltpu.VMEM((S, NB, 2 * HW), bf16),
        pltpu.VMEM((S, B, 128), f32),
        pltpu.VMEM((S, B, HW), bf16),
        pltpu.VMEM((S, 3 * B, 2 * HW), bf16),
        pltpu.VMEM((3, D, HW), bf16),
        pltpu.VMEM((S, B, D), f32),
        pltpu.VMEM((S, B, D), f32),
        pltpu.VMEM((2 * HW, 3 * B), f32),
        pltpu.VMEM((S, 2 * HW, B), f32),
        pltpu.VMEM((S, 2 * HW, NB), f32),
        pltpu.VMEM((S, B, 3 * HW), bf16),
        *[pltpu.VMEM((S, 2 * HW, B), bf16)] * 4,
        pltpu.VMEM((S, HW, NB), f32),
        pltpu.VMEM((S, 2 * HW, NB), bf16),
        pltpu.VMEM((S, 2 * HW, NB), bf16),
        pltpu.VMEM((D, S * B), bf16),
        *[pltpu.VMEM((S, B, D), bf16)] * 3,
        pltpu.VMEM((S, B, 3 * B), f32),
        pltpu.VMEM((rows, D), f32),
        sem((6 * S + 9,)),
        *[sem((S,))] * 4,
        *[sem((S, 2))] * 2,
        *[sem((S,))] * 8,
        *[sem((S, 2))] * 2,
    ]
    if gather:
        scratch += [
            pltpu.VMEM((n, Q, FW), bf16),
            pltpu.VMEM((n, 2 * Q, FW), bf16),
            *[pltpu.VMEM((n, R, HW), bf16)] * 4,
            *[pltpu.VMEM((n, 2 * Q, HW), bf16)] * 8,
            *[pltpu.VMEM((2 * Q, HW), bf16)] * 2,
            pltpu.VMEM((n, Q, HW), bf16),
            pltpu.VMEM((2 * Q, HW), bf16),
            pltpu.VMEM((n, Q, FW), bf16),
            *[pltpu.VMEM((2 * Q, HW), bf16)] * 2,
            pltpu.VMEM((n, Q, HW), bf16),
            pltpu.VMEM((2 * Q, HW), bf16),
            pltpu.VMEM((n, Q, FW), bf16),
            *[pltpu.VMEM((n - 1, 2 * Q, HW), bf16)] * 2,
            pltpu.VMEM((n - 1, Q, HW), bf16),
            pltpu.VMEM((n - 1, 2 * Q, HW), bf16),
            *[pltpu.VMEM((n - 1, Q, FW), bf16)] * 2,
            *[pltpu.VMEM((4, rows, D), f32)] * 2,
            *[pltpu.VMEM((4, *late), f32)] * 2,
            *[sem((6, 2))] * 2,
            *[sem((6, n - 1))] * 2,
            *[sem((6, 3))] * 2,
            *[sem((4, 3))] * 2,
        ]
    args = [bias, places, q, kv, mem, lse, gmixed, turned, wq, hid, gres, residual, mlp_part, pbias, gain, cw, sw, fit, sums,
            fsum, *owned]
    far = (0, 2, 3, 4, 5, 6, 20, 21, 22, 7, 8, 9, 10, 11, 12)
    return pl.pallas_call(
        lambda *refs: backward_kernel(gather, refs),
        out_shape=out,
        in_specs=[hb if i in far else vm for i in range(len(args))],
        out_specs=[vm] * len(out),
        scratch_shapes=scratch,
        compiler_params=pltpu.CompilerParams(
            collective_id=2, has_side_effects=True, vmem_limit_bytes=VMEM_LIMIT
        ),
        cost_estimate=pl.CostEstimate(flops=12_000_000_000, bytes_accessed=40_000_000, transcendentals=6_000_000),
        name="backward_part",
    )(*args)


def finish_kernel(fqkv, fo, ff, fp, early, late, block_in, grad_in, qkv, out, fc, proj, block, grad, qb, cgrad, sgrad, *vectors):
    HW = fqkv.shape[2]
    D = vectors[0].shape[0]
    H, NB = cgrad.shape
    per = D // HW
    for k in range(3):
        qb[k : k + 1] = late[2 * per + k : 2 * per + k + 1]
    qkv[...] = fqkv[...].astype(f32)
    out[...] = fo[...].astype(f32)
    fc[...] = ff[...].astype(f32)
    proj[...] = fp[...].astype(f32)
    block[...] = block_in[...]
    grad[...] = grad_in[...]
    cgrad[...] = early[8 : 8 + H, 0:NB]
    sgrad[...] = early[8 : 8 + H, NB : 2 * NB]
    for which in range(2):
        for k in range(per):
            vectors[which][k * HW : (k + 1) * HW] = late[which * per + k : which * per + k + 1].reshape(HW)
    for k in range(4):
        vectors[2 + k][...] = early[k : k + 1, 0:D].reshape(D)
    for k in range(vectors[6].shape[0] // D):
        vectors[6][k * D : (k + 1) * D] = early[4 + k : 5 + k].reshape(D)


def finish(parts, early, late, block_out, input_grad, D, H, NB):
    _, R, HW = parts[0].shape
    FW = parts[2].shape[1]
    vm = pl.BlockSpec(memory_space=pltpu.VMEM)
    shapes = [(3, R, HW), (R, HW), (R, FW), (R, FW)]
    more = [(3, HW), (H, NB), (H, NB)] + [(D,)] * 6 + [(FW,)]
    copied = [jax.ShapeDtypeStruct(v.shape, v.dtype) for v in (block_out, input_grad)]
    return pl.pallas_call(
        finish_kernel,
        out_shape=[jax.ShapeDtypeStruct(v, f32) for v in shapes] + copied + [jax.ShapeDtypeStruct(v, f32) for v in more],
        in_specs=[vm] * 8,
        out_specs=[vm] * (len(shapes) + 2 + len(more)),
        compiler_params=pltpu.CompilerParams(vmem_limit_bytes=VMEM_LIMIT),
        name="finish_part",
    )(*parts, early, late, block_out, input_grad)


def per_device(hidden_in, doc_lengths, sticky_places, attn_gain, attn_shift, qkv_weight, qkv_bias, center_weight,
               spread_weight, out_weight, out_bias, mlp_gain, mlp_shift, fc_weight, fc_bias, proj_weight, proj_bias,
               cotangent):
    S, B, D = hidden_in.shape
    n = lax.axis_size("dp")
    HW = qkv_bias.shape[1]
    H, NB = center_weight.shape
    M = sticky_places.shape[1]
    fit = jnp.asarray(ridge_fit(NB, 2 * M))
    gather = n == 4 and D % (64 * n) == 0
    weights = [jnp.transpose(qkv_weight, (1, 0, 2)), out_weight.T, fc_weight, proj_weight.T]
    if not gather:
        full = [lax.all_gather(w, "dp", axis=w.ndim - 2, tiled=True) for w in weights]
        weights = full[:1]
    made = forward(gather, hidden_in, doc_lengths, sticky_places, attn_gain, attn_shift, weights,
                   qkv_bias, center_weight, spread_weight, fit, cotangent)
    turned, cot_turned, bias, q, kv, mem, lse, mixed = made[:8]
    if gather:
        wq, wo, wf, wp = made[8:]
    else:
        wq, wo, wf, wp = full
        wo = lax.all_gather(wo, "tp", axis=0)
    made = mlp(gather, hidden_in, mixed, wo, wf, wp, out_bias, mlp_gain, mlp_shift, fc_bias, cotangent, cot_turned)
    residual, mlp_part, gres, gmixed, og, pg, fg, sums, fsum = made
    owned = [pg, fg, og] if gather else []
    made = backward(gather, bias, sticky_places, q, kv, mem, lse, gmixed, turned, wq, hidden_in, gres, residual, mlp_part,
                    proj_bias, attn_gain, center_weight, spread_weight, fit, sums, fsum, owned)
    block_out, input_grad, early, late = made[:4]
    if gather:
        made = finish(made[4:], early, late, block_out, input_grad, D, H, NB)
        qkv_grad, out_grad, fc_grad, proj_grad, block_out, input_grad, qkv_bias_grad, center_grad, spread_grad = made[:9]
        gain_grad, shift_grad, out_bias_grad, mlp_gain_grad, mlp_shift_grad, proj_bias_grad, fc_bias_grad = made[9:]
        qkv_grad, out_grad, proj_grad = jnp.transpose(qkv_grad, (1, 0, 2)), out_grad.T, proj_grad.T
    else:
        early, late = lax.psum((early, late), ("dp", "ctx"))

        def reduced(grad):
            part = lax.psum_scatter(grad.reshape(D, -1), "dp", scatter_dimension=0, tiled=True)
            return lax.psum(part, "ctx").astype(f32)

        qkv_grad = jnp.stack([reduced(g) for g in made[4:]], axis=1)
        out_grad, fc_grad, proj_grad = reduced(og).T, reduced(fg), reduced(pg).T
        per = D // HW
        qkv_bias_grad = late[2 * per : 2 * per + 3]
        center_grad, spread_grad = early[8 : 8 + H, :NB], early[8 : 8 + H, NB : 2 * NB]
        gain_grad, shift_grad = late[:per].reshape(-1), late[per : 2 * per].reshape(-1)
        out_bias_grad, mlp_gain_grad, mlp_shift_grad, proj_bias_grad = [early[k, :D] for k in range(4)]
        fc_bias_grad = early[4 : 4 + fc_bias.shape[0] // D].reshape(-1)
    return (
        block_out,
        input_grad,
        gain_grad,
        shift_grad,
        qkv_grad,
        qkv_bias_grad,
        center_grad,
        spread_grad,
        out_grad,
        out_bias_grad,
        mlp_gain_grad,
        mlp_shift_grad,
        fc_grad,
        fc_bias_grad,
        proj_grad,
        proj_bias_grad,
    )


def solution(mesh):
    in_specs = (
        P("dp", "ctx", None),
        P("dp", None),
        P("dp", None),
        P(),
        P(),
        P("dp", None, "tp"),
        P(None, "tp"),
        P("tp", None),
        P("tp", None),
        P("tp", "dp"),
        P(),
        P(),
        P(),
        P("dp", "tp"),
        P("tp"),
        P("tp", "dp"),
        P(),
        P("dp", "ctx", None),
    )
    out_specs = (
        P("dp", "ctx", None),
        P("dp", "ctx", None),
        P(),
        P(),
        P("dp", None, "tp"),
        P(None, "tp"),
        P("tp", None),
        P("tp", None),
        P("tp", "dp"),
        P(),
        P(),
        P(),
        P("dp", "tp"),
        P("tp"),
        P("tp", "dp"),
        P(),
    )
    return jax.shard_map(
        per_device, mesh=mesh, in_specs=in_specs, out_specs=out_specs, check_vma=False
    )
```
